32 devices in a mesh: grp: 4 (over y, x), dev: 8 (over z, core).
Axes of the slice: x: 2, y: 2, z: 4, core: 2. Of those that a mesh axis runs over, the one named last changes fastest.
Arguments:
- embedded: bfloat16 [32, 320, 768], P(('grp', 'dev')), may hold values from -6 to 6
- mask_order: int32 [32, 256], P(('grp', 'dev')), may hold values from 0 to 255, each once within a row
- counts: int32 [32], P(('grp', 'dev')), may hold values from 180 to 256, as said below
- targets: float32 [32, 256, 16], P(('grp', 'dev')), may hold values from -6 to 6
- noise_copies: bfloat16 [32, 256, 4, 16], P(('grp', 'dev')), may hold values from -6 to 6
- timesteps: int32 [32, 256, 4], P(('grp', 'dev')), may hold values from 0 to 999
- enc_gain_one: bfloat16 [768], P('dev'), may hold values from 0.5 to 1.5
- enc_qkv: bfloat16 [768, 2304], P('dev'), may hold values from -0.21875 to 0.21875
- enc_proj: bfloat16 [768, 768], P('dev'), may hold values from -0.875 to 0.875
- enc_gain_two: bfloat16 [768], P('dev'), may hold values from 0.5 to 1.5
- enc_up: bfloat16 [768, 3072], P('dev'), may hold values from -0.21875 to 0.21875
- enc_down: bfloat16 [3072, 768], P('dev'), may hold values from -0.109375 to 0.109375
- dec_gain_one: bfloat16 [768], P('dev'), may hold values from 0.5 to 1.5
- dec_qkv: bfloat16 [768, 2304], P('dev'), may hold values from -0.21875 to 0.21875
- dec_proj: bfloat16 [768, 768], P('dev'), may hold values from -0.875 to 0.875
- dec_gain_two: bfloat16 [768], P('dev'), may hold values from 0.5 to 1.5
- dec_up: bfloat16 [768, 3072], P('dev'), may hold values from -0.21875 to 0.21875
- dec_down: bfloat16 [3072, 768], P('dev'), may hold values from -0.109375 to 0.109375
- mask_token: bfloat16 [768], P('dev'), may hold values from -6 to 6
- head_in: bfloat16 [16, 1024], P(None, 'dev'), may hold values from -1.5 to 1.5
- head_cond: bfloat16 [768, 1024], P('dev'), may hold values from -0.21875 to 0.21875
- head_ada: bfloat16 [1024, 3072], P('dev'), may hold values from -0.1875 to 0.1875
- head_inner: bfloat16 [1024, 1024], P('dev'), may hold values from -0.1875 to 0.1875
- head_outer: bfloat16 [1024, 1024], P('dev'), may hold values from -0.1875 to 0.1875
- head_out: bfloat16 [1024, 16], P('dev'), may hold values from -0.1875 to 0.1875
Outputs:
- image_loss: float32 [32], P(('grp', 'dev'))
- activations: bfloat16 [32, 320, 768], P(('grp', 'dev'))
- embed_grad: float32 [32, 320, 768], P(('grp', 'dev'))
- enc_gain_one_grad: float32 [768], P('dev')
- enc_qkv_grad: float32 [768, 2304], P('dev')
- enc_proj_grad: float32 [768, 768], P('dev')
- enc_gain_two_grad: float32 [768], P('dev')
- enc_up_grad: float32 [768, 3072], P('dev')
- enc_down_grad: float32 [3072, 768], P('dev')
- dec_gain_one_grad: float32 [768], P('dev')
- dec_qkv_grad: float32 [768, 2304], P('dev')
- dec_proj_grad: float32 [768, 768], P('dev')
- dec_gain_two_grad: float32 [768], P('dev')
- dec_up_grad: float32 [768, 3072], P('dev')
- dec_down_grad: float32 [3072, 768], P('dev')
- mask_token_grad: float32 [768], P('dev')
- head_in_grad: float32 [16, 1024], P(None, 'dev')
- head_cond_grad: float32 [768, 1024], P('dev')
- head_ada_grad: float32 [1024, 3072], P('dev')
- head_inner_grad: float32 [1024, 1024], P('dev')
- head_outer_grad: float32 [1024, 1024], P('dev')
- head_out_grad: float32 [1024, 16], P('dev')
The draws below stay inside these ranges and needn't reach their ends.
Inputs may be any that keep to these rules, and one draw needn't show every extreme that they name: `mask_order`: each row is a permutation of the token positions; the first counts entries of a row are that image's masked tokens. The masked counts of each aligned group of 8 images (the images of one index of grp) sum to exactly 1664; in every group one image has all 256 tokens masked and one has exactly 180.
All inputs are finite; a program needn't handle non-finite values.
Results may differ from the reference program's by a relative error of at most 0.02.
Values may be sent and summed in bfloat16 or wider, within the bound.
A program may use at most 320 MiB of HBM per device.

```python
import math
import jax
import jax.numpy as jnp
from jax import lax

D = 768
HEADS = 12
HD = 64
FF = 3072
HW = 1024
CH = 16
BUF = 64
SEQ = 256
COPIES = 4
STEPS_T = 1000
GROUP_IMG = 8
IMAGES = 32
TOKENS = 320
MASK_MIN = 180
MASK_MEAN = 208
ENC = 140


def group_perm(key_one):
    return jax.random.permutation(key_one, GROUP_IMG).astype(jnp.int32)


def place_counts(base_row, perm_row, extra_row):
    return base_row.at[perm_row].set(MASK_MIN + extra_row)


def draw_counts(key, part):
    key = jax.random.fold_in(key, 7)
    groups = IMAGES // GROUP_IMG
    spare_rows = MASK_MEAN - MASK_MIN
    lift_rows = SEQ - MASK_MIN - 2 * spare_rows
    key_perm, key_move = jax.random.split(key)
    group_perms = jax.vmap(group_perm)(jax.random.split(key_perm, groups))
    move_rows = jax.random.randint(key_move, (groups, GROUP_IMG // 2), -spare_rows, spare_rows + 1).astype(jnp.int32)
    move_rows = move_rows.at[:, 0].set(spare_rows).at[:, 1].set(spare_rows)
    extra_rows = jnp.stack([spare_rows + move_rows, spare_rows - move_rows], axis=-1).reshape(groups, GROUP_IMG)
    extra_rows = extra_rows.at[:, 0].add(lift_rows).at[:, 2].add(-lift_rows)
    base_rows = jnp.zeros((groups, GROUP_IMG), jnp.int32)
    result = jax.vmap(place_counts)(base_rows, group_perms, extra_rows.astype(jnp.int32))
    return result.reshape(IMAGES).astype(jnp.int32)


def plant(drawn, rng, smallest, largest):
    place = [jax.random.randint(jax.random.fold_in(rng, axis), (), 0, length) for axis, length in enumerate(drawn.shape)]
    longest = drawn.shape.index(max(drawn.shape))
    beside = place[:longest] + [(place[longest] + 1) % drawn.shape[longest]] + place[longest + 1:]
    return drawn.at[tuple(place)].set(smallest).at[tuple(beside)].set(largest)


def steps_of(key, shape, pieces, low, high):
    loudness, own = 1.0, jax.random.fold_in(key, 6)
    for axis_at, parts in pieces:
        draws = jnp.exp(jax.random.uniform(jax.random.fold_in(own, axis_at), (parts,), jnp.float32, low / len(pieces), high / len(pieces)))
        loudness = loudness * jnp.repeat(draws, shape[axis_at] // parts).reshape([-1 if axis == axis_at else 1 for axis in range(len(shape))])
    return loudness


def centred(key, extent, spread, bound, pieces=(), kind=jnp.bfloat16):
    level = steps_of(key, extent, pieces, -0.22, 0.18) if pieces else 1.0
    values = jax.random.normal(key, extent, jnp.float32) * spread * level
    return jnp.minimum(jnp.maximum(values, -bound), bound).astype(kind)


def setup_inputs(seed: int = 0) -> dict:
    streams_of = jax.random.split(jax.random.key(seed), 26)
    embedded = centred(streams_of[0], (IMAGES, TOKENS, D), 1.0, 6.0, ((0, 32),))
    mask_order = jax.vmap(lambda own: jax.random.permutation(own, SEQ))(jax.random.split(streams_of[1], IMAGES)).reshape((IMAGES, SEQ)).astype(jnp.int32)
    counts = draw_counts(jax.random.fold_in(streams_of[25], 71), 0)
    targets = centred(streams_of[3], (IMAGES, SEQ, CH), 1.0, 6.0, ((0, 32),), jnp.float32)
    noise_copies = centred(streams_of[4], (IMAGES, SEQ, COPIES, CH), 1.0, 6.0, ((0, 32),))
    timesteps = plant(jax.random.randint(streams_of[5], (IMAGES, SEQ, COPIES), 0, STEPS_T), jax.random.fold_in(streams_of[5], 1), 0, STEPS_T - 1).astype(jnp.int32)
    enc_gain_one = jnp.clip(1.0 + 0.1 * jax.random.normal(streams_of[6], (D,), jnp.float32), 0.5, 1.5).astype(jnp.bfloat16)
    enc_qkv = centred(streams_of[7], (D, 3 * D), D ** -0.5, 0.21875, ((0, 8),))
    enc_proj = centred(streams_of[8], (D, D), (D // 16) ** -0.5, 0.875, ((0, 8),))
    enc_gain_two = jnp.clip(1.0 + 0.1 * jax.random.normal(streams_of[9], (D,), jnp.float32), 0.5, 1.5).astype(jnp.bfloat16)
    enc_up = centred(streams_of[10], (D, FF), D ** -0.5, 0.21875, ((0, 8),))
    enc_down = centred(streams_of[11], (FF, D), FF ** -0.5, 0.109375, ((0, 8),))
    dec_gain_one = jnp.clip(1.0 + 0.1 * jax.random.normal(streams_of[12], (D,), jnp.float32), 0.5, 1.5).astype(jnp.bfloat16)
    dec_qkv = centred(streams_of[13], (D, 3 * D), D ** -0.5, 0.21875, ((0, 8),))
    dec_proj = centred(streams_of[14], (D, D), (D // 16) ** -0.5, 0.875, ((0, 8),))
    dec_gain_two = jnp.clip(1.0 + 0.1 * jax.random.normal(streams_of[15], (D,), jnp.float32), 0.5, 1.5).astype(jnp.bfloat16)
    dec_up = centred(streams_of[16], (D, FF), D ** -0.5, 0.21875, ((0, 8),))
    dec_down = centred(streams_of[17], (FF, D), FF ** -0.5, 0.109375, ((0, 8),))
    mask_token = centred(streams_of[18], (D,), 1.0, 6.0, ((0, 8),))
    head_in = centred(streams_of[19], (CH, HW), CH ** -0.5, 1.5, ((1, 8),))
    head_cond = centred(streams_of[20], (D, HW), D ** -0.5, 0.21875, ((0, 8),))
    head_ada = centred(streams_of[21], (HW, 3 * HW), HW ** -0.5, 0.1875, ((0, 8),))
    head_inner = centred(streams_of[22], (HW, HW), HW ** -0.5, 0.1875, ((0, 8),))
    head_outer = centred(streams_of[23], (HW, HW), HW ** -0.5, 0.1875, ((0, 8),))
    head_out = centred(streams_of[24], (HW, CH), HW ** -0.5, 0.1875, ((0, 8),))
    return {"embedded": embedded, "mask_order": mask_order, "counts": counts, "targets": targets, "noise_copies": noise_copies, "timesteps": timesteps, "enc_gain_one": enc_gain_one, "enc_qkv": enc_qkv, "enc_proj": enc_proj, "enc_gain_two": enc_gain_two, "enc_up": enc_up, "enc_down": enc_down, "dec_gain_one": dec_gain_one, "dec_qkv": dec_qkv, "dec_proj": dec_proj, "dec_gain_two": dec_gain_two, "dec_up": dec_up, "dec_down": dec_down, "mask_token": mask_token, "head_in": head_in, "head_cond": head_cond, "head_ada": head_ada, "head_inner": head_inner, "head_outer": head_outer, "head_out": head_out}


EPSILON = 1e-06
NEG_FILL = -1e+30

@jax.custom_vjp
def low(v):
    return lax.optimization_barrier(v.astype(jnp.bfloat16)).astype(jnp.float32)

@jax.custom_vjp
def low_back(v):
    return v

def low_keep(v):
    return (low(v), None)

def low_pass(kept, grad):
    return (grad,)

def back_keep(v):
    return (v, None)

def back_low(kept, grad):
    return (low(grad),)
low.defvjp(low_keep, low_pass)
low_back.defvjp(back_keep, back_low)

def matmul(left, right):
    return jnp.dot(left, right, precision=lax.Precision.HIGHEST)

def norm_rows(values):
    centre = values - lax.optimization_barrier(jnp.mean(values, axis=-1, keepdims=True))
    return centre * lax.rsqrt(lax.optimization_barrier(jnp.mean(centre * centre, axis=-1, keepdims=True)) + EPSILON)

def vit_block(stream, key_valid, weights):
    gain_one, w_qkv, w_proj, gain_two, w_up, w_down = weights
    row_count = stream.shape[0]
    normed_one = low(norm_rows(stream) * gain_one)
    qkv_proj = low(low_back(matmul(normed_one, w_qkv))).reshape(row_count, 3, HEADS, HD)
    raw_scores = low_back(jnp.einsum('qhd,khd->hqk', qkv_proj[:, 0], qkv_proj[:, 1], precision=lax.Precision.HIGHEST))
    scores = jnp.where(key_valid[None, None, :], raw_scores * HD ** (-0.5), NEG_FILL)
    top_score = lax.optimization_barrier(jnp.max(scores, axis=-1, keepdims=True))
    exp_scores = jnp.exp(scores - top_score)
    attn_probs = low(exp_scores / lax.optimization_barrier(jnp.sum(exp_scores, axis=-1, keepdims=True)))
    mixed = jnp.einsum('hqk,khd->qhd', attn_probs, qkv_proj[:, 2], precision=lax.Precision.HIGHEST)
    mixed = low(low_back(mixed)).reshape(row_count, D)
    middle = stream + low_back(matmul(mixed, w_proj))
    normed_two = low(norm_rows(middle) * gain_two)
    up_proj = low_back(matmul(normed_two, w_up))
    return middle + low_back(matmul(low(jax.nn.gelu(up_proj, approximate=False)), w_down))

def time_embed(steps):
    half_width = HW // 2
    freqs = jnp.exp(-math.log(10000.0) * jnp.arange(half_width, dtype=jnp.float32) / half_width)
    phase = steps.astype(jnp.float32)[..., None] * freqs
    return jnp.concatenate([jnp.cos(phase), jnp.sin(phase)], axis=-1)

def noise_angle(steps):
    return (steps.astype(jnp.float32) / STEPS_T + 0.008) / 1.008 * (math.pi / 2)

def diffusion_head(cond_rows, noisy, noise_vals, steps, weights):
    w_in, w_cond, w_ada, w_inner, w_outer, w_out = weights
    row_count = cond_rows.shape[0]
    flat_count = row_count * COPIES
    cond = low_back(matmul(cond_rows, w_cond))
    cond_full = (cond[:, None, :] + time_embed(steps)).reshape(flat_count, HW)
    modulate = low_back(matmul(low(jax.nn.silu(cond_full)), w_ada))
    shift_part = modulate[:, :HW]
    scale_part = modulate[:, HW:2 * HW]
    gate_part = modulate[:, 2 * HW:]
    hidden = low_back(matmul(noisy.reshape(flat_count, CH), w_in))
    inner = low_back(matmul(low(norm_rows(hidden) * (1.0 + scale_part) + shift_part), w_inner))
    hidden = hidden + gate_part * low_back(matmul(low(jax.nn.silu(inner)), w_outer))
    predicted = low_back(matmul(low(norm_rows(hidden)), w_out))
    error = predicted - noise_vals.reshape(flat_count, CH)
    return lax.optimization_barrier(jnp.sum((error * error).reshape(row_count, COPIES * CH), axis=1))

def image_pass(weight_set, embed_row, order_row, count, target, noise_row, steps):
    enc_weights, dec_weights, token_fill, head_weights = weight_set
    spots = jnp.arange(ENC - BUF, dtype=jnp.int32)
    vis_pos = BUF + order_row[jnp.minimum(count + spots, SEQ - 1)]
    enc_rows = jnp.concatenate([jnp.arange(BUF, dtype=jnp.int32), vis_pos])
    enc_valid = jnp.concatenate([jnp.ones((BUF,), bool), spots < SEQ - count])
    enc_out = vit_block(embed_row[enc_rows], enc_valid, enc_weights)
    rank = jnp.zeros((SEQ,), jnp.int32).at[order_row].set(jnp.arange(SEQ, dtype=jnp.int32))
    visible = rank >= count
    source = BUF + jnp.clip(rank - count, 0, ENC - BUF - 1)
    tok_rows = jnp.where(visible[:, None], enc_out[source], token_fill[None, :])
    dec_in = jnp.concatenate([enc_out[:BUF], tok_rows], axis=0)
    dec_out = low(low_back(vit_block(dec_in, jnp.ones((BUF + SEQ,), bool), dec_weights)))
    step_sel = steps[order_row]
    noise_sel = noise_row[order_row]
    angle = noise_angle(step_sel)
    noisy = low(jnp.cos(angle)[..., None] * target[order_row][:, None, :] + jnp.sin(angle)[..., None] * noise_sel)
    row_err = diffusion_head(dec_out[BUF + order_row], noisy, noise_sel, step_sel, head_weights)
    live = jnp.arange(SEQ, dtype=jnp.int32) < count
    objective = jnp.sum(jnp.where(live, row_err, 0.0)) / COPIES
    loss = jnp.sum(jnp.where(live, low(row_err), 0.0)) / (count.astype(jnp.float32) * (COPIES * CH))
    return (objective, (dec_out, loss))

def reference(embedded, mask_order, counts, targets, noise_copies, timesteps, enc_gain_one, enc_qkv, enc_proj, enc_gain_two, enc_up, enc_down, dec_gain_one, dec_qkv, dec_proj, dec_gain_two, dec_up, dec_down, mask_token, head_in, head_cond, head_ada, head_inner, head_outer, head_out):

    def to_float(values):
        return tuple((v.astype(jnp.float32) for v in values))
    weight_set = (to_float((enc_gain_one, enc_qkv, enc_proj, enc_gain_two, enc_up, enc_down)), to_float((dec_gain_one, dec_qkv, dec_proj, dec_gain_two, dec_up, dec_down)), mask_token.astype(jnp.float32), to_float((head_in, head_cond, head_ada, head_inner, head_outer, head_out)))
    noise_all = noise_copies.astype(jnp.float32)
    checked = jax.checkpoint(image_pass)

    def forward(embed_all, weights_now):

        def step(total, item):
            embed_row, order_row, count, target, noise_row, steps = item
            objective, extra = checked(weights_now, embed_row, order_row, count, target, noise_row, steps)
            return (total + objective, extra)
        total, extra = lax.scan(step, jnp.zeros((), jnp.float32), (embed_all, mask_order, counts, targets, noise_all, timesteps))
        return (total, extra)
    _, pull_back, (acts, losses) = jax.vjp(forward, embedded.astype(jnp.float32), weight_set, has_aux=True)
    embed_grad, weight_grads = pull_back(jnp.ones((), jnp.float32))
    enc_grads, dec_grads, fill_grad, head_grads = weight_grads
    return (losses, acts.astype(jnp.bfloat16), embed_grad, enc_grads[0], enc_grads[1], enc_grads[2], enc_grads[3], enc_grads[4], enc_grads[5], dec_grads[0], dec_grads[1], dec_grads[2], dec_grads[3], dec_grads[4], dec_grads[5], fill_grad, head_grads[0], head_grads[1], head_grads[2], head_grads[3], head_grads[4], head_grads[5])
```

```python
import functools
import math

import jax
import jax.numpy as jnp
from jax import lax
from jax.experimental import pallas as pl
from jax.experimental.pallas import tpu as pltpu
from jax.sharding import PartitionSpec as P

MESH = pl.DeviceIdType.MESH
SUM_VMEM = 60 * 1024 * 1024
HEADS = 12
HW = 1024
CH = 16
COPIES = 4
STEPS_T = 1000
ENC = 140

EPSILON = 1e-06
NEG_FILL = -1e30


def matmul(left, right):
    return jnp.dot(left, right, preferred_element_type=jnp.float32)


def left_trans(left, right):
    return lax.dot_general(
        left, right, (((0,), (0,)), ((), ())), preferred_element_type=jnp.float32
    )


def right_trans(left, right):
    return lax.dot_general(
        left, right, (((1,), (1,)), ((), ())), preferred_element_type=jnp.float32
    )


def norm_rows(values):
    centre = values - jnp.mean(values, axis=-1, keepdims=True)
    inv_std = lax.rsqrt(jnp.mean(centre * centre, axis=-1, keepdims=True) + EPSILON)
    return (centre * inv_std, inv_std)


def norm_back(grad, normed, inv_std):
    mean_grad = jnp.mean(grad, axis=-1, keepdims=True)
    mean_cross = jnp.mean(grad * normed, axis=-1, keepdims=True)
    return inv_std * (grad - mean_grad - normed * mean_cross)


def silu_slope(values):
    sigma = jax.nn.sigmoid(values)
    return sigma * (1.0 + values * (1.0 - sigma))


def gelu_slope(values):
    cumul = 0.5 * (1.0 + lax.erf(values * (1.0 / math.sqrt(2.0))))
    density = jnp.exp(-0.5 * values * values) * (1.0 / math.sqrt(2.0 * math.pi))
    return cumul + values * density


def time_embed(steps):
    half_width = HW // 2
    freqs = jnp.exp(-math.log(10000.0) * jnp.arange(half_width, dtype=jnp.float32) / half_width)
    phase = steps.astype(jnp.float32)[..., None] * freqs
    return jnp.concatenate([jnp.cos(phase), jnp.sin(phase)], axis=-1)


def noise_angle(steps):
    return (steps.astype(jnp.float32) / STEPS_T + 0.008) / 1.008 * (math.pi / 2)


def pick_rows(table, index):
    return table[index]


def place_rows(base, index, values):
    return base.at[index].set(values, mode="drop")


def inverse_order(order_row):
    return (
        jnp.zeros(order_row.shape, jnp.int32)
        .at[order_row]
        .set(jnp.arange(order_row.shape[0], dtype=jnp.int32))
    )


def attention_scores(qkv_proj, key_valid, head_size):
    raw_scores = jnp.einsum(
        "iqhd,ikhd->ihqk", qkv_proj[:, :, 0], qkv_proj[:, :, 1], preferred_element_type=jnp.float32
    )
    return jnp.where(key_valid[:, None, None, :], raw_scores * head_size ** (-0.5), NEG_FILL)


def block_forward(stream, key_valid, weights):
    gain_one, w_qkv, w_proj, gain_two, w_up, w_down = weights
    images, row_count, width = stream.shape
    head_size = width // HEADS
    flat = stream.reshape(images * row_count, width)
    normed_one, inv_one = norm_rows(flat)
    ln_one = (normed_one * gain_one.astype(jnp.float32)).astype(jnp.bfloat16)
    qkv_proj = (
        matmul(ln_one, w_qkv).astype(jnp.bfloat16).reshape(images, row_count, 3, HEADS, head_size)
    )
    scores = attention_scores(qkv_proj, key_valid, head_size)
    top_score = jnp.max(scores, axis=-1, keepdims=True)
    exp_scores = jnp.exp(scores - top_score)
    exp_total = jnp.sum(exp_scores, axis=-1, keepdims=True)
    log_total = top_score + jnp.log(exp_total)
    attn_probs = (exp_scores / exp_total).astype(jnp.bfloat16)
    mixed = jnp.einsum(
        "ihqk,ikhd->iqhd", attn_probs, qkv_proj[:, :, 2], preferred_element_type=jnp.float32
    )
    mixed = mixed.astype(jnp.bfloat16).reshape(images * row_count, width)
    middle = flat + matmul(mixed, w_proj)
    normed_two, inv_two = norm_rows(middle)
    ln_two = (normed_two * gain_two.astype(jnp.float32)).astype(jnp.bfloat16)
    up_proj = matmul(ln_two, w_up)
    up_act = jax.nn.gelu(up_proj, approximate=False).astype(jnp.bfloat16)
    result = middle + matmul(up_act, w_down)
    kept = (
        normed_one,
        inv_one,
        ln_one,
        qkv_proj,
        log_total,
        mixed,
        normed_two,
        inv_two,
        ln_two,
        up_proj,
        up_act,
    )
    return (result.reshape(images, row_count, width), kept)


def block_backward(grad_out, key_valid, weights, kept):
    gain_one, w_qkv, w_proj, gain_two, w_up, w_down = weights
    (
        normed_one,
        inv_one,
        ln_one,
        qkv_proj,
        log_total,
        mixed,
        normed_two,
        inv_two,
        ln_two,
        up_proj,
        up_act,
    ) = kept
    images, row_count, width = grad_out.shape
    head_size = width // HEADS
    grad_flat = grad_out.reshape(images * row_count, width)
    grad_low = grad_flat.astype(jnp.bfloat16)
    grad_w_down = left_trans(up_act, grad_low)
    grad_act = right_trans(grad_low, w_down)
    grad_up = (grad_act * gelu_slope(up_proj)).astype(jnp.bfloat16)
    grad_w_up = left_trans(ln_two, grad_up)
    grad_ln_two = right_trans(grad_up, w_up)
    grad_gain_two = jnp.sum(grad_ln_two * normed_two, axis=0)
    grad_mid = grad_flat + norm_back(
        grad_ln_two * gain_two.astype(jnp.float32), normed_two, inv_two
    )
    grad_mid_low = grad_mid.astype(jnp.bfloat16)
    grad_w_proj = left_trans(mixed, grad_mid_low)
    grad_mixed = (
        right_trans(grad_mid_low, w_proj)
        .astype(jnp.bfloat16)
        .reshape(images, row_count, HEADS, head_size)
    )
    scores = attention_scores(qkv_proj, key_valid, head_size)
    attn_probs = jnp.exp(scores - log_total)
    grad_probs = jnp.einsum(
        "iqhd,ikhd->ihqk", grad_mixed, qkv_proj[:, :, 2], preferred_element_type=jnp.float32
    )
    row_dot = jnp.sum(grad_probs * attn_probs, axis=-1, keepdims=True)
    grad_scores = (attn_probs * (grad_probs - row_dot) * head_size ** (-0.5)).astype(jnp.bfloat16)
    grad_query = jnp.einsum(
        "ihqk,ikhd->iqhd", grad_scores, qkv_proj[:, :, 1], preferred_element_type=jnp.float32
    )
    grad_key = jnp.einsum(
        "ihqk,iqhd->ikhd", grad_scores, qkv_proj[:, :, 0], preferred_element_type=jnp.float32
    )
    grad_value = jnp.einsum(
        "ihqk,iqhd->ikhd",
        attn_probs.astype(jnp.bfloat16),
        grad_mixed,
        preferred_element_type=jnp.float32,
    )
    grad_qkv = jnp.stack([grad_query, grad_key, grad_value], axis=2)
    grad_qkv = grad_qkv.reshape(images * row_count, 3 * width).astype(jnp.bfloat16)
    grad_w_qkv = left_trans(ln_one, grad_qkv)
    grad_ln_one = right_trans(grad_qkv, w_qkv)
    grad_gain_one = jnp.sum(grad_ln_one * normed_one, axis=0)
    grad_in = grad_mid + norm_back(grad_ln_one * gain_one.astype(jnp.float32), normed_one, inv_one)
    grads = (grad_gain_one, grad_w_qkv, grad_w_proj, grad_gain_two, grad_w_up, grad_w_down)
    return (grad_in.reshape(images, row_count, width), grads)


def head_step(cond_rows, live, noisy, noise_vals, steps, weights):
    w_in, w_cond, w_ada, w_inner, w_outer, w_out = weights
    row_count = cond_rows.shape[0]
    flat_count = row_count * COPIES
    cond = matmul(cond_rows, w_cond)
    cond_full = (cond[:, None, :] + time_embed(steps)).reshape(flat_count, HW)
    cond_act = jax.nn.silu(cond_full).astype(jnp.bfloat16)
    modulate = matmul(cond_act, w_ada)
    shift_part = modulate[:, :HW]
    scale_part = modulate[:, HW : 2 * HW]
    gate_part = modulate[:, 2 * HW :]
    hidden = matmul(noisy, w_in)
    normed_in, inv_in = norm_rows(hidden)
    mlp_in = (normed_in * (1.0 + scale_part) + shift_part).astype(jnp.bfloat16)
    inner = matmul(mlp_in, w_inner)
    inner_act = jax.nn.silu(inner).astype(jnp.bfloat16)
    branch = matmul(inner_act, w_outer)
    hidden_two = hidden + gate_part * branch
    normed_out, inv_out = norm_rows(hidden_two)
    final_in = normed_out.astype(jnp.bfloat16)
    error = matmul(final_in, w_out) - noise_vals
    row_loss = jnp.sum((error * error).reshape(row_count, COPIES * CH), axis=1).astype(jnp.bfloat16)
    live_flat = jnp.broadcast_to(live[:, None], (row_count, COPIES)).reshape(flat_count, 1)
    grad_pred = jnp.where(live_flat, error * (2.0 / COPIES), 0.0).astype(jnp.bfloat16)
    grad_w_out = left_trans(final_in, grad_pred)
    grad_two = norm_back(right_trans(grad_pred, w_out), normed_out, inv_out)
    grad_branch = (grad_two * gate_part).astype(jnp.bfloat16)
    grad_gate = grad_two * branch
    grad_w_outer = left_trans(inner_act, grad_branch)
    grad_inner = (right_trans(grad_branch, w_outer) * silu_slope(inner)).astype(jnp.bfloat16)
    grad_w_inner = left_trans(mlp_in, grad_inner)
    grad_mlp_in = right_trans(grad_inner, w_inner)
    grad_hidden = (
        grad_two + norm_back(grad_mlp_in * (1.0 + scale_part), normed_in, inv_in)
    ).astype(jnp.bfloat16)
    grad_w_in = left_trans(noisy, grad_hidden)
    grad_mod = jnp.concatenate([grad_mlp_in, grad_mlp_in * normed_in, grad_gate], axis=1).astype(
        jnp.bfloat16
    )
    grad_w_ada = left_trans(cond_act, grad_mod)
    grad_cond_full = right_trans(grad_mod, w_ada) * silu_slope(cond_full)
    grad_cond = jnp.sum(grad_cond_full.reshape(row_count, COPIES, HW), axis=1).astype(jnp.bfloat16)
    grad_w_cond = left_trans(cond_rows, grad_cond)
    grad_rows = right_trans(grad_cond, w_cond).astype(jnp.bfloat16)
    grads = (grad_w_in, grad_w_cond, grad_w_ada, grad_w_inner, grad_w_outer, grad_w_out)
    return (grads, grad_rows, row_loss)


class Slab:
    def __init__(self, rows, cols, by_rows):
        self.rows, self.cols, self.by_rows = rows, cols, by_rows
        self.piece = (rows // 4, cols) if by_rows else (rows, cols // 4)

    def spot(self, shard, quarter, half=None):
        piece_rows, piece_cols = self.piece
        row = shard * self.rows
        if self.by_rows:
            row = row + quarter * piece_rows
        height = piece_rows
        if half is not None:
            height = piece_rows // 2
            row = row + half * height
        col = 0 if self.by_rows else quarter * piece_cols
        return (pl.ds(aligned(row, 16), height), pl.ds(aligned(col, 128), piece_cols))

    def shard(self, shard):
        return (pl.ds(aligned(shard * self.rows, 16), self.rows), pl.ds(0, self.cols))

    def within(self, quarter):
        return self.spot(0, quarter)


def aligned(value, multiple):
    return value if isinstance(value, int) else pl.multiple_of(value, multiple)


def place(depth):
    group, device = lax.axis_index("grp"), lax.axis_index("dev")
    level, core = device // 2, device % 2
    flip = lambda bit: group + (1 << bit) * (1 - 2 * ((group // (1 << bit)) % 2))
    return group, level, core, flip


def greet(peers):
    barrier = pltpu.get_barrier_semaphore()
    for peer in peers:
        pl.semaphore_signal(barrier, inc=1, device_id=peer, device_id_type=MESH)
    pl.semaphore_wait(barrier, len(peers))


def gather_kernel(slabs, depth, *refs):
    count = len(slabs)
    mine, whole = refs[:count], refs[count : 2 * count]
    sent, got, own_sent, own_got, own_copy = refs[2 * count :]
    group, level, core, flip = place(depth)
    x_peer, y_peer = (flip(0), 2 * level + core), (flip(1), 2 * level + core)
    partner = (group, 2 * level + 1 - core)

    def level_at(step):
        return lax.rem(level + step + depth, depth)

    z_peers = [(group, 2 * level_at(step) + core) for step in range(1, depth)]
    greet([x_peer, y_peer, partner] + z_peers)

    def move(kind, item, source, target, device):
        return pltpu.make_async_remote_copy(
            src_ref=source,
            dst_ref=target,
            send_sem=sent.at[kind, item],
            recv_sem=got.at[kind, item],
            device_id=device,
            device_id_type=MESH,
        )

    Z, X, Y, XH, YH, CORE = range(6)
    items = [(k, step) for k in range(count) for step in range(1, depth)]

    def by_z(item):
        k, step = items[item]
        slab = slabs[k]
        target = whole[k].at[slab.spot(2 * level + core, group)]
        return move(Z, item, mine[k].at[slab.within(group)], target, z_peers[step - 1])

    def shard_of(item):
        return 2 * level_at(-items[item][1]) + core

    def forward(kind, item, quarter, half, device):
        k = items[item][0]
        here = whole[k].at[slabs[k].spot(shard_of(item), quarter, half)]
        return move(kind, item, here, here, device)

    def core_copy(item, core_of):
        k, step = items[item]
        here = whole[k].at[slabs[k].shard(2 * level_at(-step) + core_of)]
        return move(CORE, item, here, here, partner)

    own = []
    for k, slab in enumerate(slabs):
        for step in range(1, depth):
            by_z(k * (depth - 1) + step - 1).start()
        target = whole[k].at[slab.shard(2 * level + core)]
        keep = pltpu.make_async_copy(mine[k], target, own_copy.at[k])
        keep.start()
        share = pltpu.make_async_remote_copy(
            src_ref=mine[k],
            dst_ref=target,
            send_sem=own_sent.at[k],
            recv_sem=own_got.at[k],
            device_id=partner,
            device_id_type=MESH,
        )
        share.start()
        own.append((keep, share))

    total = len(items)
    for turn in range(total + 2):
        if turn < total:
            k = items[turn][0]
            here = whole[k].at[slabs[k].spot(shard_of(turn), group)]
            move(Z, turn, here, here, x_peer).wait_recv()
            forward(X, turn, group, None, x_peer).start()
            forward(Y, turn, group, None, y_peer).start()
        item = turn - 1
        if 0 <= item < total:
            forward(X, item, flip(0), None, x_peer).wait_recv()
            forward(YH, item, flip(0), 0, y_peer).start()
            forward(Y, item, flip(1), None, y_peer).wait_recv()
            forward(XH, item, flip(1), 1, x_peer).start()
        item = turn - 2
        if 0 <= item < total:
            far = 3 - group
            forward(YH, item, far, 0, y_peer).wait_recv()
            forward(XH, item, far, 1, x_peer).wait_recv()
            core_copy(item, core).start()
    for item in range(total):
        by_z(item).wait_send()
        forward(X, item, group, None, x_peer).wait_send()
        forward(Y, item, group, None, y_peer).wait_send()
        forward(YH, item, flip(0), 0, y_peer).wait_send()
        forward(XH, item, flip(1), 1, x_peer).wait_send()
        core_copy(item, core).wait_send()
        core_copy(item, 1 - core).wait_recv()
    for keep, share in own:
        keep.wait()
        share.wait()


def gather_slabs(shards, slabs, depth):
    count, items = len(slabs), len(slabs) * (depth - 1)
    return pl.pallas_call(
        functools.partial(gather_kernel, slabs, depth),
        out_shape=[
            jax.ShapeDtypeStruct((2 * depth * s.rows, s.cols), jnp.bfloat16) for s in slabs
        ],
        in_specs=[pl.BlockSpec(memory_space=pl.ANY)] * count,
        out_specs=[pl.BlockSpec(memory_space=pl.ANY)] * count,
        scratch_shapes=[
            pltpu.SemaphoreType.DMA((6, items)),
            pltpu.SemaphoreType.DMA((6, items)),
            pltpu.SemaphoreType.DMA((count,)),
            pltpu.SemaphoreType.DMA((count,)),
            pltpu.SemaphoreType.DMA((count,)),
        ],
        compiler_params=pltpu.CompilerParams(collective_id=0, has_side_effects=True),
        name="gather_weights",
    )(*shards)


def sum_kernel(slabs, orders, depth, *refs):
    count = len(slabs)
    grads, outs = refs[:count], refs[count : 2 * count]
    rest = refs[2 * count :]
    take = lambda: (rest[:count], rest[count:])
    held, rest = take()
    from_first, rest = take()
    from_second, rest = take()
    from_level, rest = take()
    result, rest = take()
    stage, rest = take()
    stage_sem, out_sem, core_sent, core_got, sent, got, z_sent, z_got = rest
    group, level, core, flip = place(depth)
    me = 2 * level + core
    partner = (group, 2 * level + 1 - core)
    bit = lambda b: (group // (1 << b)) % 2

    def level_at(step):
        return lax.rem(level + step + depth, depth)

    z_peers = [(group, 2 * level_at(step) + core) for step in range(1, depth)]
    greet([(flip(0), me), (flip(1), me), partner] + z_peers)

    def move(pair, k, kind, source, target, device):
        send, receive = pair
        return pltpu.make_async_remote_copy(
            src_ref=source,
            dst_ref=target,
            send_sem=send.at[kind, k],
            recv_sem=receive.at[kind, k],
            device_id=device,
            device_id_type=MESH,
        )

    def core_move(k, lev):
        source = grads[k].at[slabs[k].shard(2 * lev + 1 - core)]
        return move((core_sent, core_got), k, lev, source, held[k].at[lev], partner)

    def rows_loop(height, body):
        step = 32 if height % 32 == 0 else 16

        def turn(i, carry):
            body(pl.ds(aligned(i * step, 16), step))
            return carry

        lax.fori_loop(0, height // step, turn, 0)

    def shifted(rows, by):
        return pl.ds(aligned(rows.start + by, 16), rows.size)

    def first_bit(k):
        return 1 if orders[k] == "yx" else 0

    def quarter(k, first, second):
        b = first_bit(k)
        return first * (1 << b) + second * (1 << (1 - b))

    def first_move(k, j):
        b = first_bit(k)
        where = slabs[k].within(quarter(k, 1 - bit(b), j))
        source = held[k].at[(level,) + where] if orders[k][0] == "z" else held[k].at[(slice(None),) + where]
        return move((sent, got), k, j, source, from_first[k].at[j], (flip(b), me))

    def second_move(k):
        b = first_bit(k)
        where = slabs[k].within(quarter(k, bit(b), 1 - bit(1 - b)))
        source = held[k].at[(level,) + where] if orders[k][0] == "z" else held[k].at[(slice(None),) + where]
        return move((sent, got), k, 2, source, from_second[k], (flip(1 - b), me))

    def level_move(k, step):
        lev = level_at(step)
        source = held[k].at[lev] if orders[k][0] == "z" else held[k].at[(lev,) + slabs[k].within(group)]
        return move((z_sent, z_got), k, step - 1, source, from_level[k].at[step - 1], z_peers[step - 1])

    def spread_second(k, whose):
        here = result[k].at[slabs[k].within(whose)]
        return move((sent, got), k, 3, here, here, (flip(1 - first_bit(k)), me))

    def spread_first(k, j, whose):
        here = result[k].at[slabs[k].within(whose)]
        return move((sent, got), k, 4 + j, here, here, (flip(first_bit(k)), me))

    def out_copy(k):
        return pltpu.make_async_copy(result[k], outs[k], out_sem.at[k])

    def stage_copy(k, lev):
        source = grads[k].at[slabs[k].shard(2 * lev + core)]
        return pltpu.make_async_copy(source, stage[k].at[lev % 2], stage_sem.at[k, lev % 2])

    def add_core(k):
        slab = slabs[k]
        stage_copy(k, 0).start()
        for lev in range(depth):
            if lev + 1 < depth:
                stage_copy(k, lev + 1).start()
            core_move(k, lev).wait_recv()
            stage_copy(k, lev).wait()

            def body(rows):
                total = held[k][lev, rows, :].astype(jnp.float32) + stage[k][lev % 2, rows, :].astype(jnp.float32)
                held[k][lev, rows, :] = total.astype(jnp.bfloat16)

            rows_loop(slab.rows, body)

    def levels_of(k):
        return [level] if orders[k][0] == "z" else list(range(depth))

    def add_first(k):
        slab = slabs[k]
        for j in range(2):
            first_move(k, j).wait_recv()
            rows_of, cols = slab.within(quarter(k, bit(first_bit(k)), j))
            for lev in levels_of(k):

                def body(rows):
                    at = (lev, shifted(rows, rows_of.start), cols)
                    extra = from_first[k][j, rows, :] if orders[k][0] == "z" else from_first[k][j, lev, rows, :]
                    held[k][at] = (held[k][at].astype(jnp.float32) + extra.astype(jnp.float32)).astype(jnp.bfloat16)

                rows_loop(slab.piece[0], body)

    def add_second(k):
        slab = slabs[k]
        second_move(k).wait_recv()
        rows_of, cols = slab.within(group)
        for lev in levels_of(k):

            def body(rows):
                at = (lev, shifted(rows, rows_of.start), cols)
                extra = from_second[k][rows, :] if orders[k][0] == "z" else from_second[k][lev, rows, :]
                total = held[k][at].astype(jnp.float32) + extra.astype(jnp.float32)
                target = result[k].at[shifted(rows, rows_of.start), cols] if orders[k][0] == "z" else held[k].at[at]
                target[...] = total.astype(jnp.bfloat16)

            rows_loop(slab.piece[0], body)

    def add_level(k):
        slab = slabs[k]
        for step in range(1, depth):
            level_move(k, step).wait_recv()
        if orders[k][0] == "z":

            def body(rows):
                total = held[k][level, rows, :].astype(jnp.float32)
                for step in range(depth - 1):
                    total = total + from_level[k][step, rows, :].astype(jnp.float32)
                held[k][level, rows, :] = total.astype(jnp.bfloat16)

            rows_loop(slab.rows, body)
            return
        rows_of, cols = slab.within(group)

        def body(rows):
            at = (shifted(rows, rows_of.start), cols)
            total = held[k][(level,) + at].astype(jnp.float32)
            for step in range(depth - 1):
                total = total + from_level[k][step, rows, :].astype(jnp.float32)
            result[k][at] = total.astype(jnp.bfloat16)

        rows_loop(slab.piece[0], body)

    def begin_core(k):
        for lev in range(depth):
            core_move(k, lev).start()

    def begin_first(k):
        first_move(k, 0).start()
        first_move(k, 1).start()

    def begin_level(k):
        for step in range(1, depth):
            level_move(k, step).start()

    def end_spread_second(k):
        spread_second(k, flip(1 - first_bit(k))).wait_recv()
        spread_first(k, 0, group).start()
        spread_first(k, 1, flip(1 - first_bit(k))).start()

    def end_spread_first(k):
        b = first_bit(k)
        spread_first(k, 0, flip(b)).wait_recv()
        spread_first(k, 1, 3 - group).wait_recv()
        out_copy(k).start()

    def steps(k):
        if orders[k][0] == "z":
            return [
                lambda: (add_core(k), begin_level(k)),
                lambda: (add_level(k), begin_first(k)),
                lambda: (add_first(k), second_move(k).start()),
                lambda: (add_second(k), spread_second(k, group).start()),
                lambda: end_spread_second(k),
                lambda: end_spread_first(k),
            ]
        return [
            lambda: (add_core(k), begin_first(k)),
            lambda: (add_first(k), second_move(k).start()),
            lambda: (add_second(k), begin_level(k)),
            lambda: (add_level(k), spread_second(k, group).start()),
            lambda: end_spread_second(k),
            lambda: end_spread_first(k),
        ]

    plans = [steps(k) for k in range(count)]
    begin_core(0)
    for turn in range(count + 5):
        if turn + 1 < count:
            begin_core(turn + 1)
        for place_in in range(6):
            k = turn - place_in
            if 0 <= k < count:
                plans[k][place_in]()
    for k in range(count):
        for lev in range(depth):
            core_move(k, lev).wait_send()
        first_move(k, 0).wait_send()
        first_move(k, 1).wait_send()
        second_move(k).wait_send()
        for step in range(1, depth):
            level_move(k, step).wait_send()
        spread_second(k, group).wait_send()
        spread_first(k, 0, group).wait_send()
        spread_first(k, 1, flip(1 - first_bit(k))).wait_send()
        out_copy(k).wait()


def sum_slabs(grads, slabs, orders, depth):
    count = len(slabs)
    half = jnp.bfloat16
    held, first, second, lev, result, stage = [], [], [], [], [], []
    for slab, order in zip(slabs, orders, strict=True):
        shard = (slab.rows, slab.cols)
        held.append(pltpu.VMEM((depth,) + shard, half))
        result.append(pltpu.VMEM(shard, half))
        stage.append(pltpu.VMEM((2,) + shard, half))
        if order[0] == "z":
            first.append(pltpu.VMEM((2,) + slab.piece, half))
            second.append(pltpu.VMEM(slab.piece, half))
            lev.append(pltpu.VMEM((depth - 1,) + shard, half))
        else:
            first.append(pltpu.VMEM((2, depth) + slab.piece, half))
            second.append(pltpu.VMEM((depth,) + slab.piece, half))
            lev.append(pltpu.VMEM((depth - 1,) + slab.piece, half))
    dma = pltpu.SemaphoreType.DMA
    return pl.pallas_call(
        functools.partial(sum_kernel, slabs, orders, depth),
        out_shape=[jax.ShapeDtypeStruct((s.rows, s.cols), half) for s in slabs],
        in_specs=[pl.BlockSpec(memory_space=pl.ANY)] * count,
        out_specs=[pl.BlockSpec(memory_space=pl.ANY)] * count,
        scratch_shapes=held
        + first
        + second
        + lev
        + result
        + stage
        + [
            dma((count, 2)),
            dma((count,)),
            dma((depth, count)),
            dma((depth, count)),
            dma((6, count)),
            dma((6, count)),
            dma((depth - 1, count)),
            dma((depth - 1, count)),
        ],
        compiler_params=pltpu.CompilerParams(
            collective_id=1, has_side_effects=True, vmem_limit_bytes=SUM_VMEM
        ),
        name="sum_gradients",
    )(*grads)


SMALL_ROWS, SMALL_COLS = 32, 512


def pack_small(vectors, first, last):
    parts = vectors[0].shape[0] // 96
    lanes = jnp.stack([v.reshape(parts, 96) for v in vectors], axis=1)
    lanes = jnp.pad(lanes, ((0, 0), (0, 16 - len(vectors)), (0, 128 - 96)))
    first = first.reshape(CH, parts, 128).transpose(1, 0, 2)
    last = last.reshape(parts, 128, CH).transpose(0, 2, 1)
    packed = jnp.concatenate([lanes, first, last], axis=2)
    packed = jnp.pad(packed, ((0, 0), (0, SMALL_ROWS - 16), (0, SMALL_COLS - 384)))
    return packed.reshape(parts * SMALL_ROWS, SMALL_COLS)


def unpack_small(packed):
    parts = packed.shape[0] // SMALL_ROWS
    packed = packed.reshape(parts, SMALL_ROWS, SMALL_COLS)
    vectors = [packed[:, i, :96].reshape(parts * 96) for i in range(5)]
    first = packed[:, :CH, 128:256].transpose(1, 0, 2).reshape(CH, parts * 128)
    last = packed[:, :CH, 256:384].transpose(0, 2, 1).reshape(parts * 128, CH)
    return vectors, first, last


SLABS = (
    Slab(96, 3072, False),
    Slab(96, 3072, False),
    Slab(384, 768, True),
    Slab(96, 3072, False),
    Slab(96, 3072, False),
    Slab(384, 768, True),
    Slab(96, 1024, False),
    Slab(128, 3072, False),
    Slab(128, 2048, False),
    Slab(32, 512, False),
)


def gather_weights(shards):
    (e_one, e_qkv, e_proj, e_two, e_up, e_down, d_one, d_qkv, d_proj, d_two, d_up, d_down, fill, h_in, h_cond, h_ada, h_inner, h_outer, h_out) = shards
    if lax.axis_size("dev") != 8 or lax.axis_size("grp") != 4:
        whole = [lax.all_gather(w, "dev", axis=0, tiled=True) for w in shards]
        whole[13] = lax.all_gather(h_in, "dev", axis=1, tiled=True)
        return whole
    depth = lax.axis_size("dev") // 2
    packed = (
        jnp.concatenate([e_qkv, e_proj], axis=1), e_up, e_down,
        jnp.concatenate([d_qkv, d_proj], axis=1), d_up, d_down,
        h_cond, h_ada, jnp.concatenate([h_inner, h_outer], axis=1),
        pack_small([e_one, e_two, d_one, d_two, fill], h_in, h_out),
    )
    ea, eu, ed, da, du, dd, hc, ha, hio, small = gather_slabs(packed, SLABS, depth)
    (e_one, e_two, d_one, d_two, fill), h_in, h_out = unpack_small(small)
    split = e_qkv.shape[1]
    return [e_one, ea[:, :split], ea[:, split:], e_two, eu, ed, d_one, da[:, :split], da[:, split:], d_two, du, dd, fill,
            h_in, hc, ha, hio[:, :HW], hio[:, HW:], h_out]


def sum_gradients(grads):
    low = [g.astype(jnp.bfloat16) for g in grads]
    (e_one, e_qkv, e_proj, e_two, e_up, e_down, d_one, d_qkv, d_proj, d_two, d_up, d_down, fill, h_in, h_cond, h_ada, h_inner, h_outer, h_out) = low
    if lax.axis_size("dev") != 8 or lax.axis_size("grp") != 4:
        sums = [lax.psum_scatter(g, "dev", scatter_dimension=int(i == 13), tiled=True) for i, g in enumerate(grads)]
        return [lax.psum(g.astype(jnp.bfloat16), "grp").astype(jnp.float32) for g in sums]
    depth = lax.axis_size("dev") // 2
    packed = (
        jnp.concatenate([e_qkv, e_proj], axis=1), e_up, e_down,
        jnp.concatenate([d_qkv, d_proj], axis=1), d_up, d_down,
        h_cond, h_ada, jnp.concatenate([h_inner, h_outer], axis=1),
        pack_small([e_one, e_two, d_one, d_two, fill], h_in, h_out),
    )
    turn = (7, 8, 6, 3, 4, 5, 0, 1, 2, 9)
    orders = ("xy", "yx", "zx", "xy", "yx", "zx", "yx", "xy", "yx", "xy")
    sums = sum_slabs([packed[t] for t in turn], [SLABS[t] for t in turn], [orders[t] for t in turn], depth)
    back = [None] * len(turn)
    for t, s in zip(turn, sums, strict=True):
        back[t] = s.astype(jnp.float32)
    ea, eu, ed, da, du, dd, hc, ha, hio, small = back
    (e_one, e_two, d_one, d_two, fill), h_in, h_out = unpack_small(small)
    split = e_qkv.shape[1]
    return [e_one, ea[:, :split], ea[:, split:], e_two, eu, ed, d_one, da[:, :split], da[:, split:], d_two, du, dd, fill,
            h_in, hc, ha, hio[:, :HW], hio[:, HW:], h_out]


def per_device(
    embedded,
    mask_order,
    counts,
    targets,
    noise_copies,
    timesteps,
    enc_gain_one,
    enc_qkv,
    enc_proj,
    enc_gain_two,
    enc_up,
    enc_down,
    dec_gain_one,
    dec_qkv,
    dec_proj,
    dec_gain_two,
    dec_up,
    dec_down,
    mask_token,
    head_in,
    head_cond,
    head_ada,
    head_inner,
    head_outer,
    head_out,
):
    images, tokens, width = embedded.shape
    seq_len = mask_order.shape[1]
    buffer = tokens - seq_len
    visible_max = ENC - buffer
    seen = gather_weights(
        (enc_gain_one, enc_qkv, enc_proj, enc_gain_two, enc_up, enc_down,
         dec_gain_one, dec_qkv, dec_proj, dec_gain_two, dec_up, dec_down, mask_token,
         head_in, head_cond, head_ada, head_inner, head_outer, head_out)
    )
    enc_weights, dec_weights, token_fill = seen[:6], seen[6:12], seen[12].astype(jnp.float32)
    head_weights = seen[13:]
    spots = jnp.arange(visible_max, dtype=jnp.int32)
    spot_src = jnp.minimum(counts[:, None] + spots[None, :], seq_len - 1)
    vis_tokens = jnp.take_along_axis(mask_order, spot_src, axis=1)
    spot_live = spots[None, :] < (seq_len - counts)[:, None]
    buffer_rows = jnp.arange(buffer, dtype=jnp.int32)[None, :]
    enc_rows = jnp.concatenate([buffer_rows, buffer + vis_tokens], axis=1)
    enc_in = jax.vmap(pick_rows)(embedded, enc_rows).astype(jnp.float32)
    enc_valid = jnp.concatenate([jnp.ones((images, buffer), bool), spot_live], axis=1)
    enc_out, enc_kept = block_forward(enc_in, enc_valid, enc_weights)
    rank = jax.vmap(inverse_order)(mask_order)
    visible = rank >= counts[:, None]
    enc_source = buffer + jnp.clip(rank - counts[:, None], 0, visible_max - 1)
    tok_rows = jnp.where(
        visible[..., None], jax.vmap(pick_rows)(enc_out, enc_source), token_fill[None, None, :]
    )
    dec_in = jnp.concatenate([enc_out[:, :buffer], tok_rows], axis=1)
    dec_valid = jnp.ones((images, tokens), bool)
    dec_out, dec_kept = block_forward(dec_in, dec_valid, dec_weights)
    activations = dec_out.astype(jnp.bfloat16)
    masked = ~visible.reshape(images * seq_len)
    angle = noise_angle(timesteps)
    noise_vals = noise_copies.astype(jnp.float32)
    noisy = jnp.cos(angle)[..., None] * targets[:, :, None, :] + jnp.sin(angle)[..., None] * noise_vals
    flat_count = images * seq_len * COPIES
    head_grads, grad_rows, row_loss = head_step(
        activations[:, buffer:].reshape(images * seq_len, width),
        masked,
        noisy.astype(jnp.bfloat16).reshape(flat_count, CH),
        noise_vals.reshape(flat_count, CH),
        timesteps.reshape(images * seq_len, COPIES),
        head_weights,
    )
    image_loss = jnp.sum(jnp.where(masked, row_loss.astype(jnp.float32), 0.0).reshape(images, seq_len), axis=1)
    image_loss = image_loss / (counts.astype(jnp.float32) * (COPIES * CH))
    grad_dec = jnp.concatenate(
        [jnp.zeros((images, buffer, width), jnp.float32), grad_rows.astype(jnp.float32).reshape(images, seq_len, width)],
        axis=1,
    )
    grad_dec_in, dec_grads = block_backward(
        grad_dec, dec_valid, dec_weights, dec_kept
    )
    grad_tok = grad_dec_in[:, buffer:]
    fill_grad = jnp.sum(jnp.where(visible[..., None], 0.0, grad_tok), axis=(0, 1))
    grad_vis = jnp.where(spot_live[..., None], jax.vmap(pick_rows)(grad_tok, vis_tokens), 0.0)
    grad_enc_out = jnp.concatenate([grad_dec_in[:, :buffer], grad_vis], axis=1)
    grad_enc_in, enc_grads = block_backward(grad_enc_out, enc_valid, enc_weights, enc_kept)
    token_grad = jax.vmap(place_rows)(
        jnp.zeros((images, seq_len, width), jnp.float32),
        jnp.where(spot_live, vis_tokens, seq_len),
        grad_enc_in[:, buffer:],
    )
    embed_grad = jnp.concatenate([grad_enc_in[:, :buffer], token_grad], axis=1)
    final_grads = sum_gradients([*enc_grads, *dec_grads, fill_grad, *head_grads])
    return (image_loss, activations, embed_grad, *final_grads)


def solution(mesh):
    return jax.shard_map(
        per_device,
        mesh=mesh,
        in_specs=(
            P(("grp", "dev"), None, None),
            P(("grp", "dev"), None),
            P(("grp", "dev")),
            P(("grp", "dev"), None, None),
            P(("grp", "dev"), None, None, None),
            P(("grp", "dev"), None, None),
            P("dev"),
            P("dev", None),
            P("dev", None),
            P("dev"),
            P("dev", None),
            P("dev", None),
            P("dev"),
            P("dev", None),
            P("dev", None),
            P("dev"),
            P("dev", None),
            P("dev", None),
            P("dev"),
            P(None, "dev"),
            P("dev", None),
            P("dev", None),
            P("dev", None),
            P("dev", None),
            P("dev", None),
        ),
        out_specs=(
            P(("grp", "dev")),
            P(("grp", "dev"), None, None),
            P(("grp", "dev"), None, None),
            P("dev"),
            P("dev", None),
            P("dev", None),
            P("dev"),
            P("dev", None),
            P("dev", None),
            P("dev"),
            P("dev", None),
            P("dev", None),
            P("dev"),
            P("dev", None),
            P("dev", None),
            P("dev"),
            P(None, "dev"),
            P("dev", None),
            P("dev", None),
            P("dev", None),
            P("dev", None),
            P("dev", None),
        ),
        check_vma=False,
    )
```

```python
import functools
import math

import jax
import jax.numpy as jnp
from jax import lax
from jax.experimental import pallas as pl
from jax.experimental.pallas import tpu as pltpu
from jax.sharding import PartitionSpec as P

MESH = pl.DeviceIdType.MESH
SUM_VMEM = 60 * 1024 * 1024
HW = 1024
CH = 16
COPIES = 4
STEPS_T = 1000
BUFFER = 64
SPOTS = 80
EPSILON = 1e-06
NEG_FILL = -1e30


def matmul(left, right):
    return jnp.dot(left, right, preferred_element_type=jnp.float32)


def right_trans(left, right):
    return lax.dot_general(
        left, right, (((1,), (1,)), ((), ())), preferred_element_type=jnp.float32
    )


def norm_rows(values):
    centre = values - jnp.mean(values, axis=-1, keepdims=True)
    inv_std = lax.rsqrt(jnp.mean(centre * centre, axis=-1, keepdims=True) + EPSILON)
    return (centre * inv_std, inv_std)


def norm_back(grad, normed, inv_std):
    mean_grad = jnp.mean(grad, axis=-1, keepdims=True)
    mean_cross = jnp.mean(grad * normed, axis=-1, keepdims=True)
    return inv_std * (grad - mean_grad - normed * mean_cross)


def silu_slope(values):
    sigma = jax.nn.sigmoid(values)
    return sigma * (1.0 + values * (1.0 - sigma))


def noise_angle(steps):
    return (steps.astype(jnp.float32) / STEPS_T + 0.008) / 1.008 * (math.pi / 2)


ROOT_HALF = 1.0 / math.sqrt(2.0)
TILE = 512
STEP = 16


def rows_dot(left, right):
    return lax.dot_general(left, right, (((0,), (0,)), ((), ())), preferred_element_type=jnp.float32)


def loop(count, body):
    def turn(i, carry):
        body(i)
        return carry

    lax.fori_loop(0, count, turn, 0)


def at_step(i, size=STEP):
    return pl.ds(pl.multiple_of(i * size, size), size)


def at_col(i, size):
    return pl.ds(pl.multiple_of(i * size, 128), size)


def exact_dot(ones, values):
    high = values.astype(jnp.bfloat16)
    rest = values - high.astype(jnp.float32)
    middle = rest.astype(jnp.bfloat16)
    low = (rest - middle.astype(jnp.float32)).astype(jnp.bfloat16)
    return matmul(ones, high) + matmul(ones, middle) + matmul(ones, low)


def scale_norm(source, gain, target):
    normed, _ = norm_rows(source[...])
    target[...] = (normed * gain).astype(jnp.bfloat16)


def head_mask(half):
    lane = lax.broadcasted_iota(jnp.int32, (1, 128), 1)
    return (lane < 64) if half == 0 else (lane >= 64)


def keep_half(values, half):
    return jnp.where(head_mask(half), values, jnp.zeros((), values.dtype))


def probabilities(query, key, half, bias):
    scores = right_trans(keep_half(query, half), key) * 0.125
    if bias is not None:
        scores = jnp.where(bias, scores, NEG_FILL)
    grown = jnp.exp(scores - jnp.max(scores, axis=-1, keepdims=True))
    return grown / jnp.sum(grown, axis=-1, keepdims=True)


def forward_steps(width, stream, gain_one, gain_two, w_a, w_up, w_down, qkv, mixed, middle, up, out, low, live=None):
    def project(j):
        cols = pl.ds(j * width, width)
        qkv[:, cols] = matmul(low[...], w_a[:, cols]).astype(jnp.bfloat16)

    def attend(pair):
        query, key, value = (qkv[:, pl.ds(pair * 128 + part * width, 128)] for part in range(3))
        parts = [
            matmul(probabilities(query, key, half, live).astype(jnp.bfloat16), value) for half in range(2)
        ]
        mixed[:, pl.ds(pair * 128, 128)] = jnp.where(head_mask(0), parts[0], parts[1]).astype(jnp.bfloat16)

    def mix():
        middle[...] = stream[...] + matmul(mixed[...], w_a[:, 3 * width :])
        scale_norm(middle, gain_two, low)

    def feed(j):
        cols = pl.ds(j * TILE, TILE)
        raised = matmul(low[...], w_up[:, cols])
        up[:, cols] = raised
        act = (raised * (0.5 + 0.5 * lax.erf(raised * ROOT_HALF))).astype(jnp.bfloat16)
        out[...] = (middle[...] if j == 0 else out[...]) + matmul(act, w_down[cols, :])

    yield lambda: scale_norm(stream, gain_one, low)
    for j in range(3):
        yield functools.partial(project, j)
    for pair in range(width // 128):
        yield functools.partial(attend, pair)
    yield mix
    for j in range(w_up.shape[1] // TILE):
        yield functools.partial(feed, j)


def forward_block(*args):
    for step in forward_steps(*args):
        step()


def forward_kernel(*refs):
    (embedded, vis_col, vis_row, vec, e_a_hbm, e_u_hbm, e_d_hbm, d_a_hbm, d_u_hbm, d_d_hbm,
     e_in, e_qkv, e_mixed, e_mid, e_up, d_in, d_qkv, d_mixed, d_mid, d_up, acts,
     e_a, e_u, e_d, d_a, d_u, d_d, e_out, d_out, e_low, d_low, sems) = refs
    width = embedded.shape[1]
    loads = [
        pltpu.make_async_copy(a, b, sems.at[i])
        for i, (a, b) in enumerate(
            [(e_a_hbm, e_a), (e_u_hbm, e_u), (e_d_hbm, e_d), (d_a_hbm, d_a), (d_u_hbm, d_u), (d_d_hbm, d_d)]
        )
    ]
    for load in loads:
        load.start()
    encode(embedded, vis_col, vec, e_in)
    for load in loads[:3]:
        load.wait()
    live = live_keys(vis_row)
    forward_block(width, e_in, vec[0:1, :], vec[1:2, :], e_a, e_u, e_d, e_qkv, e_mixed, e_mid, e_up, e_out, e_low, live)
    spread_rows(vis_row, e_out, vec, d_in)
    for load in loads[3:]:
        load.wait()
    forward_block(width, d_in, vec[2:3, :], vec[3:4, :], d_a, d_u, d_d, d_qkv, d_mixed, d_mid, d_up, d_out, d_low)
    acts[...] = d_out[...].astype(jnp.bfloat16)


def token_hot(vis_col, count):
    return (lax.broadcasted_iota(jnp.int32, (vis_col.shape[0], count), 1) == vis_col[...]).astype(jnp.bfloat16)


def spot_hot(vis_row, count):
    return (lax.broadcasted_iota(jnp.int32, (count, vis_row.shape[1]), 0) == vis_row[...]).astype(jnp.bfloat16)


def live_keys(vis_row):
    ones = jnp.ones((1, BUFFER), jnp.int32)
    return jnp.concatenate([ones, (vis_row[...] >= 0).astype(jnp.int32)], axis=1) > 0


def encode(embedded, vis_col, vec, target):
    tokens = embedded.shape[0] - BUFFER
    target[:BUFFER, :] = embedded[:BUFFER, :].astype(jnp.float32)
    target[BUFFER:, :] = matmul(token_hot(vis_col, tokens), embedded[BUFFER:, :])


def spread_rows(vis_row, enc_out, vec, target):
    tokens = target.shape[0] - BUFFER
    hot = spot_hot(vis_row, tokens)
    masked = 1.0 - jnp.sum(hot.astype(jnp.float32), axis=1, keepdims=True)
    target[:BUFFER, :] = enc_out[:BUFFER, :]
    target[BUFFER:, :] = exact_dot(hot, enc_out[BUFFER:, :]) + masked * vec[4:5, :]


def forward_blocks(embedded, vis_col, vis_row, vec, weights):
    tokens, width = embedded.shape
    inner = weights[1].shape[1]
    rows = BUFFER + vis_col.shape[0]
    f32, half = jnp.float32, jnp.bfloat16

    def kept(count):
        return [
            jax.ShapeDtypeStruct((count, width), f32),
            jax.ShapeDtypeStruct((count, 3 * width), half),
            jax.ShapeDtypeStruct((count, width), half),
            jax.ShapeDtypeStruct((count, width), f32),
            jax.ShapeDtypeStruct((count, inner), f32),
        ]

    outs = kept(rows) + kept(tokens) + [jax.ShapeDtypeStruct((tokens, width), half)]
    whole = pl.BlockSpec(memory_space=pltpu.VMEM)
    found = pl.pallas_call(
        forward_kernel,
        out_shape=outs,
        in_specs=[whole] * 4 + [pl.BlockSpec(memory_space=pl.ANY)] * 6,
        out_specs=[whole] * len(outs),
        scratch_shapes=[pltpu.VMEM(w.shape, half) for w in weights]
        + [
            pltpu.VMEM((rows, width), f32),
            pltpu.VMEM((tokens, width), f32),
            pltpu.VMEM((rows, width), half),
            pltpu.VMEM((tokens, width), half),
            pltpu.SemaphoreType.DMA((6,)),
        ],
        compiler_params=pltpu.CompilerParams(vmem_limit_bytes=SUM_VMEM),
        name="forward_blocks",
    )(embedded, vis_col, vis_row, vec, *weights)
    return found[:5], found[5:10], found[10]


def norm_back_into(grads, source, gain, add, target, gain_grad):
    normed, inv_std = norm_rows(source[...])
    grad = grads[...]
    gain_grad[...] = jnp.sum(grad * normed, axis=0, keepdims=True)
    target[...] = add[...] + norm_back(grad * gain, normed, inv_std)


class Tiles:
    def __init__(self, slots, sems):
        self.slots, self.sems = slots, sems

    def put(self, i, value, target):
        slot = i % 2 if isinstance(i, int) else lax.rem(i, 2)
        copy = pltpu.make_async_copy(self.slots.at[slot], target, self.sems.at[slot])

        @pl.when(i >= 2)
        def _():
            copy.wait()

        self.slots[slot] = value.astype(jnp.bfloat16)
        copy.start()

    def flush(self, like):
        for slot in range(2):
            pltpu.make_async_copy(self.slots.at[slot], like, self.sems.at[slot]).wait()


def backward_block(width, grad, stream, gain_one, gain_two, w_a, w_up, w_down, qkv, mixed, middle, up,
                   d_a, d_up, d_down, d_one, d_two, grad_low, low, grad_qkv, acc, grad_mid, out, tiles, live=None):
    rows = grad.shape[0]
    wide, narrow, square = tiles
    grad_low[...] = grad[...].astype(jnp.bfloat16)
    scale_norm(middle, gain_two, low)
    acc[...] = jnp.zeros_like(acc)
    count = w_up.shape[1] // TILE

    def feed(j):
        raised = up[:, at_col(j, TILE)]
        cumul = 0.5 + 0.5 * lax.erf(raised * ROOT_HALF)
        slope = cumul + raised * (jnp.exp(-0.5 * raised * raised) * (1.0 / math.sqrt(2.0 * math.pi)))
        act = (raised * cumul).astype(jnp.bfloat16)
        down = w_down[at_step(j, TILE), :]
        narrow.put(j, rows_dot(act, grad_low[...]), d_down.at[at_step(j, TILE), :])
        grad_up = (right_trans(grad_low[...], down) * slope).astype(jnp.bfloat16)
        wide.put(j, rows_dot(low[...], grad_up), d_up.at[:, at_col(j, TILE)])
        acc[...] += right_trans(grad_up, w_up[:, at_col(j, TILE)])

    loop(count, feed)
    narrow.flush(d_down.at[pl.ds(0, TILE), :])
    wide.flush(d_up.at[:, pl.ds(0, TILE)])
    norm_back_into(acc, middle, gain_two, grad, grad_mid, d_two)
    grad_low[...] = grad_mid[...].astype(jnp.bfloat16)
    for j in range(width // 256):
        square.put(j, rows_dot(mixed[...], grad_low[:, pl.ds(j * 256, 256)]), d_a.at[:, pl.ds(3 * width + j * 256, 256)])
    for j in range(width // 256):
        low[:, pl.ds(j * 256, 256)] = right_trans(grad_low[...], w_a[pl.ds(j * 256, 256), pl.ds(3 * width, width)]).astype(jnp.bfloat16)

    def attend(pair):
        where = [pl.ds(pl.multiple_of(pair * 128 + part * width, 128), 128) for part in range(3)]
        query, key, value = (qkv[:, at] for at in where)
        grad_mixed = low[:, at_col(pair, 128)]
        found = []
        for half in range(2):
            probs = probabilities(query, key, half, live)
            grad_half = keep_half(grad_mixed, half)
            grad_probs = right_trans(grad_half, value)
            dots = jnp.sum(grad_probs * probs, axis=-1, keepdims=True)
            grad_scores = (probs * (grad_probs - dots) * 0.125).astype(jnp.bfloat16)
            found.append(
                (matmul(grad_scores, key), rows_dot(grad_scores, query), rows_dot(probs.astype(jnp.bfloat16), grad_half))
            )
        for part in range(3):
            both = jnp.where(head_mask(0), found[0][part], found[1][part])
            grad_qkv[:, where[part]] = both.astype(jnp.bfloat16)

    loop(width // 128, attend)
    scale_norm(stream, gain_one, low)
    acc[...] = jnp.zeros_like(acc)
    first = width // 256

    def project(j):
        piece = grad_qkv[:, at_col(j, 256)]
        square.put(j + first, rows_dot(low[...], piece), d_a.at[:, at_col(j, 256)])
        acc[...] += right_trans(piece, w_a[:, at_col(j, 256)])

    loop(3 * width // 256, project)
    square.flush(d_a.at[:, pl.ds(0, 256)])
    norm_back_into(acc, stream, gain_one, grad_mid, out, d_one)


def backward_kernel(*refs):
    (grad_rows, vis_col, vis_row, vec, e_in, e_qkv, e_mixed, e_mid, e_up, d_in, d_qkv, d_mixed, d_mid, d_up,
     e_a_hbm, e_u_hbm, e_d_hbm, d_a_hbm, d_u_hbm, d_d_hbm,
     embed_grad, small, de_a, de_u, de_d, dd_a, dd_u, dd_d,
     e_a, e_u, e_d, d_a, d_u, d_d, d_grad, e_grad, low_a, low_b, grad_qkv, acc, grad_mid,
     wide, narrow, square, load_sems, tile_sems) = refs
    tokens, width = d_in.shape
    rows = e_in.shape[0]
    loads = [
        pltpu.make_async_copy(a, b, load_sems.at[i])
        for i, (a, b) in enumerate(
            [(d_d_hbm, d_d), (d_u_hbm, d_u), (d_a_hbm, d_a), (e_d_hbm, e_d), (e_u_hbm, e_u), (e_a_hbm, e_a)]
        )
    ]
    for load in loads:
        load.start()
    tiles = (Tiles(wide, tile_sems.at[0]), Tiles(narrow, tile_sems.at[1]), Tiles(square, tile_sems.at[2]))
    d_grad[:BUFFER, :] = jnp.zeros((BUFFER, width), jnp.float32)
    d_grad[BUFFER:, :] = grad_rows[...].astype(jnp.float32)
    for load in loads[:3]:
        load.wait()
    backward_block(width, d_grad, d_in, vec[2:3, :], vec[3:4, :], d_a, d_u, d_d, d_qkv, d_mixed, d_mid, d_up,
                   dd_a, dd_u, dd_d, small.at[2:3, :], small.at[3:4, :], low_a, low_b, grad_qkv, acc, grad_mid, d_grad, tiles)
    hot = spot_hot(vis_row, tokens - BUFFER)
    masked = 1.0 - jnp.sum(hot.astype(jnp.float32), axis=1, keepdims=True)
    small[4:5, :] = jnp.sum(d_grad[BUFFER:, :] * masked, axis=0, keepdims=True)
    e_grad[:BUFFER, :] = d_grad[:BUFFER, :]
    e_grad[BUFFER:, :] = exact_dot(token_hot(vis_col, tokens - BUFFER), d_grad[BUFFER:, :])
    for load in loads[3:]:
        load.wait()
    part = pl.ds(0, rows)
    backward_block(width, e_grad, e_in, vec[0:1, :], vec[1:2, :], e_a, e_u, e_d, e_qkv, e_mixed, e_mid, e_up,
                   de_a, de_u, de_d, small.at[0:1, :], small.at[1:2, :], low_a.at[part], low_b.at[part],
                   grad_qkv.at[part], acc.at[part], grad_mid.at[part], e_grad, tiles, live_keys(vis_row))
    embed_grad[:BUFFER, :] = e_grad[:BUFFER, :]
    embed_grad[BUFFER:, :] = exact_dot(hot, e_grad[BUFFER:, :])


def backward_blocks(grad_rows, vis_col, vis_row, vec, enc_kept, dec_kept, weights):
    tokens, width = dec_kept[0].shape
    rows = enc_kept[0].shape[0]
    f32, half = jnp.float32, jnp.bfloat16
    whole, anywhere = pl.BlockSpec(memory_space=pltpu.VMEM), pl.BlockSpec(memory_space=pl.ANY)
    outs = [jax.ShapeDtypeStruct((tokens, width), f32), jax.ShapeDtypeStruct((8, width), f32)]
    outs += [jax.ShapeDtypeStruct(w.shape, half) for w in weights]
    found = pl.pallas_call(
        backward_kernel,
        out_shape=outs,
        in_specs=[whole] * 14 + [anywhere] * 6,
        out_specs=[whole] * 2 + [anywhere] * 6,
        scratch_shapes=[pltpu.VMEM(w.shape, half) for w in weights]
        + [
            pltpu.VMEM((tokens, width), f32),
            pltpu.VMEM((rows, width), f32),
            pltpu.VMEM((tokens, width), half),
            pltpu.VMEM((tokens, width), half),
            pltpu.VMEM((tokens, 3 * width), half),
            pltpu.VMEM((tokens, width), f32),
            pltpu.VMEM((tokens, width), f32),
            pltpu.VMEM((2, width, TILE), half),
            pltpu.VMEM((2, TILE, width), half),
            pltpu.VMEM((2, width, 256), half),
            pltpu.SemaphoreType.DMA((6,)),
            pltpu.SemaphoreType.DMA((3, 2)),
        ],
        compiler_params=pltpu.CompilerParams(vmem_limit_bytes=SUM_VMEM),
        name="backward_blocks",
    )(grad_rows, vis_col, vis_row, vec, *enc_kept, *dec_kept, *weights)
    return found[0], found[1], found[2:]


def embed_steps(steps, freqs, target):
    half = freqs.shape[1]

    def body(i):
        phase = steps[at_step(i), :].astype(jnp.float32) * freqs[...]
        target[at_step(i), :half] = jnp.cos(phase)
        target[at_step(i), half:] = jnp.sin(phase)

    loop(steps.shape[0] // STEP, body)


ROWS = 128


def at_rows(i):
    return pl.ds(pl.multiple_of(i * ROWS, 16), ROWS)


def head_kernel(*refs):
    (acts, vis_row, targets, noise, steps, embeds, w_cond_hbm, w_ada_hbm, w_io_hbm, w_in, w_out,
     grad_rows, losses, d_in, d_out, d_cond, d_ada, d_io,
     w_cond, w_ada, w_io, cond, cond_full, mod, hidden, normed_in, inv_in, inner, branch, normed_out, inv_out,
     work, grad_two, grad_sum, noisy, cond_act, mlp_in, inner_act, final_in, grad_pred, grad_branch, grad_inner,
     grad_hidden, grad_mod, wide, load_sems, tile_sems) = refs
    tokens, wide_cols = targets.shape[0], w_in.shape[1]
    loads = [
        pltpu.make_async_copy(a, b, load_sems.at[i])
        for i, (a, b) in enumerate([(w_cond_hbm, w_cond), (w_ada_hbm, w_ada), (w_io_hbm, w_io)])
    ]
    for load in loads:
        load.start()
    hot = spot_hot(vis_row, tokens)
    masked = jnp.sum(hot.astype(jnp.float32), axis=1, keepdims=True) < 0.5
    loads[0].wait()
    cond[...] = matmul(acts[BUFFER:, :], w_cond[...])
    loads[1].wait()
    loads[2].wait()
    grad_sum[...] = jnp.zeros_like(grad_sum)
    columns = wide_cols // 256

    def copy_pass(c, loss):
        rows = pl.ds(pl.multiple_of(c * tokens, 16), tokens)

        def at(i):
            return pl.ds(pl.multiple_of(c * tokens + i * ROWS, 16), ROWS)

        angle = noise_angle(steps[rows, :])
        noise_vals = noise[rows, :].astype(jnp.float32)
        noisy[rows, :] = (jnp.cos(angle) * targets[...] + jnp.sin(angle) * noise_vals).astype(jnp.bfloat16)

        def condition(i):
            full = cond[at_rows(i), :] + embeds[at(i), :]
            cond_full[at_rows(i), :] = full
            cond_act[at(i), :] = (full * jax.nn.sigmoid(full)).astype(jnp.bfloat16)

        loop(tokens // ROWS, condition)

        def modulate(j):
            mod[:, at_col(j, wide_cols)] = matmul(cond_act[rows, :], w_ada[:, at_col(j, wide_cols)])

        loop(3, modulate)
        hidden[...] = matmul(noisy[rows, :], w_in[...])

        def enter(i):
            normed, inv_std = norm_rows(hidden[at_rows(i), :])
            normed_in[at_rows(i), :] = normed
            inv_in[at_rows(i), :] = inv_std
            shift, scale = mod[at_rows(i), :wide_cols], mod[at_rows(i), wide_cols : 2 * wide_cols]
            mlp_in[at(i), :] = (normed * (1.0 + scale) + shift).astype(jnp.bfloat16)

        loop(tokens // ROWS, enter)

        inner[...] = matmul(mlp_in[rows, :], w_io[:, :wide_cols])

        def activate(i):
            values = inner[at_rows(i), :]
            inner_act[at(i), :] = (values * jax.nn.sigmoid(values)).astype(jnp.bfloat16)

        loop(tokens // ROWS, activate)

        branch[...] = matmul(inner_act[rows, :], w_io[:, wide_cols:])

        def leave(i):
            gate = mod[at_rows(i), 2 * wide_cols :]
            normed, inv_std = norm_rows(hidden[at_rows(i), :] + gate * branch[at_rows(i), :])
            normed_out[at_rows(i), :] = normed
            inv_out[at_rows(i), :] = inv_std
            final_in[at(i), :] = normed.astype(jnp.bfloat16)

        loop(tokens // ROWS, leave)
        error = right_trans(final_in[rows, :], w_out[...]) - noise_vals
        loss = loss + jnp.sum(error * error, axis=1, keepdims=True)
        low_error = jnp.where(masked, error * (2.0 / COPIES), 0.0).astype(jnp.bfloat16)
        grad_pred[rows, :] = low_error
        work[...] = matmul(low_error, w_out[...])

        def back_out(i):
            gate = mod[at_rows(i), 2 * wide_cols :]
            grad = norm_back(work[at_rows(i), :], normed_out[at_rows(i), :], inv_out[at_rows(i), :])
            grad_two[at_rows(i), :] = grad
            grad_branch[at(i), :] = (grad * gate).astype(jnp.bfloat16)
            grad_mod[at(i), 2 * wide_cols :] = (grad * branch[at_rows(i), :]).astype(jnp.bfloat16)

        loop(tokens // ROWS, back_out)

        work[...] = right_trans(grad_branch[rows, :], w_io[:, wide_cols:])

        def back_act(i):
            grad_inner[at(i), :] = (work[at_rows(i), :] * silu_slope(inner[at_rows(i), :])).astype(jnp.bfloat16)

        loop(tokens // ROWS, back_act)

        work[...] = right_trans(grad_inner[rows, :], w_io[:, :wide_cols])

        def back_in(i):
            grad, normed = work[at_rows(i), :], normed_in[at_rows(i), :]
            scale = mod[at_rows(i), wide_cols : 2 * wide_cols]
            grad_mod[at(i), :wide_cols] = grad.astype(jnp.bfloat16)
            grad_mod[at(i), wide_cols : 2 * wide_cols] = (grad * normed).astype(jnp.bfloat16)
            total = grad_two[at_rows(i), :] + norm_back(grad * (1.0 + scale), normed, inv_in[at_rows(i), :])
            grad_hidden[at(i), :] = total.astype(jnp.bfloat16)

        loop(tokens // ROWS, back_in)

        def back_mod(j):
            work[:, at_col(j, 256)] = right_trans(grad_mod[rows, :], w_ada[at_step(j, 256), :])

        loop(columns, back_mod)

        def back_cond(i):
            grad_sum[at_rows(i), :] += work[at_rows(i), :] * silu_slope(cond_full[at_rows(i), :])

        loop(tokens // ROWS, back_cond)
        return loss

    loss = lax.fori_loop(0, COPIES, copy_pass, jnp.zeros((tokens, 1), jnp.float32))
    loss = jnp.where(masked, loss.astype(jnp.bfloat16).astype(jnp.float32), 0.0)
    losses[...] = jnp.broadcast_to(jnp.sum(loss, axis=0, keepdims=True), losses.shape)
    grad_cond = grad_sum[...].astype(jnp.bfloat16)
    grad_rows[...] = right_trans(grad_cond, w_cond[...]).astype(jnp.bfloat16)
    tiles = Tiles(wide, tile_sems)

    def out_ada(j):
        tiles.put(j, rows_dot(cond_act[...], grad_mod[:, at_col(j, TILE)]), d_ada.at[:, at_col(j, TILE)])

    count = 3 * wide_cols // TILE
    loop(count, out_ada)
    half = wide_cols // TILE

    def out_inner(j):
        tiles.put(j + count, rows_dot(mlp_in[...], grad_inner[:, at_col(j, TILE)]), d_io.at[:, at_col(j, TILE)])

    def out_outer(j):
        tiles.put(j + count + half, rows_dot(inner_act[...], grad_branch[:, at_col(j, TILE)]), d_io.at[:, at_col(j + half, TILE)])

    loop(half, out_inner)
    loop(half, out_outer)
    d_cond[...] = rows_dot(acts[BUFFER:, :], grad_cond).astype(jnp.bfloat16)
    d_in[...] = rows_dot(noisy[...], grad_hidden[...])
    d_out[...] = rows_dot(grad_pred[...], final_in[...])
    tiles.flush(d_ada.at[:, pl.ds(0, TILE)])


def head_pass(acts, vis_row, targets, noise, steps, embeds, w_cond, w_ada, w_io, w_in, w_out):
    tokens, width = targets.shape[0], acts.shape[1]
    wide, flat = w_in.shape[1], noise.shape[0]
    f32, half = jnp.float32, jnp.bfloat16
    whole, anywhere = pl.BlockSpec(memory_space=pltpu.VMEM), pl.BlockSpec(memory_space=pl.ANY)
    shape = jax.ShapeDtypeStruct
    outs = [
        shape((tokens, width), half), shape((8, 128), f32), shape((CH, wide), f32), shape((CH, wide), f32),
        shape(w_cond.shape, half), shape(w_ada.shape, half), shape(w_io.shape, half),
    ]
    tile = lambda cols, kind=f32: pltpu.VMEM((tokens, cols), kind)
    long = lambda cols: pltpu.VMEM((flat, cols), half)
    return pl.pallas_call(
        head_kernel,
        out_shape=outs,
        in_specs=[whole] * 6 + [anywhere] * 3 + [whole] * 2,
        out_specs=[whole] * 5 + [anywhere] * 2,
        scratch_shapes=[pltpu.VMEM(w.shape, half) for w in (w_cond, w_ada, w_io)]
        + [
            tile(wide), tile(wide), tile(3 * wide), tile(wide), tile(wide), tile(1), tile(wide), tile(wide), tile(wide), tile(1),
            tile(wide), tile(wide), tile(wide),
            long(CH), long(wide), long(wide), long(wide), long(wide), long(CH), long(wide), long(wide), long(wide), long(3 * wide),
            pltpu.VMEM((2, wide, TILE), half),
            pltpu.SemaphoreType.DMA((3,)),
            pltpu.SemaphoreType.DMA((2,)),
        ],
        compiler_params=pltpu.CompilerParams(vmem_limit_bytes=SUM_VMEM),
        name="head_pass",
    )(acts, vis_row, targets, noise, steps, embeds, w_cond, w_ada, w_io, w_in, w_out)


class Slab:
    def __init__(self, rows, cols, by_rows):
        self.rows, self.cols, self.by_rows = rows, cols, by_rows
        self.piece = (rows // 4, cols) if by_rows else (rows, cols // 4)

    def spot(self, shard, quarter, half=None):
        piece_rows, piece_cols = self.piece
        row = shard * self.rows
        if self.by_rows:
            row = row + quarter * piece_rows
        height = piece_rows
        if half is not None:
            height = piece_rows // 2
            row = row + half * height
        col = 0 if self.by_rows else quarter * piece_cols
        return (pl.ds(aligned(row, 16), height), pl.ds(aligned(col, 128), piece_cols))

    def shard(self, shard):
        return (pl.ds(aligned(shard * self.rows, 16), self.rows), pl.ds(0, self.cols))

    def within(self, quarter):
        return self.spot(0, quarter)


def aligned(value, multiple):
    return value if isinstance(value, int) else pl.multiple_of(value, multiple)


def place(depth):
    group, device = lax.axis_index("grp"), lax.axis_index("dev")
    level, core = device // 2, device % 2
    flip = lambda bit: group + (1 << bit) * (1 - 2 * ((group // (1 << bit)) % 2))
    return group, level, core, flip


def greet(peers):
    barrier = pltpu.get_barrier_semaphore()
    for peer in peers:
        pl.semaphore_signal(barrier, inc=1, device_id=peer, device_id_type=MESH)
    pl.semaphore_wait(barrier, len(peers))


def gather_kernel(slabs, depth, *refs):
    count = len(slabs)
    mine, whole = refs[:count], refs[count : 2 * count]
    sent, got, own_sent, own_got, own_copy = refs[2 * count :]
    group, level, core, flip = place(depth)
    x_peer, y_peer = (flip(0), 2 * level + core), (flip(1), 2 * level + core)
    partner = (group, 2 * level + 1 - core)

    def level_at(step):
        return lax.rem(level + step + depth, depth)

    z_peers = [(group, 2 * level_at(step) + core) for step in range(1, depth)]
    greet([x_peer, y_peer, partner] + z_peers)

    def move(kind, item, source, target, device):
        return pltpu.make_async_remote_copy(
            src_ref=source,
            dst_ref=target,
            send_sem=sent.at[kind, item],
            recv_sem=got.at[kind, item],
            device_id=device,
            device_id_type=MESH,
        )

    Z, X, Y, XH, YH, CORE = range(6)
    items = [(k, step) for k in range(count) for step in range(1, depth)]

    def by_z(item):
        k, step = items[item]
        slab = slabs[k]
        target = whole[k].at[slab.spot(2 * level + core, group)]
        return move(Z, item, mine[k].at[slab.within(group)], target, z_peers[step - 1])

    def shard_of(item):
        return 2 * level_at(-items[item][1]) + core

    def forward(kind, item, quarter, half, device):
        k = items[item][0]
        here = whole[k].at[slabs[k].spot(shard_of(item), quarter, half)]
        return move(kind, item, here, here, device)

    def core_copy(item, core_of):
        k, step = items[item]
        here = whole[k].at[slabs[k].shard(2 * level_at(-step) + core_of)]
        return move(CORE, item, here, here, partner)

    own = []
    for k, slab in enumerate(slabs):
        for step in range(1, depth):
            by_z(k * (depth - 1) + step - 1).start()
        target = whole[k].at[slab.shard(2 * level + core)]
        keep = pltpu.make_async_copy(mine[k], target, own_copy.at[k])
        keep.start()
        share = pltpu.make_async_remote_copy(
            src_ref=mine[k],
            dst_ref=target,
            send_sem=own_sent.at[k],
            recv_sem=own_got.at[k],
            device_id=partner,
            device_id_type=MESH,
        )
        share.start()
        own.append((keep, share))

    total = len(items)
    for turn in range(total + 2):
        if turn < total:
            k = items[turn][0]
            here = whole[k].at[slabs[k].spot(shard_of(turn), group)]
            move(Z, turn, here, here, x_peer).wait_recv()
            forward(X, turn, group, None, x_peer).start()
            forward(Y, turn, group, None, y_peer).start()
        item = turn - 1
        if 0 <= item < total:
            forward(X, item, flip(0), None, x_peer).wait_recv()
            forward(YH, item, flip(0), 0, y_peer).start()
            forward(Y, item, flip(1), None, y_peer).wait_recv()
            forward(XH, item, flip(1), 1, x_peer).start()
        item = turn - 2
        if 0 <= item < total:
            far = 3 - group
            forward(YH, item, far, 0, y_peer).wait_recv()
            forward(XH, item, far, 1, x_peer).wait_recv()
            core_copy(item, core).start()
    for item in range(total):
        by_z(item).wait_send()
        forward(X, item, group, None, x_peer).wait_send()
        forward(Y, item, group, None, y_peer).wait_send()
        forward(YH, item, flip(0), 0, y_peer).wait_send()
        forward(XH, item, flip(1), 1, x_peer).wait_send()
        core_copy(item, core).wait_send()
        core_copy(item, 1 - core).wait_recv()
    for keep, share in own:
        keep.wait()
        share.wait()


def gather_slabs(shards, slabs, depth):
    count, items = len(slabs), len(slabs) * (depth - 1)
    return pl.pallas_call(
        functools.partial(gather_kernel, slabs, depth),
        out_shape=[
            jax.ShapeDtypeStruct((2 * depth * s.rows, s.cols), jnp.bfloat16) for s in slabs
        ],
        in_specs=[pl.BlockSpec(memory_space=pl.ANY)] * count,
        out_specs=[pl.BlockSpec(memory_space=pl.ANY)] * count,
        scratch_shapes=[
            pltpu.SemaphoreType.DMA((6, items)),
            pltpu.SemaphoreType.DMA((6, items)),
            pltpu.SemaphoreType.DMA((count,)),
            pltpu.SemaphoreType.DMA((count,)),
            pltpu.SemaphoreType.DMA((count,)),
        ],
        compiler_params=pltpu.CompilerParams(collective_id=0, has_side_effects=True),
        name="gather_weights",
    )(*shards)


def sum_kernel(slabs, orders, depth, *refs):
    count = len(slabs)
    grads, outs = refs[:count], refs[count : 2 * count]
    rest = refs[2 * count :]
    take = lambda: (rest[:count], rest[count:])
    held, rest = take()
    from_first, rest = take()
    from_second, rest = take()
    from_level, rest = take()
    result, rest = take()
    stage, rest = take()
    stage_sem, out_sem, core_sent, core_got, sent, got, z_sent, z_got = rest
    group, level, core, flip = place(depth)
    me = 2 * level + core
    partner = (group, 2 * level + 1 - core)
    bit = lambda b: (group // (1 << b)) % 2

    def level_at(step):
        return lax.rem(level + step + depth, depth)

    z_peers = [(group, 2 * level_at(step) + core) for step in range(1, depth)]
    greet([(flip(0), me), (flip(1), me), partner] + z_peers)

    def move(pair, k, kind, source, target, device):
        send, receive = pair
        return pltpu.make_async_remote_copy(
            src_ref=source,
            dst_ref=target,
            send_sem=send.at[kind, k],
            recv_sem=receive.at[kind, k],
            device_id=device,
            device_id_type=MESH,
        )

    def core_move(k, lev):
        source = grads[k].at[slabs[k].shard(2 * lev + 1 - core)]
        return move((core_sent, core_got), k, lev, source, held[k].at[lev], partner)

    def rows_loop(height, body):
        step = 32 if height % 32 == 0 else 16

        def turn(i, carry):
            body(pl.ds(aligned(i * step, 16), step))
            return carry

        lax.fori_loop(0, height // step, turn, 0)

    def shifted(rows, by):
        return pl.ds(aligned(rows.start + by, 16), rows.size)

    def first_bit(k):
        return 1 if orders[k] == "yx" else 0

    def quarter(k, first, second):
        b = first_bit(k)
        return first * (1 << b) + second * (1 << (1 - b))

    def first_move(k, j):
        b = first_bit(k)
        where = slabs[k].within(quarter(k, 1 - bit(b), j))
        source = held[k].at[(level,) + where] if orders[k][0] == "z" else held[k].at[(slice(None),) + where]
        return move((sent, got), k, j, source, from_first[k].at[j], (flip(b), me))

    def second_move(k):
        b = first_bit(k)
        where = slabs[k].within(quarter(k, bit(b), 1 - bit(1 - b)))
        source = held[k].at[(level,) + where] if orders[k][0] == "z" else held[k].at[(slice(None),) + where]
        return move((sent, got), k, 2, source, from_second[k], (flip(1 - b), me))

    def level_move(k, step):
        lev = level_at(step)
        source = held[k].at[lev] if orders[k][0] == "z" else held[k].at[(lev,) + slabs[k].within(group)]
        return move((z_sent, z_got), k, step - 1, source, from_level[k].at[step - 1], z_peers[step - 1])

    def spread_second(k, whose):
        here = result[k].at[slabs[k].within(whose)]
        return move((sent, got), k, 3, here, here, (flip(1 - first_bit(k)), me))

    def spread_first(k, j, whose):
        here = result[k].at[slabs[k].within(whose)]
        return move((sent, got), k, 4 + j, here, here, (flip(first_bit(k)), me))

    def out_copy(k):
        return pltpu.make_async_copy(result[k], outs[k], out_sem.at[k])

    def stage_copy(k, lev):
        source = grads[k].at[slabs[k].shard(2 * lev + core)]
        return pltpu.make_async_copy(source, stage[k].at[lev % 2], stage_sem.at[k, lev % 2])

    def add_core(k):
        slab = slabs[k]
        stage_copy(k, 0).start()
        for lev in range(depth):
            if lev + 1 < depth:
                stage_copy(k, lev + 1).start()
            core_move(k, lev).wait_recv()
            stage_copy(k, lev).wait()

            def body(rows):
                total = held[k][lev, rows, :].astype(jnp.float32) + stage[k][lev % 2, rows, :].astype(jnp.float32)
                held[k][lev, rows, :] = total.astype(jnp.bfloat16)

            rows_loop(slab.rows, body)

    def levels_of(k):
        return [level] if orders[k][0] == "z" else list(range(depth))

    def add_first(k):
        slab = slabs[k]
        for j in range(2):
            first_move(k, j).wait_recv()
            rows_of, cols = slab.within(quarter(k, bit(first_bit(k)), j))
            for lev in levels_of(k):

                def body(rows):
                    at = (lev, shifted(rows, rows_of.start), cols)
                    extra = from_first[k][j, rows, :] if orders[k][0] == "z" else from_first[k][j, lev, rows, :]
                    held[k][at] = (held[k][at].astype(jnp.float32) + extra.astype(jnp.float32)).astype(jnp.bfloat16)

                rows_loop(slab.piece[0], body)

    def add_second(k):
        slab = slabs[k]
        second_move(k).wait_recv()
        rows_of, cols = slab.within(group)
        for lev in levels_of(k):

            def body(rows):
                at = (lev, shifted(rows, rows_of.start), cols)
                extra = from_second[k][rows, :] if orders[k][0] == "z" else from_second[k][lev, rows, :]
                total = held[k][at].astype(jnp.float32) + extra.astype(jnp.float32)
                target = result[k].at[shifted(rows, rows_of.start), cols] if orders[k][0] == "z" else held[k].at[at]
                target[...] = total.astype(jnp.bfloat16)

            rows_loop(slab.piece[0], body)

    def add_level(k):
        slab = slabs[k]
        for step in range(1, depth):
            level_move(k, step).wait_recv()
        if orders[k][0] == "z":

            def body(rows):
                total = held[k][level, rows, :].astype(jnp.float32)
                for step in range(depth - 1):
                    total = total + from_level[k][step, rows, :].astype(jnp.float32)
                held[k][level, rows, :] = total.astype(jnp.bfloat16)

            rows_loop(slab.rows, body)
            return
        rows_of, cols = slab.within(group)

        def body(rows):
            at = (shifted(rows, rows_of.start), cols)
            total = held[k][(level,) + at].astype(jnp.float32)
            for step in range(depth - 1):
                total = total + from_level[k][step, rows, :].astype(jnp.float32)
            result[k][at] = total.astype(jnp.bfloat16)

        rows_loop(slab.piece[0], body)

    def begin_core(k):
        for lev in range(depth):
            core_move(k, lev).start()

    def begin_first(k):
        first_move(k, 0).start()
        first_move(k, 1).start()

    def begin_level(k):
        for step in range(1, depth):
            level_move(k, step).start()

    def end_spread_second(k):
        spread_second(k, flip(1 - first_bit(k))).wait_recv()
        spread_first(k, 0, group).start()
        spread_first(k, 1, flip(1 - first_bit(k))).start()

    def end_spread_first(k):
        b = first_bit(k)
        spread_first(k, 0, flip(b)).wait_recv()
        spread_first(k, 1, 3 - group).wait_recv()
        out_copy(k).start()

    def steps(k):
        if orders[k][0] == "z":
            return [
                lambda: (add_core(k), begin_level(k)),
                lambda: (add_level(k), begin_first(k)),
                lambda: (add_first(k), second_move(k).start()),
                lambda: (add_second(k), spread_second(k, group).start()),
                lambda: end_spread_second(k),
                lambda: end_spread_first(k),
            ]
        return [
            lambda: (add_core(k), begin_first(k)),
            lambda: (add_first(k), second_move(k).start()),
            lambda: (add_second(k), begin_level(k)),
            lambda: (add_level(k), spread_second(k, group).start()),
            lambda: end_spread_second(k),
            lambda: end_spread_first(k),
        ]

    plans = [steps(k) for k in range(count)]
    begin_core(0)
    for turn in range(count + 5):
        if turn + 1 < count:
            begin_core(turn + 1)
        for place_in in range(6):
            k = turn - place_in
            if 0 <= k < count:
                plans[k][place_in]()
    for k in range(count):
        for lev in range(depth):
            core_move(k, lev).wait_send()
        first_move(k, 0).wait_send()
        first_move(k, 1).wait_send()
        second_move(k).wait_send()
        for step in range(1, depth):
            level_move(k, step).wait_send()
        spread_second(k, group).wait_send()
        spread_first(k, 0, group).wait_send()
        spread_first(k, 1, flip(1 - first_bit(k))).wait_send()
        out_copy(k).wait()


def sum_slabs(grads, slabs, orders, depth):
    count = len(slabs)
    half = jnp.bfloat16
    held, first, second, lev, result, stage = [], [], [], [], [], []
    for slab, order in zip(slabs, orders, strict=True):
        shard = (slab.rows, slab.cols)
        held.append(pltpu.VMEM((depth,) + shard, half))
        result.append(pltpu.VMEM(shard, half))
        stage.append(pltpu.VMEM((2,) + shard, half))
        if order[0] == "z":
            first.append(pltpu.VMEM((2,) + slab.piece, half))
            second.append(pltpu.VMEM(slab.piece, half))
            lev.append(pltpu.VMEM((depth - 1,) + shard, half))
        else:
            first.append(pltpu.VMEM((2, depth) + slab.piece, half))
            second.append(pltpu.VMEM((depth,) + slab.piece, half))
            lev.append(pltpu.VMEM((depth - 1,) + slab.piece, half))
    dma = pltpu.SemaphoreType.DMA
    return pl.pallas_call(
        functools.partial(sum_kernel, slabs, orders, depth),
        out_shape=[jax.ShapeDtypeStruct((s.rows, s.cols), half) for s in slabs],
        in_specs=[pl.BlockSpec(memory_space=pl.ANY)] * count,
        out_specs=[pl.BlockSpec(memory_space=pl.ANY)] * count,
        scratch_shapes=held
        + first
        + second
        + lev
        + result
        + stage
        + [
            dma((count, 2)),
            dma((count,)),
            dma((depth, count)),
            dma((depth, count)),
            dma((6, count)),
            dma((6, count)),
            dma((depth - 1, count)),
            dma((depth - 1, count)),
        ],
        compiler_params=pltpu.CompilerParams(
            collective_id=1, has_side_effects=True, vmem_limit_bytes=SUM_VMEM
        ),
        name="sum_gradients",
    )(*grads)


class Gathering:
    def __init__(self, slabs, depth, mine, whole, sems):
        self.slabs, self.depth, self.mine, self.whole = slabs, depth, mine, whole
        self.sent, self.got, self.own_sent, self.own_got, self.own_copy = sems
        self.group, self.level, self.core, self.flip = place(depth)
        me = 2 * self.level + self.core
        self.peers = ((self.flip(0), me), (self.flip(1), me), (self.group, 2 * self.level + 1 - self.core))
        self.items = [(k, step) for k in range(len(slabs)) for step in range(1, depth)]
        self.turn = 0
        self.turns = len(self.items) + 2

    def level_at(self, step):
        return lax.rem(self.level + step + self.depth, self.depth)

    def move(self, kind, item, source, target, device):
        return pltpu.make_async_remote_copy(
            src_ref=source,
            dst_ref=target,
            send_sem=self.sent.at[kind, item],
            recv_sem=self.got.at[kind, item],
            device_id=device,
            device_id_type=MESH,
        )

    def z_peer(self, step):
        return (self.group, 2 * self.level_at(step) + self.core)

    def along_z(self, item):
        k, step = self.items[item]
        slab = self.slabs[k]
        target = self.whole[k].at[slab.spot(2 * self.level + self.core, self.group)]
        return self.move(0, item, self.mine[k].at[slab.within(self.group)], target, self.z_peer(step))

    def onward(self, kind, item, quarter, half, device):
        k, step = self.items[item]
        shard = 2 * self.level_at(-step) + self.core
        here = self.whole[k].at[self.slabs[k].spot(shard, quarter, half)]
        return self.move(kind, item, here, here, device)

    def to_core(self, item, core):
        k, step = self.items[item]
        here = self.whole[k].at[self.slabs[k].shard(2 * self.level_at(-step) + core)]
        return self.move(5, item, here, here, self.peers[2])

    def own(self, k):
        target = self.whole[k].at[self.slabs[k].shard(2 * self.level + self.core)]
        share = pltpu.make_async_remote_copy(
            src_ref=self.mine[k],
            dst_ref=target,
            send_sem=self.own_sent.at[k],
            recv_sem=self.own_got.at[k],
            device_id=self.peers[2],
            device_id_type=MESH,
        )
        return pltpu.make_async_copy(self.mine[k], target, self.own_copy.at[k]), share

    def start(self):
        greet([*self.peers, *(self.z_peer(step) for step in range(1, self.depth))])
        for item in range(len(self.items)):
            self.along_z(item).start()
            if self.items[item][1] == 1:
                for copy in self.own(self.items[item][0]):
                    copy.start()

    def pump(self, until):
        group, flip = self.group, self.flip
        x_peer, y_peer, _ = self.peers
        total = len(self.items)
        while self.turn < min(until, self.turns):
            item = self.turn
            if item < total:
                self.onward(0, item, group, None, x_peer).wait_recv()
                self.onward(1, item, group, None, x_peer).start()
                self.onward(2, item, group, None, y_peer).start()
            item = self.turn - 1
            if 0 <= item < total:
                self.onward(1, item, flip(0), None, x_peer).wait_recv()
                self.onward(4, item, flip(0), 0, y_peer).start()
                self.onward(2, item, flip(1), None, y_peer).wait_recv()
                self.onward(3, item, flip(1), 1, x_peer).start()
            item = self.turn - 2
            if 0 <= item < total:
                self.onward(4, item, 3 - group, 0, y_peer).wait_recv()
                self.onward(3, item, 3 - group, 1, x_peer).wait_recv()
                self.to_core(item, self.core).start()
            self.turn += 1

    def ready_at(self, k):
        return (k + 1) * (self.depth - 1) + 2

    def take(self, k):
        self.pump(self.ready_at(k))
        for item, (slab, _) in enumerate(self.items):
            if slab == k:
                self.to_core(item, 1 - self.core).wait_recv()
        keep, share = self.own(k)
        keep.wait()
        share.wait_recv()

    def finish(self):
        group, flip = self.group, self.flip
        x_peer, y_peer, _ = self.peers
        for item in range(len(self.items)):
            self.along_z(item).wait_send()
            self.onward(1, item, group, None, x_peer).wait_send()
            self.onward(2, item, group, None, y_peer).wait_send()
            self.onward(4, item, flip(0), 0, y_peer).wait_send()
            self.onward(3, item, flip(1), 1, x_peer).wait_send()
            self.to_core(item, self.core).wait_send()
        for k in range(len(self.slabs)):
            self.own(k)[1].wait_send()


def unpack_vectors(small, parts, width, vec):
    piece = width // parts
    vec[...] = jnp.zeros_like(vec)
    lane = lax.broadcasted_iota(jnp.int32, (128, width), 0)
    col = lax.broadcasted_iota(jnp.int32, (128, width), 1)
    for part in range(parts):
        spread = ((col == lane + part * piece) & (lane < piece)).astype(jnp.bfloat16)
        vec[...] += matmul(small[pl.ds(part * SMALL_ROWS, CH), :128], spread)


def first_kernel(slabs, depth, *refs):
    count = len(slabs)
    mine, refs = refs[:count], refs[count:]
    embedded, vis_col, vis_row, steps, freqs = refs[:5]
    whole, refs = refs[5 : 5 + count], refs[5 + count :]
    kept_hbm, (acts, vec, w_in, w_out, embeds_hbm), refs = refs[:10], refs[10:15], refs[15:]
    sems, refs = refs[:5], refs[5:]
    small, (e_a, e_u, e_d, d_a, d_u, d_d) = refs[0], refs[1:7]
    e_kept, d_kept = refs[7:12], refs[12:17]
    embeds, e_out, d_out, e_low, d_low, load_sems, kept_sems = refs[17:]
    width = embedded.shape[1]
    parts = 2 * depth
    gathering = Gathering(slabs, depth, mine, whole, sems)
    gathering.start()
    half, height = freqs.shape[1], 64
    pieces = steps.shape[0] // height
    enc_turn, dec_turn = gathering.ready_at(3), gathering.ready_at(6)
    encode(embedded, vis_col, None, e_kept[0])
    for piece in range(pieces):
        gathering.pump(piece * enc_turn // pieces)
        rows = pl.ds(piece * height, height)
        phase = steps[rows, :].astype(jnp.float32) * freqs[...]
        embeds[rows, :half] = jnp.cos(phase)
        embeds[rows, half:] = jnp.sin(phase)
    copies = [pltpu.make_async_copy(embeds, embeds_hbm, kept_sems.at[10])]
    copies[0].start()

    def fetch(slots):
        loads = []
        for slab, target in slots:
            gathering.take(slab)
            load = pltpu.make_async_copy(whole[slab], target, load_sems.at[slab])
            load.start()
            loads.append(load)
        return loads

    def run(steps_of, turn, last):
        steps_of = list(steps_of)
        for i, step in enumerate(steps_of):
            step()
            gathering.pump(turn + (last - turn) * (i + 1) // len(steps_of))

    def keep(kept, at):
        for i, buffer in enumerate(kept):
            copy = pltpu.make_async_copy(buffer, kept_hbm[at + i], kept_sems.at[at + i])
            copy.start()
            copies.append(copy)

    for load in fetch([(0, small), (1, e_a), (2, e_u), (3, e_d)]):
        load.wait()
    unpack_vectors(small, parts, width, vec)
    for part in range(parts):
        block = pl.ds(part * SMALL_ROWS, CH)
        w_in[:, pl.ds(part * 128, 128)] = small[block, pl.ds(128, 128)]
        w_out[:, pl.ds(part * 128, 128)] = small[block, pl.ds(256, 128)]
    live = live_keys(vis_row)
    run(forward_steps(width, e_kept[0], vec[0:1, :], vec[1:2, :], e_a, e_u, e_d, *e_kept[1:], e_out, e_low, live), enc_turn, dec_turn)
    keep(e_kept, 0)
    spread_rows(vis_row, e_out, vec, d_kept[0])
    for load in fetch([(4, d_a), (5, d_u), (6, d_d)]):
        load.wait()
    run(forward_steps(width, d_kept[0], vec[2:3, :], vec[3:4, :], d_a, d_u, d_d, *d_kept[1:], d_out, d_low), dec_turn, gathering.turns)
    keep(d_kept, 5)
    acts[...] = d_out[...].astype(jnp.bfloat16)
    for slab in range(7, count):
        gathering.take(slab)
    gathering.finish()
    for copy in copies:
        copy.wait()


def first_part(shards, slabs, depth, embedded, vis_col, vis_row, steps, freqs):
    tokens, width = embedded.shape
    count, items = len(slabs), len(slabs) * (depth - 1)
    inner = slabs[2].cols
    rows = BUFFER + vis_col.shape[0]
    flat, wide = steps.shape[0], 2 * freqs.shape[1]
    f32, half = jnp.float32, jnp.bfloat16
    whole, anywhere = pl.BlockSpec(memory_space=pltpu.VMEM), pl.BlockSpec(memory_space=pl.ANY)
    shape, dma = jax.ShapeDtypeStruct, pltpu.SemaphoreType.DMA
    gathered = [shape((2 * depth * s.rows, s.cols), half) for s in slabs]

    def kept(height):
        return [
            shape((height, width), f32),
            shape((height, 3 * width), half),
            shape((height, width), half),
            shape((height, width), f32),
            shape((height, inner), f32),
        ]

    saved = kept(rows) + kept(tokens)
    outs = gathered + saved
    outs += [shape((tokens, width), half), shape((CH, width), f32), shape((CH, wide), half), shape((CH, wide), half), shape((flat, wide), f32)]
    found = pl.pallas_call(
        functools.partial(first_kernel, slabs, depth),
        out_shape=outs,
        in_specs=[anywhere] * count + [whole] * 5,
        out_specs=[anywhere] * (count + 10) + [whole] * 4 + [anywhere],
        scratch_shapes=[dma((6, items)), dma((6, items)), dma((count,)), dma((count,)), dma((count,))]
        + [pltpu.VMEM(s.shape, s.dtype) for s in (*gathered[:7], *saved)]
        + [
            pltpu.VMEM((flat, wide), f32),
            pltpu.VMEM((rows, width), f32),
            pltpu.VMEM((tokens, width), f32),
            pltpu.VMEM((rows, width), half),
            pltpu.VMEM((tokens, width), half),
            dma((count,)),
            dma((11,)),
        ],
        compiler_params=pltpu.CompilerParams(collective_id=0, has_side_effects=True, vmem_limit_bytes=SUM_VMEM),
        name="gather_and_forward",
    )(*shards, embedded, vis_col, vis_row, steps, freqs)
    slabs_found, found = found[:count], found[count:]
    return slabs_found, found[:5], found[5:10], *found[10:]


SMALL_ROWS, SMALL_COLS = 32, 512


def pack_small(vectors, first, last):
    parts = vectors[0].shape[0] // 96
    lanes = jnp.stack([v.reshape(parts, 96) for v in vectors], axis=1)
    lanes = jnp.pad(lanes, ((0, 0), (0, CH - len(vectors)), (0, 128 - 96)))
    wide = [w.reshape(CH, parts, 128).transpose(1, 0, 2) for w in (first, last)]
    packed = jnp.concatenate([lanes, *wide], axis=2)
    packed = jnp.pad(packed, ((0, 0), (0, SMALL_ROWS - CH), (0, SMALL_COLS - 384)))
    return packed.reshape(parts * SMALL_ROWS, SMALL_COLS)


def unpack_small(packed):
    parts = packed.shape[0] // SMALL_ROWS
    packed = packed.reshape(parts, SMALL_ROWS, SMALL_COLS)
    vectors = packed[:, :5, :96].transpose(1, 0, 2).reshape(5, parts * 96)
    wide = [packed[:, :CH, 128 * i : 128 * i + 128].transpose(1, 0, 2).reshape(CH, parts * 128) for i in (1, 2)]
    return vectors, wide[0], wide[1]


SLABS = (
    Slab(SMALL_ROWS, SMALL_COLS, False),
    Slab(96, 3072, False),
    Slab(96, 3072, False),
    Slab(384, 768, True),
    Slab(96, 3072, False),
    Slab(96, 3072, False),
    Slab(384, 768, True),
    Slab(96, 1024, False),
    Slab(128, 3072, False),
    Slab(128, 2048, False),
)


def by_links():
    return lax.axis_size("dev") == 8 and lax.axis_size("grp") == 4


def packed_shards(shards):
    (e_one, e_qkv, e_proj, e_two, e_up, e_down, d_one, d_qkv, d_proj, d_two, d_up, d_down, fill, h_in, h_cond, h_ada, h_inner, h_outer, h_out) = shards
    large = (
        jnp.concatenate([e_qkv, e_proj], axis=1), e_up, e_down,
        jnp.concatenate([d_qkv, d_proj], axis=1), d_up, d_down,
        h_cond, h_ada, jnp.concatenate([h_inner, h_outer], axis=1),
    )
    return large, [e_one, e_two, d_one, d_two, fill], h_in, h_out


def gather_weights(shards):
    packed, vectors, h_in, h_out = packed_shards(shards)
    whole = lambda w, axis=0: lax.all_gather(w, "dev", axis=axis, tiled=True)
    return [whole(w) for w in packed], whole(jnp.stack(vectors), 1), whole(h_in, 1), whole(h_out).T


def sum_gradients(slabs, vectors, d_in, d_out):
    if by_links():
        packed = (pack_small(list(vectors), d_in, d_out).astype(jnp.bfloat16), *slabs)
        turn = (8, 9, 7, 4, 5, 6, 1, 2, 3, 0)
        orders = ("xy", "yx", "zx", "xy", "yx", "zx", "yx", "xy", "yx", "xy")
        sums = sum_slabs([packed[t] for t in turn], [SLABS[t] for t in turn], [orders[t] for t in turn], lax.axis_size("dev") // 2)
        back = [None] * len(turn)
        for t, s in zip(turn, sums, strict=True):
            back[t] = s
        small, *slabs = back
        vectors, d_in, d_out = unpack_small(small)
    else:

        def scatter(grad, axis=0):
            part = lax.psum_scatter(grad.astype(jnp.float32), "dev", scatter_dimension=axis, tiled=True)
            return lax.psum(part.astype(jnp.bfloat16), "grp")

        slabs = [scatter(g) for g in slabs]
        vectors, d_in, d_out = scatter(vectors, 1), scatter(d_in, 1), scatter(d_out, 1)
    ea, eu, ed, da, du, dd, hc, ha, hio = (s.astype(jnp.float32) for s in slabs)
    vectors, d_in, d_out = (s.astype(jnp.float32) for s in (vectors, d_in, d_out))
    split = 3 * ed.shape[1]
    return (vectors[0], ea[:, :split], ea[:, split:], vectors[1], eu, ed, vectors[2], da[:, :split], da[:, split:], vectors[3], du, dd,
            vectors[4], d_in, hc, ha, hio[:, :HW], hio[:, HW:], d_out.T)


def per_device(embedded, mask_order, counts, targets, noise_copies, timesteps, *shards):
    images, tokens, width = embedded.shape
    seq_len = mask_order.shape[1]
    linked = by_links() and images == 1
    if not linked:
        slabs, vectors, w_in, w_out = gather_weights(shards)
        vec = jnp.pad(vectors.astype(jnp.float32), ((0, CH - 5), (0, 0)))
    freqs = jnp.exp(-math.log(10000.0) * jnp.arange(HW // 2, dtype=jnp.float32) / (HW // 2)).reshape(1, HW // 2)
    losses, acts_of, embed_grads, totals = [], [], [], None
    for image in range(images):
        padded = jnp.concatenate([mask_order[image], jnp.full((SPOTS,), -1, jnp.int32)])
        seen = lax.dynamic_slice(padded, (counts[image],), (SPOTS,))
        vis_col, vis_row = seen.reshape(SPOTS, 1), seen.reshape(1, SPOTS)
        steps = timesteps[image].T.reshape(COPIES * seq_len, 1)
        noise = noise_copies[image].transpose(1, 0, 2).reshape(COPIES * seq_len, CH)
        if linked:
            packed, vectors, h_in, h_out = packed_shards(shards)
            (_, *slabs), enc_kept, dec_kept, acts, vec, w_in, w_out, embeds = first_part(
                (pack_small(vectors, h_in, h_out.T), *packed), SLABS, lax.axis_size("dev") // 2,
                embedded[image], vis_col, vis_row, steps, freqs,
            )
        else:
            phase = steps.astype(jnp.float32) * freqs
            embeds = jnp.concatenate([jnp.cos(phase), jnp.sin(phase)], axis=1)
            enc_kept, dec_kept, acts = forward_blocks(embedded[image], vis_col, vis_row, vec, slabs[:6])
        grad_rows, loss, d_in, d_out, *head_grads = head_pass(
            acts, vis_row, targets[image], noise, steps, embeds, *slabs[6:], w_in, w_out
        )
        embed_grad, small, block_grads = backward_blocks(grad_rows, vis_col, vis_row, vec, enc_kept, dec_kept, slabs[:6])
        found = ([*block_grads, *head_grads], small[:5], d_in, d_out)
        totals = found if totals is None else jax.tree.map(jnp.add, totals, found)
        losses.append(loss[0, 0] / (counts[image].astype(jnp.float32) * (COPIES * CH)))
        acts_of.append(acts)
        embed_grads.append(embed_grad)
    return (jnp.stack(losses), jnp.stack(acts_of), jnp.stack(embed_grads), *sum_gradients(*totals))


def solution(mesh):
    return jax.shard_map(
        per_device,
        mesh=mesh,
        in_specs=(
            P(("grp", "dev"), None, None),
            P(("grp", "dev"), None),
            P(("grp", "dev")),
            P(("grp", "dev"), None, None),
            P(("grp", "dev"), None, None, None),
            P(("grp", "dev"), None, None),
            P("dev"),
            P("dev", None),
            P("dev", None),
            P("dev"),
            P("dev", None),
            P("dev", None),
            P("dev"),
            P("dev", None),
            P("dev", None),
            P("dev"),
            P("dev", None),
            P("dev", None),
            P("dev"),
            P(None, "dev"),
            P("dev", None),
            P("dev", None),
            P("dev", None),
            P("dev", None),
            P("dev", None),
        ),
        out_specs=(
            P(("grp", "dev")),
            P(("grp", "dev"), None, None),
            P(("grp", "dev"), None, None),
            P("dev"),
            P("dev", None),
            P("dev", None),
            P("dev"),
            P("dev", None),
            P("dev", None),
            P("dev"),
            P("dev", None),
            P("dev", None),
            P("dev"),
            P("dev", None),
            P("dev", None),
            P("dev"),
            P(None, "dev"),
            P("dev", None),
            P("dev", None),
            P("dev", None),
            P("dev", None),
            P("dev", None),
        ),
        check_vma=False,
    )
```

```python
import functools
import math

import jax
import jax.numpy as jnp
from jax import lax
from jax.experimental import pallas as pl
from jax.experimental.pallas import tpu as pltpu
from jax.sharding import PartitionSpec as P

MESH = pl.DeviceIdType.MESH
SUM_VMEM = 60 * 1024 * 1024
LAST_VMEM = 62 * 1024 * 1024
HW = 1024
CH = 16
COPIES = 4
STEPS_T = 1000
BUFFER = 64
SPOTS = 80
EPSILON = 1e-06
NEG_FILL = -1e30


def matmul(left, right):
    return jnp.dot(left, right, preferred_element_type=jnp.float32)


def right_trans(left, right):
    return lax.dot_general(
        left, right, (((1,), (1,)), ((), ())), preferred_element_type=jnp.float32
    )


def norm_rows(values):
    centre = values - jnp.mean(values, axis=-1, keepdims=True)
    inv_std = lax.rsqrt(jnp.mean(centre * centre, axis=-1, keepdims=True) + EPSILON)
    return (centre * inv_std, inv_std)


def norm_back(grad, normed, inv_std):
    mean_grad = jnp.mean(grad, axis=-1, keepdims=True)
    mean_cross = jnp.mean(grad * normed, axis=-1, keepdims=True)
    return inv_std * (grad - mean_grad - normed * mean_cross)


def silu_slope(values):
    sigma = jax.nn.sigmoid(values)
    return sigma * (1.0 + values * (1.0 - sigma))


def noise_angle(steps):
    return (steps.astype(jnp.float32) / STEPS_T + 0.008) / 1.008 * (math.pi / 2)


ROOT_HALF = 1.0 / math.sqrt(2.0)
TILE = 512
STEP = 16


def rows_dot(left, right):
    return lax.dot_general(left, right, (((0,), (0,)), ((), ())), preferred_element_type=jnp.float32)


def loop(count, body):
    def turn(i, carry):
        body(i)
        return carry

    lax.fori_loop(0, count, turn, 0)


def at_step(i, size=STEP):
    return pl.ds(pl.multiple_of(i * size, size), size)


def at_col(i, size):
    return pl.ds(pl.multiple_of(i * size, 128), size)


def exact_dot(ones, values):
    high = values.astype(jnp.bfloat16)
    rest = values - high.astype(jnp.float32)
    middle = rest.astype(jnp.bfloat16)
    low = (rest - middle.astype(jnp.float32)).astype(jnp.bfloat16)
    return matmul(ones, high) + matmul(ones, middle) + matmul(ones, low)


def scale_norm(source, gain, target):
    normed, _ = norm_rows(source[...])
    target[...] = (normed * gain).astype(jnp.bfloat16)


def head_mask(half):
    lane = lax.broadcasted_iota(jnp.int32, (1, 128), 1)
    return (lane < 64) if half == 0 else (lane >= 64)


def keep_half(values, half):
    return jnp.where(head_mask(half), values, jnp.zeros((), values.dtype))


def probabilities(query, key, half, bias):
    scores = right_trans(keep_half(query, half), key) * 0.125
    if bias is not None:
        scores = jnp.where(bias, scores, NEG_FILL)
    grown = jnp.exp(scores - jnp.max(scores, axis=-1, keepdims=True))
    return grown / jnp.sum(grown, axis=-1, keepdims=True)


def forward_steps(width, stream, gain_one, gain_two, w_a, w_up, w_down, qkv, mixed, middle, up, out, low, live=None):
    def project(j):
        cols = pl.ds(j * width, width)
        qkv[:, cols] = matmul(low[...], w_a[:, cols]).astype(jnp.bfloat16)

    def attend(pair):
        query, key, value = (qkv[:, pl.ds(pair * 128 + part * width, 128)] for part in range(3))
        parts = [
            matmul(probabilities(query, key, half, live).astype(jnp.bfloat16), value) for half in range(2)
        ]
        mixed[:, pl.ds(pair * 128, 128)] = jnp.where(head_mask(0), parts[0], parts[1]).astype(jnp.bfloat16)

    def mix():
        middle[...] = stream[...] + matmul(mixed[...], w_a[:, 3 * width :])
        scale_norm(middle, gain_two, low)

    def feed(j):
        cols = pl.ds(j * TILE, TILE)
        raised = matmul(low[...], w_up[:, cols])
        up[:, cols] = raised
        act = (raised * (0.5 + 0.5 * lax.erf(raised * ROOT_HALF))).astype(jnp.bfloat16)
        out[...] = (middle[...] if j == 0 else out[...]) + matmul(act, w_down[cols, :])

    yield lambda: scale_norm(stream, gain_one, low)
    for j in range(3):
        yield functools.partial(project, j)
    for pair in range(width // 128):
        yield functools.partial(attend, pair)
    yield mix
    for j in range(w_up.shape[1] // TILE):
        yield functools.partial(feed, j)


def forward_block(*args):
    for step in forward_steps(*args):
        step()


def forward_kernel(*refs):
    (embedded, vis_col, vis_row, vec, e_a_hbm, e_u_hbm, e_d_hbm, d_a_hbm, d_u_hbm, d_d_hbm,
     e_in, e_qkv, e_mixed, e_mid, e_up, d_in, d_qkv, d_mixed, d_mid, d_up, acts,
     e_a, e_u, e_d, d_a, d_u, d_d, e_out, d_out, e_low, d_low, sems) = refs
    width = embedded.shape[1]
    loads = [
        pltpu.make_async_copy(a, b, sems.at[i])
        for i, (a, b) in enumerate(
            [(e_a_hbm, e_a), (e_u_hbm, e_u), (e_d_hbm, e_d), (d_a_hbm, d_a), (d_u_hbm, d_u), (d_d_hbm, d_d)]
        )
    ]
    for load in loads:
        load.start()
    encode(embedded, vis_col, vec, e_in)
    for load in loads[:3]:
        load.wait()
    live = live_keys(vis_row)
    forward_block(width, e_in, vec[0:1, :], vec[1:2, :], e_a, e_u, e_d, e_qkv, e_mixed, e_mid, e_up, e_out, e_low, live)
    spread_rows(vis_row, e_out, vec, d_in)
    for load in loads[3:]:
        load.wait()
    forward_block(width, d_in, vec[2:3, :], vec[3:4, :], d_a, d_u, d_d, d_qkv, d_mixed, d_mid, d_up, d_out, d_low)
    acts[...] = d_out[...].astype(jnp.bfloat16)


def token_hot(vis_col, count):
    return (lax.broadcasted_iota(jnp.int32, (vis_col.shape[0], count), 1) == vis_col[...]).astype(jnp.bfloat16)


def spot_hot(vis_row, count):
    return (lax.broadcasted_iota(jnp.int32, (count, vis_row.shape[1]), 0) == vis_row[...]).astype(jnp.bfloat16)


def live_keys(vis_row):
    ones = jnp.ones((1, BUFFER), jnp.int32)
    return jnp.concatenate([ones, (vis_row[...] >= 0).astype(jnp.int32)], axis=1) > 0


def encode(embedded, vis_col, vec, target):
    tokens = embedded.shape[0] - BUFFER
    target[:BUFFER, :] = embedded[:BUFFER, :].astype(jnp.float32)
    target[BUFFER:, :] = matmul(token_hot(vis_col, tokens), embedded[BUFFER:, :])


def spread_rows(vis_row, enc_out, vec, target):
    tokens = target.shape[0] - BUFFER
    hot = spot_hot(vis_row, tokens)
    masked = 1.0 - jnp.sum(hot.astype(jnp.float32), axis=1, keepdims=True)
    target[:BUFFER, :] = enc_out[:BUFFER, :]
    target[BUFFER:, :] = exact_dot(hot, enc_out[BUFFER:, :]) + masked * vec[4:5, :]


def forward_blocks(embedded, vis_col, vis_row, vec, weights):
    tokens, width = embedded.shape
    inner = weights[1].shape[1]
    rows = BUFFER + vis_col.shape[0]
    f32, half = jnp.float32, jnp.bfloat16

    def kept(count):
        return [
            jax.ShapeDtypeStruct((count, width), f32),
            jax.ShapeDtypeStruct((count, 3 * width), half),
            jax.ShapeDtypeStruct((count, width), half),
            jax.ShapeDtypeStruct((count, width), f32),
            jax.ShapeDtypeStruct((count, inner), f32),
        ]

    outs = kept(rows) + kept(tokens) + [jax.ShapeDtypeStruct((tokens, width), half)]
    whole = pl.BlockSpec(memory_space=pltpu.VMEM)
    found = pl.pallas_call(
        forward_kernel,
        out_shape=outs,
        in_specs=[whole] * 4 + [pl.BlockSpec(memory_space=pl.ANY)] * 6,
        out_specs=[whole] * len(outs),
        scratch_shapes=[pltpu.VMEM(w.shape, half) for w in weights]
        + [
            pltpu.VMEM((rows, width), f32),
            pltpu.VMEM((tokens, width), f32),
            pltpu.VMEM((rows, width), half),
            pltpu.VMEM((tokens, width), half),
            pltpu.SemaphoreType.DMA((6,)),
        ],
        compiler_params=pltpu.CompilerParams(vmem_limit_bytes=SUM_VMEM),
        name="forward_blocks",
    )(embedded, vis_col, vis_row, vec, *weights)
    return found[:5], found[5:10], found[10]


def norm_back_into(grads, source, gain, add, target, gain_grad):
    gain_grad[...] = jnp.zeros_like(gain_grad)
    height = 64 if source.shape[0] % 64 == 0 else 48

    def body(i):
        rows = at_step(i, height)
        normed, inv_std = norm_rows(source[rows, :])
        grad = grads[rows, :]
        gain_grad[...] += jnp.broadcast_to(jnp.sum(grad * normed, axis=0, keepdims=True), gain_grad.shape)
        target[rows, :] = add[rows, :] + norm_back(grad * gain, normed, inv_std)

    loop(source.shape[0] // height, body)


class Tiles:
    def __init__(self, slots, sems):
        self.slots, self.sems = slots, sems

    def put(self, i, value, target):
        slot = i % 2 if isinstance(i, int) else lax.rem(i, 2)
        copy = pltpu.make_async_copy(self.slots.at[slot], target, self.sems.at[slot])

        @pl.when(i >= 2)
        def _():
            copy.wait()

        self.slots[slot] = value.astype(jnp.bfloat16)
        copy.start()

    def flush(self, like):
        for slot in range(2):
            pltpu.make_async_copy(self.slots.at[slot], like, self.sems.at[slot]).wait()


def backward_block(width, grad, stream, gain_one, gain_two, w_a, w_up, w_down, qkv, mixed, middle, up,
                   d_a, d_up, d_down, d_one, d_two, grad_low, low, grad_qkv, acc, grad_mid, out, tiles, live=None):
    rows = grad.shape[0]
    wide, narrow, square = tiles
    grad_low[...] = grad[...].astype(jnp.bfloat16)
    scale_norm(middle, gain_two, low)
    acc[...] = jnp.zeros_like(acc)
    count = w_up.shape[1] // TILE

    def feed(j):
        raised = up[:, at_col(j, TILE)]
        cumul = 0.5 + 0.5 * lax.erf(raised * ROOT_HALF)
        slope = cumul + raised * (jnp.exp(-0.5 * raised * raised) * (1.0 / math.sqrt(2.0 * math.pi)))
        act = (raised * cumul).astype(jnp.bfloat16)
        down = w_down[at_step(j, TILE), :]
        narrow.put(j, rows_dot(act, grad_low[...]), d_down.at[at_step(j, TILE), :])
        grad_up = (right_trans(grad_low[...], down) * slope).astype(jnp.bfloat16)
        wide.put(j, rows_dot(low[...], grad_up), d_up.at[:, at_col(j, TILE)])
        acc[...] += right_trans(grad_up, w_up[:, at_col(j, TILE)])

    loop(count, feed)
    narrow.flush(d_down.at[pl.ds(0, TILE), :])
    wide.flush(d_up.at[:, pl.ds(0, TILE)])
    norm_back_into(acc, middle, gain_two, grad, grad_mid, d_two)
    grad_low[...] = grad_mid[...].astype(jnp.bfloat16)
    for j in range(width // 256):
        square.put(j, rows_dot(mixed[...], grad_low[:, pl.ds(j * 256, 256)]), d_a.at[:, pl.ds(3 * width + j * 256, 256)])
    for j in range(width // 256):
        low[:, pl.ds(j * 256, 256)] = right_trans(grad_low[...], w_a[pl.ds(j * 256, 256), pl.ds(3 * width, width)]).astype(jnp.bfloat16)

    def attend(pair):
        where = [pl.ds(pl.multiple_of(pair * 128 + part * width, 128), 128) for part in range(3)]
        query, key, value = (qkv[:, at] for at in where)
        grad_mixed = low[:, at_col(pair, 128)]
        found = []
        for half in range(2):
            probs = probabilities(query, key, half, live)
            grad_half = keep_half(grad_mixed, half)
            grad_probs = right_trans(grad_half, value)
            dots = jnp.sum(grad_probs * probs, axis=-1, keepdims=True)
            grad_scores = (probs * (grad_probs - dots) * 0.125).astype(jnp.bfloat16)
            found.append(
                (matmul(grad_scores, key), rows_dot(grad_scores, query), rows_dot(probs.astype(jnp.bfloat16), grad_half))
            )
        for part in range(3):
            both = jnp.where(head_mask(0), found[0][part], found[1][part])
            grad_qkv[:, where[part]] = both.astype(jnp.bfloat16)

    loop(width // 128, attend)
    scale_norm(stream, gain_one, low)
    acc[...] = jnp.zeros_like(acc)
    first = width // 256

    def project(j):
        piece = grad_qkv[:, at_col(j, 256)]
        square.put(j + first, rows_dot(low[...], piece), d_a.at[:, at_col(j, 256)])
        acc[...] += right_trans(piece, w_a[:, at_col(j, 256)])

    loop(3 * width // 256, project)
    square.flush(d_a.at[:, pl.ds(0, 256)])
    norm_back_into(acc, stream, gain_one, grad_mid, out, d_one)


def backward_kernel(*refs):
    (grad_rows, vis_col, vis_row, vec, e_in, e_qkv, e_mixed, e_mid, e_up, d_in, d_qkv, d_mixed, d_mid, d_up,
     e_a_hbm, e_u_hbm, e_d_hbm, d_a_hbm, d_u_hbm, d_d_hbm,
     embed_grad, small, de_a, de_u, de_d, dd_a, dd_u, dd_d,
     e_a, e_u, e_d, d_a, d_u, d_d, d_grad, e_grad, low_a, low_b, grad_qkv, acc, grad_mid,
     wide, narrow, square, load_sems, tile_sems) = refs
    tokens, width = d_in.shape
    rows = e_in.shape[0]
    loads = [
        pltpu.make_async_copy(a, b, load_sems.at[i])
        for i, (a, b) in enumerate(
            [(d_d_hbm, d_d), (d_u_hbm, d_u), (d_a_hbm, d_a), (e_d_hbm, e_d), (e_u_hbm, e_u), (e_a_hbm, e_a)]
        )
    ]
    for load in loads:
        load.start()
    tiles = (Tiles(wide, tile_sems.at[0]), Tiles(narrow, tile_sems.at[1]), Tiles(square, tile_sems.at[2]))
    d_grad[:BUFFER, :] = jnp.zeros((BUFFER, width), jnp.float32)
    d_grad[BUFFER:, :] = grad_rows[...].astype(jnp.float32)
    for load in loads[:3]:
        load.wait()
    backward_block(width, d_grad, d_in, vec[2:3, :], vec[3:4, :], d_a, d_u, d_d, d_qkv, d_mixed, d_mid, d_up,
                   dd_a, dd_u, dd_d, small.at[2:3, :], small.at[3:4, :], low_a, low_b, grad_qkv, acc, grad_mid, d_grad, tiles)
    hot = spot_hot(vis_row, tokens - BUFFER)
    masked = 1.0 - jnp.sum(hot.astype(jnp.float32), axis=1, keepdims=True)
    small[4:5, :] = jnp.sum(d_grad[BUFFER:, :] * masked, axis=0, keepdims=True)
    e_grad[:BUFFER, :] = d_grad[:BUFFER, :]
    e_grad[BUFFER:, :] = exact_dot(token_hot(vis_col, tokens - BUFFER), d_grad[BUFFER:, :])
    for load in loads[3:]:
        load.wait()
    part = pl.ds(0, rows)
    backward_block(width, e_grad, e_in, vec[0:1, :], vec[1:2, :], e_a, e_u, e_d, e_qkv, e_mixed, e_mid, e_up,
                   de_a, de_u, de_d, small.at[0:1, :], small.at[1:2, :], low_a.at[part], low_b.at[part],
                   grad_qkv.at[part], acc.at[part], grad_mid.at[part], e_grad, tiles, live_keys(vis_row))
    embed_grad[:BUFFER, :] = e_grad[:BUFFER, :]
    embed_grad[BUFFER:, :] = exact_dot(hot, e_grad[BUFFER:, :])


def backward_blocks(grad_rows, vis_col, vis_row, vec, enc_kept, dec_kept, weights):
    tokens, width = dec_kept[0].shape
    rows = enc_kept[0].shape[0]
    f32, half = jnp.float32, jnp.bfloat16
    whole, anywhere = pl.BlockSpec(memory_space=pltpu.VMEM), pl.BlockSpec(memory_space=pl.ANY)
    outs = [jax.ShapeDtypeStruct((tokens, width), f32), jax.ShapeDtypeStruct((8, width), f32)]
    outs += [jax.ShapeDtypeStruct(w.shape, half) for w in weights]
    found = pl.pallas_call(
        backward_kernel,
        out_shape=outs,
        in_specs=[whole] * 14 + [anywhere] * 6,
        out_specs=[whole] * 2 + [anywhere] * 6,
        scratch_shapes=[pltpu.VMEM(w.shape, half) for w in weights]
        + [
            pltpu.VMEM((tokens, width), f32),
            pltpu.VMEM((rows, width), f32),
            pltpu.VMEM((tokens, width), half),
            pltpu.VMEM((tokens, width), half),
            pltpu.VMEM((tokens, 3 * width), half),
            pltpu.VMEM((tokens, width), f32),
            pltpu.VMEM((tokens, width), f32),
            pltpu.VMEM((2, width, TILE), half),
            pltpu.VMEM((2, TILE, width), half),
            pltpu.VMEM((2, width, 256), half),
            pltpu.SemaphoreType.DMA((6,)),
            pltpu.SemaphoreType.DMA((3, 2)),
        ],
        compiler_params=pltpu.CompilerParams(vmem_limit_bytes=SUM_VMEM),
        name="backward_blocks",
    )(grad_rows, vis_col, vis_row, vec, *enc_kept, *dec_kept, *weights)
    return found[0], found[1], found[2:]


def embed_steps(steps, freqs, target):
    half = freqs.shape[1]

    def body(i):
        phase = steps[at_step(i), :].astype(jnp.float32) * freqs[...]
        target[at_step(i), :half] = jnp.cos(phase)
        target[at_step(i), half:] = jnp.sin(phase)

    loop(steps.shape[0] // STEP, body)


ROWS = 128


def at_rows(i):
    return pl.ds(pl.multiple_of(i * ROWS, 16), ROWS)


def head_kernel(*refs):
    (acts, vis_row, targets, noise, steps, embeds, w_cond_hbm, w_ada_hbm, w_io_hbm, w_in, w_out,
     grad_rows, losses, d_in, d_out, d_cond, d_ada, d_io,
     w_cond, w_ada, w_io, cond, cond_full, mod, hidden, normed_in, inv_in, inner, branch, normed_out, inv_out,
     work, grad_two, grad_sum, noisy, cond_act, mlp_in, inner_act, final_in, grad_pred, grad_branch, grad_inner,
     grad_hidden, grad_mod, wide, load_sems, tile_sems) = refs
    tokens, wide_cols = targets.shape[0], w_in.shape[1]
    loads = [
        pltpu.make_async_copy(a, b, load_sems.at[i])
        for i, (a, b) in enumerate([(w_cond_hbm, w_cond), (w_ada_hbm, w_ada), (w_io_hbm, w_io)])
    ]
    for load in loads:
        load.start()
    hot = spot_hot(vis_row, tokens)
    masked = jnp.sum(hot.astype(jnp.float32), axis=1, keepdims=True) < 0.5
    loads[0].wait()
    cond[...] = matmul(acts[BUFFER:, :], w_cond[...])
    loads[1].wait()
    loads[2].wait()
    grad_sum[...] = jnp.zeros_like(grad_sum)
    columns = wide_cols // 256

    def copy_pass(c, loss):
        rows = pl.ds(pl.multiple_of(c * tokens, 16), tokens)

        def at(i):
            return pl.ds(pl.multiple_of(c * tokens + i * ROWS, 16), ROWS)

        angle = noise_angle(steps[rows, :])
        noise_vals = noise[rows, :].astype(jnp.float32)
        noisy[rows, :] = (jnp.cos(angle) * targets[...] + jnp.sin(angle) * noise_vals).astype(jnp.bfloat16)

        def condition(i):
            full = cond[at_rows(i), :] + embeds[at(i), :]
            cond_full[at_rows(i), :] = full
            cond_act[at(i), :] = (full * jax.nn.sigmoid(full)).astype(jnp.bfloat16)

        loop(tokens // ROWS, condition)

        def modulate(j):
            mod[:, at_col(j, wide_cols)] = matmul(cond_act[rows, :], w_ada[:, at_col(j, wide_cols)])

        loop(3, modulate)
        hidden[...] = matmul(noisy[rows, :], w_in[...])

        def enter(i):
            normed, inv_std = norm_rows(hidden[at_rows(i), :])
            normed_in[at_rows(i), :] = normed
            inv_in[at_rows(i), :] = inv_std
            shift, scale = mod[at_rows(i), :wide_cols], mod[at_rows(i), wide_cols : 2 * wide_cols]
            mlp_in[at(i), :] = (normed * (1.0 + scale) + shift).astype(jnp.bfloat16)

        loop(tokens // ROWS, enter)

        inner[...] = matmul(mlp_in[rows, :], w_io[:, :wide_cols])

        def activate(i):
            values = inner[at_rows(i), :]
            inner_act[at(i), :] = (values * jax.nn.sigmoid(values)).astype(jnp.bfloat16)

        loop(tokens // ROWS, activate)

        branch[...] = matmul(inner_act[rows, :], w_io[:, wide_cols:])

        def leave(i):
            gate = mod[at_rows(i), 2 * wide_cols :]
            normed, inv_std = norm_rows(hidden[at_rows(i), :] + gate * branch[at_rows(i), :])
            normed_out[at_rows(i), :] = normed
            inv_out[at_rows(i), :] = inv_std
            final_in[at(i), :] = normed.astype(jnp.bfloat16)

        loop(tokens // ROWS, leave)
        error = right_trans(final_in[rows, :], w_out[...]) - noise_vals
        loss = loss + jnp.sum(error * error, axis=1, keepdims=True)
        low_error = jnp.where(masked, error * (2.0 / COPIES), 0.0).astype(jnp.bfloat16)
        grad_pred[rows, :] = low_error
        work[...] = matmul(low_error, w_out[...])

        def back_out(i):
            gate = mod[at_rows(i), 2 * wide_cols :]
            grad = norm_back(work[at_rows(i), :], normed_out[at_rows(i), :], inv_out[at_rows(i), :])
            grad_two[at_rows(i), :] = grad
            grad_branch[at(i), :] = (grad * gate).astype(jnp.bfloat16)
            grad_mod[at(i), 2 * wide_cols :] = (grad * branch[at_rows(i), :]).astype(jnp.bfloat16)

        loop(tokens // ROWS, back_out)

        work[...] = right_trans(grad_branch[rows, :], w_io[:, wide_cols:])

        def back_act(i):
            grad_inner[at(i), :] = (work[at_rows(i), :] * silu_slope(inner[at_rows(i), :])).astype(jnp.bfloat16)

        loop(tokens // ROWS, back_act)

        work[...] = right_trans(grad_inner[rows, :], w_io[:, :wide_cols])

        def back_in(i):
            grad, normed = work[at_rows(i), :], normed_in[at_rows(i), :]
            scale = mod[at_rows(i), wide_cols : 2 * wide_cols]
            grad_mod[at(i), :wide_cols] = grad.astype(jnp.bfloat16)
            grad_mod[at(i), wide_cols : 2 * wide_cols] = (grad * normed).astype(jnp.bfloat16)
            total = grad_two[at_rows(i), :] + norm_back(grad * (1.0 + scale), normed, inv_in[at_rows(i), :])
            grad_hidden[at(i), :] = total.astype(jnp.bfloat16)

        loop(tokens // ROWS, back_in)

        def back_mod(j):
            work[:, at_col(j, 256)] = right_trans(grad_mod[rows, :], w_ada[at_step(j, 256), :])

        loop(columns, back_mod)

        def back_cond(i):
            grad_sum[at_rows(i), :] += work[at_rows(i), :] * silu_slope(cond_full[at_rows(i), :])

        loop(tokens // ROWS, back_cond)
        return loss

    loss = lax.fori_loop(0, COPIES, copy_pass, jnp.zeros((tokens, 1), jnp.float32))
    loss = jnp.where(masked, loss.astype(jnp.bfloat16).astype(jnp.float32), 0.0)
    losses[...] = jnp.broadcast_to(jnp.sum(loss, axis=0, keepdims=True), losses.shape)
    grad_cond = grad_sum[...].astype(jnp.bfloat16)
    grad_rows[...] = right_trans(grad_cond, w_cond[...]).astype(jnp.bfloat16)
    tiles = Tiles(wide, tile_sems)

    def out_ada(j):
        tiles.put(j, rows_dot(cond_act[...], grad_mod[:, at_col(j, TILE)]), d_ada.at[:, at_col(j, TILE)])

    count = 3 * wide_cols // TILE
    loop(count, out_ada)
    half = wide_cols // TILE

    def out_inner(j):
        tiles.put(j + count, rows_dot(mlp_in[...], grad_inner[:, at_col(j, TILE)]), d_io.at[:, at_col(j, TILE)])

    def out_outer(j):
        tiles.put(j + count + half, rows_dot(inner_act[...], grad_branch[:, at_col(j, TILE)]), d_io.at[:, at_col(j + half, TILE)])

    loop(half, out_inner)
    loop(half, out_outer)
    d_cond[...] = rows_dot(acts[BUFFER:, :], grad_cond).astype(jnp.bfloat16)
    d_in[...] = rows_dot(noisy[...], grad_hidden[...])
    d_out[...] = rows_dot(grad_pred[...], final_in[...])
    tiles.flush(d_ada.at[:, pl.ds(0, TILE)])


def head_pass(acts, vis_row, targets, noise, steps, embeds, w_cond, w_ada, w_io, w_in, w_out):
    tokens, width = targets.shape[0], acts.shape[1]
    wide, flat = w_in.shape[1], noise.shape[0]
    f32, half = jnp.float32, jnp.bfloat16
    whole, anywhere = pl.BlockSpec(memory_space=pltpu.VMEM), pl.BlockSpec(memory_space=pl.ANY)
    shape = jax.ShapeDtypeStruct
    outs = [
        shape((tokens, width), half), shape((8, 128), f32), shape((CH, wide), f32), shape((CH, wide), f32),
        shape(w_cond.shape, half), shape(w_ada.shape, half), shape(w_io.shape, half),
    ]
    tile = lambda cols, kind=f32: pltpu.VMEM((tokens, cols), kind)
    long = lambda cols: pltpu.VMEM((flat, cols), half)
    return pl.pallas_call(
        head_kernel,
        out_shape=outs,
        in_specs=[whole] * 6 + [anywhere] * 3 + [whole] * 2,
        out_specs=[whole] * 5 + [anywhere] * 2,
        scratch_shapes=[pltpu.VMEM(w.shape, half) for w in (w_cond, w_ada, w_io)]
        + [
            tile(wide), tile(wide), tile(3 * wide), tile(wide), tile(wide), tile(1), tile(wide), tile(wide), tile(wide), tile(1),
            tile(wide), tile(wide), tile(wide),
            long(CH), long(wide), long(wide), long(wide), long(wide), long(CH), long(wide), long(wide), long(wide), long(3 * wide),
            pltpu.VMEM((2, wide, TILE), half),
            pltpu.SemaphoreType.DMA((3,)),
            pltpu.SemaphoreType.DMA((2,)),
        ],
        compiler_params=pltpu.CompilerParams(vmem_limit_bytes=SUM_VMEM),
        name="head_pass",
    )(acts, vis_row, targets, noise, steps, embeds, w_cond, w_ada, w_io, w_in, w_out)


class Slab:
    def __init__(self, rows, cols, by_rows):
        self.rows, self.cols, self.by_rows = rows, cols, by_rows
        self.piece = (rows // 4, cols) if by_rows else (rows, cols // 4)

    def spot(self, shard, quarter, half=None):
        piece_rows, piece_cols = self.piece
        row = shard * self.rows
        if self.by_rows:
            row = row + quarter * piece_rows
        height = piece_rows
        if half is not None:
            height = piece_rows // 2
            row = row + half * height
        col = 0 if self.by_rows else quarter * piece_cols
        return (pl.ds(aligned(row, 16), height), pl.ds(aligned(col, 128), piece_cols))

    def shard(self, shard):
        return (pl.ds(aligned(shard * self.rows, 16), self.rows), pl.ds(0, self.cols))

    def within(self, quarter):
        return self.spot(0, quarter)


def aligned(value, multiple):
    return value if isinstance(value, int) else pl.multiple_of(value, multiple)


def place(depth):
    group, device = lax.axis_index("grp"), lax.axis_index("dev")
    level, core = device // 2, device % 2
    flip = lambda bit: group + (1 << bit) * (1 - 2 * ((group // (1 << bit)) % 2))
    return group, level, core, flip


def greet(peers):
    barrier = pltpu.get_barrier_semaphore()
    for peer in peers:
        pl.semaphore_signal(barrier, inc=1, device_id=peer, device_id_type=MESH)
    pl.semaphore_wait(barrier, len(peers))


def gather_kernel(slabs, depth, *refs):
    count = len(slabs)
    mine, whole = refs[:count], refs[count : 2 * count]
    sent, got, own_sent, own_got, own_copy = refs[2 * count :]
    group, level, core, flip = place(depth)
    x_peer, y_peer = (flip(0), 2 * level + core), (flip(1), 2 * level + core)
    partner = (group, 2 * level + 1 - core)

    def level_at(step):
        return lax.rem(level + step + depth, depth)

    z_peers = [(group, 2 * level_at(step) + core) for step in range(1, depth)]
    greet([x_peer, y_peer, partner] + z_peers)

    def move(kind, item, source, target, device):
        return pltpu.make_async_remote_copy(
            src_ref=source,
            dst_ref=target,
            send_sem=sent.at[kind, item],
            recv_sem=got.at[kind, item],
            device_id=device,
            device_id_type=MESH,
        )

    Z, X, Y, XH, YH, CORE = range(6)
    items = [(k, step) for k in range(count) for step in range(1, depth)]

    def by_z(item):
        k, step = items[item]
        slab = slabs[k]
        target = whole[k].at[slab.spot(2 * level + core, group)]
        return move(Z, item, mine[k].at[slab.within(group)], target, z_peers[step - 1])

    def shard_of(item):
        return 2 * level_at(-items[item][1]) + core

    def forward(kind, item, quarter, half, device):
        k = items[item][0]
        here = whole[k].at[slabs[k].spot(shard_of(item), quarter, half)]
        return move(kind, item, here, here, device)

    def core_copy(item, core_of):
        k, step = items[item]
        here = whole[k].at[slabs[k].shard(2 * level_at(-step) + core_of)]
        return move(CORE, item, here, here, partner)

    own = []
    for k, slab in enumerate(slabs):
        for step in range(1, depth):
            by_z(k * (depth - 1) + step - 1).start()
        target = whole[k].at[slab.shard(2 * level + core)]
        keep = pltpu.make_async_copy(mine[k], target, own_copy.at[k])
        keep.start()
        share = pltpu.make_async_remote_copy(
            src_ref=mine[k],
            dst_ref=target,
            send_sem=own_sent.at[k],
            recv_sem=own_got.at[k],
            device_id=partner,
            device_id_type=MESH,
        )
        share.start()
        own.append((keep, share))

    total = len(items)
    for turn in range(total + 2):
        if turn < total:
            k = items[turn][0]
            here = whole[k].at[slabs[k].spot(shard_of(turn), group)]
            move(Z, turn, here, here, x_peer).wait_recv()
            forward(X, turn, group, None, x_peer).start()
            forward(Y, turn, group, None, y_peer).start()
        item = turn - 1
        if 0 <= item < total:
            forward(X, item, flip(0), None, x_peer).wait_recv()
            forward(YH, item, flip(0), 0, y_peer).start()
            forward(Y, item, flip(1), None, y_peer).wait_recv()
            forward(XH, item, flip(1), 1, x_peer).start()
        item = turn - 2
        if 0 <= item < total:
            far = 3 - group
            forward(YH, item, far, 0, y_peer).wait_recv()
            forward(XH, item, far, 1, x_peer).wait_recv()
            core_copy(item, core).start()
    for item in range(total):
        by_z(item).wait_send()
        forward(X, item, group, None, x_peer).wait_send()
        forward(Y, item, group, None, y_peer).wait_send()
        forward(YH, item, flip(0), 0, y_peer).wait_send()
        forward(XH, item, flip(1), 1, x_peer).wait_send()
        core_copy(item, core).wait_send()
        core_copy(item, 1 - core).wait_recv()
    for keep, share in own:
        keep.wait()
        share.wait()


def gather_slabs(shards, slabs, depth):
    count, items = len(slabs), len(slabs) * (depth - 1)
    return pl.pallas_call(
        functools.partial(gather_kernel, slabs, depth),
        out_shape=[
            jax.ShapeDtypeStruct((2 * depth * s.rows, s.cols), jnp.bfloat16) for s in slabs
        ],
        in_specs=[pl.BlockSpec(memory_space=pl.ANY)] * count,
        out_specs=[pl.BlockSpec(memory_space=pl.ANY)] * count,
        scratch_shapes=[
            pltpu.SemaphoreType.DMA((6, items)),
            pltpu.SemaphoreType.DMA((6, items)),
            pltpu.SemaphoreType.DMA((count,)),
            pltpu.SemaphoreType.DMA((count,)),
            pltpu.SemaphoreType.DMA((count,)),
        ],
        compiler_params=pltpu.CompilerParams(collective_id=0, has_side_effects=True),
        name="gather_weights",
    )(*shards)


def sum_kernel(slabs, orders, depth, *refs):
    count = len(slabs)
    grads, outs = refs[:count], refs[count : 2 * count]
    rest = refs[2 * count :]
    take = lambda: (rest[:count], rest[count:])
    held, rest = take()
    from_first, rest = take()
    from_second, rest = take()
    from_level, rest = take()
    result, rest = take()
    stage, rest = take()
    stage_sem, out_sem, core_sent, core_got, sent, got, z_sent, z_got = rest
    group, level, core, flip = place(depth)
    me = 2 * level + core
    partner = (group, 2 * level + 1 - core)
    bit = lambda b: (group // (1 << b)) % 2

    def level_at(step):
        return lax.rem(level + step + depth, depth)

    z_peers = [(group, 2 * level_at(step) + core) for step in range(1, depth)]
    greet([(flip(0), me), (flip(1), me), partner] + z_peers)

    def move(pair, k, kind, source, target, device):
        send, receive = pair
        return pltpu.make_async_remote_copy(
            src_ref=source,
            dst_ref=target,
            send_sem=send.at[kind, k],
            recv_sem=receive.at[kind, k],
            device_id=device,
            device_id_type=MESH,
        )

    def core_move(k, lev):
        source = grads[k].at[slabs[k].shard(2 * lev + 1 - core)]
        return move((core_sent, core_got), k, lev, source, held[k].at[lev], partner)

    def rows_loop(height, body):
        step = 32 if height % 32 == 0 else 16

        def turn(i, carry):
            body(pl.ds(aligned(i * step, 16), step))
            return carry

        lax.fori_loop(0, height // step, turn, 0)

    def shifted(rows, by):
        return pl.ds(aligned(rows.start + by, 16), rows.size)

    def first_bit(k):
        return 1 if orders[k] == "yx" else 0

    def quarter(k, first, second):
        b = first_bit(k)
        return first * (1 << b) + second * (1 << (1 - b))

    def first_move(k, j):
        b = first_bit(k)
        where = slabs[k].within(quarter(k, 1 - bit(b), j))
        source = held[k].at[(level,) + where] if orders[k][0] == "z" else held[k].at[(slice(None),) + where]
        return move((sent, got), k, j, source, from_first[k].at[j], (flip(b), me))

    def second_move(k):
        b = first_bit(k)
        where = slabs[k].within(quarter(k, bit(b), 1 - bit(1 - b)))
        source = held[k].at[(level,) + where] if orders[k][0] == "z" else held[k].at[(slice(None),) + where]
        return move((sent, got), k, 2, source, from_second[k], (flip(1 - b), me))

    def level_move(k, step):
        lev = level_at(step)
        source = held[k].at[lev] if orders[k][0] == "z" else held[k].at[(lev,) + slabs[k].within(group)]
        return move((z_sent, z_got), k, step - 1, source, from_level[k].at[step - 1], z_peers[step - 1])

    def spread_second(k, whose):
        here = result[k].at[slabs[k].within(whose)]
        return move((sent, got), k, 3, here, here, (flip(1 - first_bit(k)), me))

    def spread_first(k, j, whose):
        here = result[k].at[slabs[k].within(whose)]
        return move((sent, got), k, 4 + j, here, here, (flip(first_bit(k)), me))

    def out_copy(k):
        return pltpu.make_async_copy(result[k], outs[k], out_sem.at[k])

    def stage_copy(k, lev):
        source = grads[k].at[slabs[k].shard(2 * lev + core)]
        return pltpu.make_async_copy(source, stage[k].at[lev % 2], stage_sem.at[k, lev % 2])

    def add_core(k):
        slab = slabs[k]
        stage_copy(k, 0).start()
        for lev in range(depth):
            if lev + 1 < depth:
                stage_copy(k, lev + 1).start()
            core_move(k, lev).wait_recv()
            stage_copy(k, lev).wait()

            def body(rows):
                total = held[k][lev, rows, :].astype(jnp.float32) + stage[k][lev % 2, rows, :].astype(jnp.float32)
                held[k][lev, rows, :] = total.astype(jnp.bfloat16)

            rows_loop(slab.rows, body)

    def levels_of(k):
        return [level] if orders[k][0] == "z" else list(range(depth))

    def add_first(k):
        slab = slabs[k]
        for j in range(2):
            first_move(k, j).wait_recv()
            rows_of, cols = slab.within(quarter(k, bit(first_bit(k)), j))
            for lev in levels_of(k):

                def body(rows):
                    at = (lev, shifted(rows, rows_of.start), cols)
                    extra = from_first[k][j, rows, :] if orders[k][0] == "z" else from_first[k][j, lev, rows, :]
                    held[k][at] = (held[k][at].astype(jnp.float32) + extra.astype(jnp.float32)).astype(jnp.bfloat16)

                rows_loop(slab.piece[0], body)

    def add_second(k):
        slab = slabs[k]
        second_move(k).wait_recv()
        rows_of, cols = slab.within(group)
        for lev in levels_of(k):

            def body(rows):
                at = (lev, shifted(rows, rows_of.start), cols)
                extra = from_second[k][rows, :] if orders[k][0] == "z" else from_second[k][lev, rows, :]
                total = held[k][at].astype(jnp.float32) + extra.astype(jnp.float32)
                target = result[k].at[shifted(rows, rows_of.start), cols] if orders[k][0] == "z" else held[k].at[at]
                target[...] = total.astype(jnp.bfloat16)

            rows_loop(slab.piece[0], body)

    def add_level(k):
        slab = slabs[k]
        for step in range(1, depth):
            level_move(k, step).wait_recv()
        if orders[k][0] == "z":

            def body(rows):
                total = held[k][level, rows, :].astype(jnp.float32)
                for step in range(depth - 1):
                    total = total + from_level[k][step, rows, :].astype(jnp.float32)
                held[k][level, rows, :] = total.astype(jnp.bfloat16)

            rows_loop(slab.rows, body)
            return
        rows_of, cols = slab.within(group)

        def body(rows):
            at = (shifted(rows, rows_of.start), cols)
            total = held[k][(level,) + at].astype(jnp.float32)
            for step in range(depth - 1):
                total = total + from_level[k][step, rows, :].astype(jnp.float32)
            result[k][at] = total.astype(jnp.bfloat16)

        rows_loop(slab.piece[0], body)

    def begin_core(k):
        for lev in range(depth):
            core_move(k, lev).start()

    def begin_first(k):
        first_move(k, 0).start()
        first_move(k, 1).start()

    def begin_level(k):
        for step in range(1, depth):
            level_move(k, step).start()

    def end_spread_second(k):
        spread_second(k, flip(1 - first_bit(k))).wait_recv()
        spread_first(k, 0, group).start()
        spread_first(k, 1, flip(1 - first_bit(k))).start()

    def end_spread_first(k):
        b = first_bit(k)
        spread_first(k, 0, flip(b)).wait_recv()
        spread_first(k, 1, 3 - group).wait_recv()
        out_copy(k).start()

    def steps(k):
        if orders[k][0] == "z":
            return [
                lambda: (add_core(k), begin_level(k)),
                lambda: (add_level(k), begin_first(k)),
                lambda: (add_first(k), second_move(k).start()),
                lambda: (add_second(k), spread_second(k, group).start()),
                lambda: end_spread_second(k),
                lambda: end_spread_first(k),
            ]
        return [
            lambda: (add_core(k), begin_first(k)),
            lambda: (add_first(k), second_move(k).start()),
            lambda: (add_second(k), begin_level(k)),
            lambda: (add_level(k), spread_second(k, group).start()),
            lambda: end_spread_second(k),
            lambda: end_spread_first(k),
        ]

    plans = [steps(k) for k in range(count)]
    begin_core(0)
    for turn in range(count + 5):
        if turn + 1 < count:
            begin_core(turn + 1)
        for place_in in range(6):
            k = turn - place_in
            if 0 <= k < count:
                plans[k][place_in]()
    for k in range(count):
        for lev in range(depth):
            core_move(k, lev).wait_send()
        first_move(k, 0).wait_send()
        first_move(k, 1).wait_send()
        second_move(k).wait_send()
        for step in range(1, depth):
            level_move(k, step).wait_send()
        spread_second(k, group).wait_send()
        spread_first(k, 0, group).wait_send()
        spread_first(k, 1, flip(1 - first_bit(k))).wait_send()
        out_copy(k).wait()


def sum_slabs(grads, slabs, orders, depth):
    count = len(slabs)
    half = jnp.bfloat16
    held, first, second, lev, result, stage = [], [], [], [], [], []
    for slab, order in zip(slabs, orders, strict=True):
        shard = (slab.rows, slab.cols)
        held.append(pltpu.VMEM((depth,) + shard, half))
        result.append(pltpu.VMEM(shard, half))
        stage.append(pltpu.VMEM((2,) + shard, half))
        if order[0] == "z":
            first.append(pltpu.VMEM((2,) + slab.piece, half))
            second.append(pltpu.VMEM(slab.piece, half))
            lev.append(pltpu.VMEM((depth - 1,) + shard, half))
        else:
            first.append(pltpu.VMEM((2, depth) + slab.piece, half))
            second.append(pltpu.VMEM((depth,) + slab.piece, half))
            lev.append(pltpu.VMEM((depth - 1,) + slab.piece, half))
    dma = pltpu.SemaphoreType.DMA
    return pl.pallas_call(
        functools.partial(sum_kernel, slabs, orders, depth),
        out_shape=[jax.ShapeDtypeStruct((s.rows, s.cols), half) for s in slabs],
        in_specs=[pl.BlockSpec(memory_space=pl.ANY)] * count,
        out_specs=[pl.BlockSpec(memory_space=pl.ANY)] * count,
        scratch_shapes=held
        + first
        + second
        + lev
        + result
        + stage
        + [
            dma((count, 2)),
            dma((count,)),
            dma((depth, count)),
            dma((depth, count)),
            dma((6, count)),
            dma((6, count)),
            dma((depth - 1, count)),
            dma((depth - 1, count)),
        ],
        compiler_params=pltpu.CompilerParams(
            collective_id=1, has_side_effects=True, vmem_limit_bytes=SUM_VMEM
        ),
        name="sum_gradients",
    )(*grads)


class Gathering:
    def __init__(self, slabs, depth, mine, whole, sems):
        self.slabs, self.depth, self.mine, self.whole = slabs, depth, mine, whole
        self.sent, self.got, self.own_sent, self.own_got, self.own_copy = sems
        self.group, self.level, self.core, self.flip = place(depth)
        me = 2 * self.level + self.core
        self.peers = ((self.flip(0), me), (self.flip(1), me), (self.group, 2 * self.level + 1 - self.core))
        self.items = [(k, step) for k in range(len(slabs)) for step in range(1, depth)]
        self.turn = 0
        self.turns = len(self.items) + 2

    def level_at(self, step):
        return lax.rem(self.level + step + self.depth, self.depth)

    def move(self, kind, item, source, target, device):
        return pltpu.make_async_remote_copy(
            src_ref=source,
            dst_ref=target,
            send_sem=self.sent.at[kind, item],
            recv_sem=self.got.at[kind, item],
            device_id=device,
            device_id_type=MESH,
        )

    def z_peer(self, step):
        return (self.group, 2 * self.level_at(step) + self.core)

    def along_z(self, item):
        k, step = self.items[item]
        slab = self.slabs[k]
        target = self.whole[k].at[slab.spot(2 * self.level + self.core, self.group)]
        return self.move(0, item, self.mine[k].at[slab.within(self.group)], target, self.z_peer(step))

    def onward(self, kind, item, quarter, half, device):
        k, step = self.items[item]
        shard = 2 * self.level_at(-step) + self.core
        here = self.whole[k].at[self.slabs[k].spot(shard, quarter, half)]
        return self.move(kind, item, here, here, device)

    def to_core(self, item, core):
        k, step = self.items[item]
        here = self.whole[k].at[self.slabs[k].shard(2 * self.level_at(-step) + core)]
        return self.move(5, item, here, here, self.peers[2])

    def own(self, k):
        target = self.whole[k].at[self.slabs[k].shard(2 * self.level + self.core)]
        share = pltpu.make_async_remote_copy(
            src_ref=self.mine[k],
            dst_ref=target,
            send_sem=self.own_sent.at[k],
            recv_sem=self.own_got.at[k],
            device_id=self.peers[2],
            device_id_type=MESH,
        )
        return pltpu.make_async_copy(self.mine[k], target, self.own_copy.at[k]), share

    def start(self):
        greet([*self.peers, *(self.z_peer(step) for step in range(1, self.depth))])
        for item in range(len(self.items)):
            self.along_z(item).start()
            if self.items[item][1] == 1:
                for copy in self.own(self.items[item][0]):
                    copy.start()

    def pump(self, until):
        group, flip = self.group, self.flip
        x_peer, y_peer, _ = self.peers
        total = len(self.items)
        while self.turn < min(until, self.turns):
            item = self.turn
            if item < total:
                self.onward(0, item, group, None, x_peer).wait_recv()
                self.onward(1, item, group, None, x_peer).start()
                self.onward(2, item, group, None, y_peer).start()
            item = self.turn - 1
            if 0 <= item < total:
                self.onward(1, item, flip(0), None, x_peer).wait_recv()
                self.onward(4, item, flip(0), 0, y_peer).start()
                self.onward(2, item, flip(1), None, y_peer).wait_recv()
                self.onward(3, item, flip(1), 1, x_peer).start()
            item = self.turn - 2
            if 0 <= item < total:
                self.onward(4, item, 3 - group, 0, y_peer).wait_recv()
                self.onward(3, item, 3 - group, 1, x_peer).wait_recv()
                self.to_core(item, self.core).start()
            self.turn += 1

    def ready_at(self, k):
        return (k + 1) * (self.depth - 1) + 2

    def take(self, k):
        self.pump(self.ready_at(k))
        for item, (slab, _) in enumerate(self.items):
            if slab == k:
                self.to_core(item, 1 - self.core).wait_recv()
        keep, share = self.own(k)
        keep.wait()
        share.wait_recv()

    def finish(self):
        group, flip = self.group, self.flip
        x_peer, y_peer, _ = self.peers
        for item in range(len(self.items)):
            self.along_z(item).wait_send()
            self.onward(1, item, group, None, x_peer).wait_send()
            self.onward(2, item, group, None, y_peer).wait_send()
            self.onward(4, item, flip(0), 0, y_peer).wait_send()
            self.onward(3, item, flip(1), 1, x_peer).wait_send()
            self.to_core(item, self.core).wait_send()
        for k in range(len(self.slabs)):
            self.own(k)[1].wait_send()


def unpack_vectors(small, parts, width, vec):
    piece = width // parts
    vec[...] = jnp.zeros_like(vec)
    lane = lax.broadcasted_iota(jnp.int32, (128, width), 0)
    col = lax.broadcasted_iota(jnp.int32, (128, width), 1)
    for part in range(parts):
        spread = ((col == lane + part * piece) & (lane < piece)).astype(jnp.bfloat16)
        vec[...] += matmul(small[pl.ds(part * SMALL_ROWS, CH), :128], spread)


def first_kernel(slabs, depth, *refs):
    count = len(slabs)
    mine, refs = refs[:count], refs[count:]
    embedded, vis_col, vis_row, steps, freqs = refs[:5]
    whole, refs = refs[5 : 5 + count], refs[5 + count :]
    kept_hbm, (acts, vec, w_in, w_out, embeds_hbm), refs = refs[:10], refs[10:15], refs[15:]
    sems, refs = refs[:5], refs[5:]
    small, (e_a, e_u, e_d, d_a, d_u, d_d) = refs[0], refs[1:7]
    e_kept, d_kept = refs[7:12], refs[12:17]
    embeds, e_out, d_out, e_low, d_low, load_sems, kept_sems = refs[17:]
    width = embedded.shape[1]
    parts = 2 * depth
    gathering = Gathering(slabs, depth, mine, whole, sems)
    gathering.start()
    half, height = freqs.shape[1], 64
    pieces = steps.shape[0] // height
    enc_turn, dec_turn = gathering.ready_at(3), gathering.ready_at(6)
    encode(embedded, vis_col, None, e_kept[0])
    for piece in range(pieces):
        gathering.pump(piece * enc_turn // pieces)
        rows = pl.ds(piece * height, height)
        phase = steps[rows, :].astype(jnp.float32) * freqs[...]
        embeds[rows, :half] = jnp.cos(phase)
        embeds[rows, half:] = jnp.sin(phase)
    copies = [pltpu.make_async_copy(embeds, embeds_hbm, kept_sems.at[10])]
    copies[0].start()

    def fetch(slots):
        loads = []
        for slab, target in slots:
            gathering.take(slab)
            load = pltpu.make_async_copy(whole[slab], target, load_sems.at[slab])
            load.start()
            loads.append(load)
        return loads

    def run(steps_of, turn, last):
        steps_of = list(steps_of)
        for i, step in enumerate(steps_of):
            step()
            gathering.pump(turn + (last - turn) * (i + 1) // len(steps_of))

    def keep(kept, at):
        for i, buffer in enumerate(kept):
            copy = pltpu.make_async_copy(buffer, kept_hbm[at + i], kept_sems.at[at + i])
            copy.start()
            copies.append(copy)

    for load in fetch([(0, small), (1, e_a), (2, e_u), (3, e_d)]):
        load.wait()
    unpack_vectors(small, parts, width, vec)
    for part in range(parts):
        block = pl.ds(part * SMALL_ROWS, CH)
        w_in[:, pl.ds(part * 128, 128)] = small[block, pl.ds(128, 128)]
        w_out[:, pl.ds(part * 128, 128)] = small[block, pl.ds(256, 128)]
    live = live_keys(vis_row)
    run(forward_steps(width, e_kept[0], vec[0:1, :], vec[1:2, :], e_a, e_u, e_d, *e_kept[1:], e_out, e_low, live), enc_turn, dec_turn)
    keep(e_kept, 0)
    spread_rows(vis_row, e_out, vec, d_kept[0])
    for load in fetch([(4, d_a), (5, d_u), (6, d_d)]):
        load.wait()
    run(forward_steps(width, d_kept[0], vec[2:3, :], vec[3:4, :], d_a, d_u, d_d, *d_kept[1:], d_out, d_low), dec_turn, gathering.turns)
    keep(d_kept, 5)
    acts[...] = d_out[...].astype(jnp.bfloat16)
    for slab in range(7, count):
        gathering.take(slab)
    gathering.finish()
    for copy in copies:
        copy.wait()


def first_part(shards, slabs, depth, embedded, vis_col, vis_row, steps, freqs):
    tokens, width = embedded.shape
    count, items = len(slabs), len(slabs) * (depth - 1)
    inner = slabs[2].cols
    rows = BUFFER + vis_col.shape[0]
    flat, wide = steps.shape[0], 2 * freqs.shape[1]
    f32, half = jnp.float32, jnp.bfloat16
    whole, anywhere = pl.BlockSpec(memory_space=pltpu.VMEM), pl.BlockSpec(memory_space=pl.ANY)
    shape, dma = jax.ShapeDtypeStruct, pltpu.SemaphoreType.DMA
    gathered = [shape((2 * depth * s.rows, s.cols), half) for s in slabs]

    def kept(height):
        return [
            shape((height, width), f32),
            shape((height, 3 * width), half),
            shape((height, width), half),
            shape((height, width), f32),
            shape((height, inner), f32),
        ]

    saved = kept(rows) + kept(tokens)
    outs = gathered + saved
    outs += [shape((tokens, width), half), shape((CH, width), f32), shape((CH, wide), half), shape((CH, wide), half), shape((flat, wide), f32)]
    found = pl.pallas_call(
        functools.partial(first_kernel, slabs, depth),
        out_shape=outs,
        in_specs=[anywhere] * count + [whole] * 5,
        out_specs=[anywhere] * (count + 10) + [whole] * 4 + [anywhere],
        scratch_shapes=[dma((6, items)), dma((6, items)), dma((count,)), dma((count,)), dma((count,))]
        + [pltpu.VMEM(s.shape, s.dtype) for s in (*gathered[:7], *saved)]
        + [
            pltpu.VMEM((flat, wide), f32),
            pltpu.VMEM((rows, width), f32),
            pltpu.VMEM((tokens, width), f32),
            pltpu.VMEM((rows, width), half),
            pltpu.VMEM((tokens, width), half),
            dma((count,)),
            dma((11,)),
        ],
        compiler_params=pltpu.CompilerParams(collective_id=0, has_side_effects=True, vmem_limit_bytes=SUM_VMEM),
        name="gather_and_forward",
    )(*shards, embedded, vis_col, vis_row, steps, freqs)
    slabs_found, found = found[:count], found[count:]
    return slabs_found, found[:5], found[5:10], *found[10:]


SIDE = 256
BACK_TILE = 256


class Chunk:
    def __init__(self, parent, height, row, rows, col, cols, by_rows):
        self.parent, self.height = parent, height
        self.row, self.rows, self.col, self.cols, self.by_rows = row, rows, col, cols, by_rows
        self.piece = (rows // 4, cols) if by_rows else (rows, cols // 4)
        self.set_order(False, 0)

    def set_order(self, z_first, first_bit):
        self.z_first, self.first_bit = z_first, first_bit

    def shard(self, shard):
        return (pl.ds(aligned(shard * self.height + self.row, 16), self.rows), pl.ds(self.col, self.cols))

    def out(self):
        return (pl.ds(self.row, self.rows), pl.ds(self.col, self.cols))

    def within(self, quarter):
        rows, cols = self.piece
        if self.by_rows:
            return (pl.ds(aligned(quarter * rows, 16), rows), pl.ds(0, cols))
        return (pl.ds(0, rows), pl.ds(aligned(quarter * cols, 128), cols))


def cut(parent, slab, pieces):
    for i in range(pieces):
        if slab.by_rows:
            cols = slab.cols // pieces
            yield Chunk(parent, slab.rows, 0, slab.rows, i * cols, cols, True)
        else:
            rows = slab.rows // pieces
            yield Chunk(parent, slab.rows, i * rows, rows, 0, slab.cols, False)


class Summing:
    STAGES, LAG, AHEAD = 6, 4, 2

    def __init__(self, chunks, depth, grads, outs, buffers, sems):
        self.chunks, self.depth, self.grads, self.outs = chunks, depth, grads, outs
        self.held, self.from_first, self.from_second, self.from_level, self.result, self.stage = buffers
        self.stage_sem, self.out_sem, self.core_pair, self.pair, self.z_pair = sems
        self.group, self.level, self.core, self.flip = place(depth)
        self.me = 2 * self.level + self.core
        self.partner = (self.group, 2 * self.level + 1 - self.core)
        self.z_peers = [(self.group, 2 * self.level_at(step) + self.core) for step in range(1, depth)]
        self.peers = [(self.flip(0), self.me), (self.flip(1), self.me), self.partner, *self.z_peers]

    def level_at(self, step):
        return lax.rem(self.level + step + self.depth, self.depth)

    def bit(self, b):
        return (self.group // (1 << b)) % 2

    def move(self, pair, k, kind, source, target, device):
        return pltpu.make_async_remote_copy(
            src_ref=source,
            dst_ref=target,
            send_sem=pair[0].at[kind, k],
            recv_sem=pair[1].at[kind, k],
            device_id=device,
            device_id_type=MESH,
        )

    def quarter(self, k, first, second):
        b = self.chunks[k].first_bit
        return first * (1 << b) + second * (1 << (1 - b))

    def core_move(self, k, lev):
        chunk = self.chunks[k]
        source = self.grads[chunk.parent].at[chunk.shard(2 * lev + 1 - self.core)]
        return self.move(self.core_pair, k, lev, source, self.held[k].at[lev], self.partner)

    def part(self, k, quarter):
        chunk, held = self.chunks[k], self.held[k]
        where = chunk.within(quarter)
        return held.at[(self.level,) + where] if chunk.z_first else held.at[(slice(None),) + where]

    def first_move(self, k, j):
        b = self.chunks[k].first_bit
        source = self.part(k, self.quarter(k, 1 - self.bit(b), j))
        return self.move(self.pair, k, j, source, self.from_first[k].at[j], (self.flip(b), self.me))

    def second_move(self, k):
        b = self.chunks[k].first_bit
        source = self.part(k, self.quarter(k, self.bit(b), 1 - self.bit(1 - b)))
        return self.move(self.pair, k, 2, source, self.from_second[k], (self.flip(1 - b), self.me))

    def level_move(self, k, step):
        chunk, held = self.chunks[k], self.held[k]
        lev = self.level_at(step)
        source = held.at[lev] if chunk.z_first else held.at[(lev,) + chunk.within(self.group)]
        target = self.from_level[k].at[step - 1]
        return self.move(self.z_pair, k, step - 1, source, target, self.z_peers[step - 1])

    def spread(self, k, kind, whose, b):
        here = self.result[k].at[self.chunks[k].within(whose)]
        return self.move(self.pair, k, kind, here, here, (self.flip(b), self.me))

    def spread_second(self, k, whose):
        return self.spread(k, 3, whose, 1 - self.chunks[k].first_bit)

    def spread_first(self, k, j, whose):
        return self.spread(k, 4 + j, whose, self.chunks[k].first_bit)

    def out_copy(self, k):
        chunk = self.chunks[k]
        target = self.outs[chunk.parent].at[chunk.out()]
        return pltpu.make_async_copy(self.result[k], target, self.out_sem.at[k])

    def stage_copy(self, k, lev):
        chunk = self.chunks[k]
        source = self.grads[chunk.parent].at[chunk.shard(2 * lev + self.core)]
        slot = self.stage[(chunk.rows, chunk.cols)].at[lev % 2]
        return pltpu.make_async_copy(source, slot, self.stage_sem.at[k, lev % 2])

    def rows_loop(self, height, body):
        step = 32 if height % 32 == 0 else 16
        loop(height // step + self.level // self.depth, lambda i: body(at_step(i, step)))

    def add_core(self, k):
        chunk, held = self.chunks[k], self.held[k]
        stage = self.stage[(chunk.rows, chunk.cols)]
        self.stage_copy(k, 0).start()
        for lev in range(self.depth):
            if lev + 1 < self.depth:
                self.stage_copy(k, lev + 1).start()
            self.core_move(k, lev).wait_recv()
            self.stage_copy(k, lev).wait()

            def body(rows):
                total = held[lev, rows, :].astype(jnp.float32) + stage[lev % 2, rows, :].astype(jnp.float32)
                held[lev, rows, :] = total.astype(jnp.bfloat16)

            self.rows_loop(chunk.rows, body)

    def levels_of(self, k):
        return [self.level] if self.chunks[k].z_first else list(range(self.depth))

    def shifted(self, rows, by):
        return pl.ds(aligned(rows.start + by, 16), rows.size)

    def add_first(self, k):
        chunk, slot = self.chunks[k], k
        held, arrived = self.held[slot], self.from_first[slot]
        for j in range(2):
            self.first_move(k, j).wait_recv()
            top, cols = chunk.within(self.quarter(k, self.bit(chunk.first_bit), j))
            for lev in self.levels_of(k):

                def body(rows):
                    at = (lev, self.shifted(rows, top.start), cols)
                    extra = arrived[j, rows, :] if chunk.z_first else arrived[j, lev, rows, :]
                    held[at] = (held[at].astype(jnp.float32) + extra.astype(jnp.float32)).astype(jnp.bfloat16)

                self.rows_loop(chunk.piece[0], body)

    def add_second(self, k):
        chunk, slot = self.chunks[k], k
        held, arrived, result = self.held[slot], self.from_second[slot], self.result[slot]
        self.second_move(k).wait_recv()
        top, cols = chunk.within(self.group)
        for lev in self.levels_of(k):

            def body(rows):
                at = (lev, self.shifted(rows, top.start), cols)
                extra = arrived[rows, :] if chunk.z_first else arrived[lev, rows, :]
                total = (held[at].astype(jnp.float32) + extra.astype(jnp.float32)).astype(jnp.bfloat16)
                if chunk.z_first:
                    result[at[1:]] = total
                else:
                    held[at] = total

            self.rows_loop(chunk.piece[0], body)

    def add_level(self, k):
        chunk, slot = self.chunks[k], k
        held, arrived, result = self.held[slot], self.from_level[slot], self.result[slot]
        for step in range(1, self.depth):
            self.level_move(k, step).wait_recv()
        top, cols = (pl.ds(0, chunk.rows), pl.ds(0, chunk.cols)) if chunk.z_first else chunk.within(self.group)

        def body(rows):
            at = (self.shifted(rows, top.start), cols)
            total = held[(self.level,) + at].astype(jnp.float32)
            for step in range(self.depth - 1):
                total = total + arrived[step, rows, :].astype(jnp.float32)
            if chunk.z_first:
                held[(self.level,) + at] = total.astype(jnp.bfloat16)
            else:
                result[at] = total.astype(jnp.bfloat16)

        self.rows_loop(top.size, body)

    def begin_core(self, k):
        for lev in range(self.depth):
            self.core_move(k, lev).start()

    def begin_first(self, k):
        self.first_move(k, 0).start()
        self.first_move(k, 1).start()

    def begin_level(self, k):
        for step in range(1, self.depth):
            self.level_move(k, step).start()

    def begin_spread(self, k):
        self.spread_second(k, self.group).start()

    def end_spread_second(self, k):
        other = self.flip(1 - self.chunks[k].first_bit)
        self.spread_second(k, other).wait_recv()
        self.spread_first(k, 0, self.group).start()
        self.spread_first(k, 1, other).start()

    def end_spread_first(self, k):
        self.spread_first(k, 0, self.flip(self.chunks[k].first_bit)).wait_recv()
        self.spread_first(k, 1, 3 - self.group).wait_recv()
        self.out_copy(k).start()

    def stages(self, k):
        if self.chunks[k].z_first:
            return [
                lambda: (self.add_core(k), self.begin_level(k)),
                lambda: (self.add_level(k), self.begin_first(k)),
                lambda: (self.add_first(k), self.second_move(k).start()),
                lambda: (self.add_second(k), self.begin_spread(k)),
                lambda: self.end_spread_second(k),
                lambda: self.end_spread_first(k),
            ]
        return [
            lambda: (self.add_core(k), self.begin_first(k)),
            lambda: (self.add_first(k), self.second_move(k).start()),
            lambda: (self.add_second(k), self.begin_level(k)),
            lambda: (self.add_level(k), self.begin_spread(k)),
            lambda: self.end_spread_second(k),
            lambda: self.end_spread_first(k),
        ]

    def settle(self, k):
        for lev in range(self.depth):
            self.core_move(k, lev).wait_send()
        self.first_move(k, 0).wait_send()
        self.first_move(k, 1).wait_send()
        self.second_move(k).wait_send()
        for step in range(1, self.depth):
            self.level_move(k, step).wait_send()
        self.spread_second(k, self.group).wait_send()
        self.spread_first(k, 0, self.group).wait_send()
        self.spread_first(k, 1, self.flip(1 - self.chunks[k].first_bit)).wait_send()
        self.out_copy(k).wait()

    def run(self, ready, beside):
        count = len(self.chunks)
        greet(self.peers)
        plans = [self.stages(k) for k in range(count)]
        for turn in range(-self.AHEAD, count + self.LAG * (self.STAGES - 1)):
            if turn + self.AHEAD < count:
                ready(turn + self.AHEAD)
                self.begin_core(turn + self.AHEAD)
            for stage in range(self.STAGES):
                if 0 <= turn - self.LAG * stage < count:
                    plans[turn - self.LAG * stage][stage]()
                beside()
        for k in range(count):
            self.settle(k)


class Saved:
    def __init__(self, kept, buffers, sems):
        rows = kept[0].shape[0]
        part = pl.ds(0, rows)
        self.wide, self.qkv, self.mixed = (b if b.shape[0] == rows else b.at[part] for b in buffers)
        places = (self.wide, self.qkv, self.mixed, self.wide)
        self.copies = [pltpu.make_async_copy(a, b, sems.at[i]) for i, (a, b) in enumerate(zip(kept, places, strict=True))]

    def start(self, which):
        self.copies[("x", "qkv", "mixed", "middle").index(which)].start()

    def wait(self, which):
        self.copies[("x", "qkv", "mixed", "middle").index(which)].wait()


class Stream:
    def __init__(self, sources, slots, sems):
        self.sources, self.slots, self.sems, self.used = sources, slots, sems, 0
        self.copy(0).start()

    def slot(self, i):
        height, slot = self.sources[i].shape[0], self.slots.at[i % 2]
        return slot if height == slot.shape[0] else slot.at[pl.ds(0, height)]

    def copy(self, i):
        return pltpu.make_async_copy(self.sources[i], self.slot(i), self.sems.at[i % 2])

    def next(self):
        i = self.used
        self.copy(i).wait()
        if i + 1 < len(self.sources):
            self.copy(i + 1).start()
        self.used += 1
        return self.slot(i)


def backward_steps(width, grad, gain_one, gain_two, saved, following, streams, d_a, d_up, d_down, d_one, d_two,
                   grad_low, low, grad_qkv, acc, grad_mid, out, tiles, live, reach, names):
    wide, narrow, square = tiles
    downs, ups, raiseds, heads = streams
    inner, side = d_up.shape[1], SIDE
    qkv, mixed, middle, stream = saved.qkv, saved.mixed, saved.wide, saved.wide

    def begin():
        saved.wait("middle")
        grad_low[...] = grad[...].astype(jnp.bfloat16)
        scale_norm(middle, gain_two, low)
        acc[...] = jnp.zeros_like(acc)

    yield begin
    def feed_down(j):
        raised, down = raiseds.next()[...], downs.next()
        cumul = 0.5 + 0.5 * lax.erf(raised * ROOT_HALF)
        slope = cumul + raised * (jnp.exp(-0.5 * raised * raised) * (1.0 / math.sqrt(2.0 * math.pi)))
        grad_qkv[:, :BACK_TILE] = (raised * cumul).astype(jnp.bfloat16)
        narrow.put(j, rows_dot(grad_qkv[:, :BACK_TILE], grad_low[...]), d_down.at[pl.ds(j * BACK_TILE, BACK_TILE), :])
        grad_qkv[:, BACK_TILE : 2 * BACK_TILE] = (right_trans(grad_low[...], down[...]) * slope).astype(jnp.bfloat16)

    def feed_up(j):
        wide.put(j, rows_dot(low[...], grad_qkv[:, BACK_TILE : 2 * BACK_TILE]), d_up.at[:, pl.ds(j * BACK_TILE, BACK_TILE)])
        acc[...] += right_trans(grad_qkv[:, BACK_TILE : 2 * BACK_TILE], ups.next()[...])

    for j in range(inner // BACK_TILE):
        yield functools.partial(feed_down, j)
        yield functools.partial(feed_up, j)

    def middle_back():
        narrow.flush(d_down.at[pl.ds(0, BACK_TILE), :])
        wide.flush(d_up.at[:, pl.ds(0, BACK_TILE)])
        reach(names[0])
        norm_back_into(acc, middle, gain_two, grad, grad_mid, d_two)
        saved.start("x")
        grad_low[...] = grad_mid[...].astype(jnp.bfloat16)
        saved.wait("mixed")

    yield middle_back

    def project_back(j):
        cols = pl.ds(j * side, side)
        square.put(j, rows_dot(mixed[...], grad_low[:, cols]), d_a.at[:, pl.ds(3 * width + j * side, side)])
        added = right_trans(grad_low[:, cols], heads.next()[...])
        acc[...] = added if j == 0 else acc[...] + added

    for j in range(width // side):
        yield functools.partial(project_back, j)

    def mixed_back():
        if following:
            following.start("mixed")
        low[...] = acc[...].astype(jnp.bfloat16)
        saved.wait("qkv")

    yield mixed_back

    def attend(pair):
        where = [pl.ds(pair * 128 + part * width, 128) for part in range(3)]
        query, key, value = (qkv[:, at] for at in where)
        grad_mixed = low[:, pl.ds(pair * 128, 128)]
        found = []
        for half in range(2):
            probs = probabilities(query, key, half, live)
            grad_half = keep_half(grad_mixed, half)
            grad_probs = right_trans(grad_half, value)
            dots = jnp.sum(grad_probs * probs, axis=-1, keepdims=True)
            grad_scores = (probs * (grad_probs - dots) * 0.125).astype(jnp.bfloat16)
            found.append(
                (matmul(grad_scores, key), rows_dot(grad_scores, query), rows_dot(probs.astype(jnp.bfloat16), grad_half))
            )
        for part in range(3):
            both = jnp.where(head_mask(0), found[0][part], found[1][part])
            grad_qkv[:, where[part]] = both.astype(jnp.bfloat16)

    for pair in range(width // 128):
        yield functools.partial(attend, pair)

    def normed():
        if following:
            following.start("qkv")
        saved.wait("x")
        scale_norm(stream, gain_one, low)

    yield normed

    def project(j):
        piece = grad_qkv[:, pl.ds(j * side, side)]
        square.put(j + width // side, rows_dot(low[...], piece), d_a.at[:, pl.ds(j * side, side)])
        added = right_trans(piece, heads.next()[...])
        acc[...] = added if j == 0 else acc[...] + added

    for j in range(3 * width // side):
        yield functools.partial(project, j)

    def end():
        square.flush(d_a.at[:, pl.ds(0, side)])
        reach(names[1])
        norm_back_into(acc, stream, gain_one, grad_mid, out, d_one)
        if following:
            following.start("middle")

    yield end


def last_kernel(chunks, stage_keys, depth, *refs):
    head_grads, refs = refs[:3], refs[3:]
    head_small, refs = refs[:2], refs[2:]
    (grad_rows, vis_col, vis_row, vec), e_kept, d_kept, refs = refs[:4], refs[4:8], refs[8:12], refs[12:]
    (e_up, d_up, e_a, e_u, e_d, d_a, d_u, d_d), refs = refs[:8], refs[8:]
    outs, refs = refs[:10], refs[10:]
    embed_grad, small_grad, refs = refs[0], refs[1], refs[2:]
    block_grads, refs = refs[:6], refs[6:]
    (small, small_pack, d_grad, e_grad, low_a, low_b, grad_qkv, acc, grad_mid), refs = refs[:9], refs[9:]
    saved_buffers, saved_sems, refs = refs[:3], refs[3], refs[4:]
    (wide, narrow, square, down_slots, up_slots, raised_slots, head_slots, tile_sems, load_sems, pack_sem), refs = refs[:10], refs[10:]
    count = len(chunks)
    buffers = [refs[i * count : (i + 1) * count] for i in range(5)]
    refs = refs[5 * count :]
    stage, refs = dict(zip(stage_keys, refs[: len(stage_keys)], strict=True)), refs[len(stage_keys) :]
    stage_sem, out_sem, core_sent, core_got, sent, got, z_sent, z_got = refs
    sems = (stage_sem, out_sem, (core_sent, core_got), (sent, got), (z_sent, z_got))
    tokens, width = d_kept[0].shape
    rows = e_kept[0].shape[0]
    parts = 2 * depth
    d_saved = Saved(d_kept, saved_buffers, saved_sems.at[0])
    e_saved = Saved(e_kept, saved_buffers, saved_sems.at[1])
    de_a, de_u, de_d, dd_a, dd_u, dd_d = block_grads
    grads = (small_grad, *block_grads, *head_grads)
    summing = Summing(chunks, depth, grads, outs, (*buffers, stage), sems)
    tiles = (Tiles(wide, tile_sems.at[0]), Tiles(narrow, tile_sems.at[1]), Tiles(square, tile_sems.at[2]))
    reached = {"head"}
    embed_copy = pltpu.make_async_copy(d_grad, embed_grad, pack_sem.at[1])

    def streams(inner, w_a, w_u, w_d, up):
        tile = [pl.ds(j * BACK_TILE, BACK_TILE) for j in range(inner // BACK_TILE)]
        past = width // SIDE
        sides = [pl.ds((j + 3 * past) % (4 * past) * SIDE, SIDE) for j in range(4 * past)]
        return (
            Stream([w_d.at[t, :] for t in tile], down_slots, load_sems.at[0]),
            Stream([w_u.at[:, t] for t in tile], up_slots, load_sems.at[1]),
            Stream([up.at[:, t] for t in tile], raised_slots, load_sems.at[2]),
            Stream([w_a.at[:, t] for t in sides], head_slots, load_sems.at[3]),
        )

    def work():
        inner = d_u.shape[1]
        ready_streams = []

        def begin():
            for which in ("middle", "mixed", "qkv"):
                d_saved.start(which)
            ready_streams.append(streams(inner, d_a, d_u, d_d, d_up))
            d_grad[:BUFFER, :] = jnp.zeros((BUFFER, width), jnp.float32)
            d_grad[BUFFER:, :] = grad_rows[...].astype(jnp.float32)

        yield begin
        yield from lazy_steps(lambda: backward_steps(
            width, d_grad, vec[2:3, :], vec[3:4, :], d_saved, e_saved, ready_streams[0], dd_a, dd_u, dd_d,
            small.at[2], small.at[3], low_a, low_b, grad_qkv, acc, grad_mid, d_grad, tiles, None, reached.add, ("dec feed", "dec")))

        def between():
            ready_streams.append(streams(inner, e_a, e_u, e_d, e_up))
            hot = spot_hot(vis_row, tokens - BUFFER)
            masked = 1.0 - jnp.sum(hot.astype(jnp.float32), axis=1, keepdims=True)
            small[4] = jnp.broadcast_to(jnp.sum(d_grad[BUFFER:, :] * masked, axis=0, keepdims=True), (8, width))
            e_grad[:BUFFER, :] = d_grad[:BUFFER, :]
            e_grad[BUFFER:, :] = exact_dot(token_hot(vis_col, tokens - BUFFER), d_grad[BUFFER:, :])

        yield between
        part = pl.ds(0, rows)
        yield from lazy_steps(lambda: backward_steps(
            width, e_grad, vec[0:1, :], vec[1:2, :], e_saved, None, ready_streams[1], de_a, de_u, de_d,
            small.at[0], small.at[1], low_a.at[part], low_b.at[part], grad_qkv.at[part], acc.at[part],
            grad_mid.at[part], e_grad, tiles, live_keys(vis_row), reached.add, ("enc feed", "enc")))

        def end():
            d_grad[:BUFFER, :] = e_grad[:BUFFER, :]
            d_grad[BUFFER:, :] = exact_dot(spot_hot(vis_row, tokens - BUFFER), e_grad[BUFFER:, :])
            embed_copy.start()
            pack_gradients(small, head_small, parts, small_pack)
            copy = pltpu.make_async_copy(small_pack, small_grad, pack_sem.at[0])
            copy.start()
            copy.wait()
            reached.add("all")

        yield end

    steps = work()
    needs = ["all", "enc", "enc feed", "enc feed", "dec", "dec feed", "dec feed", "head", "head", "head"]

    def beside():
        step = next(steps, None)
        if step is not None:
            step()

    def ready(k):
        while needs[chunks[k].parent] not in reached:
            beside()

    summing.run(ready, beside)
    embed_copy.wait()


def lazy_steps(make):
    yield from make()


def pack_gradients(small, head_small, parts, target):
    count, _, width = small.shape
    piece = width // parts
    target[...] = jnp.zeros_like(target)
    lane = lax.broadcasted_iota(jnp.int32, (width, 128), 1)
    row = lax.broadcasted_iota(jnp.int32, (width, 128), 0)
    which = lax.broadcasted_iota(jnp.int32, (CH, width), 0)
    rows = jnp.zeros((CH, width), jnp.float32)
    for i in range(count):
        rows = jnp.where(which == i, jnp.concatenate([small[i], small[i]], axis=0), rows)
    low = rows.astype(jnp.bfloat16)
    for part in range(parts):
        block = pl.ds(part * SMALL_ROWS, CH)
        pick = ((row == lane + part * piece) & (lane < piece)).astype(jnp.bfloat16)
        target[block, :128] = matmul(low, pick).astype(jnp.bfloat16)
        for i in range(2):
            target[block, pl.ds(128 * (i + 1), 128)] = head_small[i][:, pl.ds(part * 128, 128)].astype(jnp.bfloat16)


def last_part(slabs, chunks, depth, head_grads, head_small, grad_rows, vis_col, vis_row, vec, enc_kept, dec_kept, weights):
    tokens, width = dec_kept[0].shape
    rows = enc_kept[0].shape[0]
    parts = 2 * depth
    f32, half = jnp.float32, jnp.bfloat16
    whole, anywhere = pl.BlockSpec(memory_space=pltpu.VMEM), pl.BlockSpec(memory_space=pl.ANY)
    shape, dma = jax.ShapeDtypeStruct, pltpu.SemaphoreType.DMA
    stage_keys = sorted({(c.rows, c.cols) for c in chunks})
    held, first, second, lev, result = [], [], [], [], []
    for chunk in chunks:
        part = (chunk.rows, chunk.cols)
        held.append(pltpu.VMEM((depth,) + part, half))
        result.append(pltpu.VMEM(part, half))
        if chunk.z_first:
            first.append(pltpu.VMEM((2,) + chunk.piece, half))
            second.append(pltpu.VMEM(chunk.piece, half))
            lev.append(pltpu.VMEM((depth - 1,) + part, half))
        else:
            first.append(pltpu.VMEM((2, depth) + chunk.piece, half))
            second.append(pltpu.VMEM((depth,) + chunk.piece, half))
            lev.append(pltpu.VMEM((depth - 1,) + chunk.piece, half))
    count = len(chunks)
    outs = [shape((s.rows, s.cols), half) for s in slabs]
    outs += [shape((tokens, width), f32), shape((parts * SMALL_ROWS, SMALL_COLS), half)]
    outs += [shape(w.shape, half) for w in weights]
    e_up, d_up = enc_kept[4], dec_kept[4]
    vmem = pltpu.VMEM
    found = pl.pallas_call(
        functools.partial(last_kernel, chunks, stage_keys, depth),
        out_shape=outs,
        in_specs=[anywhere] * 3 + [whole] * 6 + [anywhere] * 16,
        out_specs=[anywhere] * (len(slabs) + 8),
        scratch_shapes=[
            vmem((5, 8, width), f32),
            vmem((parts * SMALL_ROWS, SMALL_COLS), half),
            vmem((tokens, width), f32),
            vmem((rows, width), f32),
            vmem((tokens, width), half),
            vmem((tokens, width), half),
            vmem((tokens, 3 * width), half),
            vmem((tokens, width), f32),
            vmem((tokens, width), f32),
            vmem((tokens, width), f32),
            vmem((tokens, 3 * width), half),
            vmem((tokens, width), half),
            dma((2, 4)),
            vmem((2, width, BACK_TILE), half),
            vmem((2, BACK_TILE, width), half),
            vmem((2, width, SIDE), half),
            vmem((2, BACK_TILE, width), half),
            vmem((2, width, BACK_TILE), half),
            vmem((2, tokens, BACK_TILE), f32),
            vmem((2, width, SIDE), half),
            dma((3, 2)),
            dma((4, 2)),
            dma((2,)),
        ]
        + held
        + first
        + second
        + lev
        + result
        + [vmem((2,) + key, half) for key in stage_keys]
        + [
            dma((count, 2)),
            dma((count,)),
            dma((depth, count)),
            dma((depth, count)),
            dma((6, count)),
            dma((6, count)),
            dma((depth - 1, count)),
            dma((depth - 1, count)),
        ],
        compiler_params=pltpu.CompilerParams(collective_id=1, has_side_effects=True, vmem_limit_bytes=LAST_VMEM),
        name="backward_and_sum",
    )(*head_grads, *head_small, grad_rows, vis_col, vis_row, vec, *enc_kept[:4], *dec_kept[:4], e_up, d_up, *weights)
    return found[len(slabs)], found[: len(slabs)]


SMALL_ROWS, SMALL_COLS = 32, 512


def pack_small(vectors, first, last):
    parts = vectors[0].shape[0] // 96
    lanes = jnp.stack([v.reshape(parts, 96) for v in vectors], axis=1)
    lanes = jnp.pad(lanes, ((0, 0), (0, CH - len(vectors)), (0, 128 - 96)))
    wide = [w.reshape(CH, parts, 128).transpose(1, 0, 2) for w in (first, last)]
    packed = jnp.concatenate([lanes, *wide], axis=2)
    packed = jnp.pad(packed, ((0, 0), (0, SMALL_ROWS - CH), (0, SMALL_COLS - 384)))
    return packed.reshape(parts * SMALL_ROWS, SMALL_COLS)


def unpack_small(packed):
    parts = packed.shape[0] // SMALL_ROWS
    packed = packed.reshape(parts, SMALL_ROWS, SMALL_COLS)
    vectors = packed[:, :5, :96].transpose(1, 0, 2).reshape(5, parts * 96)
    wide = [packed[:, :CH, 128 * i : 128 * i + 128].transpose(1, 0, 2).reshape(CH, parts * 128) for i in (1, 2)]
    return vectors, wide[0], wide[1]


SLABS = (
    Slab(SMALL_ROWS, SMALL_COLS, False),
    Slab(96, 3072, False),
    Slab(96, 3072, False),
    Slab(384, 768, True),
    Slab(96, 3072, False),
    Slab(96, 3072, False),
    Slab(384, 768, True),
    Slab(96, 1024, False),
    Slab(128, 3072, False),
    Slab(128, 2048, False),
)


def chunks_of():
    plan = [(8, 4, ()), (9, 2, ()), (7, 1, ()), (6, 3, (0, 2)), (5, 3, ()), (4, 3, ()), (3, 3, (0, 2)), (2, 3, ()), (1, 3, ()), (0, 1, ())]
    found = []
    for parent, pieces, z_first in plan:
        for i, chunk in enumerate(cut(parent, SLABS[parent], pieces)):
            chunk.set_order(i in z_first, len(found) % 2)
            found.append(chunk)
    return found


def by_links():
    return lax.axis_size("dev") == 8 and lax.axis_size("grp") == 4


def packed_shards(shards):
    (e_one, e_qkv, e_proj, e_two, e_up, e_down, d_one, d_qkv, d_proj, d_two, d_up, d_down, fill, h_in, h_cond, h_ada, h_inner, h_outer, h_out) = shards
    large = (
        jnp.concatenate([e_qkv, e_proj], axis=1), e_up, e_down,
        jnp.concatenate([d_qkv, d_proj], axis=1), d_up, d_down,
        h_cond, h_ada, jnp.concatenate([h_inner, h_outer], axis=1),
    )
    return large, [e_one, e_two, d_one, d_two, fill], h_in, h_out


def gather_weights(shards):
    packed, vectors, h_in, h_out = packed_shards(shards)
    whole = lambda w, axis=0: lax.all_gather(w, "dev", axis=axis, tiled=True)
    return [whole(w) for w in packed], whole(jnp.stack(vectors), 1), whole(h_in, 1), whole(h_out).T


def sum_gradients(slabs, vectors, d_in, d_out):
    def scatter(grad, axis=0):
        part = lax.psum_scatter(grad.astype(jnp.float32), "dev", scatter_dimension=axis, tiled=True)
        return lax.psum(part.astype(jnp.bfloat16), "grp")

    return unpack_gradients([scatter(g) for g in slabs], scatter(vectors, 1), scatter(d_in, 1), scatter(d_out, 1))


def unpack_gradients(slabs, vectors, d_in, d_out):
    ea, eu, ed, da, du, dd, hc, ha, hio = (s.astype(jnp.float32) for s in slabs)
    vectors, d_in, d_out = (s.astype(jnp.float32) for s in (vectors, d_in, d_out))
    split = 3 * ed.shape[1]
    return (vectors[0], ea[:, :split], ea[:, split:], vectors[1], eu, ed, vectors[2], da[:, :split], da[:, split:], vectors[3], du, dd,
            vectors[4], d_in, hc, ha, hio[:, :HW], hio[:, HW:], d_out.T)


def per_device(embedded, mask_order, counts, targets, noise_copies, timesteps, *shards):
    images, tokens, width = embedded.shape
    seq_len = mask_order.shape[1]
    linked = by_links() and images == 1
    if not linked:
        slabs, vectors, w_in, w_out = gather_weights(shards)
        vec = jnp.pad(vectors.astype(jnp.float32), ((0, CH - 5), (0, 0)))
    freqs = jnp.exp(-math.log(10000.0) * jnp.arange(HW // 2, dtype=jnp.float32) / (HW // 2)).reshape(1, HW // 2)
    losses, acts_of, embed_grads, totals = [], [], [], None
    for image in range(images):
        padded = jnp.concatenate([mask_order[image], jnp.full((SPOTS,), -1, jnp.int32)])
        seen = lax.dynamic_slice(padded, (counts[image],), (SPOTS,))
        vis_col, vis_row = seen.reshape(SPOTS, 1), seen.reshape(1, SPOTS)
        steps = timesteps[image].T.reshape(COPIES * seq_len, 1)
        noise = noise_copies[image].transpose(1, 0, 2).reshape(COPIES * seq_len, CH)
        if linked:
            packed, vectors, h_in, h_out = packed_shards(shards)
            (_, *slabs), enc_kept, dec_kept, acts, vec, w_in, w_out, embeds = first_part(
                (pack_small(vectors, h_in, h_out.T), *packed), SLABS, lax.axis_size("dev") // 2,
                embedded[image], vis_col, vis_row, steps, freqs,
            )
        else:
            phase = steps.astype(jnp.float32) * freqs
            embeds = jnp.concatenate([jnp.cos(phase), jnp.sin(phase)], axis=1)
            enc_kept, dec_kept, acts = forward_blocks(embedded[image], vis_col, vis_row, vec, slabs[:6])
        grad_rows, loss, d_in, d_out, *head_grads = head_pass(
            acts, vis_row, targets[image], noise, steps, embeds, *slabs[6:], w_in, w_out
        )
        if linked:
            embed_grad, sums = last_part(
                SLABS, chunks_of(), lax.axis_size("dev") // 2, head_grads, (d_in, d_out), grad_rows, vis_col, vis_row, vec,
                enc_kept, dec_kept, slabs[:6],
            )
        else:
            embed_grad, small, block_grads = backward_blocks(grad_rows, vis_col, vis_row, vec, enc_kept, dec_kept, slabs[:6])
            found = ([*block_grads, *head_grads], small[:5], d_in, d_out)
            totals = found if totals is None else jax.tree.map(jnp.add, totals, found)
        losses.append(loss[0, 0] / (counts[image].astype(jnp.float32) * (COPIES * CH)))
        acts_of.append(acts)
        embed_grads.append(embed_grad)
    if linked:
        small, *large = sums
        shares = unpack_gradients(large, *unpack_small(small))
    else:
        shares = sum_gradients(*totals)
    return (jnp.stack(losses), jnp.stack(acts_of), jnp.stack(embed_grads), *shares)


def solution(mesh):
    return jax.shard_map(
        per_device,
        mesh=mesh,
        in_specs=(
            P(("grp", "dev"), None, None),
            P(("grp", "dev"), None),
            P(("grp", "dev")),
            P(("grp", "dev"), None, None),
            P(("grp", "dev"), None, None, None),
            P(("grp", "dev"), None, None),
            P("dev"),
            P("dev", None),
            P("dev", None),
            P("dev"),
            P("dev", None),
            P("dev", None),
            P("dev"),
            P("dev", None),
            P("dev", None),
            P("dev"),
            P("dev", None),
            P("dev", None),
            P("dev"),
            P(None, "dev"),
            P("dev", None),
            P("dev", None),
            P("dev", None),
            P("dev", None),
            P("dev", None),
        ),
        out_specs=(
            P(("grp", "dev")),
            P(("grp", "dev"), None, None),
            P(("grp", "dev"), None, None),
            P("dev"),
            P("dev", None),
            P("dev", None),
            P("dev"),
            P("dev", None),
            P("dev", None),
            P("dev"),
            P("dev", None),
            P("dev", None),
            P("dev"),
            P("dev", None),
            P("dev", None),
            P("dev"),
            P(None, "dev"),
            P("dev", None),
            P("dev", None),
            P("dev", None),
            P("dev", None),
            P("dev", None),
        ),
        check_vma=False,
    )
```

```python
import functools
import math

import jax
import jax.numpy as jnp
from jax import lax
from jax.experimental import pallas as pl
from jax.experimental.pallas import tpu as pltpu
from jax.sharding import PartitionSpec as P

MESH = pl.DeviceIdType.MESH
SUM_VMEM = 60 * 1024 * 1024
LAST_VMEM = 62 * 1024 * 1024
HW = 1024
CH = 16
COPIES = 4
STEPS_T = 1000
BUFFER = 64
SPOTS = 80
EPSILON = 1e-06
NEG_FILL = -1e30


def matmul(left, right):
    return jnp.dot(left, right, preferred_element_type=jnp.float32)


def right_trans(left, right):
    return lax.dot_general(
        left, right, (((1,), (1,)), ((), ())), preferred_element_type=jnp.float32
    )


def norm_rows(values):
    centre = values - jnp.mean(values, axis=-1, keepdims=True)
    inv_std = lax.rsqrt(jnp.mean(centre * centre, axis=-1, keepdims=True) + EPSILON)
    return (centre * inv_std, inv_std)


def norm_back(grad, normed, inv_std):
    mean_grad = jnp.mean(grad, axis=-1, keepdims=True)
    mean_cross = jnp.mean(grad * normed, axis=-1, keepdims=True)
    return inv_std * (grad - mean_grad - normed * mean_cross)


def silu_slope(values):
    sigma = jax.nn.sigmoid(values)
    return sigma * (1.0 + values * (1.0 - sigma))


def noise_angle(steps):
    return (steps.astype(jnp.float32) / STEPS_T + 0.008) / 1.008 * (math.pi / 2)


ROOT_HALF = 1.0 / math.sqrt(2.0)
TILE = 512
STEP = 16


def rows_dot(left, right):
    return lax.dot_general(left, right, (((0,), (0,)), ((), ())), preferred_element_type=jnp.float32)


def loop(count, body):
    def turn(i, carry):
        body(i)
        return carry

    lax.fori_loop(0, count, turn, 0)


def at_step(i, size=STEP):
    return pl.ds(pl.multiple_of(i * size, size), size)


def at_col(i, size):
    return pl.ds(pl.multiple_of(i * size, 128), size)


def exact_dot(ones, values):
    high = values.astype(jnp.bfloat16)
    rest = values - high.astype(jnp.float32)
    middle = rest.astype(jnp.bfloat16)
    low = (rest - middle.astype(jnp.float32)).astype(jnp.bfloat16)
    return matmul(ones, high) + matmul(ones, middle) + matmul(ones, low)


def scale_norm(source, gain, target):
    normed, _ = norm_rows(source[...])
    target[...] = (normed * gain).astype(jnp.bfloat16)


def head_mask(half):
    lane = lax.broadcasted_iota(jnp.int32, (1, 128), 1)
    return (lane < 64) if half == 0 else (lane >= 64)


def keep_half(values, half):
    return jnp.where(head_mask(half), values, jnp.zeros((), values.dtype))


def probabilities(query, key, half, bias):
    scores = right_trans(keep_half(query, half), key) * 0.125
    if bias is not None:
        scores = jnp.where(bias, scores, NEG_FILL)
    grown = jnp.exp(scores - jnp.max(scores, axis=-1, keepdims=True))
    return grown / jnp.sum(grown, axis=-1, keepdims=True)


def forward_steps(width, stream, gain_one, gain_two, w_a, w_up, w_down, qkv, mixed, middle, acted, sloped, out, low, live=None):
    def project(j):
        cols = pl.ds(j * width, width)
        qkv[:, cols] = matmul(low[...], w_a[:, cols]).astype(jnp.bfloat16)

    def attend(pair):
        query, key, value = (qkv[:, pl.ds(pair * 128 + part * width, 128)] for part in range(3))
        parts = [
            matmul(probabilities(query, key, half, live).astype(jnp.bfloat16), value) for half in range(2)
        ]
        mixed[:, pl.ds(pair * 128, 128)] = jnp.where(head_mask(0), parts[0], parts[1]).astype(jnp.bfloat16)

    def mix():
        middle[...] = stream[...] + matmul(mixed[...], w_a[:, 3 * width :])
        scale_norm(middle, gain_two, low)

    def feed(j):
        cols = pl.ds(j * TILE, TILE)
        raised = matmul(low[...], w_up[:, cols])
        cumul = 0.5 + 0.5 * lax.erf(raised * ROOT_HALF)
        slope = cumul + raised * (jnp.exp(-0.5 * raised * raised) * (1.0 / math.sqrt(2.0 * math.pi)))
        sloped[:, cols] = slope.astype(jnp.bfloat16)
        acted[:, cols] = (raised * cumul).astype(jnp.bfloat16)
        out[...] = (middle[...] if j == 0 else out[...]) + matmul(acted[:, cols], w_down[cols, :])

    yield lambda: scale_norm(stream, gain_one, low)
    for j in range(3):
        yield functools.partial(project, j)
    for pair in range(width // 128):
        yield functools.partial(attend, pair)
    yield mix
    for j in range(w_up.shape[1] // TILE):
        yield functools.partial(feed, j)


def forward_block(*args):
    for step in forward_steps(*args):
        step()


def forward_kernel(*refs):
    (embedded, vis_col, vis_row, vec, e_a_hbm, e_u_hbm, e_d_hbm, d_a_hbm, d_u_hbm, d_d_hbm,
     e_in, e_qkv, e_mixed, e_mid, e_act, e_slope, d_in, d_qkv, d_mixed, d_mid, d_act, d_slope, acts,
     e_a, e_u, e_d, d_a, d_u, d_d, e_out, d_out, e_low, d_low, sems) = refs
    width = embedded.shape[1]
    loads = [
        pltpu.make_async_copy(a, b, sems.at[i])
        for i, (a, b) in enumerate(
            [(e_a_hbm, e_a), (e_u_hbm, e_u), (e_d_hbm, e_d), (d_a_hbm, d_a), (d_u_hbm, d_u), (d_d_hbm, d_d)]
        )
    ]
    for load in loads:
        load.start()
    encode(embedded, vis_col, vec, e_in)
    for load in loads[:3]:
        load.wait()
    live = live_keys(vis_row)
    forward_block(width, e_in, vec[0:1, :], vec[1:2, :], e_a, e_u, e_d, e_qkv, e_mixed, e_mid, e_act, e_slope, e_out, e_low, live)
    spread_rows(vis_row, e_out, vec, d_in)
    for load in loads[3:]:
        load.wait()
    forward_block(width, d_in, vec[2:3, :], vec[3:4, :], d_a, d_u, d_d, d_qkv, d_mixed, d_mid, d_act, d_slope, d_out, d_low)
    acts[...] = d_out[...].astype(jnp.bfloat16)


def token_hot(vis_col, count):
    return (lax.broadcasted_iota(jnp.int32, (vis_col.shape[0], count), 1) == vis_col[...]).astype(jnp.bfloat16)


def spot_hot(vis_row, count):
    return (lax.broadcasted_iota(jnp.int32, (count, vis_row.shape[1]), 0) == vis_row[...]).astype(jnp.bfloat16)


def live_keys(vis_row):
    ones = jnp.ones((1, BUFFER), jnp.int32)
    return jnp.concatenate([ones, (vis_row[...] >= 0).astype(jnp.int32)], axis=1) > 0


def encode(embedded, vis_col, vec, target):
    tokens = embedded.shape[0] - BUFFER
    target[:BUFFER, :] = embedded[:BUFFER, :].astype(jnp.float32)
    target[BUFFER:, :] = matmul(token_hot(vis_col, tokens), embedded[BUFFER:, :])


def spread_rows(vis_row, enc_out, vec, target):
    tokens = target.shape[0] - BUFFER
    hot = spot_hot(vis_row, tokens)
    masked = 1.0 - jnp.sum(hot.astype(jnp.float32), axis=1, keepdims=True)
    target[:BUFFER, :] = enc_out[:BUFFER, :]
    target[BUFFER:, :] = exact_dot(hot, enc_out[BUFFER:, :]) + masked * vec[4:5, :]


def forward_blocks(embedded, vis_col, vis_row, vec, weights):
    tokens, width = embedded.shape
    inner = weights[1].shape[1]
    rows = BUFFER + vis_col.shape[0]
    f32, half = jnp.float32, jnp.bfloat16

    def kept(count):
        return [
            jax.ShapeDtypeStruct((count, width), f32),
            jax.ShapeDtypeStruct((count, 3 * width), half),
            jax.ShapeDtypeStruct((count, width), half),
            jax.ShapeDtypeStruct((count, width), f32),
            jax.ShapeDtypeStruct((count, inner), half),
            jax.ShapeDtypeStruct((count, inner), half),
        ]

    outs = kept(rows) + kept(tokens) + [jax.ShapeDtypeStruct((tokens, width), half)]
    whole = pl.BlockSpec(memory_space=pltpu.VMEM)
    found = pl.pallas_call(
        forward_kernel,
        out_shape=outs,
        in_specs=[whole] * 4 + [pl.BlockSpec(memory_space=pl.ANY)] * 6,
        out_specs=[whole] * len(outs),
        scratch_shapes=[pltpu.VMEM(w.shape, half) for w in weights]
        + [
            pltpu.VMEM((rows, width), f32),
            pltpu.VMEM((tokens, width), f32),
            pltpu.VMEM((rows, width), half),
            pltpu.VMEM((tokens, width), half),
            pltpu.SemaphoreType.DMA((6,)),
        ],
        compiler_params=pltpu.CompilerParams(vmem_limit_bytes=SUM_VMEM),
        name="forward_blocks",
    )(embedded, vis_col, vis_row, vec, *weights)
    return found[:6], found[6:12], found[12]


def norm_back_into(grads, source, gain, add, target, gain_grad):
    gain_grad[...] = jnp.zeros_like(gain_grad)
    height = 64 if source.shape[0] % 64 == 0 else 48

    def body(i):
        rows = at_step(i, height)
        normed, inv_std = norm_rows(source[rows, :])
        grad = grads[rows, :]
        gain_grad[...] += jnp.broadcast_to(jnp.sum(grad * normed, axis=0, keepdims=True), gain_grad.shape)
        target[rows, :] = add[rows, :] + norm_back(grad * gain, normed, inv_std)

    loop(source.shape[0] // height, body)


class Tiles:
    def __init__(self, slots, sems):
        self.slots, self.sems = slots, sems

    def put(self, i, value, target):
        slot = i % 2 if isinstance(i, int) else lax.rem(i, 2)
        copy = pltpu.make_async_copy(self.slots.at[slot], target, self.sems.at[slot])

        @pl.when(i >= 2)
        def _():
            copy.wait()

        self.slots[slot] = value.astype(jnp.bfloat16)
        copy.start()

    def flush(self, like):
        for slot in range(2):
            pltpu.make_async_copy(self.slots.at[slot], like, self.sems.at[slot]).wait()


def backward_block(width, grad, stream, gain_one, gain_two, w_a, w_up, w_down, qkv, mixed, middle, acted, sloped,
                   d_a, d_up, d_down, d_one, d_two, grad_low, low, grad_qkv, acc, grad_mid, out, tiles, live=None):
    rows = grad.shape[0]
    wide, narrow, square = tiles
    grad_low[...] = grad[...].astype(jnp.bfloat16)
    scale_norm(middle, gain_two, low)
    acc[...] = jnp.zeros_like(acc)
    count = w_up.shape[1] // TILE

    def feed(j):
        act, slope = acted[:, at_col(j, TILE)], sloped[:, at_col(j, TILE)].astype(jnp.float32)
        down = w_down[at_step(j, TILE), :]
        narrow.put(j, rows_dot(act, grad_low[...]), d_down.at[at_step(j, TILE), :])
        grad_up = (right_trans(grad_low[...], down) * slope).astype(jnp.bfloat16)
        wide.put(j, rows_dot(low[...], grad_up), d_up.at[:, at_col(j, TILE)])
        acc[...] += right_trans(grad_up, w_up[:, at_col(j, TILE)])

    loop(count, feed)
    narrow.flush(d_down.at[pl.ds(0, TILE), :])
    wide.flush(d_up.at[:, pl.ds(0, TILE)])
    norm_back_into(acc, middle, gain_two, grad, grad_mid, d_two)
    grad_low[...] = grad_mid[...].astype(jnp.bfloat16)
    for j in range(width // 256):
        square.put(j, rows_dot(mixed[...], grad_low[:, pl.ds(j * 256, 256)]), d_a.at[:, pl.ds(3 * width + j * 256, 256)])
    for j in range(width // 256):
        low[:, pl.ds(j * 256, 256)] = right_trans(grad_low[...], w_a[pl.ds(j * 256, 256), pl.ds(3 * width, width)]).astype(jnp.bfloat16)

    def attend(pair):
        where = [pl.ds(pl.multiple_of(pair * 128 + part * width, 128), 128) for part in range(3)]
        query, key, value = (qkv[:, at] for at in where)
        grad_mixed = low[:, at_col(pair, 128)]
        found = []
        for half in range(2):
            probs = probabilities(query, key, half, live)
            grad_half = keep_half(grad_mixed, half)
            grad_probs = right_trans(grad_half, value)
            dots = jnp.sum(grad_probs * probs, axis=-1, keepdims=True)
            grad_scores = (probs * (grad_probs - dots) * 0.125).astype(jnp.bfloat16)
            found.append(
                (matmul(grad_scores, key), rows_dot(grad_scores, query), rows_dot(probs.astype(jnp.bfloat16), grad_half))
            )
        for part in range(3):
            both = jnp.where(head_mask(0), found[0][part], found[1][part])
            grad_qkv[:, where[part]] = both.astype(jnp.bfloat16)

    loop(width // 128, attend)
    scale_norm(stream, gain_one, low)
    acc[...] = jnp.zeros_like(acc)
    first = width // 256

    def project(j):
        piece = grad_qkv[:, at_col(j, 256)]
        square.put(j + first, rows_dot(low[...], piece), d_a.at[:, at_col(j, 256)])
        acc[...] += right_trans(piece, w_a[:, at_col(j, 256)])

    loop(3 * width // 256, project)
    square.flush(d_a.at[:, pl.ds(0, 256)])
    norm_back_into(acc, stream, gain_one, grad_mid, out, d_one)


def backward_kernel(*refs):
    (grad_rows, vis_col, vis_row, vec, e_in, e_qkv, e_mixed, e_mid, e_act, e_slope, d_in, d_qkv, d_mixed, d_mid, d_act, d_slope,
     e_a_hbm, e_u_hbm, e_d_hbm, d_a_hbm, d_u_hbm, d_d_hbm,
     embed_grad, small, de_a, de_u, de_d, dd_a, dd_u, dd_d,
     e_a, e_u, e_d, d_a, d_u, d_d, d_grad, e_grad, low_a, low_b, grad_qkv, acc, grad_mid,
     wide, narrow, square, load_sems, tile_sems) = refs
    tokens, width = d_in.shape
    rows = e_in.shape[0]
    loads = [
        pltpu.make_async_copy(a, b, load_sems.at[i])
        for i, (a, b) in enumerate(
            [(d_d_hbm, d_d), (d_u_hbm, d_u), (d_a_hbm, d_a), (e_d_hbm, e_d), (e_u_hbm, e_u), (e_a_hbm, e_a)]
        )
    ]
    for load in loads:
        load.start()
    tiles = (Tiles(wide, tile_sems.at[0]), Tiles(narrow, tile_sems.at[1]), Tiles(square, tile_sems.at[2]))
    d_grad[:BUFFER, :] = jnp.zeros((BUFFER, width), jnp.float32)
    d_grad[BUFFER:, :] = grad_rows[...].astype(jnp.float32)
    for load in loads[:3]:
        load.wait()
    backward_block(width, d_grad, d_in, vec[2:3, :], vec[3:4, :], d_a, d_u, d_d, d_qkv, d_mixed, d_mid, d_act, d_slope,
                   dd_a, dd_u, dd_d, small.at[2:3, :], small.at[3:4, :], low_a, low_b, grad_qkv, acc, grad_mid, d_grad, tiles)
    hot = spot_hot(vis_row, tokens - BUFFER)
    masked = 1.0 - jnp.sum(hot.astype(jnp.float32), axis=1, keepdims=True)
    small[4:5, :] = jnp.sum(d_grad[BUFFER:, :] * masked, axis=0, keepdims=True)
    e_grad[:BUFFER, :] = d_grad[:BUFFER, :]
    e_grad[BUFFER:, :] = exact_dot(token_hot(vis_col, tokens - BUFFER), d_grad[BUFFER:, :])
    for load in loads[3:]:
        load.wait()
    part = pl.ds(0, rows)
    backward_block(width, e_grad, e_in, vec[0:1, :], vec[1:2, :], e_a, e_u, e_d, e_qkv, e_mixed, e_mid, e_act, e_slope,
                   de_a, de_u, de_d, small.at[0:1, :], small.at[1:2, :], low_a.at[part], low_b.at[part],
                   grad_qkv.at[part], acc.at[part], grad_mid.at[part], e_grad, tiles, live_keys(vis_row))
    embed_grad[:BUFFER, :] = e_grad[:BUFFER, :]
    embed_grad[BUFFER:, :] = exact_dot(hot, e_grad[BUFFER:, :])


def backward_blocks(grad_rows, vis_col, vis_row, vec, enc_kept, dec_kept, weights):
    tokens, width = dec_kept[0].shape
    rows = enc_kept[0].shape[0]
    f32, half = jnp.float32, jnp.bfloat16
    whole, anywhere = pl.BlockSpec(memory_space=pltpu.VMEM), pl.BlockSpec(memory_space=pl.ANY)
    outs = [jax.ShapeDtypeStruct((tokens, width), f32), jax.ShapeDtypeStruct((8, width), f32)]
    outs += [jax.ShapeDtypeStruct(w.shape, half) for w in weights]
    found = pl.pallas_call(
        backward_kernel,
        out_shape=outs,
        in_specs=[whole] * 16 + [anywhere] * 6,
        out_specs=[whole] * 2 + [anywhere] * 6,
        scratch_shapes=[pltpu.VMEM(w.shape, half) for w in weights]
        + [
            pltpu.VMEM((tokens, width), f32),
            pltpu.VMEM((rows, width), f32),
            pltpu.VMEM((tokens, width), half),
            pltpu.VMEM((tokens, width), half),
            pltpu.VMEM((tokens, 3 * width), half),
            pltpu.VMEM((tokens, width), f32),
            pltpu.VMEM((tokens, width), f32),
            pltpu.VMEM((2, width, TILE), half),
            pltpu.VMEM((2, TILE, width), half),
            pltpu.VMEM((2, width, 256), half),
            pltpu.SemaphoreType.DMA((6,)),
            pltpu.SemaphoreType.DMA((3, 2)),
        ],
        compiler_params=pltpu.CompilerParams(vmem_limit_bytes=SUM_VMEM),
        name="backward_blocks",
    )(grad_rows, vis_col, vis_row, vec, *enc_kept, *dec_kept, *weights)
    return found[0], found[1], found[2:]


def embed_steps(steps, freqs, target):
    half = freqs.shape[1]

    def body(i):
        phase = steps[at_step(i), :].astype(jnp.float32) * freqs[...]
        target[at_step(i), :half] = jnp.cos(phase)
        target[at_step(i), half:] = jnp.sin(phase)

    loop(steps.shape[0] // STEP, body)


ROWS = 128


def at_rows(i):
    return pl.ds(pl.multiple_of(i * ROWS, 16), ROWS)


def head_kernel(*refs):
    (acts, vis_row, targets, noise, steps, embeds, w_cond_hbm, w_ada_hbm, w_io_hbm, w_in, w_out,
     grad_rows, losses, d_in, d_out, d_cond, d_ada, d_io,
     w_cond, w_ada, w_io, cond, cond_full, mod, hidden, normed_in, inv_in, inner, branch, normed_out, inv_out,
     work, grad_two, grad_sum, noisy, cond_act, mlp_in, inner_act, final_in, grad_pred, grad_branch, grad_inner,
     grad_hidden, grad_mod, wide, load_sems, tile_sems) = refs
    tokens, wide_cols = targets.shape[0], w_in.shape[1]
    loads = [
        pltpu.make_async_copy(a, b, load_sems.at[i])
        for i, (a, b) in enumerate([(w_cond_hbm, w_cond), (w_ada_hbm, w_ada), (w_io_hbm, w_io)])
    ]
    for load in loads:
        load.start()
    hot = spot_hot(vis_row, tokens)
    masked = jnp.sum(hot.astype(jnp.float32), axis=1, keepdims=True) < 0.5
    loads[0].wait()
    cond[...] = matmul(acts[BUFFER:, :], w_cond[...])
    loads[1].wait()
    loads[2].wait()
    grad_sum[...] = jnp.zeros_like(grad_sum)
    columns = wide_cols // 256

    def copy_pass(c, loss):
        rows = pl.ds(pl.multiple_of(c * tokens, 16), tokens)

        def at(i):
            return pl.ds(pl.multiple_of(c * tokens + i * ROWS, 16), ROWS)

        angle = noise_angle(steps[rows, :])
        noise_vals = noise[rows, :].astype(jnp.float32)
        noisy[rows, :] = (jnp.cos(angle) * targets[...] + jnp.sin(angle) * noise_vals).astype(jnp.bfloat16)

        def condition(i):
            full = cond[at_rows(i), :] + embeds[at(i), :]
            cond_full[at_rows(i), :] = full
            cond_act[at(i), :] = (full * jax.nn.sigmoid(full)).astype(jnp.bfloat16)

        loop(tokens // ROWS, condition)

        def modulate(j):
            mod[:, at_col(j, wide_cols)] = matmul(cond_act[rows, :], w_ada[:, at_col(j, wide_cols)])

        loop(3, modulate)
        hidden[...] = matmul(noisy[rows, :], w_in[...])

        def enter(i):
            normed, inv_std = norm_rows(hidden[at_rows(i), :])
            normed_in[at_rows(i), :] = normed
            inv_in[at_rows(i), :] = inv_std
            shift, scale = mod[at_rows(i), :wide_cols], mod[at_rows(i), wide_cols : 2 * wide_cols]
            mlp_in[at(i), :] = (normed * (1.0 + scale) + shift).astype(jnp.bfloat16)

        loop(tokens // ROWS, enter)

        inner[...] = matmul(mlp_in[rows, :], w_io[:, :wide_cols])

        def activate(i):
            values = inner[at_rows(i), :]
            inner_act[at(i), :] = (values * jax.nn.sigmoid(values)).astype(jnp.bfloat16)

        loop(tokens // ROWS, activate)

        branch[...] = matmul(inner_act[rows, :], w_io[:, wide_cols:])

        def leave(i):
            gate = mod[at_rows(i), 2 * wide_cols :]
            normed, inv_std = norm_rows(hidden[at_rows(i), :] + gate * branch[at_rows(i), :])
            normed_out[at_rows(i), :] = normed
            inv_out[at_rows(i), :] = inv_std
            final_in[at(i), :] = normed.astype(jnp.bfloat16)

        loop(tokens // ROWS, leave)
        error = right_trans(final_in[rows, :], w_out[...]) - noise_vals
        loss = loss + jnp.sum(error * error, axis=1, keepdims=True)
        low_error = jnp.where(masked, error * (2.0 / COPIES), 0.0).astype(jnp.bfloat16)
        grad_pred[rows, :] = low_error
        work[...] = matmul(low_error, w_out[...])

        def back_out(i):
            gate = mod[at_rows(i), 2 * wide_cols :]
            grad = norm_back(work[at_rows(i), :], normed_out[at_rows(i), :], inv_out[at_rows(i), :])
            grad_two[at_rows(i), :] = grad
            grad_branch[at(i), :] = (grad * gate).astype(jnp.bfloat16)
            grad_mod[at(i), 2 * wide_cols :] = (grad * branch[at_rows(i), :]).astype(jnp.bfloat16)

        loop(tokens // ROWS, back_out)

        work[...] = right_trans(grad_branch[rows, :], w_io[:, wide_cols:])

        def back_act(i):
            grad_inner[at(i), :] = (work[at_rows(i), :] * silu_slope(inner[at_rows(i), :])).astype(jnp.bfloat16)

        loop(tokens // ROWS, back_act)

        work[...] = right_trans(grad_inner[rows, :], w_io[:, :wide_cols])

        def back_in(i):
            grad, normed = work[at_rows(i), :], normed_in[at_rows(i), :]
            scale = mod[at_rows(i), wide_cols : 2 * wide_cols]
            grad_mod[at(i), :wide_cols] = grad.astype(jnp.bfloat16)
            grad_mod[at(i), wide_cols : 2 * wide_cols] = (grad * normed).astype(jnp.bfloat16)
            total = grad_two[at_rows(i), :] + norm_back(grad * (1.0 + scale), normed, inv_in[at_rows(i), :])
            grad_hidden[at(i), :] = total.astype(jnp.bfloat16)

        loop(tokens // ROWS, back_in)

        def back_mod(j):
            work[:, at_col(j, 256)] = right_trans(grad_mod[rows, :], w_ada[at_step(j, 256), :])

        loop(columns, back_mod)

        def back_cond(i):
            grad_sum[at_rows(i), :] += work[at_rows(i), :] * silu_slope(cond_full[at_rows(i), :])

        loop(tokens // ROWS, back_cond)
        return loss

    loss = lax.fori_loop(0, COPIES, copy_pass, jnp.zeros((tokens, 1), jnp.float32))
    loss = jnp.where(masked, loss.astype(jnp.bfloat16).astype(jnp.float32), 0.0)
    losses[...] = jnp.broadcast_to(jnp.sum(loss, axis=0, keepdims=True), losses.shape)
    grad_cond = grad_sum[...].astype(jnp.bfloat16)
    grad_rows[...] = right_trans(grad_cond, w_cond[...]).astype(jnp.bfloat16)
    tiles = Tiles(wide, tile_sems)

    def out_ada(j):
        tiles.put(j, rows_dot(cond_act[...], grad_mod[:, at_col(j, TILE)]), d_ada.at[:, at_col(j, TILE)])

    count = 3 * wide_cols // TILE
    loop(count, out_ada)
    half = wide_cols // TILE

    def out_inner(j):
        tiles.put(j + count, rows_dot(mlp_in[...], grad_inner[:, at_col(j, TILE)]), d_io.at[:, at_col(j, TILE)])

    def out_outer(j):
        tiles.put(j + count + half, rows_dot(inner_act[...], grad_branch[:, at_col(j, TILE)]), d_io.at[:, at_col(j + half, TILE)])

    loop(half, out_inner)
    loop(half, out_outer)
    d_cond[...] = rows_dot(acts[BUFFER:, :], grad_cond).astype(jnp.bfloat16)
    d_in[...] = rows_dot(noisy[...], grad_hidden[...])
    d_out[...] = rows_dot(grad_pred[...], final_in[...])
    tiles.flush(d_ada.at[:, pl.ds(0, TILE)])


def head_pass(acts, vis_row, targets, noise, steps, embeds, w_cond, w_ada, w_io, w_in, w_out):
    tokens, width = targets.shape[0], acts.shape[1]
    wide, flat = w_in.shape[1], noise.shape[0]
    f32, half = jnp.float32, jnp.bfloat16
    whole, anywhere = pl.BlockSpec(memory_space=pltpu.VMEM), pl.BlockSpec(memory_space=pl.ANY)
    shape = jax.ShapeDtypeStruct
    outs = [
        shape((tokens, width), half), shape((8, 128), f32), shape((CH, wide), f32), shape((CH, wide), f32),
        shape(w_cond.shape, half), shape(w_ada.shape, half), shape(w_io.shape, half),
    ]
    tile = lambda cols, kind=f32: pltpu.VMEM((tokens, cols), kind)
    long = lambda cols: pltpu.VMEM((flat, cols), half)
    return pl.pallas_call(
        head_kernel,
        out_shape=outs,
        in_specs=[whole] * 6 + [anywhere] * 3 + [whole] * 2,
        out_specs=[whole] * 5 + [anywhere] * 2,
        scratch_shapes=[pltpu.VMEM(w.shape, half) for w in (w_cond, w_ada, w_io)]
        + [
            tile(wide), tile(wide), tile(3 * wide), tile(wide), tile(wide), tile(1), tile(wide), tile(wide), tile(wide), tile(1),
            tile(wide), tile(wide), tile(wide),
            long(CH), long(wide), long(wide), long(wide), long(wide), long(CH), long(wide), long(wide), long(wide), long(3 * wide),
            pltpu.VMEM((2, wide, TILE), half),
            pltpu.SemaphoreType.DMA((3,)),
            pltpu.SemaphoreType.DMA((2,)),
        ],
        compiler_params=pltpu.CompilerParams(vmem_limit_bytes=SUM_VMEM),
        name="head_pass",
    )(acts, vis_row, targets, noise, steps, embeds, w_cond, w_ada, w_io, w_in, w_out)


class Slab:
    def __init__(self, rows, cols, by_rows, direct=False):
        self.rows, self.cols, self.by_rows, self.direct = rows, cols, by_rows, direct
        self.piece = (rows // 4, cols) if by_rows else (rows, cols // 4)

    def spot(self, shard, quarter, half=None):
        piece_rows, piece_cols = self.piece
        row = shard * self.rows
        if self.by_rows:
            row = row + quarter * piece_rows
        height = piece_rows
        if half is not None:
            height = piece_rows // 2
            row = row + half * height
        col = 0 if self.by_rows else quarter * piece_cols
        return (pl.ds(aligned(row, 16), height), pl.ds(aligned(col, 128), piece_cols))

    def shard(self, shard):
        return (pl.ds(aligned(shard * self.rows, 16), self.rows), pl.ds(0, self.cols))

    def within(self, quarter):
        return self.spot(0, quarter)


def aligned(value, multiple):
    return value if isinstance(value, int) else pl.multiple_of(value, multiple)


def place(depth):
    group, device = lax.axis_index("grp"), lax.axis_index("dev")
    level, core = device // 2, device % 2
    flip = lambda bit: group + (1 << bit) * (1 - 2 * ((group // (1 << bit)) % 2))
    return group, level, core, flip


def greet(peers):
    barrier = pltpu.get_barrier_semaphore()
    for peer in peers:
        pl.semaphore_signal(barrier, inc=1, device_id=peer, device_id_type=MESH)
    pl.semaphore_wait(barrier, len(peers))


def gather_kernel(slabs, depth, *refs):
    count = len(slabs)
    mine, whole = refs[:count], refs[count : 2 * count]
    sent, got, own_sent, own_got, own_copy = refs[2 * count :]
    group, level, core, flip = place(depth)
    x_peer, y_peer = (flip(0), 2 * level + core), (flip(1), 2 * level + core)
    partner = (group, 2 * level + 1 - core)

    def level_at(step):
        return lax.rem(level + step + depth, depth)

    z_peers = [(group, 2 * level_at(step) + core) for step in range(1, depth)]
    greet([x_peer, y_peer, partner] + z_peers)

    def move(kind, item, source, target, device):
        return pltpu.make_async_remote_copy(
            src_ref=source,
            dst_ref=target,
            send_sem=sent.at[kind, item],
            recv_sem=got.at[kind, item],
            device_id=device,
            device_id_type=MESH,
        )

    Z, X, Y, XH, YH, CORE = range(6)
    items = [(k, step) for k in range(count) for step in range(1, depth)]

    def by_z(item):
        k, step = items[item]
        slab = slabs[k]
        target = whole[k].at[slab.spot(2 * level + core, group)]
        return move(Z, item, mine[k].at[slab.within(group)], target, z_peers[step - 1])

    def shard_of(item):
        return 2 * level_at(-items[item][1]) + core

    def forward(kind, item, quarter, half, device):
        k = items[item][0]
        here = whole[k].at[slabs[k].spot(shard_of(item), quarter, half)]
        return move(kind, item, here, here, device)

    def core_copy(item, core_of):
        k, step = items[item]
        here = whole[k].at[slabs[k].shard(2 * level_at(-step) + core_of)]
        return move(CORE, item, here, here, partner)

    own = []
    for k, slab in enumerate(slabs):
        for step in range(1, depth):
            by_z(k * (depth - 1) + step - 1).start()
        target = whole[k].at[slab.shard(2 * level + core)]
        keep = pltpu.make_async_copy(mine[k], target, own_copy.at[k])
        keep.start()
        share = pltpu.make_async_remote_copy(
            src_ref=mine[k],
            dst_ref=target,
            send_sem=own_sent.at[k],
            recv_sem=own_got.at[k],
            device_id=partner,
            device_id_type=MESH,
        )
        share.start()
        own.append((keep, share))

    total = len(items)
    for turn in range(total + 2):
        if turn < total:
            k = items[turn][0]
            here = whole[k].at[slabs[k].spot(shard_of(turn), group)]
            move(Z, turn, here, here, x_peer).wait_recv()
            forward(X, turn, group, None, x_peer).start()
            forward(Y, turn, group, None, y_peer).start()
        item = turn - 1
        if 0 <= item < total:
            forward(X, item, flip(0), None, x_peer).wait_recv()
            forward(YH, item, flip(0), 0, y_peer).start()
            forward(Y, item, flip(1), None, y_peer).wait_recv()
            forward(XH, item, flip(1), 1, x_peer).start()
        item = turn - 2
        if 0 <= item < total:
            far = 3 - group
            forward(YH, item, far, 0, y_peer).wait_recv()
            forward(XH, item, far, 1, x_peer).wait_recv()
            core_copy(item, core).start()
    for item in range(total):
        by_z(item).wait_send()
        forward(X, item, group, None, x_peer).wait_send()
        forward(Y, item, group, None, y_peer).wait_send()
        forward(YH, item, flip(0), 0, y_peer).wait_send()
        forward(XH, item, flip(1), 1, x_peer).wait_send()
        core_copy(item, core).wait_send()
        core_copy(item, 1 - core).wait_recv()
    for keep, share in own:
        keep.wait()
        share.wait()


def gather_slabs(shards, slabs, depth):
    count, items = len(slabs), len(slabs) * (depth - 1)
    return pl.pallas_call(
        functools.partial(gather_kernel, slabs, depth),
        out_shape=[
            jax.ShapeDtypeStruct((2 * depth * s.rows, s.cols), jnp.bfloat16) for s in slabs
        ],
        in_specs=[pl.BlockSpec(memory_space=pl.ANY)] * count,
        out_specs=[pl.BlockSpec(memory_space=pl.ANY)] * count,
        scratch_shapes=[
            pltpu.SemaphoreType.DMA((6, items)),
            pltpu.SemaphoreType.DMA((6, items)),
            pltpu.SemaphoreType.DMA((count,)),
            pltpu.SemaphoreType.DMA((count,)),
            pltpu.SemaphoreType.DMA((count,)),
        ],
        compiler_params=pltpu.CompilerParams(collective_id=0, has_side_effects=True),
        name="gather_weights",
    )(*shards)


def sum_kernel(slabs, orders, depth, *refs):
    count = len(slabs)
    grads, outs = refs[:count], refs[count : 2 * count]
    rest = refs[2 * count :]
    take = lambda: (rest[:count], rest[count:])
    held, rest = take()
    from_first, rest = take()
    from_second, rest = take()
    from_level, rest = take()
    result, rest = take()
    stage, rest = take()
    stage_sem, out_sem, core_sent, core_got, sent, got, z_sent, z_got = rest
    group, level, core, flip = place(depth)
    me = 2 * level + core
    partner = (group, 2 * level + 1 - core)
    bit = lambda b: (group // (1 << b)) % 2

    def level_at(step):
        return lax.rem(level + step + depth, depth)

    z_peers = [(group, 2 * level_at(step) + core) for step in range(1, depth)]
    greet([(flip(0), me), (flip(1), me), partner] + z_peers)

    def move(pair, k, kind, source, target, device):
        send, receive = pair
        return pltpu.make_async_remote_copy(
            src_ref=source,
            dst_ref=target,
            send_sem=send.at[kind, k],
            recv_sem=receive.at[kind, k],
            device_id=device,
            device_id_type=MESH,
        )

    def core_move(k, lev):
        source = grads[k].at[slabs[k].shard(2 * lev + 1 - core)]
        return move((core_sent, core_got), k, lev, source, held[k].at[lev], partner)

    def rows_loop(height, body):
        step = 32 if height % 32 == 0 else 16

        def turn(i, carry):
            body(pl.ds(aligned(i * step, 16), step))
            return carry

        lax.fori_loop(0, height // step, turn, 0)

    def shifted(rows, by):
        return pl.ds(aligned(rows.start + by, 16), rows.size)

    def first_bit(k):
        return 1 if orders[k] == "yx" else 0

    def quarter(k, first, second):
        b = first_bit(k)
        return first * (1 << b) + second * (1 << (1 - b))

    def first_move(k, j):
        b = first_bit(k)
        where = slabs[k].within(quarter(k, 1 - bit(b), j))
        source = held[k].at[(level,) + where] if orders[k][0] == "z" else held[k].at[(slice(None),) + where]
        return move((sent, got), k, j, source, from_first[k].at[j], (flip(b), me))

    def second_move(k):
        b = first_bit(k)
        where = slabs[k].within(quarter(k, bit(b), 1 - bit(1 - b)))
        source = held[k].at[(level,) + where] if orders[k][0] == "z" else held[k].at[(slice(None),) + where]
        return move((sent, got), k, 2, source, from_second[k], (flip(1 - b), me))

    def level_move(k, step):
        lev = level_at(step)
        source = held[k].at[lev] if orders[k][0] == "z" else held[k].at[(lev,) + slabs[k].within(group)]
        return move((z_sent, z_got), k, step - 1, source, from_level[k].at[step - 1], z_peers[step - 1])

    def spread_second(k, whose):
        here = result[k].at[slabs[k].within(whose)]
        return move((sent, got), k, 3, here, here, (flip(1 - first_bit(k)), me))

    def spread_first(k, j, whose):
        here = result[k].at[slabs[k].within(whose)]
        return move((sent, got), k, 4 + j, here, here, (flip(first_bit(k)), me))

    def out_copy(k):
        return pltpu.make_async_copy(result[k], outs[k], out_sem.at[k])

    def stage_copy(k, lev):
        source = grads[k].at[slabs[k].shard(2 * lev + core)]
        return pltpu.make_async_copy(source, stage[k].at[lev % 2], stage_sem.at[k, lev % 2])

    def add_core(k):
        slab = slabs[k]
        stage_copy(k, 0).start()
        for lev in range(depth):
            if lev + 1 < depth:
                stage_copy(k, lev + 1).start()
            core_move(k, lev).wait_recv()
            stage_copy(k, lev).wait()

            def body(rows):
                total = held[k][lev, rows, :].astype(jnp.float32) + stage[k][lev % 2, rows, :].astype(jnp.float32)
                held[k][lev, rows, :] = total.astype(jnp.bfloat16)

            rows_loop(slab.rows, body)

    def levels_of(k):
        return [level] if orders[k][0] == "z" else list(range(depth))

    def add_first(k):
        slab = slabs[k]
        for j in range(2):
            first_move(k, j).wait_recv()
            rows_of, cols = slab.within(quarter(k, bit(first_bit(k)), j))
            for lev in levels_of(k):

                def body(rows):
                    at = (lev, shifted(rows, rows_of.start), cols)
                    extra = from_first[k][j, rows, :] if orders[k][0] == "z" else from_first[k][j, lev, rows, :]
                    held[k][at] = (held[k][at].astype(jnp.float32) + extra.astype(jnp.float32)).astype(jnp.bfloat16)

                rows_loop(slab.piece[0], body)

    def add_second(k):
        slab = slabs[k]
        second_move(k).wait_recv()
        rows_of, cols = slab.within(group)
        for lev in levels_of(k):

            def body(rows):
                at = (lev, shifted(rows, rows_of.start), cols)
                extra = from_second[k][rows, :] if orders[k][0] == "z" else from_second[k][lev, rows, :]
                total = held[k][at].astype(jnp.float32) + extra.astype(jnp.float32)
                target = result[k].at[shifted(rows, rows_of.start), cols] if orders[k][0] == "z" else held[k].at[at]
                target[...] = total.astype(jnp.bfloat16)

            rows_loop(slab.piece[0], body)

    def add_level(k):
        slab = slabs[k]
        for step in range(1, depth):
            level_move(k, step).wait_recv()
        if orders[k][0] == "z":

            def body(rows):
                total = held[k][level, rows, :].astype(jnp.float32)
                for step in range(depth - 1):
                    total = total + from_level[k][step, rows, :].astype(jnp.float32)
                held[k][level, rows, :] = total.astype(jnp.bfloat16)

            rows_loop(slab.rows, body)
            return
        rows_of, cols = slab.within(group)

        def body(rows):
            at = (shifted(rows, rows_of.start), cols)
            total = held[k][(level,) + at].astype(jnp.float32)
            for step in range(depth - 1):
                total = total + from_level[k][step, rows, :].astype(jnp.float32)
            result[k][at] = total.astype(jnp.bfloat16)

        rows_loop(slab.piece[0], body)

    def begin_core(k):
        for lev in range(depth):
            core_move(k, lev).start()

    def begin_first(k):
        first_move(k, 0).start()
        first_move(k, 1).start()

    def begin_level(k):
        for step in range(1, depth):
            level_move(k, step).start()

    def end_spread_second(k):
        spread_second(k, flip(1 - first_bit(k))).wait_recv()
        spread_first(k, 0, group).start()
        spread_first(k, 1, flip(1 - first_bit(k))).start()

    def end_spread_first(k):
        b = first_bit(k)
        spread_first(k, 0, flip(b)).wait_recv()
        spread_first(k, 1, 3 - group).wait_recv()
        out_copy(k).start()

    def steps(k):
        if orders[k][0] == "z":
            return [
                lambda: (add_core(k), begin_level(k)),
                lambda: (add_level(k), begin_first(k)),
                lambda: (add_first(k), second_move(k).start()),
                lambda: (add_second(k), spread_second(k, group).start()),
                lambda: end_spread_second(k),
                lambda: end_spread_first(k),
            ]
        return [
            lambda: (add_core(k), begin_first(k)),
            lambda: (add_first(k), second_move(k).start()),
            lambda: (add_second(k), begin_level(k)),
            lambda: (add_level(k), spread_second(k, group).start()),
            lambda: end_spread_second(k),
            lambda: end_spread_first(k),
        ]

    plans = [steps(k) for k in range(count)]
    begin_core(0)
    for turn in range(count + 5):
        if turn + 1 < count:
            begin_core(turn + 1)
        for place_in in range(6):
            k = turn - place_in
            if 0 <= k < count:
                plans[k][place_in]()
    for k in range(count):
        for lev in range(depth):
            core_move(k, lev).wait_send()
        first_move(k, 0).wait_send()
        first_move(k, 1).wait_send()
        second_move(k).wait_send()
        for step in range(1, depth):
            level_move(k, step).wait_send()
        spread_second(k, group).wait_send()
        spread_first(k, 0, group).wait_send()
        spread_first(k, 1, flip(1 - first_bit(k))).wait_send()
        out_copy(k).wait()


def sum_slabs(grads, slabs, orders, depth):
    count = len(slabs)
    half = jnp.bfloat16
    held, first, second, lev, result, stage = [], [], [], [], [], []
    for slab, order in zip(slabs, orders, strict=True):
        shard = (slab.rows, slab.cols)
        held.append(pltpu.VMEM((depth,) + shard, half))
        result.append(pltpu.VMEM(shard, half))
        stage.append(pltpu.VMEM((2,) + shard, half))
        if order[0] == "z":
            first.append(pltpu.VMEM((2,) + slab.piece, half))
            second.append(pltpu.VMEM(slab.piece, half))
            lev.append(pltpu.VMEM((depth - 1,) + shard, half))
        else:
            first.append(pltpu.VMEM((2, depth) + slab.piece, half))
            second.append(pltpu.VMEM((depth,) + slab.piece, half))
            lev.append(pltpu.VMEM((depth - 1,) + slab.piece, half))
    dma = pltpu.SemaphoreType.DMA
    return pl.pallas_call(
        functools.partial(sum_kernel, slabs, orders, depth),
        out_shape=[jax.ShapeDtypeStruct((s.rows, s.cols), half) for s in slabs],
        in_specs=[pl.BlockSpec(memory_space=pl.ANY)] * count,
        out_specs=[pl.BlockSpec(memory_space=pl.ANY)] * count,
        scratch_shapes=held
        + first
        + second
        + lev
        + result
        + stage
        + [
            dma((count, 2)),
            dma((count,)),
            dma((depth, count)),
            dma((depth, count)),
            dma((6, count)),
            dma((6, count)),
            dma((depth - 1, count)),
            dma((depth - 1, count)),
        ],
        compiler_params=pltpu.CompilerParams(
            collective_id=1, has_side_effects=True, vmem_limit_bytes=SUM_VMEM
        ),
        name="sum_gradients",
    )(*grads)


class Gathering:
    LAG, AHEAD, SKEW = 2, 2, 1

    def __init__(self, slabs, depth, mine, whole, near, sems):
        self.slabs, self.depth, self.mine, self.whole, self.near = slabs, depth, mine, whole, near
        self.sent, self.got, self.z_sent, self.z_got, self.own_sent, self.own_got, self.own_copy = sems
        self.group, self.level, self.core, self.flip = place(depth)
        me = 2 * self.level + self.core
        self.peers = ((self.flip(0), me), (self.flip(1), me), (self.group, 2 * self.level + 1 - self.core))
        by_way = [sorted((o for o in range(depth) if o != z), key=lambda o: (abs(o - z), o)) for z in range(depth)]
        self.sources = [sum((self.level == z) * by_way[z][i] for z in range(depth)) for i in range(depth - 1)]
        self.items = [(k, i) for k in range(len(slabs)) for i in range(depth - 1)]
        self.items.sort(key=lambda item: (item[0] + item[1] * self.SKEW, item[1]))
        self.turn = 0
        self.turns = len(self.items) + 2 * self.LAG

    def move(self, kind, item, source, target, device):
        return pltpu.make_async_remote_copy(
            src_ref=source,
            dst_ref=target,
            send_sem=self.sent.at[kind, item],
            recv_sem=self.got.at[kind, item],
            device_id=device,
            device_id_type=MESH,
        )

    def z_part(self, k, source):
        slab, shard = self.slabs[k], 2 * source + self.core
        return self.whole[k].at[slab.shard(shard) if slab.direct else slab.spot(shard, self.group)]

    def mine_part(self, k):
        slab = self.slabs[k]
        return self.near[k] if slab.direct else self.near[k].at[slab.within(self.group)]

    def along_z(self, k, source, step):
        here = self.z_part(k, source)
        mine = source is self.level
        way = (1 - step) // 2
        return pltpu.make_async_remote_copy(
            src_ref=self.mine_part(k) if mine else here,
            dst_ref=here,
            send_sem=self.z_sent.at[way if mine else 2, k * self.depth + source],
            recv_sem=self.z_got.at[k * self.depth + source],
            device_id=(self.group, 2 * (self.level + step) + self.core),
            device_id_type=MESH,
        )

    def pass_on(self, item, act):
        k, i = self.items[item]
        source = self.sources[i]
        pl.when((source < self.level) & (self.level < self.depth - 1))(lambda: act(self.along_z(k, source, 1)))
        pl.when((source > self.level) & (self.level > 0))(lambda: act(self.along_z(k, source, -1)))

    def send_own(self, k, act):
        pl.when(self.level < self.depth - 1)(lambda: act(self.along_z(k, self.level, 1)))
        pl.when(self.level > 0)(lambda: act(self.along_z(k, self.level, -1)))

    def onward(self, kind, item, quarter, half, device):
        k, i = self.items[item]
        shard = 2 * self.sources[i] + self.core
        here = self.whole[k].at[self.slabs[k].spot(shard, quarter, half)]
        return self.move(kind, item, here, here, device)

    def direct(self, item):
        return self.slabs[self.items[item][0]].direct

    def to_core(self, item, core):
        k, i = self.items[item]
        here = self.whole[k].at[self.slabs[k].shard(2 * self.sources[i] + core)]
        return self.move(4, item, here, here, self.peers[2])

    def own(self, k):
        target = self.whole[k].at[self.slabs[k].shard(2 * self.level + self.core)]
        share = pltpu.make_async_remote_copy(
            src_ref=self.near[k],
            dst_ref=target,
            send_sem=self.own_sent.at[k],
            recv_sem=self.own_got.at[k],
            device_id=self.peers[2],
            device_id_type=MESH,
        )
        return pltpu.make_async_copy(self.near[k], target, self.own_copy.at[k, 0]), share

    def fetch_own(self, k):
        col = 0
        for i, array in enumerate(self.mine[k]):
            part = self.near[k].at[:, pl.ds(col, array.shape[1])]
            yield pltpu.make_async_copy(array, part, self.own_copy.at[k, i])
            col += array.shape[1]

    def start(self):
        for k in range(len(self.slabs)):
            for fetch in self.fetch_own(k):
                fetch.start()
        barrier = pltpu.get_barrier_semaphore()

        def greet_one(device):
            pl.semaphore_signal(barrier, inc=1, device_id=device, device_id_type=MESH)

        for peer in self.peers:
            greet_one(peer)
        up, down = self.level < self.depth - 1, self.level > 0
        pl.when(up)(lambda: greet_one((self.group, 2 * (self.level + 1) + self.core)))
        pl.when(down)(lambda: greet_one((self.group, 2 * (self.level - 1) + self.core)))
        pl.semaphore_wait(barrier, 3 + up.astype(jnp.int32) + down.astype(jnp.int32))
        self.begun = 0
        self.begin(self.AHEAD)

    def begin(self, until):
        while self.begun < min(until, len(self.slabs)):
            for fetch in self.fetch_own(self.begun):
                fetch.wait()
            self.send_own(self.begun, lambda copy: copy.start())
            for copy in self.own(self.begun):
                copy.start()
            self.begun += 1

    def pump(self, until):
        group, flip = self.group, self.flip
        x_peer, y_peer, _ = self.peers
        total = len(self.items)
        while self.turn < min(until, self.turns):
            item = self.turn
            if item < total:
                k, i = self.items[item]
                self.begin(k + i * self.SKEW + self.AHEAD)
                here = self.z_part(k, self.sources[i])
                pltpu.make_async_remote_copy(
                    src_ref=here,
                    dst_ref=here,
                    send_sem=self.z_sent.at[2, 0],
                    recv_sem=self.z_got.at[k * self.depth + self.sources[i]],
                    device_id=x_peer,
                    device_id_type=MESH,
                ).wait_recv()
                self.pass_on(item, lambda copy: copy.start())
                if self.direct(item):
                    self.to_core(item, self.core).start()
                else:
                    self.onward(0, item, group, None, x_peer).start()
                    self.onward(1, item, group, None, y_peer).start()
            item = self.turn - self.LAG
            if 0 <= item < total and not self.direct(item):
                self.onward(0, item, flip(0), None, x_peer).wait_recv()
                self.onward(3, item, flip(0), 0, y_peer).start()
                self.onward(1, item, flip(1), None, y_peer).wait_recv()
                self.onward(2, item, flip(1), 1, x_peer).start()
            item = self.turn - 2 * self.LAG
            if 0 <= item < total and not self.direct(item):
                self.onward(3, item, 3 - group, 0, y_peer).wait_recv()
                self.onward(2, item, 3 - group, 1, x_peer).wait_recv()
                self.to_core(item, self.core).start()
            self.turn += 1

    def ready_at(self, k):
        return 1 + max(item for item, (slab, _) in enumerate(self.items) if slab == k) + 2 * self.LAG

    def take(self, k):
        self.pump(self.ready_at(k))
        for item, (slab, _) in enumerate(self.items):
            if slab == k:
                self.to_core(item, 1 - self.core).wait_recv()
        keep, share = self.own(k)
        keep.wait()
        share.wait_recv()

    def finish(self):
        group, flip = self.group, self.flip
        x_peer, y_peer, _ = self.peers
        for item in range(len(self.items)):
            self.pass_on(item, lambda copy: copy.wait_send())
            self.to_core(item, self.core).wait_send()
            if self.direct(item):
                continue
            self.onward(0, item, group, None, x_peer).wait_send()
            self.onward(1, item, group, None, y_peer).wait_send()
            self.onward(3, item, flip(0), 0, y_peer).wait_send()
            self.onward(2, item, flip(1), 1, x_peer).wait_send()
        for k in range(len(self.slabs)):
            self.send_own(k, lambda copy: copy.wait_send())
            self.own(k)[1].wait_send()


def unpack_vectors(small, parts, width, vec):
    piece = width // parts
    vec[...] = jnp.zeros_like(vec)
    lane = lax.broadcasted_iota(jnp.int32, (128, width), 0)
    col = lax.broadcasted_iota(jnp.int32, (128, width), 1)
    for part in range(parts):
        spread = ((col == lane + part * piece) & (lane < piece)).astype(jnp.bfloat16)
        vec[...] += matmul(small[pl.ds(part * SMALL_ROWS, CH), :128], spread)


def first_kernel(slabs, depth, sizes, *refs):
    count, mine = len(slabs), []
    for size in sizes:
        mine.append(refs[:size])
        refs = refs[size:]
    embedded, vis_col, vis_row, steps, freqs = refs[:5]
    whole, refs = refs[5 : 5 + count], refs[5 + count :]
    kept_hbm, (acts, vec, w_in, w_out, embeds_hbm), refs = refs[:12], refs[12:17], refs[17:]
    sems, refs = refs[:7], refs[7:]
    near, refs = refs[:count], refs[count:]
    small, (e_a, e_u, e_d, d_a, d_u, d_d) = refs[0], refs[1:7]
    e_kept, d_kept = refs[7:13], refs[13:19]
    embeds, e_out, d_out, e_low, d_low, load_sems, kept_sems = refs[19:]
    width = embedded.shape[1]
    parts = 2 * depth
    gathering = Gathering(slabs, depth, mine, whole, near, sems)
    gathering.start()
    half, height = freqs.shape[1], 64
    pieces = steps.shape[0] // height
    enc_turn, dec_turn = gathering.ready_at(3), gathering.ready_at(6)
    encode(embedded, vis_col, None, e_kept[0])
    for piece in range(pieces):
        gathering.pump(piece * enc_turn // pieces)
        rows = pl.ds(piece * height, height)
        phase = steps[rows, :].astype(jnp.float32) * freqs[...]
        embeds[rows, :half] = jnp.cos(phase)
        embeds[rows, half:] = jnp.sin(phase)
    copies = [pltpu.make_async_copy(embeds, embeds_hbm, kept_sems.at[12])]
    copies[0].start()

    def fetch(slots):
        loads = []
        for slab, target in slots:
            gathering.take(slab)
            load = pltpu.make_async_copy(whole[slab], target, load_sems.at[slab])
            load.start()
            loads.append(load)
        return loads

    def run(steps_of, turn, last):
        steps_of = list(steps_of)
        for i, step in enumerate(steps_of):
            step()
            gathering.pump(turn + (last - turn) * (i + 1) // len(steps_of))

    def keep(kept, at):
        for i, buffer in enumerate(kept):
            copy = pltpu.make_async_copy(buffer, kept_hbm[at + i], kept_sems.at[at + i])
            copy.start()
            copies.append(copy)

    for load in fetch([(0, small), (1, e_a), (2, e_u), (3, e_d)]):
        load.wait()
    unpack_vectors(small, parts, width, vec)
    for part in range(parts):
        block = pl.ds(part * SMALL_ROWS, CH)
        w_in[:, pl.ds(part * 128, 128)] = small[block, pl.ds(128, 128)]
        w_out[:, pl.ds(part * 128, 128)] = small[block, pl.ds(256, 128)]
    live = live_keys(vis_row)
    run(forward_steps(width, e_kept[0], vec[0:1, :], vec[1:2, :], e_a, e_u, e_d, *e_kept[1:], e_out, e_low, live), enc_turn, dec_turn)
    keep(e_kept, 0)
    spread_rows(vis_row, e_out, vec, d_kept[0])
    for load in fetch([(4, d_a), (5, d_u), (6, d_d)]):
        load.wait()
    run(forward_steps(width, d_kept[0], vec[2:3, :], vec[3:4, :], d_a, d_u, d_d, *d_kept[1:], d_out, d_low), dec_turn, gathering.turns)
    keep(d_kept, 6)
    acts[...] = d_out[...].astype(jnp.bfloat16)
    for slab in range(7, count):
        gathering.take(slab)
    gathering.finish()
    for copy in copies:
        copy.wait()


def first_part(shards, slabs, depth, embedded, vis_col, vis_row, steps, freqs):
    tokens, width = embedded.shape
    count, items = len(slabs), len(slabs) * (depth - 1)
    inner = slabs[2].cols
    rows = BUFFER + vis_col.shape[0]
    flat, wide = steps.shape[0], 2 * freqs.shape[1]
    f32, half = jnp.float32, jnp.bfloat16
    whole, anywhere = pl.BlockSpec(memory_space=pltpu.VMEM), pl.BlockSpec(memory_space=pl.ANY)
    shape, dma = jax.ShapeDtypeStruct, pltpu.SemaphoreType.DMA
    gathered = [shape((2 * depth * s.rows, s.cols), half) for s in slabs]

    def kept(height):
        return [
            shape((height, width), f32),
            shape((height, 3 * width), half),
            shape((height, width), half),
            shape((height, width), f32),
            shape((height, inner), half),
            shape((height, inner), half),
        ]

    saved = kept(rows) + kept(tokens)
    outs = gathered + saved
    outs += [shape((tokens, width), half), shape((CH, width), f32), shape((CH, wide), half), shape((CH, wide), half), shape((flat, wide), f32)]
    found = pl.pallas_call(
        functools.partial(first_kernel, slabs, depth, [len(arrays) for arrays in shards]),
        out_shape=outs,
        in_specs=[anywhere] * sum(len(arrays) for arrays in shards) + [whole] * 5,
        out_specs=[anywhere] * (count + 12) + [whole] * 4 + [anywhere],
        scratch_shapes=[dma((5, items)), dma((5, items)), dma((3, count * depth)), dma((count * depth,)), dma((count,)), dma((count,)), dma((count, 2))]
        + [pltpu.VMEM((s.rows, s.cols), half) for s in slabs]
        + [pltpu.VMEM(s.shape, s.dtype) for s in (*gathered[:7], *saved)]
        + [
            pltpu.VMEM((flat, wide), f32),
            pltpu.VMEM((rows, width), f32),
            pltpu.VMEM((tokens, width), f32),
            pltpu.VMEM((rows, width), half),
            pltpu.VMEM((tokens, width), half),
            dma((count,)),
            dma((13,)),
        ],
        compiler_params=pltpu.CompilerParams(collective_id=0, has_side_effects=True, vmem_limit_bytes=SUM_VMEM),
        name="gather_and_forward",
    )(*(array for arrays in shards for array in arrays), embedded, vis_col, vis_row, steps, freqs)
    slabs_found, found = found[:count], found[count:]
    return slabs_found, found[:6], found[6:12], *found[12:]


SIDE = 256
BACK_TILE = 256


class Chunk:
    def __init__(self, parent, height, row, rows, col, cols, by_rows):
        self.parent, self.height = parent, height
        self.row, self.rows, self.col, self.cols, self.by_rows = row, rows, col, cols, by_rows
        self.piece = (rows // 4, cols) if by_rows else (rows, cols // 4)
        self.set_order(False, 0)

    def set_order(self, z_first, first_bit):
        self.z_first, self.first_bit = z_first, first_bit

    def shard(self, shard):
        return (pl.ds(aligned(shard * self.height + self.row, 16), self.rows), pl.ds(self.col, self.cols))

    def out(self):
        return (pl.ds(self.row, self.rows), pl.ds(self.col, self.cols))

    def within(self, quarter):
        rows, cols = self.piece
        if self.by_rows:
            return (pl.ds(aligned(quarter * rows, 16), rows), pl.ds(0, cols))
        return (pl.ds(0, rows), pl.ds(aligned(quarter * cols, 128), cols))


def cut(parent, slab, pieces):
    for i in range(pieces):
        if slab.by_rows:
            cols = slab.cols // pieces
            yield Chunk(parent, slab.rows, 0, slab.rows, i * cols, cols, True)
        else:
            rows = slab.rows // pieces
            yield Chunk(parent, slab.rows, i * rows, rows, 0, slab.cols, False)


class Summing:
    STAGES, LAG, AHEAD = 6, 5, 2

    def __init__(self, chunks, depth, grads, outs, buffers, sems):
        self.chunks, self.depth, self.grads, self.outs = chunks, depth, grads, outs
        self.held, self.from_first, self.from_second, self.from_level, self.result, self.stage = buffers
        self.stage_sem, self.out_sem, self.core_pair, self.pair, self.z_pair = sems
        self.group, self.level, self.core, self.flip = place(depth)
        self.me = 2 * self.level + self.core
        self.partner = (self.group, 2 * self.level + 1 - self.core)
        self.z_peers = [(self.group, 2 * self.level_at(step) + self.core) for step in range(1, depth)]
        self.peers = [(self.flip(0), self.me), (self.flip(1), self.me), self.partner, *self.z_peers]

    def level_at(self, step):
        return lax.rem(self.level + step + self.depth, self.depth)

    def bit(self, b):
        return (self.group // (1 << b)) % 2

    def move(self, pair, k, kind, source, target, device):
        return pltpu.make_async_remote_copy(
            src_ref=source,
            dst_ref=target,
            send_sem=pair[0].at[kind, k],
            recv_sem=pair[1].at[kind, k],
            device_id=device,
            device_id_type=MESH,
        )

    def quarter(self, k, first, second):
        b = self.chunks[k].first_bit
        return first * (1 << b) + second * (1 << (1 - b))

    def core_move(self, k, lev):
        chunk = self.chunks[k]
        source = self.grads[chunk.parent].at[chunk.shard(2 * lev + 1 - self.core)]
        return self.move(self.core_pair, k, lev, source, self.held[k].at[lev], self.partner)

    def part(self, k, quarter):
        chunk, held = self.chunks[k], self.held[k]
        where = chunk.within(quarter)
        return held.at[(self.level,) + where] if chunk.z_first else held.at[(slice(None),) + where]

    def first_move(self, k, j):
        b = self.chunks[k].first_bit
        source = self.part(k, self.quarter(k, 1 - self.bit(b), j))
        return self.move(self.pair, k, j, source, self.from_first[k].at[j], (self.flip(b), self.me))

    def second_move(self, k):
        b = self.chunks[k].first_bit
        source = self.part(k, self.quarter(k, self.bit(b), 1 - self.bit(1 - b)))
        return self.move(self.pair, k, 2, source, self.from_second[k], (self.flip(1 - b), self.me))

    def level_move(self, k, step):
        chunk, held = self.chunks[k], self.held[k]
        lev = self.level_at(step)
        source = held.at[lev] if chunk.z_first else held.at[(lev,) + chunk.within(self.group)]
        target = self.from_level[k].at[step - 1]
        return self.move(self.z_pair, k, step - 1, source, target, self.z_peers[step - 1])

    def spread(self, k, kind, whose, b):
        here = self.result[k].at[self.chunks[k].within(whose)]
        return self.move(self.pair, k, kind, here, here, (self.flip(b), self.me))

    def spread_second(self, k, whose):
        return self.spread(k, 3, whose, 1 - self.chunks[k].first_bit)

    def spread_first(self, k, j, whose):
        return self.spread(k, 4 + j, whose, self.chunks[k].first_bit)

    def out_copy(self, k):
        chunk = self.chunks[k]
        target = self.outs[chunk.parent].at[chunk.out()]
        return pltpu.make_async_copy(self.result[k], target, self.out_sem.at[k])

    def stage_copy(self, k, lev):
        chunk = self.chunks[k]
        source = self.grads[chunk.parent].at[chunk.shard(2 * lev + self.core)]
        slot = self.stage[(chunk.rows, chunk.cols)].at[lev % 2]
        return pltpu.make_async_copy(source, slot, self.stage_sem.at[k, lev % 2])

    def rows_loop(self, height, body):
        step = 32 if height % 32 == 0 else 16
        loop(height // step + self.level // self.depth, lambda i: body(at_step(i, step)))

    def add_core(self, k):
        chunk, held = self.chunks[k], self.held[k]
        stage = self.stage[(chunk.rows, chunk.cols)]
        self.stage_copy(k, 0).start()
        for lev in range(self.depth):
            if lev + 1 < self.depth:
                self.stage_copy(k, lev + 1).start()
            self.core_move(k, lev).wait_recv()
            self.stage_copy(k, lev).wait()

            def body(rows):
                total = held[lev, rows, :].astype(jnp.float32) + stage[lev % 2, rows, :].astype(jnp.float32)
                held[lev, rows, :] = total.astype(jnp.bfloat16)

            self.rows_loop(chunk.rows, body)

    def levels_of(self, k):
        return [self.level] if self.chunks[k].z_first else list(range(self.depth))

    def shifted(self, rows, by):
        return pl.ds(aligned(rows.start + by, 16), rows.size)

    def add_first(self, k):
        chunk, slot = self.chunks[k], k
        held, arrived = self.held[slot], self.from_first[slot]
        for j in range(2):
            self.first_move(k, j).wait_recv()
            top, cols = chunk.within(self.quarter(k, self.bit(chunk.first_bit), j))
            for lev in self.levels_of(k):

                def body(rows):
                    at = (lev, self.shifted(rows, top.start), cols)
                    extra = arrived[j, rows, :] if chunk.z_first else arrived[j, lev, rows, :]
                    held[at] = (held[at].astype(jnp.float32) + extra.astype(jnp.float32)).astype(jnp.bfloat16)

                self.rows_loop(chunk.piece[0], body)

    def add_second(self, k):
        chunk, slot = self.chunks[k], k
        held, arrived, result = self.held[slot], self.from_second[slot], self.result[slot]
        self.second_move(k).wait_recv()
        top, cols = chunk.within(self.group)
        for lev in self.levels_of(k):

            def body(rows):
                at = (lev, self.shifted(rows, top.start), cols)
                extra = arrived[rows, :] if chunk.z_first else arrived[lev, rows, :]
                total = (held[at].astype(jnp.float32) + extra.astype(jnp.float32)).astype(jnp.bfloat16)
                if chunk.z_first:
                    result[at[1:]] = total
                else:
                    held[at] = total

            self.rows_loop(chunk.piece[0], body)

    def add_level(self, k):
        chunk, slot = self.chunks[k], k
        held, arrived, result = self.held[slot], self.from_level[slot], self.result[slot]
        for step in range(1, self.depth):
            self.level_move(k, step).wait_recv()
        top, cols = (pl.ds(0, chunk.rows), pl.ds(0, chunk.cols)) if chunk.z_first else chunk.within(self.group)

        def body(rows):
            at = (self.shifted(rows, top.start), cols)
            total = held[(self.level,) + at].astype(jnp.float32)
            for step in range(self.depth - 1):
                total = total + arrived[step, rows, :].astype(jnp.float32)
            if chunk.z_first:
                held[(self.level,) + at] = total.astype(jnp.bfloat16)
            else:
                result[at] = total.astype(jnp.bfloat16)

        self.rows_loop(top.size, body)

    def begin_core(self, k):
        for lev in range(self.depth):
            self.core_move(k, lev).start()

    def begin_first(self, k):
        self.first_move(k, 0).start()
        self.first_move(k, 1).start()

    def begin_level(self, k):
        for step in range(1, self.depth):
            self.level_move(k, step).start()

    def begin_spread(self, k):
        self.spread_second(k, self.group).start()

    def end_spread_second(self, k):
        other = self.flip(1 - self.chunks[k].first_bit)
        self.spread_second(k, other).wait_recv()
        self.spread_first(k, 0, self.group).start()
        self.spread_first(k, 1, other).start()

    def end_spread_first(self, k):
        self.spread_first(k, 0, self.flip(self.chunks[k].first_bit)).wait_recv()
        self.spread_first(k, 1, 3 - self.group).wait_recv()
        self.out_copy(k).start()

    def stages(self, k):
        if self.chunks[k].z_first:
            return [
                lambda: (self.add_core(k), self.begin_level(k)),
                lambda: (self.add_level(k), self.begin_first(k)),
                lambda: (self.add_first(k), self.second_move(k).start()),
                lambda: (self.add_second(k), self.begin_spread(k)),
                lambda: self.end_spread_second(k),
                lambda: self.end_spread_first(k),
            ]
        return [
            lambda: (self.add_core(k), self.begin_first(k)),
            lambda: (self.add_first(k), self.second_move(k).start()),
            lambda: (self.add_second(k), self.begin_level(k)),
            lambda: (self.add_level(k), self.begin_spread(k)),
            lambda: self.end_spread_second(k),
            lambda: self.end_spread_first(k),
        ]

    def settle(self, k):
        for lev in range(self.depth):
            self.core_move(k, lev).wait_send()
        self.first_move(k, 0).wait_send()
        self.first_move(k, 1).wait_send()
        self.second_move(k).wait_send()
        for step in range(1, self.depth):
            self.level_move(k, step).wait_send()
        self.spread_second(k, self.group).wait_send()
        self.spread_first(k, 0, self.group).wait_send()
        self.spread_first(k, 1, self.flip(1 - self.chunks[k].first_bit)).wait_send()
        self.out_copy(k).wait()

    def run(self, ready, beside):
        count = len(self.chunks)
        greet(self.peers)
        plans = [self.stages(k) for k in range(count)]
        for turn in range(-self.AHEAD, count + self.LAG * (self.STAGES - 1)):
            if turn + self.AHEAD < count:
                ready(turn + self.AHEAD)
                self.begin_core(turn + self.AHEAD)
            for stage in range(self.STAGES):
                if 0 <= turn - self.LAG * stage < count:
                    plans[turn - self.LAG * stage][stage]()
                beside()
        for k in range(count):
            self.settle(k)


class Saved:
    def __init__(self, kept, buffers, sems):
        rows = kept[0].shape[0]
        part = pl.ds(0, rows)
        self.wide, self.qkv, self.mixed = (b if b.shape[0] == rows else b.at[part] for b in buffers)
        places = (self.wide, self.qkv, self.mixed, self.wide)
        self.copies = [pltpu.make_async_copy(a, b, sems.at[i]) for i, (a, b) in enumerate(zip(kept, places, strict=True))]

    def start(self, which):
        self.copies[("x", "qkv", "mixed", "middle").index(which)].start()

    def wait(self, which):
        self.copies[("x", "qkv", "mixed", "middle").index(which)].wait()


class Stream:
    SLOTS = 3

    def __init__(self, sources, slots, sems):
        self.sources, self.slots, self.sems, self.used = sources, slots, sems, 0
        for i in range(self.SLOTS - 1):
            self.copy(i).start()

    def slot(self, i):
        height, slot = self.sources[i].shape[0], self.slots.at[i % self.SLOTS]
        return slot if height == slot.shape[0] else slot.at[pl.ds(0, height)]

    def copy(self, i):
        return pltpu.make_async_copy(self.sources[i], self.slot(i), self.sems.at[i % self.SLOTS])

    def next(self):
        i = self.used
        self.copy(i).wait()
        if i + self.SLOTS - 1 < len(self.sources):
            self.copy(i + self.SLOTS - 1).start()
        self.used += 1
        return self.slot(i)


def backward_steps(width, grad, gain_one, gain_two, saved, following, streams, d_a, d_up, d_down, d_one, d_two,
                   grad_low, low, grad_qkv, acc, grad_mid, out, tiles, live, reach, names):
    wide, narrow, square = tiles
    downs, ups, acts, slopes, heads = streams
    inner, side = d_up.shape[1], SIDE
    qkv, mixed, middle, stream = saved.qkv, saved.mixed, saved.wide, saved.wide

    def begin():
        saved.wait("middle")
        grad_low[...] = grad[...].astype(jnp.bfloat16)
        scale_norm(middle, gain_two, low)
        acc[...] = jnp.zeros_like(acc)

    yield begin
    def feed_down(j):
        narrow.put(j, rows_dot(acts.next()[...], grad_low[...]), d_down.at[pl.ds(j * BACK_TILE, BACK_TILE), :])

    def feed_slope(j):
        slope = slopes.next()[...].astype(jnp.float32)
        grad_qkv[:, :BACK_TILE] = (right_trans(grad_low[...], downs.next()[...]) * slope).astype(jnp.bfloat16)

    def feed_up(j):
        wide.put(j, rows_dot(low[...], grad_qkv[:, :BACK_TILE]), d_up.at[:, pl.ds(j * BACK_TILE, BACK_TILE)])
        acc[...] += right_trans(grad_qkv[:, :BACK_TILE], ups.next()[...])

    def down_done():
        narrow.flush(d_down.at[pl.ds(0, BACK_TILE), :])
        reach(names[0])

    for j in range(inner // BACK_TILE):
        yield functools.partial(feed_down, j)
    yield down_done
    for j in range(inner // BACK_TILE):
        yield functools.partial(feed_slope, j)
        yield functools.partial(feed_up, j)

    def middle_back():
        wide.flush(d_up.at[:, pl.ds(0, BACK_TILE)])
        reach(names[1])
        norm_back_into(acc, middle, gain_two, grad, grad_mid, d_two)
        saved.start("x")
        grad_low[...] = grad_mid[...].astype(jnp.bfloat16)
        saved.wait("mixed")

    yield middle_back

    def project_back(j):
        cols = pl.ds(j * side, side)
        square.put(j, rows_dot(mixed[...], grad_low[:, cols]), d_a.at[:, pl.ds(3 * width + j * side, side)])
        added = right_trans(grad_low[:, cols], heads.next()[...])
        acc[...] = added if j == 0 else acc[...] + added

    for j in range(width // side):
        yield functools.partial(project_back, j)

    def mixed_back():
        if following:
            following.start("mixed")
        low[...] = acc[...].astype(jnp.bfloat16)
        saved.wait("qkv")

    yield mixed_back

    def attend(pair):
        where = [pl.ds(pair * 128 + part * width, 128) for part in range(3)]
        query, key, value = (qkv[:, at] for at in where)
        grad_mixed = low[:, pl.ds(pair * 128, 128)]
        found = []
        for half in range(2):
            probs = probabilities(query, key, half, live)
            grad_half = keep_half(grad_mixed, half)
            grad_probs = right_trans(grad_half, value)
            dots = jnp.sum(grad_probs * probs, axis=-1, keepdims=True)
            grad_scores = (probs * (grad_probs - dots) * 0.125).astype(jnp.bfloat16)
            found.append(
                (matmul(grad_scores, key), rows_dot(grad_scores, query), rows_dot(probs.astype(jnp.bfloat16), grad_half))
            )
        for part in range(3):
            both = jnp.where(head_mask(0), found[0][part], found[1][part])
            grad_qkv[:, where[part]] = both.astype(jnp.bfloat16)

    for pair in range(width // 128):
        yield functools.partial(attend, pair)

    def normed():
        if following:
            following.start("qkv")
        saved.wait("x")
        scale_norm(stream, gain_one, low)

    yield normed

    def project(j):
        piece = grad_qkv[:, pl.ds(j * side, side)]
        square.put(j + width // side, rows_dot(low[...], piece), d_a.at[:, pl.ds(j * side, side)])
        added = right_trans(piece, heads.next()[...])
        acc[...] = added if j == 0 else acc[...] + added

    for j in range(3 * width // side):
        yield functools.partial(project, j)

    def end():
        square.flush(d_a.at[:, pl.ds(0, side)])
        reach(names[2])
        norm_back_into(acc, stream, gain_one, grad_mid, out, d_one)
        if following:
            following.start("middle")

    yield end


def last_kernel(chunks, stage_keys, depth, *refs):
    head_grads, refs = refs[:3], refs[3:]
    head_small, refs = refs[:2], refs[2:]
    (vis_col, vis_row, vec, grad_rows), e_kept, d_kept, refs = refs[:4], refs[4:10], refs[10:16], refs[16:]
    (e_a, e_u, e_d, d_a, d_u, d_d), refs = refs[:6], refs[6:]
    outs, refs = refs[:10], refs[10:]
    embed_grad, small_grad, refs = refs[0], refs[1], refs[2:]
    block_grads, refs = refs[:6], refs[6:]
    (small, small_pack, d_grad, low_a, low_b, grad_qkv, acc, grad_mid), refs = refs[:8], refs[8:]
    saved_buffers, saved_sems, refs = refs[:3], refs[3], refs[4:]
    (wide, narrow, square, down_slots, up_slots, act_slots, slope_slots, head_slots, tile_sems, load_sems, pack_sem), refs = refs[:11], refs[11:]
    count = len(chunks)
    buffers = [refs[i * count : (i + 1) * count] for i in range(5)]
    refs = refs[5 * count :]
    stage, refs = dict(zip(stage_keys, refs[: len(stage_keys)], strict=True)), refs[len(stage_keys) :]
    stage_sem, out_sem, core_sent, core_got, sent, got, z_sent, z_got = refs
    sems = (stage_sem, out_sem, (core_sent, core_got), (sent, got), (z_sent, z_got))
    tokens, width = d_kept[0].shape
    rows = e_kept[0].shape[0]
    parts = 2 * depth
    d_saved = Saved(d_kept[:4], saved_buffers, saved_sems.at[0])
    e_saved = Saved(e_kept[:4], saved_buffers, saved_sems.at[1])
    de_a, de_u, de_d, dd_a, dd_u, dd_d = block_grads
    grads = (small_grad, *block_grads, *head_grads)
    summing = Summing(chunks, depth, grads, outs, (*buffers, stage), sems)
    tiles = (Tiles(wide, tile_sems.at[0]), Tiles(narrow, tile_sems.at[1]), Tiles(square, tile_sems.at[2]))
    reached = {"head"}
    e_grad = d_grad.at[pl.ds(0, rows)]
    embed_copy = pltpu.make_async_copy(d_grad, embed_grad, pack_sem.at[1])

    def streams(inner, w_a, w_u, w_d, acted, sloped):
        tile = [pl.ds(j * BACK_TILE, BACK_TILE) for j in range(inner // BACK_TILE)]
        past = width // SIDE
        sides = [pl.ds((j + 3 * past) % (4 * past) * SIDE, SIDE) for j in range(4 * past)]
        return (
            Stream([w_d.at[t, :] for t in tile], down_slots, load_sems.at[0]),
            Stream([w_u.at[:, t] for t in tile], up_slots, load_sems.at[1]),
            Stream([acted.at[:, t] for t in tile], act_slots, load_sems.at[2]),
            Stream([sloped.at[:, t] for t in tile], slope_slots, load_sems.at[3]),
            Stream([w_a.at[:, t] for t in sides], head_slots, load_sems.at[4]),
        )

    def work():
        inner = d_u.shape[1]
        ready_streams = []

        def begin():
            for which in ("middle", "mixed", "qkv"):
                d_saved.start(which)
            ready_streams.append(streams(inner, d_a, d_u, d_d, *d_kept[4:]))
            arrived = low_b.at[pl.ds(BUFFER, tokens - BUFFER)]
            fetch = pltpu.make_async_copy(grad_rows, arrived, pack_sem.at[2])
            fetch.start()
            fetch.wait()
            d_grad[:BUFFER, :] = jnp.zeros((BUFFER, width), jnp.float32)
            d_grad[BUFFER:, :] = arrived[...].astype(jnp.float32)

        yield begin
        yield from lazy_steps(lambda: backward_steps(
            width, d_grad, vec[2:3, :], vec[3:4, :], d_saved, e_saved, ready_streams[0], dd_a, dd_u, dd_d,
            small.at[2], small.at[3], low_a, low_b, grad_qkv, acc, grad_mid, d_grad, tiles, None, reached.add, ("dec down", "dec up", "dec")))

        def between():
            ready_streams.append(streams(inner, e_a, e_u, e_d, *e_kept[4:]))
            hot = spot_hot(vis_row, tokens - BUFFER)
            masked = 1.0 - jnp.sum(hot.astype(jnp.float32), axis=1, keepdims=True)
            small[4] = jnp.broadcast_to(jnp.sum(d_grad[BUFFER:, :] * masked, axis=0, keepdims=True), (8, width))
            e_grad[BUFFER:, :] = exact_dot(token_hot(vis_col, tokens - BUFFER), d_grad[BUFFER:, :])

        yield between
        part = pl.ds(0, rows)
        yield from lazy_steps(lambda: backward_steps(
            width, e_grad, vec[0:1, :], vec[1:2, :], e_saved, None, ready_streams[1], de_a, de_u, de_d,
            small.at[0], small.at[1], low_a.at[part], low_b.at[part], grad_qkv.at[part], acc.at[part],
            grad_mid.at[part], e_grad, tiles, live_keys(vis_row), reached.add, ("enc down", "enc up", "enc")))

        def end():
            d_grad[BUFFER:, :] = exact_dot(spot_hot(vis_row, tokens - BUFFER), e_grad[BUFFER:, :])
            embed_copy.start()
            pack_gradients(small, head_small, parts, small_pack)
            copy = pltpu.make_async_copy(small_pack, small_grad, pack_sem.at[0])
            copy.start()
            copy.wait()
            reached.add("all")

        yield end

    steps = work()
    needs = ["all", "enc", "enc up", "enc down", "dec", "dec up", "dec down", "head", "head", "head"]

    def beside():
        step = next(steps, None)
        if step is not None:
            step()

    def ready(k):
        while needs[chunks[k].parent] not in reached:
            beside()

    summing.run(ready, beside)
    embed_copy.wait()


def lazy_steps(make):
    yield from make()


def pack_gradients(small, head_small, parts, target):
    count, _, width = small.shape
    piece = width // parts
    target[...] = jnp.zeros_like(target)
    lane = lax.broadcasted_iota(jnp.int32, (width, 128), 1)
    row = lax.broadcasted_iota(jnp.int32, (width, 128), 0)
    which = lax.broadcasted_iota(jnp.int32, (CH, width), 0)
    rows = jnp.zeros((CH, width), jnp.float32)
    for i in range(count):
        rows = jnp.where(which == i, jnp.concatenate([small[i], small[i]], axis=0), rows)
    low = rows.astype(jnp.bfloat16)
    for part in range(parts):
        block = pl.ds(part * SMALL_ROWS, CH)
        pick = ((row == lane + part * piece) & (lane < piece)).astype(jnp.bfloat16)
        target[block, :128] = matmul(low, pick).astype(jnp.bfloat16)
        for i in range(2):
            target[block, pl.ds(128 * (i + 1), 128)] = head_small[i][:, pl.ds(part * 128, 128)].astype(jnp.bfloat16)


def last_part(slabs, chunks, depth, head_grads, head_small, grad_rows, vis_col, vis_row, vec, enc_kept, dec_kept, weights):
    tokens, width = dec_kept[0].shape
    rows = enc_kept[0].shape[0]
    parts = 2 * depth
    f32, half = jnp.float32, jnp.bfloat16
    whole, anywhere = pl.BlockSpec(memory_space=pltpu.VMEM), pl.BlockSpec(memory_space=pl.ANY)
    shape, dma = jax.ShapeDtypeStruct, pltpu.SemaphoreType.DMA
    stage_keys = sorted({(c.rows, c.cols) for c in chunks})
    held, first, second, lev, result = [], [], [], [], []
    for chunk in chunks:
        part = (chunk.rows, chunk.cols)
        held.append(pltpu.VMEM((depth,) + part, half))
        result.append(pltpu.VMEM(part, half))
        if chunk.z_first:
            first.append(pltpu.VMEM((2,) + chunk.piece, half))
            second.append(pltpu.VMEM(chunk.piece, half))
            lev.append(pltpu.VMEM((depth - 1,) + part, half))
        else:
            first.append(pltpu.VMEM((2, depth) + chunk.piece, half))
            second.append(pltpu.VMEM((depth,) + chunk.piece, half))
            lev.append(pltpu.VMEM((depth - 1,) + chunk.piece, half))
    count = len(chunks)
    outs = [shape((s.rows, s.cols), half) for s in slabs]
    outs += [shape((tokens, width), f32), shape((parts * SMALL_ROWS, SMALL_COLS), half)]
    outs += [shape(w.shape, half) for w in weights]
    vmem = pltpu.VMEM
    found = pl.pallas_call(
        functools.partial(last_kernel, chunks, stage_keys, depth),
        out_shape=outs,
        in_specs=[anywhere] * 3 + [whole] * 5 + [anywhere] * 19,
        out_specs=[anywhere] * (len(slabs) + 8),
        scratch_shapes=[
            vmem((5, 8, width), f32),
            vmem((parts * SMALL_ROWS, SMALL_COLS), half),
            vmem((tokens, width), f32),
            vmem((tokens, width), half),
            vmem((tokens, width), half),
            vmem((tokens, 3 * width), half),
            vmem((tokens, width), f32),
            vmem((tokens, width), f32),
            vmem((tokens, width), f32),
            vmem((tokens, 3 * width), half),
            vmem((tokens, width), half),
            dma((2, 4)),
            vmem((2, width, BACK_TILE), half),
            vmem((2, BACK_TILE, width), half),
            vmem((2, width, SIDE), half),
            vmem((Stream.SLOTS, BACK_TILE, width), half),
            vmem((Stream.SLOTS, width, BACK_TILE), half),
            vmem((Stream.SLOTS, tokens, BACK_TILE), half),
            vmem((Stream.SLOTS, tokens, BACK_TILE), half),
            vmem((Stream.SLOTS, width, SIDE), half),
            dma((3, 2)),
            dma((5, Stream.SLOTS)),
            dma((3,)),
        ]
        + held
        + first
        + second
        + lev
        + result
        + [vmem((2,) + key, half) for key in stage_keys]
        + [
            dma((count, 2)),
            dma((count,)),
            dma((depth, count)),
            dma((depth, count)),
            dma((6, count)),
            dma((6, count)),
            dma((depth - 1, count)),
            dma((depth - 1, count)),
        ],
        compiler_params=pltpu.CompilerParams(collective_id=1, has_side_effects=True, vmem_limit_bytes=LAST_VMEM),
        name="backward_and_sum",
    )(*head_grads, *head_small, vis_col, vis_row, vec, grad_rows, *enc_kept, *dec_kept, *weights)
    return found[len(slabs)], found[: len(slabs)]


SMALL_ROWS, SMALL_COLS = 32, 512


def pack_small(vectors, first, last):
    parts = vectors[0].shape[0] // 96
    lanes = jnp.stack([v.reshape(parts, 96) for v in vectors], axis=1)
    lanes = jnp.pad(lanes, ((0, 0), (0, CH - len(vectors)), (0, 128 - 96)))
    wide = [w.reshape(CH, parts, 128).transpose(1, 0, 2) for w in (first, last)]
    packed = jnp.concatenate([lanes, *wide], axis=2)
    packed = jnp.pad(packed, ((0, 0), (0, SMALL_ROWS - CH), (0, SMALL_COLS - 384)))
    return packed.reshape(parts * SMALL_ROWS, SMALL_COLS)


def unpack_small(packed):
    parts = packed.shape[0] // SMALL_ROWS
    packed = packed.reshape(parts, SMALL_ROWS, SMALL_COLS)
    vectors = packed[:, :5, :96].transpose(1, 0, 2).reshape(5, parts * 96)
    wide = [packed[:, :CH, 128 * i : 128 * i + 128].transpose(1, 0, 2).reshape(CH, parts * 128) for i in (1, 2)]
    return vectors, wide[0], wide[1]


SLABS = (
    Slab(SMALL_ROWS, SMALL_COLS, False, True),
    Slab(96, 3072, False),
    Slab(96, 3072, False),
    Slab(384, 768, True),
    Slab(96, 3072, False),
    Slab(96, 3072, False),
    Slab(384, 768, True),
    Slab(128, 3072, False),
    Slab(128, 2048, False),
    Slab(96, 1024, False, True),
)


def chunks_of():
    plan = [(7, 4, ()), (8, 2, ()), (9, 1, ()), (6, 3, (0, 2)), (5, 3, ()), (4, 3, ()), (3, 3, (0, 2)), (2, 3, ()), (1, 3, ()), (0, 1, ())]
    found = []
    for parent, pieces, z_first in plan:
        for i, chunk in enumerate(cut(parent, SLABS[parent], pieces)):
            chunk.set_order(i in z_first, len(found) % 2)
            found.append(chunk)
    return found


def by_links():
    return lax.axis_size("dev") == 8 and lax.axis_size("grp") == 4


def packed_shards(shards):
    (e_one, e_qkv, e_proj, e_two, e_up, e_down, d_one, d_qkv, d_proj, d_two, d_up, d_down, fill, h_in, h_cond, h_ada, h_inner, h_outer, h_out) = shards
    large = ((e_qkv, e_proj), (e_up,), (e_down,), (d_qkv, d_proj), (d_up,), (d_down,), (h_ada,), (h_inner, h_outer), (h_cond,))
    return large, [e_one, e_two, d_one, d_two, fill], h_in, h_out


def gather_weights(shards):
    packed, vectors, h_in, h_out = packed_shards(shards)
    whole = lambda w, axis=0: lax.all_gather(w, "dev", axis=axis, tiled=True)
    return [whole(jnp.concatenate(w, axis=1)) for w in packed], whole(jnp.stack(vectors), 1), whole(h_in, 1), whole(h_out).T


def sum_gradients(slabs, vectors, d_in, d_out):
    def scatter(grad, axis=0):
        part = lax.psum_scatter(grad.astype(jnp.float32), "dev", scatter_dimension=axis, tiled=True)
        return lax.psum(part.astype(jnp.bfloat16), "grp")

    return unpack_gradients([scatter(g) for g in slabs], scatter(vectors, 1), scatter(d_in, 1), scatter(d_out, 1))


def widen_kernel(count, *refs):
    sources, targets = refs[:count], list(refs[count:])
    for source in sources:
        col = 0
        while col < source.shape[1]:
            target = targets.pop(0)
            width = target.shape[1]
            target[...] = source[:, col : col + width].astype(jnp.float32)
            col += width


def widen(slabs, cuts):
    shape = jax.ShapeDtypeStruct
    outs = [shape((s.shape[0], width), jnp.float32) for s, widths in zip(slabs, cuts, strict=True) for width in widths]
    whole = pl.BlockSpec(memory_space=pltpu.VMEM)
    return pl.pallas_call(
        functools.partial(widen_kernel, len(slabs)),
        out_shape=outs,
        in_specs=[whole] * len(slabs),
        out_specs=[whole] * len(outs),
        compiler_params=pltpu.CompilerParams(vmem_limit_bytes=SUM_VMEM),
        name="widen_gradients",
    )(*slabs)


def unpack_gradients(slabs, vectors, d_in, d_out):
    vectors, d_in, d_out = (s.astype(jnp.float32) for s in (vectors, d_in, d_out))
    width = slabs[2].shape[1]
    head = slabs[8].shape[1]
    cuts = [(3 * width, width), (4 * width,), (width,)] * 2 + [(3 * head,), (head, head), (head,)]
    e_qkv, e_proj, e_up, e_down, d_qkv, d_proj, d_up, d_down, ada, inner, outer, cond = widen(slabs, cuts)
    return (vectors[0], e_qkv, e_proj, vectors[1], e_up, e_down, vectors[2], d_qkv, d_proj, vectors[3], d_up, d_down,
            vectors[4], d_in, cond, ada, inner, outer, d_out.T)


def per_device(embedded, mask_order, counts, targets, noise_copies, timesteps, *shards):
    images, tokens, width = embedded.shape
    seq_len = mask_order.shape[1]
    linked = by_links() and images == 1
    if not linked:
        slabs, vectors, w_in, w_out = gather_weights(shards)
        vec = jnp.pad(vectors.astype(jnp.float32), ((0, CH - 5), (0, 0)))
    freqs = jnp.exp(-math.log(10000.0) * jnp.arange(HW // 2, dtype=jnp.float32) / (HW // 2)).reshape(1, HW // 2)
    losses, acts_of, embed_grads, totals = [], [], [], None
    for image in range(images):
        padded = jnp.concatenate([mask_order[image], jnp.full((SPOTS,), -1, jnp.int32)])
        seen = lax.dynamic_slice(padded, (counts[image],), (SPOTS,))
        vis_col, vis_row = seen.reshape(SPOTS, 1), seen.reshape(1, SPOTS)
        steps = timesteps[image].T.reshape(COPIES * seq_len, 1)
        noise = noise_copies[image].transpose(1, 0, 2).reshape(COPIES * seq_len, CH)
        if linked:
            packed, vectors, h_in, h_out = packed_shards(shards)
            (_, *slabs), enc_kept, dec_kept, acts, vec, w_in, w_out, embeds = first_part(
                ((pack_small(vectors, h_in, h_out.T),), *packed), SLABS, lax.axis_size("dev") // 2,
                embedded[image], vis_col, vis_row, steps, freqs,
            )
        else:
            phase = steps.astype(jnp.float32) * freqs
            embeds = jnp.concatenate([jnp.cos(phase), jnp.sin(phase)], axis=1)
            enc_kept, dec_kept, acts = forward_blocks(embedded[image], vis_col, vis_row, vec, slabs[:6])
        grad_rows, loss, d_in, d_out, d_cond, d_ada, d_io = head_pass(
            acts, vis_row, targets[image], noise, steps, embeds, slabs[8], slabs[6], slabs[7], w_in, w_out
        )
        head_grads = (d_ada, d_io, d_cond)
        if linked:
            embed_grad, sums = last_part(
                SLABS, chunks_of(), lax.axis_size("dev") // 2, head_grads, (d_in, d_out), grad_rows, vis_col, vis_row, vec,
                enc_kept, dec_kept, slabs[:6],
            )
        else:
            embed_grad, small, block_grads = backward_blocks(grad_rows, vis_col, vis_row, vec, enc_kept, dec_kept, slabs[:6])
            found = ([*block_grads, *head_grads], small[:5], d_in, d_out)
            totals = found if totals is None else jax.tree.map(jnp.add, totals, found)
        losses.append(loss[0, 0] / (counts[image].astype(jnp.float32) * (COPIES * CH)))
        acts_of.append(acts)
        embed_grads.append(embed_grad)
    if linked:
        small, *large = sums
        shares = unpack_gradients(large, *unpack_small(small))
    else:
        shares = sum_gradients(*totals)
    return (jnp.stack(losses), jnp.stack(acts_of), jnp.stack(embed_grads), *shares)


def solution(mesh):
    return jax.shard_map(
        per_device,
        mesh=mesh,
        in_specs=(
            P(("grp", "dev"), None, None),
            P(("grp", "dev"), None),
            P(("grp", "dev")),
            P(("grp", "dev"), None, None),
            P(("grp", "dev"), None, None, None),
            P(("grp", "dev"), None, None),
            P("dev"),
            P("dev", None),
            P("dev", None),
            P("dev"),
            P("dev", None),
            P("dev", None),
            P("dev"),
            P("dev", None),
            P("dev", None),
            P("dev"),
            P("dev", None),
            P("dev", None),
            P("dev"),
            P(None, "dev"),
            P("dev", None),
            P("dev", None),
            P("dev", None),
            P("dev", None),
            P("dev", None),
        ),
        out_specs=(
            P(("grp", "dev")),
            P(("grp", "dev"), None, None),
            P(("grp", "dev"), None, None),
            P("dev"),
            P("dev", None),
            P("dev", None),
            P("dev"),
            P("dev", None),
            P("dev", None),
            P("dev"),
            P("dev", None),
            P("dev", None),
            P("dev"),
            P("dev", None),
            P("dev", None),
            P("dev"),
            P(None, "dev"),
            P("dev", None),
            P("dev", None),
            P("dev", None),
            P("dev", None),
            P("dev", None),
        ),
        check_vma=False,
    )
```

```python
import functools
import math

import jax
import jax.numpy as jnp
from jax import lax
from jax.experimental import pallas as pl
from jax.experimental.pallas import tpu as pltpu
from jax.sharding import PartitionSpec as P

MESH = pl.DeviceIdType.MESH
SUM_VMEM = 60 * 1024 * 1024
LAST_VMEM = 62 * 1024 * 1024
HW = 1024
CH = 16
COPIES = 4
STEPS_T = 1000
BUFFER = 64
SPOTS = 80
EPSILON = 1e-06
NEG_FILL = -1e30


def matmul(left, right):
    return jnp.dot(left, right, preferred_element_type=jnp.float32)


def right_trans(left, right):
    return lax.dot_general(
        left, right, (((1,), (1,)), ((), ())), preferred_element_type=jnp.float32
    )


def norm_rows(values):
    centre = values - jnp.mean(values, axis=-1, keepdims=True)
    inv_std = lax.rsqrt(jnp.mean(centre * centre, axis=-1, keepdims=True) + EPSILON)
    return (centre * inv_std, inv_std)


def norm_back(grad, normed, inv_std):
    mean_grad = jnp.mean(grad, axis=-1, keepdims=True)
    mean_cross = jnp.mean(grad * normed, axis=-1, keepdims=True)
    return inv_std * (grad - mean_grad - normed * mean_cross)


def silu_slope(values):
    sigma = jax.nn.sigmoid(values)
    return sigma * (1.0 + values * (1.0 - sigma))


def noise_angle(steps):
    return (steps.astype(jnp.float32) / STEPS_T + 0.008) / 1.008 * (math.pi / 2)


ROOT_HALF = 1.0 / math.sqrt(2.0)
TILE = 512
STEP = 16


def rows_dot(left, right):
    return lax.dot_general(left, right, (((0,), (0,)), ((), ())), preferred_element_type=jnp.float32)


def loop(count, body):
    def turn(i, carry):
        body(i)
        return carry

    lax.fori_loop(0, count, turn, 0)


def at_step(i, size=STEP):
    return pl.ds(pl.multiple_of(i * size, size), size)


def at_col(i, size):
    return pl.ds(pl.multiple_of(i * size, 128), size)


def exact_dot(ones, values):
    high = values.astype(jnp.bfloat16)
    rest = values - high.astype(jnp.float32)
    middle = rest.astype(jnp.bfloat16)
    low = (rest - middle.astype(jnp.float32)).astype(jnp.bfloat16)
    return matmul(ones, high) + matmul(ones, middle) + matmul(ones, low)


def scale_norm(source, gain, target):
    normed, _ = norm_rows(source[...])
    target[...] = (normed * gain).astype(jnp.bfloat16)


def head_mask(half):
    lane = lax.broadcasted_iota(jnp.int32, (1, 128), 1)
    return (lane < 64) if half == 0 else (lane >= 64)


def keep_half(values, half):
    return jnp.where(head_mask(half), values, jnp.zeros((), values.dtype))


def probabilities(query, key, half, bias):
    scores = right_trans(keep_half(query, half), key) * 0.125
    if bias is not None:
        scores = jnp.where(bias, scores, NEG_FILL)
    grown = jnp.exp(scores - jnp.max(scores, axis=-1, keepdims=True))
    return grown / jnp.sum(grown, axis=-1, keepdims=True)


def forward_steps(width, stream, gain_one, gain_two, w_a, w_up, w_down, qkv, mixed, middle, acted, sloped, out, low, live=None):
    def project(j):
        cols = pl.ds(j * width, width)
        qkv[:, cols] = matmul(low[...], w_a[:, cols]).astype(jnp.bfloat16)

    def attend(pair):
        query, key, value = (qkv[:, pl.ds(pair * 128 + part * width, 128)] for part in range(3))
        parts = [
            matmul(probabilities(query, key, half, live).astype(jnp.bfloat16), value) for half in range(2)
        ]
        mixed[:, pl.ds(pair * 128, 128)] = jnp.where(head_mask(0), parts[0], parts[1]).astype(jnp.bfloat16)

    def mix():
        middle[...] = stream[...] + matmul(mixed[...], w_a[:, 3 * width :])
        scale_norm(middle, gain_two, low)

    def feed(j):
        cols = pl.ds(j * TILE, TILE)
        raised = matmul(low[...], w_up[:, cols])
        cumul = 0.5 + 0.5 * lax.erf(raised * ROOT_HALF)
        slope = cumul + raised * (jnp.exp(-0.5 * raised * raised) * (1.0 / math.sqrt(2.0 * math.pi)))
        sloped[:, cols] = slope.astype(jnp.bfloat16)
        acted[:, cols] = (raised * cumul).astype(jnp.bfloat16)
        out[...] = (middle[...] if j == 0 else out[...]) + matmul(acted[:, cols], w_down[cols, :])

    yield lambda: scale_norm(stream, gain_one, low)
    for j in range(3):
        yield functools.partial(project, j)
    for pair in range(width // 128):
        yield functools.partial(attend, pair)
    yield mix
    for j in range(w_up.shape[1] // TILE):
        yield functools.partial(feed, j)


def forward_block(*args):
    for step in forward_steps(*args):
        step()


def forward_kernel(*refs):
    (embedded, vis_col, vis_row, vec, e_a_hbm, e_u_hbm, e_d_hbm, d_a_hbm, d_u_hbm, d_d_hbm,
     e_in, e_qkv, e_mixed, e_mid, e_act, e_slope, d_in, d_qkv, d_mixed, d_mid, d_act, d_slope, acts,
     e_a, e_u, e_d, d_a, d_u, d_d, e_out, d_out, e_low, d_low, sems) = refs
    width = embedded.shape[1]
    loads = [
        pltpu.make_async_copy(a, b, sems.at[i])
        for i, (a, b) in enumerate(
            [(e_a_hbm, e_a), (e_u_hbm, e_u), (e_d_hbm, e_d), (d_a_hbm, d_a), (d_u_hbm, d_u), (d_d_hbm, d_d)]
        )
    ]
    for load in loads:
        load.start()
    encode(embedded, vis_col, vec, e_in)
    for load in loads[:3]:
        load.wait()
    live = live_keys(vis_row)
    forward_block(width, e_in, vec[0:1, :], vec[1:2, :], e_a, e_u, e_d, e_qkv, e_mixed, e_mid, e_act, e_slope, e_out, e_low, live)
    spread_rows(vis_row, e_out, vec, d_in)
    for load in loads[3:]:
        load.wait()
    forward_block(width, d_in, vec[2:3, :], vec[3:4, :], d_a, d_u, d_d, d_qkv, d_mixed, d_mid, d_act, d_slope, d_out, d_low)
    acts[...] = d_out[...].astype(jnp.bfloat16)


def token_hot(vis_col, count):
    return (lax.broadcasted_iota(jnp.int32, (vis_col.shape[0], count), 1) == vis_col[...]).astype(jnp.bfloat16)


def spot_hot(vis_row, count):
    return (lax.broadcasted_iota(jnp.int32, (count, vis_row.shape[1]), 0) == vis_row[...]).astype(jnp.bfloat16)


def live_keys(vis_row):
    ones = jnp.ones((1, BUFFER), jnp.int32)
    return jnp.concatenate([ones, (vis_row[...] >= 0).astype(jnp.int32)], axis=1) > 0


def encode(embedded, vis_col, vec, target):
    tokens = embedded.shape[0] - BUFFER
    target[:BUFFER, :] = embedded[:BUFFER, :].astype(jnp.float32)
    target[BUFFER:, :] = matmul(token_hot(vis_col, tokens), embedded[BUFFER:, :])


def spread_rows(vis_row, enc_out, vec, target):
    tokens = target.shape[0] - BUFFER
    hot = spot_hot(vis_row, tokens)
    masked = 1.0 - jnp.sum(hot.astype(jnp.float32), axis=1, keepdims=True)
    target[:BUFFER, :] = enc_out[:BUFFER, :]
    target[BUFFER:, :] = exact_dot(hot, enc_out[BUFFER:, :]) + masked * vec[4:5, :]


def forward_blocks(embedded, vis_col, vis_row, vec, weights):
    tokens, width = embedded.shape
    inner = weights[1].shape[1]
    rows = BUFFER + vis_col.shape[0]
    f32, half = jnp.float32, jnp.bfloat16

    def kept(count):
        return [
            jax.ShapeDtypeStruct((count, width), f32),
            jax.ShapeDtypeStruct((count, 3 * width), half),
            jax.ShapeDtypeStruct((count, width), half),
            jax.ShapeDtypeStruct((count, width), f32),
            jax.ShapeDtypeStruct((count, inner), half),
            jax.ShapeDtypeStruct((count, inner), half),
        ]

    outs = kept(rows) + kept(tokens) + [jax.ShapeDtypeStruct((tokens, width), half)]
    whole = pl.BlockSpec(memory_space=pltpu.VMEM)
    found = pl.pallas_call(
        forward_kernel,
        out_shape=outs,
        in_specs=[whole] * 4 + [pl.BlockSpec(memory_space=pl.ANY)] * 6,
        out_specs=[whole] * len(outs),
        scratch_shapes=[pltpu.VMEM(w.shape, half) for w in weights]
        + [
            pltpu.VMEM((rows, width), f32),
            pltpu.VMEM((tokens, width), f32),
            pltpu.VMEM((rows, width), half),
            pltpu.VMEM((tokens, width), half),
            pltpu.SemaphoreType.DMA((6,)),
        ],
        compiler_params=pltpu.CompilerParams(vmem_limit_bytes=SUM_VMEM),
        name="forward_blocks",
    )(embedded, vis_col, vis_row, vec, *weights)
    return found[:6], found[6:12], found[12]


def norm_back_into(grads, source, gain, add, target, gain_grad):
    gain_grad[...] = jnp.zeros_like(gain_grad)
    height = 64 if source.shape[0] % 64 == 0 else 48

    def body(i):
        rows = at_step(i, height)
        normed, inv_std = norm_rows(source[rows, :])
        grad = grads[rows, :]
        gain_grad[...] += jnp.broadcast_to(jnp.sum(grad * normed, axis=0, keepdims=True), gain_grad.shape)
        target[rows, :] = add[rows, :] + norm_back(grad * gain, normed, inv_std)

    loop(source.shape[0] // height, body)


class Tiles:
    def __init__(self, slots, sems):
        self.slots, self.sems = slots, sems

    def put(self, i, value, target):
        slot = i % 2 if isinstance(i, int) else lax.rem(i, 2)
        copy = pltpu.make_async_copy(self.slots.at[slot], target, self.sems.at[slot])

        @pl.when(i >= 2)
        def _():
            copy.wait()

        self.slots[slot] = value.astype(jnp.bfloat16)
        copy.start()

    def flush(self, like):
        for slot in range(2):
            pltpu.make_async_copy(self.slots.at[slot], like, self.sems.at[slot]).wait()


def backward_block(width, grad, stream, gain_one, gain_two, w_a, w_up, w_down, qkv, mixed, middle, acted, sloped,
                   d_a, d_up, d_down, d_one, d_two, grad_low, low, grad_qkv, acc, grad_mid, out, tiles, live=None):
    rows = grad.shape[0]
    wide, narrow, square = tiles
    grad_low[...] = grad[...].astype(jnp.bfloat16)
    scale_norm(middle, gain_two, low)
    acc[...] = jnp.zeros_like(acc)
    count = w_up.shape[1] // TILE

    def feed(j):
        act, slope = acted[:, at_col(j, TILE)], sloped[:, at_col(j, TILE)].astype(jnp.float32)
        down = w_down[at_step(j, TILE), :]
        narrow.put(j, rows_dot(act, grad_low[...]), d_down.at[at_step(j, TILE), :])
        grad_up = (right_trans(grad_low[...], down) * slope).astype(jnp.bfloat16)
        wide.put(j, rows_dot(low[...], grad_up), d_up.at[:, at_col(j, TILE)])
        acc[...] += right_trans(grad_up, w_up[:, at_col(j, TILE)])

    loop(count, feed)
    narrow.flush(d_down.at[pl.ds(0, TILE), :])
    wide.flush(d_up.at[:, pl.ds(0, TILE)])
    norm_back_into(acc, middle, gain_two, grad, grad_mid, d_two)
    grad_low[...] = grad_mid[...].astype(jnp.bfloat16)
    for j in range(width // 256):
        square.put(j, rows_dot(mixed[...], grad_low[:, pl.ds(j * 256, 256)]), d_a.at[:, pl.ds(3 * width + j * 256, 256)])
    for j in range(width // 256):
        low[:, pl.ds(j * 256, 256)] = right_trans(grad_low[...], w_a[pl.ds(j * 256, 256), pl.ds(3 * width, width)]).astype(jnp.bfloat16)

    def attend(pair):
        where = [pl.ds(pl.multiple_of(pair * 128 + part * width, 128), 128) for part in range(3)]
        query, key, value = (qkv[:, at] for at in where)
        grad_mixed = low[:, at_col(pair, 128)]
        found = []
        for half in range(2):
            probs = probabilities(query, key, half, live)
            grad_half = keep_half(grad_mixed, half)
            grad_probs = right_trans(grad_half, value)
            dots = jnp.sum(grad_probs * probs, axis=-1, keepdims=True)
            grad_scores = (probs * (grad_probs - dots) * 0.125).astype(jnp.bfloat16)
            found.append(
                (matmul(grad_scores, key), rows_dot(grad_scores, query), rows_dot(probs.astype(jnp.bfloat16), grad_half))
            )
        for part in range(3):
            both = jnp.where(head_mask(0), found[0][part], found[1][part])
            grad_qkv[:, where[part]] = both.astype(jnp.bfloat16)

    loop(width // 128, attend)
    scale_norm(stream, gain_one, low)
    acc[...] = jnp.zeros_like(acc)
    first = width // 256

    def project(j):
        piece = grad_qkv[:, at_col(j, 256)]
        square.put(j + first, rows_dot(low[...], piece), d_a.at[:, at_col(j, 256)])
        acc[...] += right_trans(piece, w_a[:, at_col(j, 256)])

    loop(3 * width // 256, project)
    square.flush(d_a.at[:, pl.ds(0, 256)])
    norm_back_into(acc, stream, gain_one, grad_mid, out, d_one)


def backward_kernel(*refs):
    (grad_rows, vis_col, vis_row, vec, e_in, e_qkv, e_mixed, e_mid, e_act, e_slope, d_in, d_qkv, d_mixed, d_mid, d_act, d_slope,
     e_a_hbm, e_u_hbm, e_d_hbm, d_a_hbm, d_u_hbm, d_d_hbm,
     embed_grad, small, de_a, de_u, de_d, dd_a, dd_u, dd_d,
     e_a, e_u, e_d, d_a, d_u, d_d, d_grad, e_grad, low_a, low_b, grad_qkv, acc, grad_mid,
     wide, narrow, square, load_sems, tile_sems) = refs
    tokens, width = d_in.shape
    rows = e_in.shape[0]
    loads = [
        pltpu.make_async_copy(a, b, load_sems.at[i])
        for i, (a, b) in enumerate(
            [(d_d_hbm, d_d), (d_u_hbm, d_u), (d_a_hbm, d_a), (e_d_hbm, e_d), (e_u_hbm, e_u), (e_a_hbm, e_a)]
        )
    ]
    for load in loads:
        load.start()
    tiles = (Tiles(wide, tile_sems.at[0]), Tiles(narrow, tile_sems.at[1]), Tiles(square, tile_sems.at[2]))
    d_grad[:BUFFER, :] = jnp.zeros((BUFFER, width), jnp.float32)
    d_grad[BUFFER:, :] = grad_rows[...].astype(jnp.float32)
    for load in loads[:3]:
        load.wait()
    backward_block(width, d_grad, d_in, vec[2:3, :], vec[3:4, :], d_a, d_u, d_d, d_qkv, d_mixed, d_mid, d_act, d_slope,
                   dd_a, dd_u, dd_d, small.at[2:3, :], small.at[3:4, :], low_a, low_b, grad_qkv, acc, grad_mid, d_grad, tiles)
    hot = spot_hot(vis_row, tokens - BUFFER)
    masked = 1.0 - jnp.sum(hot.astype(jnp.float32), axis=1, keepdims=True)
    small[4:5, :] = jnp.sum(d_grad[BUFFER:, :] * masked, axis=0, keepdims=True)
    e_grad[:BUFFER, :] = d_grad[:BUFFER, :]
    e_grad[BUFFER:, :] = exact_dot(token_hot(vis_col, tokens - BUFFER), d_grad[BUFFER:, :])
    for load in loads[3:]:
        load.wait()
    part = pl.ds(0, rows)
    backward_block(width, e_grad, e_in, vec[0:1, :], vec[1:2, :], e_a, e_u, e_d, e_qkv, e_mixed, e_mid, e_act, e_slope,
                   de_a, de_u, de_d, small.at[0:1, :], small.at[1:2, :], low_a.at[part], low_b.at[part],
                   grad_qkv.at[part], acc.at[part], grad_mid.at[part], e_grad, tiles, live_keys(vis_row))
    embed_grad[:BUFFER, :] = e_grad[:BUFFER, :]
    embed_grad[BUFFER:, :] = exact_dot(hot, e_grad[BUFFER:, :])


def backward_blocks(grad_rows, vis_col, vis_row, vec, enc_kept, dec_kept, weights):
    tokens, width = dec_kept[0].shape
    rows = enc_kept[0].shape[0]
    f32, half = jnp.float32, jnp.bfloat16
    whole, anywhere = pl.BlockSpec(memory_space=pltpu.VMEM), pl.BlockSpec(memory_space=pl.ANY)
    outs = [jax.ShapeDtypeStruct((tokens, width), f32), jax.ShapeDtypeStruct((8, width), f32)]
    outs += [jax.ShapeDtypeStruct(w.shape, half) for w in weights]
    found = pl.pallas_call(
        backward_kernel,
        out_shape=outs,
        in_specs=[whole] * 16 + [anywhere] * 6,
        out_specs=[whole] * 2 + [anywhere] * 6,
        scratch_shapes=[pltpu.VMEM(w.shape, half) for w in weights]
        + [
            pltpu.VMEM((tokens, width), f32),
            pltpu.VMEM((rows, width), f32),
            pltpu.VMEM((tokens, width), half),
            pltpu.VMEM((tokens, width), half),
            pltpu.VMEM((tokens, 3 * width), half),
            pltpu.VMEM((tokens, width), f32),
            pltpu.VMEM((tokens, width), f32),
            pltpu.VMEM((2, width, TILE), half),
            pltpu.VMEM((2, TILE, width), half),
            pltpu.VMEM((2, width, 256), half),
            pltpu.SemaphoreType.DMA((6,)),
            pltpu.SemaphoreType.DMA((3, 2)),
        ],
        compiler_params=pltpu.CompilerParams(vmem_limit_bytes=SUM_VMEM),
        name="backward_blocks",
    )(grad_rows, vis_col, vis_row, vec, *enc_kept, *dec_kept, *weights)
    return found[0], found[1], found[2:]


def embed_steps(steps, freqs, target):
    half = freqs.shape[1]

    def body(i):
        phase = steps[at_step(i), :].astype(jnp.float32) * freqs[...]
        target[at_step(i), :half] = jnp.cos(phase)
        target[at_step(i), half:] = jnp.sin(phase)

    loop(steps.shape[0] // STEP, body)


ROWS = 256


def at_rows(i):
    return pl.ds(pl.multiple_of(i * ROWS, 16), ROWS)


def head_kernel(*refs):
    (acts, vis_row, targets, noise, steps, embeds, w_cond_hbm, w_ada_hbm, w_io_hbm, w_in, w_out,
     grad_rows, losses, d_in, d_out, d_cond, d_ada, d_io,
     w_cond, w_ada, w_io, cond, cond_full, mod, hidden, normed_in, inv_in, inner, branch, normed_out, inv_out,
     work, grad_two, grad_sum, noisy, cond_act, mlp_in, inner_act, final_in, grad_pred, grad_branch, grad_inner,
     grad_hidden, grad_mod, wide, load_sems, tile_sems) = refs
    tokens, wide_cols = targets.shape[0], w_in.shape[1]
    loads = [
        pltpu.make_async_copy(a, b, load_sems.at[i])
        for i, (a, b) in enumerate([(w_cond_hbm, w_cond), (w_ada_hbm, w_ada), (w_io_hbm, w_io)])
    ]
    for load in loads:
        load.start()
    hot = spot_hot(vis_row, tokens)
    masked = jnp.sum(hot.astype(jnp.float32), axis=1, keepdims=True) < 0.5
    loads[0].wait()
    cond[...] = matmul(acts[BUFFER:, :], w_cond[...])
    loads[1].wait()
    loads[2].wait()
    grad_sum[...] = jnp.zeros_like(grad_sum)
    columns = wide_cols // 256

    def copy_pass(c, loss):
        rows = pl.ds(pl.multiple_of(c * tokens, 16), tokens)

        def at(i):
            return pl.ds(pl.multiple_of(c * tokens + i * ROWS, 16), ROWS)

        angle = noise_angle(steps[rows, :])
        noise_vals = noise[rows, :].astype(jnp.float32)
        noisy[rows, :] = (jnp.cos(angle) * targets[...] + jnp.sin(angle) * noise_vals).astype(jnp.bfloat16)

        def condition(i):
            full = cond[at_rows(i), :] + embeds[at(i), :]
            cond_full[at_rows(i), :] = full
            cond_act[at(i), :] = (full * jax.nn.sigmoid(full)).astype(jnp.bfloat16)

        loop(tokens // ROWS, condition)

        mod[...] = matmul(cond_act[rows, :], w_ada[...])
        hidden[...] = matmul(noisy[rows, :], w_in[...])

        def enter(i):
            normed, inv_std = norm_rows(hidden[at_rows(i), :])
            normed_in[at_rows(i), :] = normed
            inv_in[at_rows(i), :] = inv_std
            shift, scale = mod[at_rows(i), :wide_cols], mod[at_rows(i), wide_cols : 2 * wide_cols]
            mlp_in[at(i), :] = (normed * (1.0 + scale) + shift).astype(jnp.bfloat16)

        loop(tokens // ROWS, enter)

        inner[...] = matmul(mlp_in[rows, :], w_io[:, :wide_cols])

        def activate(i):
            values = inner[at_rows(i), :]
            inner_act[at(i), :] = (values * jax.nn.sigmoid(values)).astype(jnp.bfloat16)

        loop(tokens // ROWS, activate)

        branch[...] = matmul(inner_act[rows, :], w_io[:, wide_cols:])

        def leave(i):
            gate = mod[at_rows(i), 2 * wide_cols :]
            normed, inv_std = norm_rows(hidden[at_rows(i), :] + gate * branch[at_rows(i), :])
            normed_out[at_rows(i), :] = normed
            inv_out[at_rows(i), :] = inv_std
            final_in[at(i), :] = normed.astype(jnp.bfloat16)

        loop(tokens // ROWS, leave)
        error = right_trans(final_in[rows, :], w_out[...]) - noise_vals
        loss = loss + jnp.sum(error * error, axis=1, keepdims=True)
        low_error = jnp.where(masked, error * (2.0 / COPIES), 0.0).astype(jnp.bfloat16)
        grad_pred[rows, :] = low_error
        work[...] = matmul(low_error, w_out[...])

        def back_out(i):
            gate = mod[at_rows(i), 2 * wide_cols :]
            grad = norm_back(work[at_rows(i), :], normed_out[at_rows(i), :], inv_out[at_rows(i), :])
            grad_two[at_rows(i), :] = grad
            grad_branch[at(i), :] = (grad * gate).astype(jnp.bfloat16)
            grad_mod[at(i), 2 * wide_cols :] = (grad * branch[at_rows(i), :]).astype(jnp.bfloat16)

        loop(tokens // ROWS, back_out)

        work[...] = right_trans(grad_branch[rows, :], w_io[:, wide_cols:])

        def back_act(i):
            grad_inner[at(i), :] = (work[at_rows(i), :] * silu_slope(inner[at_rows(i), :])).astype(jnp.bfloat16)

        loop(tokens // ROWS, back_act)

        work[...] = right_trans(grad_inner[rows, :], w_io[:, :wide_cols])

        def back_in(i):
            grad, normed = work[at_rows(i), :], normed_in[at_rows(i), :]
            scale = mod[at_rows(i), wide_cols : 2 * wide_cols]
            grad_mod[at(i), :wide_cols] = grad.astype(jnp.bfloat16)
            grad_mod[at(i), wide_cols : 2 * wide_cols] = (grad * normed).astype(jnp.bfloat16)
            total = grad_two[at_rows(i), :] + norm_back(grad * (1.0 + scale), normed, inv_in[at_rows(i), :])
            grad_hidden[at(i), :] = total.astype(jnp.bfloat16)

        loop(tokens // ROWS, back_in)

        work[...] = right_trans(grad_mod[rows, :], w_ada[...])

        def back_cond(i):
            grad_sum[at_rows(i), :] += work[at_rows(i), :] * silu_slope(cond_full[at_rows(i), :])

        loop(tokens // ROWS, back_cond)
        return loss

    loss = lax.fori_loop(0, COPIES, copy_pass, jnp.zeros((tokens, 1), jnp.float32))
    loss = jnp.where(masked, loss.astype(jnp.bfloat16).astype(jnp.float32), 0.0)
    losses[...] = jnp.broadcast_to(jnp.sum(loss, axis=0, keepdims=True), losses.shape)
    grad_cond = grad_sum[...].astype(jnp.bfloat16)
    grad_rows[...] = right_trans(grad_cond, w_cond[...]).astype(jnp.bfloat16)
    tiles = Tiles(wide, tile_sems)

    def out_ada(j):
        tiles.put(j, rows_dot(cond_act[...], grad_mod[:, at_col(j, TILE)]), d_ada.at[:, at_col(j, TILE)])

    count = 3 * wide_cols // TILE
    loop(count, out_ada)
    half = wide_cols // TILE

    def out_inner(j):
        tiles.put(j + count, rows_dot(mlp_in[...], grad_inner[:, at_col(j, TILE)]), d_io.at[:, at_col(j, TILE)])

    def out_outer(j):
        tiles.put(j + count + half, rows_dot(inner_act[...], grad_branch[:, at_col(j, TILE)]), d_io.at[:, at_col(j + half, TILE)])

    loop(half, out_inner)
    loop(half, out_outer)
    d_cond[...] = rows_dot(acts[BUFFER:, :], grad_cond).astype(jnp.bfloat16)
    d_in[...] = rows_dot(noisy[...], grad_hidden[...])
    d_out[...] = rows_dot(grad_pred[...], final_in[...])
    tiles.flush(d_ada.at[:, pl.ds(0, TILE)])


def head_pass(acts, vis_row, targets, noise, steps, embeds, w_cond, w_ada, w_io, w_in, w_out):
    tokens, width = targets.shape[0], acts.shape[1]
    wide, flat = w_in.shape[1], noise.shape[0]
    f32, half = jnp.float32, jnp.bfloat16
    whole, anywhere = pl.BlockSpec(memory_space=pltpu.VMEM), pl.BlockSpec(memory_space=pl.ANY)
    shape = jax.ShapeDtypeStruct
    outs = [
        shape((tokens, width), half), shape((8, 128), f32), shape((CH, wide), f32), shape((CH, wide), f32),
        shape(w_cond.shape, half), shape(w_ada.shape, half), shape(w_io.shape, half),
    ]
    tile = lambda cols, kind=f32: pltpu.VMEM((tokens, cols), kind)
    long = lambda cols: pltpu.VMEM((flat, cols), half)
    return pl.pallas_call(
        head_kernel,
        out_shape=outs,
        in_specs=[whole] * 6 + [anywhere] * 3 + [whole] * 2,
        out_specs=[whole] * 5 + [anywhere] * 2,
        scratch_shapes=[pltpu.VMEM(w.shape, half) for w in (w_cond, w_ada, w_io)]
        + [
            tile(wide), tile(wide), tile(3 * wide), tile(wide), tile(wide), tile(1), tile(wide), tile(wide), tile(wide), tile(1),
            tile(wide), tile(wide), tile(wide),
            long(CH), long(wide), long(wide), long(wide), long(wide), long(CH), long(wide), long(wide), long(wide), long(3 * wide),
            pltpu.VMEM((2, wide, TILE), half),
            pltpu.SemaphoreType.DMA((3,)),
            pltpu.SemaphoreType.DMA((2,)),
        ],
        compiler_params=pltpu.CompilerParams(vmem_limit_bytes=SUM_VMEM),
        name="head_pass",
    )(acts, vis_row, targets, noise, steps, embeds, w_cond, w_ada, w_io, w_in, w_out)


class Slab:
    def __init__(self, rows, cols, by_rows, direct=False):
        self.rows, self.cols, self.by_rows, self.direct = rows, cols, by_rows, direct
        self.piece = (rows // 4, cols) if by_rows else (rows, cols // 4)

    def spot(self, shard, quarter, half=None):
        piece_rows, piece_cols = self.piece
        row = shard * self.rows
        if self.by_rows:
            row = row + quarter * piece_rows
        height = piece_rows
        if half is not None:
            height = piece_rows // 2
            row = row + half * height
        col = 0 if self.by_rows else quarter * piece_cols
        return (pl.ds(aligned(row, 16), height), pl.ds(aligned(col, 128), piece_cols))

    def shard(self, shard):
        return (pl.ds(aligned(shard * self.rows, 16), self.rows), pl.ds(0, self.cols))

    def within(self, quarter):
        return self.spot(0, quarter)


def aligned(value, multiple):
    return value if isinstance(value, int) else pl.multiple_of(value, multiple)


def place(depth):
    group, device = lax.axis_index("grp"), lax.axis_index("dev")
    level, core = device // 2, device % 2
    flip = lambda bit: group + (1 << bit) * (1 - 2 * ((group // (1 << bit)) % 2))
    return group, level, core, flip


def greet(peers):
    barrier = pltpu.get_barrier_semaphore()
    for peer in peers:
        pl.semaphore_signal(barrier, inc=1, device_id=peer, device_id_type=MESH)
    pl.semaphore_wait(barrier, len(peers))


def gather_kernel(slabs, depth, *refs):
    count = len(slabs)
    mine, whole = refs[:count], refs[count : 2 * count]
    sent, got, own_sent, own_got, own_copy = refs[2 * count :]
    group, level, core, flip = place(depth)
    x_peer, y_peer = (flip(0), 2 * level + core), (flip(1), 2 * level + core)
    partner = (group, 2 * level + 1 - core)

    def level_at(step):
        return lax.rem(level + step + depth, depth)

    z_peers = [(group, 2 * level_at(step) + core) for step in range(1, depth)]
    greet([x_peer, y_peer, partner] + z_peers)

    def move(kind, item, source, target, device):
        return pltpu.make_async_remote_copy(
            src_ref=source,
            dst_ref=target,
            send_sem=sent.at[kind, item],
            recv_sem=got.at[kind, item],
            device_id=device,
            device_id_type=MESH,
        )

    Z, X, Y, XH, YH, CORE = range(6)
    items = [(k, step) for k in range(count) for step in range(1, depth)]

    def by_z(item):
        k, step = items[item]
        slab = slabs[k]
        target = whole[k].at[slab.spot(2 * level + core, group)]
        return move(Z, item, mine[k].at[slab.within(group)], target, z_peers[step - 1])

    def shard_of(item):
        return 2 * level_at(-items[item][1]) + core

    def forward(kind, item, quarter, half, device):
        k = items[item][0]
        here = whole[k].at[slabs[k].spot(shard_of(item), quarter, half)]
        return move(kind, item, here, here, device)

    def core_copy(item, core_of):
        k, step = items[item]
        here = whole[k].at[slabs[k].shard(2 * level_at(-step) + core_of)]
        return move(CORE, item, here, here, partner)

    own = []
    for k, slab in enumerate(slabs):
        for step in range(1, depth):
            by_z(k * (depth - 1) + step - 1).start()
        target = whole[k].at[slab.shard(2 * level + core)]
        keep = pltpu.make_async_copy(mine[k], target, own_copy.at[k])
        keep.start()
        share = pltpu.make_async_remote_copy(
            src_ref=mine[k],
            dst_ref=target,
            send_sem=own_sent.at[k],
            recv_sem=own_got.at[k],
            device_id=partner,
            device_id_type=MESH,
        )
        share.start()
        own.append((keep, share))

    total = len(items)
    for turn in range(total + 2):
        if turn < total:
            k = items[turn][0]
            here = whole[k].at[slabs[k].spot(shard_of(turn), group)]
            move(Z, turn, here, here, x_peer).wait_recv()
            forward(X, turn, group, None, x_peer).start()
            forward(Y, turn, group, None, y_peer).start()
        item = turn - 1
        if 0 <= item < total:
            forward(X, item, flip(0), None, x_peer).wait_recv()
            forward(YH, item, flip(0), 0, y_peer).start()
            forward(Y, item, flip(1), None, y_peer).wait_recv()
            forward(XH, item, flip(1), 1, x_peer).start()
        item = turn - 2
        if 0 <= item < total:
            far = 3 - group
            forward(YH, item, far, 0, y_peer).wait_recv()
            forward(XH, item, far, 1, x_peer).wait_recv()
            core_copy(item, core).start()
    for item in range(total):
        by_z(item).wait_send()
        forward(X, item, group, None, x_peer).wait_send()
        forward(Y, item, group, None, y_peer).wait_send()
        forward(YH, item, flip(0), 0, y_peer).wait_send()
        forward(XH, item, flip(1), 1, x_peer).wait_send()
        core_copy(item, core).wait_send()
        core_copy(item, 1 - core).wait_recv()
    for keep, share in own:
        keep.wait()
        share.wait()


def gather_slabs(shards, slabs, depth):
    count, items = len(slabs), len(slabs) * (depth - 1)
    return pl.pallas_call(
        functools.partial(gather_kernel, slabs, depth),
        out_shape=[
            jax.ShapeDtypeStruct((2 * depth * s.rows, s.cols), jnp.bfloat16) for s in slabs
        ],
        in_specs=[pl.BlockSpec(memory_space=pl.ANY)] * count,
        out_specs=[pl.BlockSpec(memory_space=pl.ANY)] * count,
        scratch_shapes=[
            pltpu.SemaphoreType.DMA((6, items)),
            pltpu.SemaphoreType.DMA((6, items)),
            pltpu.SemaphoreType.DMA((count,)),
            pltpu.SemaphoreType.DMA((count,)),
            pltpu.SemaphoreType.DMA((count,)),
        ],
        compiler_params=pltpu.CompilerParams(collective_id=0, has_side_effects=True),
        name="gather_weights",
    )(*shards)


def sum_kernel(slabs, orders, depth, *refs):
    count = len(slabs)
    grads, outs = refs[:count], refs[count : 2 * count]
    rest = refs[2 * count :]
    take = lambda: (rest[:count], rest[count:])
    held, rest = take()
    from_first, rest = take()
    from_second, rest = take()
    from_level, rest = take()
    result, rest = take()
    stage, rest = take()
    stage_sem, out_sem, core_sent, core_got, sent, got, z_sent, z_got = rest
    group, level, core, flip = place(depth)
    me = 2 * level + core
    partner = (group, 2 * level + 1 - core)
    bit = lambda b: (group // (1 << b)) % 2

    def level_at(step):
        return lax.rem(level + step + depth, depth)

    z_peers = [(group, 2 * level_at(step) + core) for step in range(1, depth)]
    greet([(flip(0), me), (flip(1), me), partner] + z_peers)

    def move(pair, k, kind, source, target, device):
        send, receive = pair
        return pltpu.make_async_remote_copy(
            src_ref=source,
            dst_ref=target,
            send_sem=send.at[kind, k],
            recv_sem=receive.at[kind, k],
            device_id=device,
            device_id_type=MESH,
        )

    def core_move(k, lev):
        source = grads[k].at[slabs[k].shard(2 * lev + 1 - core)]
        return move((core_sent, core_got), k, lev, source, held[k].at[lev], partner)

    def rows_loop(height, body):
        step = 32 if height % 32 == 0 else 16

        def turn(i, carry):
            body(pl.ds(aligned(i * step, 16), step))
            return carry

        lax.fori_loop(0, height // step, turn, 0)

    def shifted(rows, by):
        return pl.ds(aligned(rows.start + by, 16), rows.size)

    def first_bit(k):
        return 1 if orders[k] == "yx" else 0

    def quarter(k, first, second):
        b = first_bit(k)
        return first * (1 << b) + second * (1 << (1 - b))

    def first_move(k, j):
        b = first_bit(k)
        where = slabs[k].within(quarter(k, 1 - bit(b), j))
        source = held[k].at[(level,) + where] if orders[k][0] == "z" else held[k].at[(slice(None),) + where]
        return move((sent, got), k, j, source, from_first[k].at[j], (flip(b), me))

    def second_move(k):
        b = first_bit(k)
        where = slabs[k].within(quarter(k, bit(b), 1 - bit(1 - b)))
        source = held[k].at[(level,) + where] if orders[k][0] == "z" else held[k].at[(slice(None),) + where]
        return move((sent, got), k, 2, source, from_second[k], (flip(1 - b), me))

    def level_move(k, step):
        lev = level_at(step)
        source = held[k].at[lev] if orders[k][0] == "z" else held[k].at[(lev,) + slabs[k].within(group)]
        return move((z_sent, z_got), k, step - 1, source, from_level[k].at[step - 1], z_peers[step - 1])

    def spread_second(k, whose):
        here = result[k].at[slabs[k].within(whose)]
        return move((sent, got), k, 3, here, here, (flip(1 - first_bit(k)), me))

    def spread_first(k, j, whose):
        here = result[k].at[slabs[k].within(whose)]
        return move((sent, got), k, 4 + j, here, here, (flip(first_bit(k)), me))

    def out_copy(k):
        return pltpu.make_async_copy(result[k], outs[k], out_sem.at[k])

    def stage_copy(k, lev):
        source = grads[k].at[slabs[k].shard(2 * lev + core)]
        return pltpu.make_async_copy(source, stage[k].at[lev % 2], stage_sem.at[k, lev % 2])

    def add_core(k):
        slab = slabs[k]
        stage_copy(k, 0).start()
        for lev in range(depth):
            if lev + 1 < depth:
                stage_copy(k, lev + 1).start()
            core_move(k, lev).wait_recv()
            stage_copy(k, lev).wait()

            def body(rows):
                total = held[k][lev, rows, :].astype(jnp.float32) + stage[k][lev % 2, rows, :].astype(jnp.float32)
                held[k][lev, rows, :] = total.astype(jnp.bfloat16)

            rows_loop(slab.rows, body)

    def levels_of(k):
        return [level] if orders[k][0] == "z" else list(range(depth))

    def add_first(k):
        slab = slabs[k]
        for j in range(2):
            first_move(k, j).wait_recv()
            rows_of, cols = slab.within(quarter(k, bit(first_bit(k)), j))
            for lev in levels_of(k):

                def body(rows):
                    at = (lev, shifted(rows, rows_of.start), cols)
                    extra = from_first[k][j, rows, :] if orders[k][0] == "z" else from_first[k][j, lev, rows, :]
                    held[k][at] = (held[k][at].astype(jnp.float32) + extra.astype(jnp.float32)).astype(jnp.bfloat16)

                rows_loop(slab.piece[0], body)

    def add_second(k):
        slab = slabs[k]
        second_move(k).wait_recv()
        rows_of, cols = slab.within(group)
        for lev in levels_of(k):

            def body(rows):
                at = (lev, shifted(rows, rows_of.start), cols)
                extra = from_second[k][rows, :] if orders[k][0] == "z" else from_second[k][lev, rows, :]
                total = held[k][at].astype(jnp.float32) + extra.astype(jnp.float32)
                target = result[k].at[shifted(rows, rows_of.start), cols] if orders[k][0] == "z" else held[k].at[at]
                target[...] = total.astype(jnp.bfloat16)

            rows_loop(slab.piece[0], body)

    def add_level(k):
        slab = slabs[k]
        for step in range(1, depth):
            level_move(k, step).wait_recv()
        if orders[k][0] == "z":

            def body(rows):
                total = held[k][level, rows, :].astype(jnp.float32)
                for step in range(depth - 1):
                    total = total + from_level[k][step, rows, :].astype(jnp.float32)
                held[k][level, rows, :] = total.astype(jnp.bfloat16)

            rows_loop(slab.rows, body)
            return
        rows_of, cols = slab.within(group)

        def body(rows):
            at = (shifted(rows, rows_of.start), cols)
            total = held[k][(level,) + at].astype(jnp.float32)
            for step in range(depth - 1):
                total = total + from_level[k][step, rows, :].astype(jnp.float32)
            result[k][at] = total.astype(jnp.bfloat16)

        rows_loop(slab.piece[0], body)

    def begin_core(k):
        for lev in range(depth):
            core_move(k, lev).start()

    def begin_first(k):
        first_move(k, 0).start()
        first_move(k, 1).start()

    def begin_level(k):
        for step in range(1, depth):
            level_move(k, step).start()

    def end_spread_second(k):
        spread_second(k, flip(1 - first_bit(k))).wait_recv()
        spread_first(k, 0, group).start()
        spread_first(k, 1, flip(1 - first_bit(k))).start()

    def end_spread_first(k):
        b = first_bit(k)
        spread_first(k, 0, flip(b)).wait_recv()
        spread_first(k, 1, 3 - group).wait_recv()
        out_copy(k).start()

    def steps(k):
        if orders[k][0] == "z":
            return [
                lambda: (add_core(k), begin_level(k)),
                lambda: (add_level(k), begin_first(k)),
                lambda: (add_first(k), second_move(k).start()),
                lambda: (add_second(k), spread_second(k, group).start()),
                lambda: end_spread_second(k),
                lambda: end_spread_first(k),
            ]
        return [
            lambda: (add_core(k), begin_first(k)),
            lambda: (add_first(k), second_move(k).start()),
            lambda: (add_second(k), begin_level(k)),
            lambda: (add_level(k), spread_second(k, group).start()),
            lambda: end_spread_second(k),
            lambda: end_spread_first(k),
        ]

    plans = [steps(k) for k in range(count)]
    begin_core(0)
    for turn in range(count + 5):
        if turn + 1 < count:
            begin_core(turn + 1)
        for place_in in range(6):
            k = turn - place_in
            if 0 <= k < count:
                plans[k][place_in]()
    for k in range(count):
        for lev in range(depth):
            core_move(k, lev).wait_send()
        first_move(k, 0).wait_send()
        first_move(k, 1).wait_send()
        second_move(k).wait_send()
        for step in range(1, depth):
            level_move(k, step).wait_send()
        spread_second(k, group).wait_send()
        spread_first(k, 0, group).wait_send()
        spread_first(k, 1, flip(1 - first_bit(k))).wait_send()
        out_copy(k).wait()


def sum_slabs(grads, slabs, orders, depth):
    count = len(slabs)
    half = jnp.bfloat16
    held, first, second, lev, result, stage = [], [], [], [], [], []
    for slab, order in zip(slabs, orders, strict=True):
        shard = (slab.rows, slab.cols)
        held.append(pltpu.VMEM((depth,) + shard, half))
        result.append(pltpu.VMEM(shard, half))
        stage.append(pltpu.VMEM((2,) + shard, half))
        if order[0] == "z":
            first.append(pltpu.VMEM((2,) + slab.piece, half))
            second.append(pltpu.VMEM(slab.piece, half))
            lev.append(pltpu.VMEM((depth - 1,) + shard, half))
        else:
            first.append(pltpu.VMEM((2, depth) + slab.piece, half))
            second.append(pltpu.VMEM((depth,) + slab.piece, half))
            lev.append(pltpu.VMEM((depth - 1,) + slab.piece, half))
    dma = pltpu.SemaphoreType.DMA
    return pl.pallas_call(
        functools.partial(sum_kernel, slabs, orders, depth),
        out_shape=[jax.ShapeDtypeStruct((s.rows, s.cols), half) for s in slabs],
        in_specs=[pl.BlockSpec(memory_space=pl.ANY)] * count,
        out_specs=[pl.BlockSpec(memory_space=pl.ANY)] * count,
        scratch_shapes=held
        + first
        + second
        + lev
        + result
        + stage
        + [
            dma((count, 2)),
            dma((count,)),
            dma((depth, count)),
            dma((depth, count)),
            dma((6, count)),
            dma((6, count)),
            dma((depth - 1, count)),
            dma((depth - 1, count)),
        ],
        compiler_params=pltpu.CompilerParams(
            collective_id=1, has_side_effects=True, vmem_limit_bytes=SUM_VMEM
        ),
        name="sum_gradients",
    )(*grads)


class Gathering:
    LAG, AHEAD, SKEW = 2, 2, 1

    def __init__(self, slabs, depth, mine, whole, near, sems):
        self.slabs, self.depth, self.mine, self.whole, self.near = slabs, depth, mine, whole, near
        self.sent, self.got, self.z_sent, self.z_got, self.own_sent, self.own_got, self.own_copy = sems
        self.group, self.level, self.core, self.flip = place(depth)
        me = 2 * self.level + self.core
        self.peers = ((self.flip(0), me), (self.flip(1), me), (self.group, 2 * self.level + 1 - self.core))
        by_way = [sorted((o for o in range(depth) if o != z), key=lambda o: (abs(o - z), o)) for z in range(depth)]
        self.sources = [sum((self.level == z) * by_way[z][i] for z in range(depth)) for i in range(depth - 1)]
        self.items = [(k, i) for k in range(len(slabs)) for i in range(depth - 1)]
        self.items.sort(key=lambda item: (item[0] + item[1] * self.SKEW, item[1]))
        self.turn = self.settled = 0
        self.turns = len(self.items) + 2 * self.LAG

    def move(self, kind, item, source, target, device):
        return pltpu.make_async_remote_copy(
            src_ref=source,
            dst_ref=target,
            send_sem=self.sent.at[kind, item],
            recv_sem=self.got.at[kind, item],
            device_id=device,
            device_id_type=MESH,
        )

    def z_part(self, k, source):
        slab, shard = self.slabs[k], 2 * source + self.core
        return self.whole[k].at[slab.shard(shard) if slab.direct else slab.spot(shard, self.group)]

    def mine_part(self, k):
        slab = self.slabs[k]
        return self.near[k] if slab.direct else self.near[k].at[slab.within(self.group)]

    def along_z(self, k, source, step):
        here = self.z_part(k, source)
        mine = source is self.level
        way = (1 - step) // 2
        return pltpu.make_async_remote_copy(
            src_ref=self.mine_part(k) if mine else here,
            dst_ref=here,
            send_sem=self.z_sent.at[way if mine else 2, k * self.depth + source],
            recv_sem=self.z_got.at[k * self.depth + source],
            device_id=(self.group, 2 * (self.level + step) + self.core),
            device_id_type=MESH,
        )

    def pass_on(self, item, act):
        k, i = self.items[item]
        source = self.sources[i]
        pl.when((source < self.level) & (self.level < self.depth - 1))(lambda: act(self.along_z(k, source, 1)))
        pl.when((source > self.level) & (self.level > 0))(lambda: act(self.along_z(k, source, -1)))

    def send_own(self, k, act):
        pl.when(self.level < self.depth - 1)(lambda: act(self.along_z(k, self.level, 1)))
        pl.when(self.level > 0)(lambda: act(self.along_z(k, self.level, -1)))

    def onward(self, kind, item, quarter, half, device):
        k, i = self.items[item]
        shard = 2 * self.sources[i] + self.core
        here = self.whole[k].at[self.slabs[k].spot(shard, quarter, half)]
        return self.move(kind, item, here, here, device)

    def direct(self, item):
        return self.slabs[self.items[item][0]].direct

    def to_core(self, item, core):
        k, i = self.items[item]
        here = self.whole[k].at[self.slabs[k].shard(2 * self.sources[i] + core)]
        return self.move(4, item, here, here, self.peers[2])

    def own(self, k):
        target = self.whole[k].at[self.slabs[k].shard(2 * self.level + self.core)]
        share = pltpu.make_async_remote_copy(
            src_ref=self.near[k],
            dst_ref=target,
            send_sem=self.own_sent.at[k],
            recv_sem=self.own_got.at[k],
            device_id=self.peers[2],
            device_id_type=MESH,
        )
        return pltpu.make_async_copy(self.near[k], target, self.own_copy.at[k, 0]), share

    def fetch_own(self, k):
        col = 0
        for i, array in enumerate(self.mine[k]):
            part = self.near[k].at[:, pl.ds(col, array.shape[1])]
            yield pltpu.make_async_copy(array, part, self.own_copy.at[k, i])
            col += array.shape[1]

    def start(self):
        for k in range(len(self.slabs)):
            for fetch in self.fetch_own(k):
                fetch.start()
        barrier = pltpu.get_barrier_semaphore()

        def greet_one(device):
            pl.semaphore_signal(barrier, inc=1, device_id=device, device_id_type=MESH)

        for peer in self.peers:
            greet_one(peer)
        up, down = self.level < self.depth - 1, self.level > 0
        pl.when(up)(lambda: greet_one((self.group, 2 * (self.level + 1) + self.core)))
        pl.when(down)(lambda: greet_one((self.group, 2 * (self.level - 1) + self.core)))
        pl.semaphore_wait(barrier, 3 + up.astype(jnp.int32) + down.astype(jnp.int32))
        self.begun = 0
        self.begin(self.AHEAD)

    def begin(self, until):
        while self.begun < min(until, len(self.slabs)):
            for fetch in self.fetch_own(self.begun):
                fetch.wait()
            self.send_own(self.begun, lambda copy: copy.start())
            for copy in self.own(self.begun):
                copy.start()
            self.begun += 1

    def pump(self, until):
        group, flip = self.group, self.flip
        x_peer, y_peer, _ = self.peers
        total = len(self.items)
        while self.turn < min(until, self.turns):
            item = self.turn
            if item < total:
                k, i = self.items[item]
                self.begin(k + i * self.SKEW + self.AHEAD)
                here = self.z_part(k, self.sources[i])
                pltpu.make_async_remote_copy(
                    src_ref=here,
                    dst_ref=here,
                    send_sem=self.z_sent.at[2, 0],
                    recv_sem=self.z_got.at[k * self.depth + self.sources[i]],
                    device_id=x_peer,
                    device_id_type=MESH,
                ).wait_recv()
                self.pass_on(item, lambda copy: copy.start())
                if self.direct(item):
                    self.to_core(item, self.core).start()
                else:
                    self.onward(0, item, group, None, x_peer).start()
                    self.onward(1, item, group, None, y_peer).start()
            item = self.turn - self.LAG
            if 0 <= item < total and not self.direct(item):
                self.onward(0, item, flip(0), None, x_peer).wait_recv()
                self.onward(3, item, flip(0), 0, y_peer).start()
                self.onward(1, item, flip(1), None, y_peer).wait_recv()
                self.onward(2, item, flip(1), 1, x_peer).start()
            item = self.turn - 2 * self.LAG
            if 0 <= item < total and not self.direct(item):
                self.onward(3, item, 3 - group, 0, y_peer).wait_recv()
                self.onward(2, item, 3 - group, 1, x_peer).wait_recv()
                self.to_core(item, self.core).start()
            if self.settled < self.turn - 2 * self.LAG - 2:
                self.settle(self.settled)
                self.settled += 1
            self.turn += 1

    def ready_at(self, k):
        return 1 + max(item for item, (slab, _) in enumerate(self.items) if slab == k) + 2 * self.LAG

    def take(self, k):
        self.pump(self.ready_at(k))
        for item, (slab, _) in enumerate(self.items):
            if slab == k:
                self.to_core(item, 1 - self.core).wait_recv()
        keep, share = self.own(k)
        keep.wait()
        share.wait_recv()

    def settle(self, item):
        group, flip = self.group, self.flip
        x_peer, y_peer, _ = self.peers
        self.pass_on(item, lambda copy: copy.wait_send())
        self.to_core(item, self.core).wait_send()
        if self.direct(item):
            return
        self.onward(0, item, group, None, x_peer).wait_send()
        self.onward(1, item, group, None, y_peer).wait_send()
        self.onward(3, item, flip(0), 0, y_peer).wait_send()
        self.onward(2, item, flip(1), 1, x_peer).wait_send()

    def finish(self):
        for item in range(self.settled, len(self.items)):
            self.settle(item)
        for k in range(len(self.slabs)):
            self.send_own(k, lambda copy: copy.wait_send())
            self.own(k)[1].wait_send()


def unpack_vectors(small, parts, width, vec):
    piece = width // parts
    vec[...] = jnp.zeros_like(vec)
    lane = lax.broadcasted_iota(jnp.int32, (128, width), 0)
    col = lax.broadcasted_iota(jnp.int32, (128, width), 1)
    for part in range(parts):
        spread = ((col == lane + part * piece) & (lane < piece)).astype(jnp.bfloat16)
        vec[...] += matmul(small[pl.ds(part * SMALL_ROWS, CH), :128], spread)


def first_kernel(slabs, depth, sizes, *refs):
    count, mine = len(slabs), []
    for size in sizes:
        mine.append(refs[:size])
        refs = refs[size:]
    embedded, vis_col, vis_row, steps, freqs = refs[:5]
    whole, refs = refs[5 : 5 + count], refs[5 + count :]
    kept_hbm, (acts, vec, w_in, w_out, embeds_hbm), refs = refs[:12], refs[12:17], refs[17:]
    sems, refs = refs[:7], refs[7:]
    near, refs = refs[:count], refs[count:]
    small, (e_a, e_u, e_d, d_a, d_u, d_d) = refs[0], refs[1:7]
    e_kept, d_kept = refs[7:13], refs[13:19]
    embeds, e_out, d_out, e_low, d_low, load_sems, kept_sems = refs[19:]
    width = embedded.shape[1]
    parts = 2 * depth
    gathering = Gathering(slabs, depth, mine, whole, near, sems)
    gathering.start()
    half, height = freqs.shape[1], 64
    pieces = steps.shape[0] // height
    enc_turn, dec_turn = gathering.ready_at(3), gathering.ready_at(6)
    encode(embedded, vis_col, None, e_kept[0])
    for piece in range(pieces):
        gathering.pump(piece * enc_turn // pieces)
        rows = pl.ds(piece * height, height)
        phase = steps[rows, :].astype(jnp.float32) * freqs[...]
        embeds[rows, :half] = jnp.cos(phase)
        embeds[rows, half:] = jnp.sin(phase)
    copies = [pltpu.make_async_copy(embeds, embeds_hbm, kept_sems.at[12])]
    copies[0].start()

    def fetch(slots):
        loads = []
        for slab, target in slots:
            gathering.take(slab)
            load = pltpu.make_async_copy(whole[slab], target, load_sems.at[slab])
            load.start()
            loads.append(load)
        return loads

    def run(steps_of, turn, last):
        steps_of = list(steps_of)
        for i, step in enumerate(steps_of):
            step()
            gathering.pump(turn + (last - turn) * (i + 1) // len(steps_of))

    def keep(kept, at):
        for i, buffer in enumerate(kept):
            copy = pltpu.make_async_copy(buffer, kept_hbm[at + i], kept_sems.at[at + i])
            copy.start()
            copies.append(copy)

    for load in fetch([(0, small), (1, e_a), (2, e_u), (3, e_d)]):
        load.wait()
    unpack_vectors(small, parts, width, vec)
    for part in range(parts):
        block = pl.ds(part * SMALL_ROWS, CH)
        w_in[:, pl.ds(part * 128, 128)] = small[block, pl.ds(128, 128)]
        w_out[:, pl.ds(part * 128, 128)] = small[block, pl.ds(256, 128)]
    live = live_keys(vis_row)
    run(forward_steps(width, e_kept[0], vec[0:1, :], vec[1:2, :], e_a, e_u, e_d, *e_kept[1:], e_out, e_low, live), enc_turn, dec_turn)
    keep(e_kept, 0)
    spread_rows(vis_row, e_out, vec, d_kept[0])
    for load in fetch([(4, d_a), (5, d_u), (6, d_d)]):
        load.wait()
    run(forward_steps(width, d_kept[0], vec[2:3, :], vec[3:4, :], d_a, d_u, d_d, *d_kept[1:], d_out, d_low), dec_turn, gathering.turns)
    keep(d_kept, 6)
    acts[...] = d_out[...].astype(jnp.bfloat16)
    for slab in range(7, count):
        gathering.take(slab)
    gathering.finish()
    for copy in copies:
        copy.wait()


def first_part(shards, slabs, depth, embedded, vis_col, vis_row, steps, freqs):
    tokens, width = embedded.shape
    count, items = len(slabs), len(slabs) * (depth - 1)
    inner = slabs[2].cols
    rows = BUFFER + vis_col.shape[0]
    flat, wide = steps.shape[0], 2 * freqs.shape[1]
    f32, half = jnp.float32, jnp.bfloat16
    whole, anywhere = pl.BlockSpec(memory_space=pltpu.VMEM), pl.BlockSpec(memory_space=pl.ANY)
    shape, dma = jax.ShapeDtypeStruct, pltpu.SemaphoreType.DMA
    gathered = [shape((2 * depth * s.rows, s.cols), half) for s in slabs]

    def kept(height):
        return [
            shape((height, width), f32),
            shape((height, 3 * width), half),
            shape((height, width), half),
            shape((height, width), f32),
            shape((height, inner), half),
            shape((height, inner), half),
        ]

    saved = kept(rows) + kept(tokens)
    outs = gathered + saved
    outs += [shape((tokens, width), half), shape((CH, width), f32), shape((CH, wide), half), shape((CH, wide), half), shape((flat, wide), f32)]
    found = pl.pallas_call(
        functools.partial(first_kernel, slabs, depth, [len(arrays) for arrays in shards]),
        out_shape=outs,
        in_specs=[anywhere] * sum(len(arrays) for arrays in shards) + [whole] * 5,
        out_specs=[anywhere] * (count + 12) + [whole] * 4 + [anywhere],
        scratch_shapes=[dma((5, items)), dma((5, items)), dma((3, count * depth)), dma((count * depth,)), dma((count,)), dma((count,)), dma((count, 2))]
        + [pltpu.VMEM((s.rows, s.cols), half) for s in slabs]
        + [pltpu.VMEM(s.shape, s.dtype) for s in (*gathered[:7], *saved)]
        + [
            pltpu.VMEM((flat, wide), f32),
            pltpu.VMEM((rows, width), f32),
            pltpu.VMEM((tokens, width), f32),
            pltpu.VMEM((rows, width), half),
            pltpu.VMEM((tokens, width), half),
            dma((count,)),
            dma((13,)),
        ],
        compiler_params=pltpu.CompilerParams(collective_id=0, has_side_effects=True, vmem_limit_bytes=SUM_VMEM),
        name="gather_and_forward",
    )(*(array for arrays in shards for array in arrays), embedded, vis_col, vis_row, steps, freqs)
    slabs_found, found = found[:count], found[count:]
    return slabs_found, found[:6], found[6:12], *found[12:]


SIDE = 256
BACK_TILE = 256


class Chunk:
    def __init__(self, parent, height, row, rows, col, cols, by_rows):
        self.parent, self.height = parent, height
        self.row, self.rows, self.col, self.cols, self.by_rows = row, rows, col, cols, by_rows
        self.piece = (rows // 4, cols) if by_rows else (rows, cols // 4)
        self.set_order(False, 0)

    def set_order(self, z_first, first_bit):
        self.z_first, self.first_bit = z_first, first_bit

    def shard(self, shard):
        return (pl.ds(aligned(shard * self.height + self.row, 16), self.rows), pl.ds(self.col, self.cols))

    def out(self):
        return (pl.ds(self.row, self.rows), pl.ds(self.col, self.cols))

    def within(self, quarter):
        rows, cols = self.piece
        if self.by_rows:
            return (pl.ds(aligned(quarter * rows, 16), rows), pl.ds(0, cols))
        return (pl.ds(0, rows), pl.ds(aligned(quarter * cols, 128), cols))


def cut(parent, slab, pieces):
    for i in range(pieces):
        if slab.by_rows:
            cols = slab.cols // pieces
            yield Chunk(parent, slab.rows, 0, slab.rows, i * cols, cols, True)
        else:
            rows = slab.rows // pieces
            yield Chunk(parent, slab.rows, i * rows, rows, 0, slab.cols, False)


class Summing:
    STAGES, LAG, AHEAD, BESIDE = 6, 5, 2, 5

    def __init__(self, chunks, depth, grads, outs, buffers, sems):
        self.chunks, self.depth, self.grads, self.outs = chunks, depth, grads, outs
        self.held, self.from_first, self.from_second, self.from_level, self.result, self.stage = buffers
        self.stage_sem, self.out_sem, self.core_pair, self.pair, self.z_pair = sems
        self.group, self.level, self.core, self.flip = place(depth)
        self.me = 2 * self.level + self.core
        self.partner = (self.group, 2 * self.level + 1 - self.core)
        self.z_peers = [(self.group, 2 * self.level_at(step) + self.core) for step in range(1, depth)]
        self.peers = [(self.flip(0), self.me), (self.flip(1), self.me), self.partner, *self.z_peers]

    def level_at(self, step):
        return lax.rem(self.level + step + self.depth, self.depth)

    def bit(self, b):
        return (self.group // (1 << b)) % 2

    def move(self, pair, k, kind, source, target, device):
        return pltpu.make_async_remote_copy(
            src_ref=source,
            dst_ref=target,
            send_sem=pair[0].at[kind, k],
            recv_sem=pair[1].at[kind, k],
            device_id=device,
            device_id_type=MESH,
        )

    def quarter(self, k, first, second):
        b = self.chunks[k].first_bit
        return first * (1 << b) + second * (1 << (1 - b))

    def core_move(self, k, lev):
        chunk = self.chunks[k]
        source = self.grads[chunk.parent].at[chunk.shard(2 * lev + 1 - self.core)]
        return self.move(self.core_pair, k, lev, source, self.held[k].at[lev], self.partner)

    def part(self, k, quarter):
        chunk, held = self.chunks[k], self.held[k]
        where = chunk.within(quarter)
        return held.at[(self.level,) + where] if chunk.z_first else held.at[(slice(None),) + where]

    def first_move(self, k, j):
        b = self.chunks[k].first_bit
        source = self.part(k, self.quarter(k, 1 - self.bit(b), j))
        return self.move(self.pair, k, j, source, self.from_first[k].at[j], (self.flip(b), self.me))

    def second_move(self, k):
        b = self.chunks[k].first_bit
        source = self.part(k, self.quarter(k, self.bit(b), 1 - self.bit(1 - b)))
        return self.move(self.pair, k, 2, source, self.from_second[k], (self.flip(1 - b), self.me))

    def level_move(self, k, step):
        chunk, held = self.chunks[k], self.held[k]
        lev = self.level_at(step)
        source = held.at[lev] if chunk.z_first else held.at[(lev,) + chunk.within(self.group)]
        target = self.from_level[k].at[step - 1]
        return self.move(self.z_pair, k, step - 1, source, target, self.z_peers[step - 1])

    def spread(self, k, kind, whose, b):
        here = self.result[k].at[self.chunks[k].within(whose)]
        return self.move(self.pair, k, kind, here, here, (self.flip(b), self.me))

    def spread_second(self, k, whose):
        return self.spread(k, 3, whose, 1 - self.chunks[k].first_bit)

    def spread_first(self, k, j, whose):
        return self.spread(k, 4 + j, whose, self.chunks[k].first_bit)

    def out_copy(self, k):
        chunk = self.chunks[k]
        target = self.outs[chunk.parent].at[chunk.out()]
        return pltpu.make_async_copy(self.result[k], target, self.out_sem.at[k])

    def stage_copy(self, k, lev):
        chunk = self.chunks[k]
        source = self.grads[chunk.parent].at[chunk.shard(2 * lev + self.core)]
        slot = self.stage[(chunk.rows, chunk.cols)].at[lev % 2]
        return pltpu.make_async_copy(source, slot, self.stage_sem.at[k, lev % 2])

    def rows_loop(self, height, body):
        step = 32 if height % 32 == 0 else 16
        loop(height // step + self.level // self.depth, lambda i: body(at_step(i, step)))

    def add_core(self, k):
        chunk, held = self.chunks[k], self.held[k]
        stage = self.stage[(chunk.rows, chunk.cols)]
        self.stage_copy(k, 0).start()
        for lev in range(self.depth):
            if lev + 1 < self.depth:
                self.stage_copy(k, lev + 1).start()
            self.core_move(k, lev).wait_recv()
            self.stage_copy(k, lev).wait()

            def body(rows):
                total = held[lev, rows, :].astype(jnp.float32) + stage[lev % 2, rows, :].astype(jnp.float32)
                held[lev, rows, :] = total.astype(jnp.bfloat16)

            self.rows_loop(chunk.rows, body)

    def levels_of(self, k):
        return [self.level] if self.chunks[k].z_first else list(range(self.depth))

    def shifted(self, rows, by):
        return pl.ds(aligned(rows.start + by, 16), rows.size)

    def add_first(self, k):
        chunk, slot = self.chunks[k], k
        held, arrived = self.held[slot], self.from_first[slot]
        for j in range(2):
            self.first_move(k, j).wait_recv()
            top, cols = chunk.within(self.quarter(k, self.bit(chunk.first_bit), j))
            for lev in self.levels_of(k):

                def body(rows):
                    at = (lev, self.shifted(rows, top.start), cols)
                    extra = arrived[j, rows, :] if chunk.z_first else arrived[j, lev, rows, :]
                    held[at] = (held[at].astype(jnp.float32) + extra.astype(jnp.float32)).astype(jnp.bfloat16)

                self.rows_loop(chunk.piece[0], body)

    def add_second(self, k):
        chunk, slot = self.chunks[k], k
        held, arrived, result = self.held[slot], self.from_second[slot], self.result[slot]
        self.second_move(k).wait_recv()
        top, cols = chunk.within(self.group)
        for lev in self.levels_of(k):

            def body(rows):
                at = (lev, self.shifted(rows, top.start), cols)
                extra = arrived[rows, :] if chunk.z_first else arrived[lev, rows, :]
                total = (held[at].astype(jnp.float32) + extra.astype(jnp.float32)).astype(jnp.bfloat16)
                if chunk.z_first:
                    result[at[1:]] = total
                else:
                    held[at] = total

            self.rows_loop(chunk.piece[0], body)

    def add_level(self, k):
        chunk, slot = self.chunks[k], k
        held, arrived, result = self.held[slot], self.from_level[slot], self.result[slot]
        for step in range(1, self.depth):
            self.level_move(k, step).wait_recv()
        top, cols = (pl.ds(0, chunk.rows), pl.ds(0, chunk.cols)) if chunk.z_first else chunk.within(self.group)

        def body(rows):
            at = (self.shifted(rows, top.start), cols)
            total = held[(self.level,) + at].astype(jnp.float32)
            for step in range(self.depth - 1):
                total = total + arrived[step, rows, :].astype(jnp.float32)
            if chunk.z_first:
                held[(self.level,) + at] = total.astype(jnp.bfloat16)
            else:
                result[at] = total.astype(jnp.bfloat16)

        self.rows_loop(top.size, body)

    def begin_core(self, k):
        for lev in range(self.depth):
            self.core_move(k, lev).start()

    def begin_first(self, k):
        self.first_move(k, 0).start()
        self.first_move(k, 1).start()

    def begin_level(self, k):
        for step in range(1, self.depth):
            self.level_move(k, step).start()

    def begin_spread(self, k):
        self.spread_second(k, self.group).start()

    def end_spread_second(self, k):
        other = self.flip(1 - self.chunks[k].first_bit)
        self.spread_second(k, other).wait_recv()
        self.spread_first(k, 0, self.group).start()
        self.spread_first(k, 1, other).start()

    def end_spread_first(self, k):
        self.spread_first(k, 0, self.flip(self.chunks[k].first_bit)).wait_recv()
        self.spread_first(k, 1, 3 - self.group).wait_recv()
        self.out_copy(k).start()

    def stages(self, k):
        if self.chunks[k].z_first:
            return [
                lambda: (self.add_core(k), self.begin_level(k)),
                lambda: (self.add_level(k), self.begin_first(k)),
                lambda: (self.add_first(k), self.second_move(k).start()),
                lambda: (self.add_second(k), self.begin_spread(k)),
                lambda: self.end_spread_second(k),
                lambda: self.end_spread_first(k),
            ]
        return [
            lambda: (self.add_core(k), self.begin_first(k)),
            lambda: (self.add_first(k), self.second_move(k).start()),
            lambda: (self.add_second(k), self.begin_level(k)),
            lambda: (self.add_level(k), self.begin_spread(k)),
            lambda: self.end_spread_second(k),
            lambda: self.end_spread_first(k),
        ]

    def settle(self, k):
        for lev in range(self.depth):
            self.core_move(k, lev).wait_send()
        self.first_move(k, 0).wait_send()
        self.first_move(k, 1).wait_send()
        self.second_move(k).wait_send()
        for step in range(1, self.depth):
            self.level_move(k, step).wait_send()
        self.spread_second(k, self.group).wait_send()
        self.spread_first(k, 0, self.group).wait_send()
        self.spread_first(k, 1, self.flip(1 - self.chunks[k].first_bit)).wait_send()
        self.out_copy(k).wait()

    def run(self, ready, beside):
        count = len(self.chunks)
        greet(self.peers)
        plans = [self.stages(k) for k in range(count)]
        for turn in range(-self.AHEAD, count + self.LAG * (self.STAGES - 1)):
            if turn + self.AHEAD < count:
                ready(turn + self.AHEAD)
                self.begin_core(turn + self.AHEAD)
            for stage in range(self.STAGES):
                if 0 <= turn - self.LAG * stage < count:
                    plans[turn - self.LAG * stage][stage]()
                if stage < self.BESIDE:
                    beside()
            done = turn - self.LAG * (self.STAGES - 1) - 2
            if 0 <= done < count:
                self.settle(done)
        for k in range(max(0, done + 1), count):
            self.settle(k)


class Saved:
    def __init__(self, kept, buffers, sems):
        rows = kept[0].shape[0]
        part = pl.ds(0, rows)
        self.wide, self.qkv, self.mixed = (b if b.shape[0] == rows else b.at[part] for b in buffers)
        places = (self.wide, self.qkv, self.mixed, self.wide)
        self.copies = [pltpu.make_async_copy(a, b, sems.at[i]) for i, (a, b) in enumerate(zip(kept, places, strict=True))]

    def start(self, which):
        self.copies[("x", "qkv", "mixed", "middle").index(which)].start()

    def wait(self, which):
        self.copies[("x", "qkv", "mixed", "middle").index(which)].wait()


class Stream:
    SLOTS = 3

    def __init__(self, sources, slots, sems):
        self.sources, self.slots, self.sems, self.used = sources, slots, sems, 0
        for i in range(self.SLOTS - 1):
            self.copy(i).start()

    def slot(self, i):
        height, slot = self.sources[i].shape[0], self.slots.at[i % self.SLOTS]
        return slot if height == slot.shape[0] else slot.at[pl.ds(0, height)]

    def copy(self, i):
        return pltpu.make_async_copy(self.sources[i], self.slot(i), self.sems.at[i % self.SLOTS])

    def next(self):
        i = self.used
        self.copy(i).wait()
        if i + self.SLOTS - 1 < len(self.sources):
            self.copy(i + self.SLOTS - 1).start()
        self.used += 1
        return self.slot(i)


def backward_steps(width, grad, gain_one, gain_two, saved, following, streams, d_a, d_up, d_down, d_one, d_two,
                   grad_low, low, grad_qkv, acc, grad_mid, out, tiles, live, reach, names):
    wide, narrow, square = tiles
    downs, ups, acts, slopes, heads = streams
    inner, side = d_up.shape[1], SIDE
    qkv, mixed, middle, stream = saved.qkv, saved.mixed, saved.wide, saved.wide

    def begin():
        saved.wait("middle")
        grad_low[...] = grad[...].astype(jnp.bfloat16)
        scale_norm(middle, gain_two, low)
        acc[...] = jnp.zeros_like(acc)

    yield begin
    def feed_down(j):
        narrow.put(j, rows_dot(acts.next()[...], grad_low[...]), d_down.at[pl.ds(j * BACK_TILE, BACK_TILE), :])

    def feed_slope(j):
        slope = slopes.next()[...].astype(jnp.float32)
        grad_qkv[:, :BACK_TILE] = (right_trans(grad_low[...], downs.next()[...]) * slope).astype(jnp.bfloat16)

    def feed_up(j):
        wide.put(j, rows_dot(low[...], grad_qkv[:, :BACK_TILE]), d_up.at[:, pl.ds(j * BACK_TILE, BACK_TILE)])
        acc[...] += right_trans(grad_qkv[:, :BACK_TILE], ups.next()[...])

    def down_done():
        narrow.flush(d_down.at[pl.ds(0, BACK_TILE), :])
        reach(names[0])

    for j in range(inner // BACK_TILE):
        yield functools.partial(feed_down, j)
    yield down_done
    for j in range(inner // BACK_TILE):
        yield functools.partial(feed_slope, j)
        yield functools.partial(feed_up, j)

    def middle_back():
        wide.flush(d_up.at[:, pl.ds(0, BACK_TILE)])
        reach(names[1])
        norm_back_into(acc, middle, gain_two, grad, grad_mid, d_two)
        saved.start("x")
        grad_low[...] = grad_mid[...].astype(jnp.bfloat16)
        saved.wait("mixed")

    yield middle_back

    def project_back(j):
        cols = pl.ds(j * side, side)
        square.put(j, rows_dot(mixed[...], grad_low[:, cols]), d_a.at[:, pl.ds(3 * width + j * side, side)])
        added = right_trans(grad_low[:, cols], heads.next()[...])
        acc[...] = added if j == 0 else acc[...] + added

    for j in range(width // side):
        yield functools.partial(project_back, j)

    def mixed_back():
        if following:
            following.start("mixed")
        low[...] = acc[...].astype(jnp.bfloat16)
        saved.wait("qkv")

    yield mixed_back

    def attend(pair):
        where = [pl.ds(pair * 128 + part * width, 128) for part in range(3)]
        query, key, value = (qkv[:, at] for at in where)
        grad_mixed = low[:, pl.ds(pair * 128, 128)]
        found = []
        for half in range(2):
            probs = probabilities(query, key, half, live)
            grad_half = keep_half(grad_mixed, half)
            grad_probs = right_trans(grad_half, value)
            dots = jnp.sum(grad_probs * probs, axis=-1, keepdims=True)
            grad_scores = (probs * (grad_probs - dots) * 0.125).astype(jnp.bfloat16)
            found.append(
                (matmul(grad_scores, key), rows_dot(grad_scores, query), rows_dot(probs.astype(jnp.bfloat16), grad_half))
            )
        for part in range(3):
            both = jnp.where(head_mask(0), found[0][part], found[1][part])
            grad_qkv[:, where[part]] = both.astype(jnp.bfloat16)

    for pair in range(width // 128):
        yield functools.partial(attend, pair)

    def normed():
        if following:
            following.start("qkv")
        saved.wait("x")
        scale_norm(stream, gain_one, low)

    yield normed

    def project(j):
        piece = grad_qkv[:, pl.ds(j * side, side)]
        square.put(j + width // side, rows_dot(low[...], piece), d_a.at[:, pl.ds(j * side, side)])
        added = right_trans(piece, heads.next()[...])
        acc[...] = added if j == 0 else acc[...] + added

    for j in range(3 * width // side):
        yield functools.partial(project, j)

    def end():
        square.flush(d_a.at[:, pl.ds(0, side)])
        reach(names[2])
        norm_back_into(acc, stream, gain_one, grad_mid, out, d_one)
        if following:
            following.start("middle")

    yield end


def last_kernel(chunks, stage_keys, depth, *refs):
    head_grads, refs = refs[:3], refs[3:]
    head_small, refs = refs[:2], refs[2:]
    (vis_col, vis_row, vec, grad_rows), e_kept, d_kept, refs = refs[:4], refs[4:10], refs[10:16], refs[16:]
    (e_a, e_u, e_d, d_a, d_u, d_d), refs = refs[:6], refs[6:]
    outs, refs = refs[:10], refs[10:]
    embed_grad, small_grad, refs = refs[0], refs[1], refs[2:]
    block_grads, refs = refs[:6], refs[6:]
    (small, small_pack, d_grad, low_a, low_b, grad_qkv, acc, grad_mid), refs = refs[:8], refs[8:]
    saved_buffers, saved_sems, refs = refs[:3], refs[3], refs[4:]
    (wide, narrow, square, down_slots, up_slots, act_slots, slope_slots, head_slots, tile_sems, load_sems, pack_sem), refs = refs[:11], refs[11:]
    count = len(chunks)
    buffers = [refs[i * count : (i + 1) * count] for i in range(5)]
    refs = refs[5 * count :]
    stage, refs = dict(zip(stage_keys, refs[: len(stage_keys)], strict=True)), refs[len(stage_keys) :]
    stage_sem, out_sem, core_sent, core_got, sent, got, z_sent, z_got = refs
    sems = (stage_sem, out_sem, (core_sent, core_got), (sent, got), (z_sent, z_got))
    tokens, width = d_kept[0].shape
    rows = e_kept[0].shape[0]
    parts = 2 * depth
    d_saved = Saved(d_kept[:4], saved_buffers, saved_sems.at[0])
    e_saved = Saved(e_kept[:4], saved_buffers, saved_sems.at[1])
    de_a, de_u, de_d, dd_a, dd_u, dd_d = block_grads
    grads = (small_grad, *block_grads, *head_grads)
    summing = Summing(chunks, depth, grads, outs, (*buffers, stage), sems)
    tiles = (Tiles(wide, tile_sems.at[0]), Tiles(narrow, tile_sems.at[1]), Tiles(square, tile_sems.at[2]))
    reached = {"head"}
    e_grad = d_grad.at[pl.ds(0, rows)]
    embed_copy = pltpu.make_async_copy(d_grad, embed_grad, pack_sem.at[1])

    def streams(inner, w_a, w_u, w_d, acted, sloped):
        tile = [pl.ds(j * BACK_TILE, BACK_TILE) for j in range(inner // BACK_TILE)]
        past = width // SIDE
        sides = [pl.ds((j + 3 * past) % (4 * past) * SIDE, SIDE) for j in range(4 * past)]
        return (
            Stream([w_d.at[t, :] for t in tile], down_slots, load_sems.at[0]),
            Stream([w_u.at[:, t] for t in tile], up_slots, load_sems.at[1]),
            Stream([acted.at[:, t] for t in tile], act_slots, load_sems.at[2]),
            Stream([sloped.at[:, t] for t in tile], slope_slots, load_sems.at[3]),
            Stream([w_a.at[:, t] for t in sides], head_slots, load_sems.at[4]),
        )

    def work():
        inner = d_u.shape[1]
        ready_streams = []

        def begin():
            for which in ("middle", "mixed", "qkv"):
                d_saved.start(which)
            ready_streams.append(streams(inner, d_a, d_u, d_d, *d_kept[4:]))
            arrived = low_b.at[pl.ds(BUFFER, tokens - BUFFER)]
            fetch = pltpu.make_async_copy(grad_rows, arrived, pack_sem.at[2])
            fetch.start()
            fetch.wait()
            d_grad[:BUFFER, :] = jnp.zeros((BUFFER, width), jnp.float32)
            d_grad[BUFFER:, :] = arrived[...].astype(jnp.float32)

        yield begin
        yield from lazy_steps(lambda: backward_steps(
            width, d_grad, vec[2:3, :], vec[3:4, :], d_saved, e_saved, ready_streams[0], dd_a, dd_u, dd_d,
            small.at[2], small.at[3], low_a, low_b, grad_qkv, acc, grad_mid, d_grad, tiles, None, reached.add, ("dec down", "dec up", "dec")))

        def between():
            ready_streams.append(streams(inner, e_a, e_u, e_d, *e_kept[4:]))
            hot = spot_hot(vis_row, tokens - BUFFER)
            masked = 1.0 - jnp.sum(hot.astype(jnp.float32), axis=1, keepdims=True)
            small[4] = jnp.broadcast_to(jnp.sum(d_grad[BUFFER:, :] * masked, axis=0, keepdims=True), (8, width))
            e_grad[BUFFER:, :] = exact_dot(token_hot(vis_col, tokens - BUFFER), d_grad[BUFFER:, :])

        yield between
        part = pl.ds(0, rows)
        yield from lazy_steps(lambda: backward_steps(
            width, e_grad, vec[0:1, :], vec[1:2, :], e_saved, None, ready_streams[1], de_a, de_u, de_d,
            small.at[0], small.at[1], low_a.at[part], low_b.at[part], grad_qkv.at[part], acc.at[part],
            grad_mid.at[part], e_grad, tiles, live_keys(vis_row), reached.add, ("enc down", "enc up", "enc")))

        def end():
            d_grad[BUFFER:, :] = exact_dot(spot_hot(vis_row, tokens - BUFFER), e_grad[BUFFER:, :])
            embed_copy.start()
            pack_gradients(small, head_small, parts, small_pack)
            copy = pltpu.make_async_copy(small_pack, small_grad, pack_sem.at[0])
            copy.start()
            copy.wait()
            reached.add("all")

        yield end

    steps = work()
    needs = ["all", "enc", "enc up", "enc down", "dec", "dec up", "dec down", "head", "head", "head"]

    def beside():
        step = next(steps, None)
        if step is not None:
            step()

    def ready(k):
        while needs[chunks[k].parent] not in reached:
            beside()

    summing.run(ready, beside)
    embed_copy.wait()


def lazy_steps(make):
    yield from make()


def pack_gradients(small, head_small, parts, target):
    count, _, width = small.shape
    piece = width // parts
    target[...] = jnp.zeros_like(target)
    lane = lax.broadcasted_iota(jnp.int32, (width, 128), 1)
    row = lax.broadcasted_iota(jnp.int32, (width, 128), 0)
    which = lax.broadcasted_iota(jnp.int32, (CH, width), 0)
    rows = jnp.zeros((CH, width), jnp.float32)
    for i in range(count):
        rows = jnp.where(which == i, jnp.concatenate([small[i], small[i]], axis=0), rows)
    low = rows.astype(jnp.bfloat16)
    for part in range(parts):
        block = pl.ds(part * SMALL_ROWS, CH)
        pick = ((row == lane + part * piece) & (lane < piece)).astype(jnp.bfloat16)
        target[block, :128] = matmul(low, pick).astype(jnp.bfloat16)
        for i in range(2):
            target[block, pl.ds(128 * (i + 1), 128)] = head_small[i][:, pl.ds(part * 128, 128)].astype(jnp.bfloat16)


def last_part(slabs, chunks, depth, head_grads, head_small, grad_rows, vis_col, vis_row, vec, enc_kept, dec_kept, weights):
    tokens, width = dec_kept[0].shape
    rows = enc_kept[0].shape[0]
    parts = 2 * depth
    f32, half = jnp.float32, jnp.bfloat16
    whole, anywhere = pl.BlockSpec(memory_space=pltpu.VMEM), pl.BlockSpec(memory_space=pl.ANY)
    shape, dma = jax.ShapeDtypeStruct, pltpu.SemaphoreType.DMA
    stage_keys = sorted({(c.rows, c.cols) for c in chunks})
    held, first, second, lev, result = [], [], [], [], []
    for chunk in chunks:
        part = (chunk.rows, chunk.cols)
        held.append(pltpu.VMEM((depth,) + part, half))
        result.append(pltpu.VMEM(part, half))
        if chunk.z_first:
            first.append(pltpu.VMEM((2,) + chunk.piece, half))
            second.append(pltpu.VMEM(chunk.piece, half))
            lev.append(pltpu.VMEM((depth - 1,) + part, half))
        else:
            first.append(pltpu.VMEM((2, depth) + chunk.piece, half))
            second.append(pltpu.VMEM((depth,) + chunk.piece, half))
            lev.append(pltpu.VMEM((depth - 1,) + chunk.piece, half))
    count = len(chunks)
    outs = [shape((s.rows, s.cols), half) for s in slabs]
    outs += [shape((tokens, width), f32), shape((parts * SMALL_ROWS, SMALL_COLS), half)]
    outs += [shape(w.shape, half) for w in weights]
    vmem = pltpu.VMEM
    found = pl.pallas_call(
        functools.partial(last_kernel, chunks, stage_keys, depth),
        out_shape=outs,
        in_specs=[anywhere] * 3 + [whole] * 5 + [anywhere] * 19,
        out_specs=[anywhere] * (len(slabs) + 8),
        scratch_shapes=[
            vmem((5, 8, width), f32),
            vmem((parts * SMALL_ROWS, SMALL_COLS), half),
            vmem((tokens, width), f32),
            vmem((tokens, width), half),
            vmem((tokens, width), half),
            vmem((tokens, 3 * width), half),
            vmem((tokens, width), f32),
            vmem((tokens, width), f32),
            vmem((tokens, width), f32),
            vmem((tokens, 3 * width), half),
            vmem((tokens, width), half),
            dma((2, 4)),
            vmem((2, width, BACK_TILE), half),
            vmem((2, BACK_TILE, width), half),
            vmem((2, width, SIDE), half),
            vmem((Stream.SLOTS, BACK_TILE, width), half),
            vmem((Stream.SLOTS, width, BACK_TILE), half),
            vmem((Stream.SLOTS, tokens, BACK_TILE), half),
            vmem((Stream.SLOTS, tokens, BACK_TILE), half),
            vmem((Stream.SLOTS, width, SIDE), half),
            dma((3, 2)),
            dma((5, Stream.SLOTS)),
            dma((3,)),
        ]
        + held
        + first
        + second
        + lev
        + result
        + [vmem((2,) + key, half) for key in stage_keys]
        + [
            dma((count, 2)),
            dma((count,)),
            dma((depth, count)),
            dma((depth, count)),
            dma((6, count)),
            dma((6, count)),
            dma((depth - 1, count)),
            dma((depth - 1, count)),
        ],
        compiler_params=pltpu.CompilerParams(collective_id=1, has_side_effects=True, vmem_limit_bytes=LAST_VMEM),
        name="backward_and_sum",
    )(*head_grads, *head_small, vis_col, vis_row, vec, grad_rows, *enc_kept, *dec_kept, *weights)
    return found[len(slabs)], found[: len(slabs)]


SMALL_ROWS, SMALL_COLS = 32, 512


def pack_small(vectors, first, last):
    parts = vectors[0].shape[0] // 96
    lanes = jnp.stack([v.reshape(parts, 96) for v in vectors], axis=1)
    lanes = jnp.pad(lanes, ((0, 0), (0, CH - len(vectors)), (0, 128 - 96)))
    wide = [w.reshape(CH, parts, 128).transpose(1, 0, 2) for w in (first, last)]
    packed = jnp.concatenate([lanes, *wide], axis=2)
    packed = jnp.pad(packed, ((0, 0), (0, SMALL_ROWS - CH), (0, SMALL_COLS - 384)))
    return packed.reshape(parts * SMALL_ROWS, SMALL_COLS)


def unpack_small(packed):
    parts = packed.shape[0] // SMALL_ROWS
    packed = packed.reshape(parts, SMALL_ROWS, SMALL_COLS)
    vectors = packed[:, :5, :96].transpose(1, 0, 2).reshape(5, parts * 96)
    wide = [packed[:, :CH, 128 * i : 128 * i + 128].transpose(1, 0, 2).reshape(CH, parts * 128) for i in (1, 2)]
    return vectors, wide[0], wide[1]


SLABS = (
    Slab(SMALL_ROWS, SMALL_COLS, False, True),
    Slab(96, 3072, False),
    Slab(96, 3072, False),
    Slab(384, 768, True),
    Slab(96, 3072, False),
    Slab(96, 3072, False),
    Slab(384, 768, True),
    Slab(128, 3072, False),
    Slab(128, 2048, False),
    Slab(96, 1024, False, True),
)


def chunks_of():
    plan = [(7, 4, ()), (8, 2, ()), (9, 1, ()), (6, 3, (0, 2)), (5, 3, ()), (4, 3, ()), (3, 3, (0, 2)), (2, 3, ()), (1, 3, ()), (0, 1, ())]
    found = []
    for parent, pieces, z_first in plan:
        for i, chunk in enumerate(cut(parent, SLABS[parent], pieces)):
            chunk.set_order(i in z_first, len(found) % 2)
            found.append(chunk)
    return found


def by_links():
    return lax.axis_size("dev") == 8 and lax.axis_size("grp") == 4


def packed_shards(shards):
    (e_one, e_qkv, e_proj, e_two, e_up, e_down, d_one, d_qkv, d_proj, d_two, d_up, d_down, fill, h_in, h_cond, h_ada, h_inner, h_outer, h_out) = shards
    large = ((e_qkv, e_proj), (e_up,), (e_down,), (d_qkv, d_proj), (d_up,), (d_down,), (h_ada,), (h_inner, h_outer), (h_cond,))
    return large, [e_one, e_two, d_one, d_two, fill], h_in, h_out


def gather_weights(shards):
    packed, vectors, h_in, h_out = packed_shards(shards)
    whole = lambda w, axis=0: lax.all_gather(w, "dev", axis=axis, tiled=True)
    return [whole(jnp.concatenate(w, axis=1)) for w in packed], whole(jnp.stack(vectors), 1), whole(h_in, 1), whole(h_out).T


def sum_gradients(slabs, vectors, d_in, d_out):
    def scatter(grad, axis=0):
        part = lax.psum_scatter(grad.astype(jnp.float32), "dev", scatter_dimension=axis, tiled=True)
        return lax.psum(part.astype(jnp.bfloat16), "grp")

    return unpack_gradients([scatter(g) for g in slabs], scatter(vectors, 1), scatter(d_in, 1), scatter(d_out, 1))


def widen_kernel(count, *refs):
    sources, targets = refs[:count], list(refs[count:])
    for source in sources:
        col = 0
        while col < source.shape[1]:
            target = targets.pop(0)
            width = target.shape[1]
            target[...] = source[:, col : col + width].astype(jnp.float32)
            col += width


def widen(slabs, cuts):
    shape = jax.ShapeDtypeStruct
    outs = [shape((s.shape[0], width), jnp.float32) for s, widths in zip(slabs, cuts, strict=True) for width in widths]
    whole = pl.BlockSpec(memory_space=pltpu.VMEM)
    return pl.pallas_call(
        functools.partial(widen_kernel, len(slabs)),
        out_shape=outs,
        in_specs=[whole] * len(slabs),
        out_specs=[whole] * len(outs),
        compiler_params=pltpu.CompilerParams(vmem_limit_bytes=SUM_VMEM),
        name="widen_gradients",
    )(*slabs)


def unpack_gradients(slabs, vectors, d_in, d_out):
    vectors, d_in, d_out = (s.astype(jnp.float32) for s in (vectors, d_in, d_out))
    width = slabs[2].shape[1]
    head = slabs[8].shape[1]
    cuts = [(3 * width, width), (4 * width,), (width,)] * 2 + [(3 * head,), (head, head), (head,)]
    e_qkv, e_proj, e_up, e_down, d_qkv, d_proj, d_up, d_down, ada, inner, outer, cond = widen(slabs, cuts)
    return (vectors[0], e_qkv, e_proj, vectors[1], e_up, e_down, vectors[2], d_qkv, d_proj, vectors[3], d_up, d_down,
            vectors[4], d_in, cond, ada, inner, outer, d_out.T)


def per_device(embedded, mask_order, counts, targets, noise_copies, timesteps, *shards):
    images, tokens, width = embedded.shape
    seq_len = mask_order.shape[1]
    linked = by_links() and images == 1
    if not linked:
        slabs, vectors, w_in, w_out = gather_weights(shards)
        vec = jnp.pad(vectors.astype(jnp.float32), ((0, CH - 5), (0, 0)))
    freqs = jnp.exp(-math.log(10000.0) * jnp.arange(HW // 2, dtype=jnp.float32) / (HW // 2)).reshape(1, HW // 2)
    losses, acts_of, embed_grads, totals = [], [], [], None
    for image in range(images):
        padded = jnp.concatenate([mask_order[image], jnp.full((SPOTS,), -1, jnp.int32)])
        seen = lax.dynamic_slice(padded, (counts[image],), (SPOTS,))
        vis_col, vis_row = seen.reshape(SPOTS, 1), seen.reshape(1, SPOTS)
        steps = timesteps[image].T.reshape(COPIES * seq_len, 1)
        noise = noise_copies[image].transpose(1, 0, 2).reshape(COPIES * seq_len, CH)
        if linked:
            packed, vectors, h_in, h_out = packed_shards(shards)
            (_, *slabs), enc_kept, dec_kept, acts, vec, w_in, w_out, embeds = first_part(
                ((pack_small(vectors, h_in, h_out.T),), *packed), SLABS, lax.axis_size("dev") // 2,
                embedded[image], vis_col, vis_row, steps, freqs,
            )
        else:
            phase = steps.astype(jnp.float32) * freqs
            embeds = jnp.concatenate([jnp.cos(phase), jnp.sin(phase)], axis=1)
            enc_kept, dec_kept, acts = forward_blocks(embedded[image], vis_col, vis_row, vec, slabs[:6])
        grad_rows, loss, d_in, d_out, d_cond, d_ada, d_io = head_pass(
            acts, vis_row, targets[image], noise, steps, embeds, slabs[8], slabs[6], slabs[7], w_in, w_out
        )
        head_grads = (d_ada, d_io, d_cond)
        if linked:
            embed_grad, sums = last_part(
                SLABS, chunks_of(), lax.axis_size("dev") // 2, head_grads, (d_in, d_out), grad_rows, vis_col, vis_row, vec,
                enc_kept, dec_kept, slabs[:6],
            )
        else:
            embed_grad, small, block_grads = backward_blocks(grad_rows, vis_col, vis_row, vec, enc_kept, dec_kept, slabs[:6])
            found = ([*block_grads, *head_grads], small[:5], d_in, d_out)
            totals = found if totals is None else jax.tree.map(jnp.add, totals, found)
        losses.append(loss[0, 0] / (counts[image].astype(jnp.float32) * (COPIES * CH)))
        acts_of.append(acts)
        embed_grads.append(embed_grad)
    if linked:
        small, *large = sums
        shares = unpack_gradients(large, *unpack_small(small))
    else:
        shares = sum_gradients(*totals)
    return (jnp.stack(losses), jnp.stack(acts_of), jnp.stack(embed_grads), *shares)


def solution(mesh):
    return jax.shard_map(
        per_device,
        mesh=mesh,
        in_specs=(
            P(("grp", "dev"), None, None),
            P(("grp", "dev"), None),
            P(("grp", "dev")),
            P(("grp", "dev"), None, None),
            P(("grp", "dev"), None, None, None),
            P(("grp", "dev"), None, None),
            P("dev"),
            P("dev", None),
            P("dev", None),
            P("dev"),
            P("dev", None),
            P("dev", None),
            P("dev"),
            P("dev", None),
            P("dev", None),
            P("dev"),
            P("dev", None),
            P("dev", None),
            P("dev"),
            P(None, "dev"),
            P("dev", None),
            P("dev", None),
            P("dev", None),
            P("dev", None),
            P("dev", None),
        ),
        out_specs=(
            P(("grp", "dev")),
            P(("grp", "dev"), None, None),
            P(("grp", "dev"), None, None),
            P("dev"),
            P("dev", None),
            P("dev", None),
            P("dev"),
            P("dev", None),
            P("dev", None),
            P("dev"),
            P("dev", None),
            P("dev", None),
            P("dev"),
            P("dev", None),
            P("dev", None),
            P("dev"),
            P(None, "dev"),
            P("dev", None),
            P("dev", None),
            P("dev", None),
            P("dev", None),
            P("dev", None),
        ),
        check_vma=False,
    )
```

```python
import functools
import math

import jax
import jax.numpy as jnp
from jax import lax
from jax.experimental import pallas as pl
from jax.experimental.pallas import tpu as pltpu
from jax.sharding import PartitionSpec as P

MESH = pl.DeviceIdType.MESH
SUM_VMEM = 60 * 1024 * 1024
LAST_VMEM = 62 * 1024 * 1024
HW = 1024
CH = 16
COPIES = 4
STEPS_T = 1000
BUFFER = 64
SPOTS = 80
EPSILON = 1e-06
NEG_FILL = -1e30


def matmul(left, right):
    return jnp.dot(left, right, preferred_element_type=jnp.float32)


def right_trans(left, right):
    return lax.dot_general(
        left, right, (((1,), (1,)), ((), ())), preferred_element_type=jnp.float32
    )


def norm_rows(values):
    centre = values - jnp.mean(values, axis=-1, keepdims=True)
    inv_std = lax.rsqrt(jnp.mean(centre * centre, axis=-1, keepdims=True) + EPSILON)
    return (centre * inv_std, inv_std)


def norm_back(grad, normed, inv_std):
    mean_grad = jnp.mean(grad, axis=-1, keepdims=True)
    mean_cross = jnp.mean(grad * normed, axis=-1, keepdims=True)
    return inv_std * (grad - mean_grad - normed * mean_cross)


def silu_slope(values):
    sigma = jax.nn.sigmoid(values)
    return sigma * (1.0 + values * (1.0 - sigma))


def noise_angle(steps):
    return (steps.astype(jnp.float32) / STEPS_T + 0.008) / 1.008 * (math.pi / 2)


ROOT_HALF = 1.0 / math.sqrt(2.0)
TILE = 512
STEP = 16


def rows_dot(left, right):
    return lax.dot_general(left, right, (((0,), (0,)), ((), ())), preferred_element_type=jnp.float32)


def loop(count, body):
    def turn(i, carry):
        body(i)
        return carry

    lax.fori_loop(0, count, turn, 0)


def at_step(i, size=STEP):
    return pl.ds(pl.multiple_of(i * size, size), size)


def at_col(i, size):
    return pl.ds(pl.multiple_of(i * size, 128), size)


def exact_dot(ones, values):
    high = values.astype(jnp.bfloat16)
    rest = values - high.astype(jnp.float32)
    middle = rest.astype(jnp.bfloat16)
    low = (rest - middle.astype(jnp.float32)).astype(jnp.bfloat16)
    return matmul(ones, high) + matmul(ones, middle) + matmul(ones, low)


def scale_norm(source, gain, target):
    normed, _ = norm_rows(source[...])
    target[...] = (normed * gain).astype(jnp.bfloat16)


def head_mask(half):
    lane = lax.broadcasted_iota(jnp.int32, (1, 128), 1)
    return (lane < 64) if half == 0 else (lane >= 64)


def keep_half(values, half):
    return jnp.where(head_mask(half), values, jnp.zeros((), values.dtype))


def probabilities(query, key, half, bias):
    scores = right_trans(keep_half(query, half), key) * 0.125
    if bias is not None:
        scores = jnp.where(bias, scores, NEG_FILL)
    grown = jnp.exp(scores - jnp.max(scores, axis=-1, keepdims=True))
    return grown / jnp.sum(grown, axis=-1, keepdims=True)


def forward_steps(width, stream, gain_one, gain_two, w_a, w_up, w_down, qkv, mixed, middle, acted, sloped, out, low, live=None):
    def project(j):
        cols = pl.ds(j * width, width)
        qkv[:, cols] = matmul(low[...], w_a[:, cols]).astype(jnp.bfloat16)

    def attend(pair):
        query, key, value = (qkv[:, pl.ds(pair * 128 + part * width, 128)] for part in range(3))
        parts = [
            matmul(probabilities(query, key, half, live).astype(jnp.bfloat16), value) for half in range(2)
        ]
        mixed[:, pl.ds(pair * 128, 128)] = jnp.where(head_mask(0), parts[0], parts[1]).astype(jnp.bfloat16)

    def mix():
        middle[...] = stream[...] + matmul(mixed[...], w_a[:, 3 * width :])
        scale_norm(middle, gain_two, low)

    def feed(j):
        cols = pl.ds(j * TILE, TILE)
        raised = matmul(low[...], w_up[:, cols])
        cumul = 0.5 + 0.5 * lax.erf(raised * ROOT_HALF)
        slope = cumul + raised * (jnp.exp(-0.5 * raised * raised) * (1.0 / math.sqrt(2.0 * math.pi)))
        sloped[:, cols] = slope.astype(jnp.bfloat16)
        acted[:, cols] = (raised * cumul).astype(jnp.bfloat16)
        out[...] = (middle[...] if j == 0 else out[...]) + matmul(acted[:, cols], w_down[cols, :])

    yield lambda: scale_norm(stream, gain_one, low)
    for j in range(3):
        yield functools.partial(project, j)
    for pair in range(width // 128):
        yield functools.partial(attend, pair)
    yield mix
    for j in range(w_up.shape[1] // TILE):
        yield functools.partial(feed, j)


def forward_block(*args):
    for step in forward_steps(*args):
        step()


def forward_kernel(*refs):
    (embedded, vis_col, vis_row, vec, e_a_hbm, e_u_hbm, e_d_hbm, d_a_hbm, d_u_hbm, d_d_hbm,
     e_in, e_qkv, e_mixed, e_mid, e_act, e_slope, d_in, d_qkv, d_mixed, d_mid, d_act, d_slope, acts,
     e_a, e_u, e_d, d_a, d_u, d_d, e_out, d_out, e_low, d_low, sems) = refs
    width = embedded.shape[1]
    loads = [
        pltpu.make_async_copy(a, b, sems.at[i])
        for i, (a, b) in enumerate(
            [(e_a_hbm, e_a), (e_u_hbm, e_u), (e_d_hbm, e_d), (d_a_hbm, d_a), (d_u_hbm, d_u), (d_d_hbm, d_d)]
        )
    ]
    for load in loads:
        load.start()
    encode(embedded, vis_col, vec, e_in)
    for load in loads[:3]:
        load.wait()
    live = live_keys(vis_row)
    forward_block(width, e_in, vec[0:1, :], vec[1:2, :], e_a, e_u, e_d, e_qkv, e_mixed, e_mid, e_act, e_slope, e_out, e_low, live)
    spread_rows(vis_row, e_out, vec, d_in)
    for load in loads[3:]:
        load.wait()
    forward_block(width, d_in, vec[2:3, :], vec[3:4, :], d_a, d_u, d_d, d_qkv, d_mixed, d_mid, d_act, d_slope, d_out, d_low)
    acts[...] = d_out[...].astype(jnp.bfloat16)


def token_hot(vis_col, count):
    return (lax.broadcasted_iota(jnp.int32, (vis_col.shape[0], count), 1) == vis_col[...]).astype(jnp.bfloat16)


def spot_hot(vis_row, count):
    return (lax.broadcasted_iota(jnp.int32, (count, vis_row.shape[1]), 0) == vis_row[...]).astype(jnp.bfloat16)


def live_keys(vis_row):
    ones = jnp.ones((1, BUFFER), jnp.int32)
    return jnp.concatenate([ones, (vis_row[...] >= 0).astype(jnp.int32)], axis=1) > 0


def encode(embedded, vis_col, vec, target):
    tokens = embedded.shape[0] - BUFFER
    target[:BUFFER, :] = embedded[:BUFFER, :].astype(jnp.float32)
    target[BUFFER:, :] = matmul(token_hot(vis_col, tokens), embedded[BUFFER:, :])


def spread_rows(vis_row, enc_out, vec, target):
    tokens = target.shape[0] - BUFFER
    hot = spot_hot(vis_row, tokens)
    masked = 1.0 - jnp.sum(hot.astype(jnp.float32), axis=1, keepdims=True)
    target[:BUFFER, :] = enc_out[:BUFFER, :]
    target[BUFFER:, :] = exact_dot(hot, enc_out[BUFFER:, :]) + masked * vec[4:5, :]


def forward_blocks(embedded, vis_col, vis_row, vec, weights):
    tokens, width = embedded.shape
    inner = weights[1].shape[1]
    rows = BUFFER + vis_col.shape[0]
    f32, half = jnp.float32, jnp.bfloat16

    def kept(count):
        return [
            jax.ShapeDtypeStruct((count, width), f32),
            jax.ShapeDtypeStruct((count, 3 * width), half),
            jax.ShapeDtypeStruct((count, width), half),
            jax.ShapeDtypeStruct((count, width), f32),
            jax.ShapeDtypeStruct((count, inner), half),
            jax.ShapeDtypeStruct((count, inner), half),
        ]

    outs = kept(rows) + kept(tokens) + [jax.ShapeDtypeStruct((tokens, width), half)]
    whole = pl.BlockSpec(memory_space=pltpu.VMEM)
    found = pl.pallas_call(
        forward_kernel,
        out_shape=outs,
        in_specs=[whole] * 4 + [pl.BlockSpec(memory_space=pl.ANY)] * 6,
        out_specs=[whole] * len(outs),
        scratch_shapes=[pltpu.VMEM(w.shape, half) for w in weights]
        + [
            pltpu.VMEM((rows, width), f32),
            pltpu.VMEM((tokens, width), f32),
            pltpu.VMEM((rows, width), half),
            pltpu.VMEM((tokens, width), half),
            pltpu.SemaphoreType.DMA((6,)),
        ],
        compiler_params=pltpu.CompilerParams(vmem_limit_bytes=SUM_VMEM),
        name="forward_blocks",
    )(embedded, vis_col, vis_row, vec, *weights)
    return found[:6], found[6:12], found[12]


def norm_back_into(grads, source, gain, add, target, gain_grad):
    normed, inv_std = norm_rows(source[...])
    grad = grads[...]
    gain_grad[...] = jnp.broadcast_to(jnp.sum(grad * normed, axis=0, keepdims=True), gain_grad.shape)
    target[...] = add[...] + norm_back(grad * gain, normed, inv_std)


class Tiles:
    def __init__(self, slots, sems):
        self.slots, self.sems = slots, sems

    def put(self, i, value, target):
        slot = i % 2 if isinstance(i, int) else lax.rem(i, 2)
        copy = pltpu.make_async_copy(self.slots.at[slot], target, self.sems.at[slot])

        @pl.when(i >= 2)
        def _():
            copy.wait()

        self.slots[slot] = value.astype(jnp.bfloat16)
        copy.start()

    def flush(self, like):
        for slot in range(2):
            pltpu.make_async_copy(self.slots.at[slot], like, self.sems.at[slot]).wait()


def backward_block(width, grad, stream, gain_one, gain_two, w_a, w_up, w_down, qkv, mixed, middle, acted, sloped,
                   d_a, d_up, d_down, d_one, d_two, grad_low, low, grad_qkv, acc, grad_mid, out, tiles, live=None):
    rows = grad.shape[0]
    wide, narrow, square = tiles
    grad_low[...] = grad[...].astype(jnp.bfloat16)
    scale_norm(middle, gain_two, low)
    acc[...] = jnp.zeros_like(acc)
    count = w_up.shape[1] // TILE

    def feed(j):
        act, slope = acted[:, at_col(j, TILE)], sloped[:, at_col(j, TILE)].astype(jnp.float32)
        down = w_down[at_step(j, TILE), :]
        narrow.put(j, rows_dot(act, grad_low[...]), d_down.at[at_step(j, TILE), :])
        grad_up = (right_trans(grad_low[...], down) * slope).astype(jnp.bfloat16)
        wide.put(j, rows_dot(low[...], grad_up), d_up.at[:, at_col(j, TILE)])
        acc[...] += right_trans(grad_up, w_up[:, at_col(j, TILE)])

    loop(count, feed)
    narrow.flush(d_down.at[pl.ds(0, TILE), :])
    wide.flush(d_up.at[:, pl.ds(0, TILE)])
    norm_back_into(acc, middle, gain_two, grad, grad_mid, d_two)
    grad_low[...] = grad_mid[...].astype(jnp.bfloat16)
    for j in range(width // 256):
        square.put(j, rows_dot(mixed[...], grad_low[:, pl.ds(j * 256, 256)]), d_a.at[:, pl.ds(3 * width + j * 256, 256)])
    for j in range(width // 256):
        low[:, pl.ds(j * 256, 256)] = right_trans(grad_low[...], w_a[pl.ds(j * 256, 256), pl.ds(3 * width, width)]).astype(jnp.bfloat16)

    def attend(pair):
        where = [pl.ds(pl.multiple_of(pair * 128 + part * width, 128), 128) for part in range(3)]
        query, key, value = (qkv[:, at] for at in where)
        grad_mixed = low[:, at_col(pair, 128)]
        found = []
        for half in range(2):
            probs = probabilities(query, key, half, live)
            grad_half = keep_half(grad_mixed, half)
            grad_probs = right_trans(grad_half, value)
            dots = jnp.sum(grad_probs * probs, axis=-1, keepdims=True)
            grad_scores = (probs * (grad_probs - dots) * 0.125).astype(jnp.bfloat16)
            found.append(
                (matmul(grad_scores, key), rows_dot(grad_scores, query), rows_dot(probs.astype(jnp.bfloat16), grad_half))
            )
        for part in range(3):
            both = jnp.where(head_mask(0), found[0][part], found[1][part])
            grad_qkv[:, where[part]] = both.astype(jnp.bfloat16)

    loop(width // 128, attend)
    scale_norm(stream, gain_one, low)
    acc[...] = jnp.zeros_like(acc)
    first = width // 256

    def project(j):
        piece = grad_qkv[:, at_col(j, 256)]
        square.put(j + first, rows_dot(low[...], piece), d_a.at[:, at_col(j, 256)])
        acc[...] += right_trans(piece, w_a[:, at_col(j, 256)])

    loop(3 * width // 256, project)
    square.flush(d_a.at[:, pl.ds(0, 256)])
    norm_back_into(acc, stream, gain_one, grad_mid, out, d_one)


def backward_kernel(*refs):
    (grad_rows, vis_col, vis_row, vec, e_in, e_qkv, e_mixed, e_mid, e_act, e_slope, d_in, d_qkv, d_mixed, d_mid, d_act, d_slope,
     e_a_hbm, e_u_hbm, e_d_hbm, d_a_hbm, d_u_hbm, d_d_hbm,
     embed_grad, small, de_a, de_u, de_d, dd_a, dd_u, dd_d,
     e_a, e_u, e_d, d_a, d_u, d_d, d_grad, e_grad, low_a, low_b, grad_qkv, acc, grad_mid,
     wide, narrow, square, load_sems, tile_sems) = refs
    tokens, width = d_in.shape
    rows = e_in.shape[0]
    loads = [
        pltpu.make_async_copy(a, b, load_sems.at[i])
        for i, (a, b) in enumerate(
            [(d_d_hbm, d_d), (d_u_hbm, d_u), (d_a_hbm, d_a), (e_d_hbm, e_d), (e_u_hbm, e_u), (e_a_hbm, e_a)]
        )
    ]
    for load in loads:
        load.start()
    tiles = (Tiles(wide, tile_sems.at[0]), Tiles(narrow, tile_sems.at[1]), Tiles(square, tile_sems.at[2]))
    d_grad[:BUFFER, :] = jnp.zeros((BUFFER, width), jnp.float32)
    d_grad[BUFFER:, :] = grad_rows[...].astype(jnp.float32)
    for load in loads[:3]:
        load.wait()
    backward_block(width, d_grad, d_in, vec[2:3, :], vec[3:4, :], d_a, d_u, d_d, d_qkv, d_mixed, d_mid, d_act, d_slope,
                   dd_a, dd_u, dd_d, small.at[2:3, :], small.at[3:4, :], low_a, low_b, grad_qkv, acc, grad_mid, d_grad, tiles)
    hot = spot_hot(vis_row, tokens - BUFFER)
    masked = 1.0 - jnp.sum(hot.astype(jnp.float32), axis=1, keepdims=True)
    small[4:5, :] = jnp.sum(d_grad[BUFFER:, :] * masked, axis=0, keepdims=True)
    e_grad[:BUFFER, :] = d_grad[:BUFFER, :]
    e_grad[BUFFER:, :] = exact_dot(token_hot(vis_col, tokens - BUFFER), d_grad[BUFFER:, :])
    for load in loads[3:]:
        load.wait()
    part = pl.ds(0, rows)
    backward_block(width, e_grad, e_in, vec[0:1, :], vec[1:2, :], e_a, e_u, e_d, e_qkv, e_mixed, e_mid, e_act, e_slope,
                   de_a, de_u, de_d, small.at[0:1, :], small.at[1:2, :], low_a.at[part], low_b.at[part],
                   grad_qkv.at[part], acc.at[part], grad_mid.at[part], e_grad, tiles, live_keys(vis_row))
    embed_grad[:BUFFER, :] = e_grad[:BUFFER, :]
    embed_grad[BUFFER:, :] = exact_dot(hot, e_grad[BUFFER:, :])


def backward_blocks(grad_rows, vis_col, vis_row, vec, enc_kept, dec_kept, weights):
    tokens, width = dec_kept[0].shape
    rows = enc_kept[0].shape[0]
    f32, half = jnp.float32, jnp.bfloat16
    whole, anywhere = pl.BlockSpec(memory_space=pltpu.VMEM), pl.BlockSpec(memory_space=pl.ANY)
    outs = [jax.ShapeDtypeStruct((tokens, width), f32), jax.ShapeDtypeStruct((8, width), f32)]
    outs += [jax.ShapeDtypeStruct(w.shape, half) for w in weights]
    found = pl.pallas_call(
        backward_kernel,
        out_shape=outs,
        in_specs=[whole] * 16 + [anywhere] * 6,
        out_specs=[whole] * 2 + [anywhere] * 6,
        scratch_shapes=[pltpu.VMEM(w.shape, half) for w in weights]
        + [
            pltpu.VMEM((tokens, width), f32),
            pltpu.VMEM((rows, width), f32),
            pltpu.VMEM((tokens, width), half),
            pltpu.VMEM((tokens, width), half),
            pltpu.VMEM((tokens, 3 * width), half),
            pltpu.VMEM((tokens, width), f32),
            pltpu.VMEM((tokens, width), f32),
            pltpu.VMEM((2, width, TILE), half),
            pltpu.VMEM((2, TILE, width), half),
            pltpu.VMEM((2, width, 256), half),
            pltpu.SemaphoreType.DMA((6,)),
            pltpu.SemaphoreType.DMA((3, 2)),
        ],
        compiler_params=pltpu.CompilerParams(vmem_limit_bytes=SUM_VMEM),
        name="backward_blocks",
    )(grad_rows, vis_col, vis_row, vec, *enc_kept, *dec_kept, *weights)
    return found[0], found[1], found[2:]


def embed_steps(steps, freqs, target):
    half = freqs.shape[1]

    def body(i):
        phase = steps[at_step(i), :].astype(jnp.float32) * freqs[...]
        target[at_step(i), :half] = jnp.cos(phase)
        target[at_step(i), half:] = jnp.sin(phase)

    loop(steps.shape[0] // STEP, body)


ROWS = 256


def at_rows(i):
    return pl.ds(pl.multiple_of(i * ROWS, 16), ROWS)


def head_kernel(*refs):
    (acts, vis_row, targets, noise, steps, embeds, w_cond_hbm, w_ada_hbm, w_io_hbm, w_in, w_out,
     grad_rows, losses, d_in, d_out, d_cond, d_ada, d_io,
     w_cond, w_ada, w_io, cond, cond_full, mod, hidden, normed_in, inv_in, inner, branch, normed_out, inv_out,
     work, grad_two, grad_sum, noisy, cond_act, mlp_in, inner_act, final_in, grad_pred, grad_branch, grad_inner,
     grad_hidden, grad_mod, wide, load_sems, tile_sems) = refs
    tokens, wide_cols = targets.shape[0], w_in.shape[1]
    loads = [
        pltpu.make_async_copy(a, b, load_sems.at[i])
        for i, (a, b) in enumerate([(w_cond_hbm, w_cond), (w_ada_hbm, w_ada), (w_io_hbm, w_io)])
    ]
    for load in loads:
        load.start()
    hot = spot_hot(vis_row, tokens)
    masked = jnp.sum(hot.astype(jnp.float32), axis=1, keepdims=True) < 0.5
    loads[0].wait()
    cond[...] = matmul(acts[BUFFER:, :], w_cond[...])
    loads[1].wait()
    loads[2].wait()
    grad_sum[...] = jnp.zeros_like(grad_sum)
    columns = wide_cols // 256

    def copy_pass(c, loss):
        rows = pl.ds(pl.multiple_of(c * tokens, 16), tokens)

        def at(i):
            return pl.ds(pl.multiple_of(c * tokens + i * ROWS, 16), ROWS)

        angle = noise_angle(steps[rows, :])
        noise_vals = noise[rows, :].astype(jnp.float32)
        noisy[rows, :] = (jnp.cos(angle) * targets[...] + jnp.sin(angle) * noise_vals).astype(jnp.bfloat16)

        def condition(i):
            full = cond[at_rows(i), :] + embeds[at(i), :]
            cond_full[at_rows(i), :] = full
            cond_act[at(i), :] = (full * jax.nn.sigmoid(full)).astype(jnp.bfloat16)

        loop(tokens // ROWS, condition)

        mod[...] = matmul(cond_act[rows, :], w_ada[...])
        hidden[...] = matmul(noisy[rows, :], w_in[...])

        def enter(i):
            normed, inv_std = norm_rows(hidden[at_rows(i), :])
            normed_in[at_rows(i), :] = normed
            inv_in[at_rows(i), :] = inv_std
            shift, scale = mod[at_rows(i), :wide_cols], mod[at_rows(i), wide_cols : 2 * wide_cols]
            mlp_in[at(i), :] = (normed * (1.0 + scale) + shift).astype(jnp.bfloat16)

        loop(tokens // ROWS, enter)

        inner[...] = matmul(mlp_in[rows, :], w_io[:, :wide_cols])

        def activate(i):
            values = inner[at_rows(i), :]
            inner_act[at(i), :] = (values * jax.nn.sigmoid(values)).astype(jnp.bfloat16)

        loop(tokens // ROWS, activate)

        branch[...] = matmul(inner_act[rows, :], w_io[:, wide_cols:])

        def leave(i):
            gate = mod[at_rows(i), 2 * wide_cols :]
            normed, inv_std = norm_rows(hidden[at_rows(i), :] + gate * branch[at_rows(i), :])
            normed_out[at_rows(i), :] = normed
            inv_out[at_rows(i), :] = inv_std
            final_in[at(i), :] = normed.astype(jnp.bfloat16)

        loop(tokens // ROWS, leave)
        error = right_trans(final_in[rows, :], w_out[...]) - noise_vals
        loss = loss + jnp.sum(error * error, axis=1, keepdims=True)
        low_error = jnp.where(masked, error * (2.0 / COPIES), 0.0).astype(jnp.bfloat16)
        grad_pred[rows, :] = low_error
        work[...] = matmul(low_error, w_out[...])

        def back_out(i):
            gate = mod[at_rows(i), 2 * wide_cols :]
            grad = norm_back(work[at_rows(i), :], normed_out[at_rows(i), :], inv_out[at_rows(i), :])
            grad_two[at_rows(i), :] = grad
            grad_branch[at(i), :] = (grad * gate).astype(jnp.bfloat16)
            grad_mod[at(i), 2 * wide_cols :] = (grad * branch[at_rows(i), :]).astype(jnp.bfloat16)

        loop(tokens // ROWS, back_out)

        work[...] = right_trans(grad_branch[rows, :], w_io[:, wide_cols:])

        def back_act(i):
            grad_inner[at(i), :] = (work[at_rows(i), :] * silu_slope(inner[at_rows(i), :])).astype(jnp.bfloat16)

        loop(tokens // ROWS, back_act)

        work[...] = right_trans(grad_inner[rows, :], w_io[:, :wide_cols])

        def back_in(i):
            grad, normed = work[at_rows(i), :], normed_in[at_rows(i), :]
            scale = mod[at_rows(i), wide_cols : 2 * wide_cols]
            grad_mod[at(i), :wide_cols] = grad.astype(jnp.bfloat16)
            grad_mod[at(i), wide_cols : 2 * wide_cols] = (grad * normed).astype(jnp.bfloat16)
            total = grad_two[at_rows(i), :] + norm_back(grad * (1.0 + scale), normed, inv_in[at_rows(i), :])
            grad_hidden[at(i), :] = total.astype(jnp.bfloat16)

        loop(tokens // ROWS, back_in)

        work[...] = right_trans(grad_mod[rows, :], w_ada[...])

        def back_cond(i):
            grad_sum[at_rows(i), :] += work[at_rows(i), :] * silu_slope(cond_full[at_rows(i), :])

        loop(tokens // ROWS, back_cond)
        return loss

    loss = lax.fori_loop(0, COPIES, copy_pass, jnp.zeros((tokens, 1), jnp.float32))
    loss = jnp.where(masked, loss.astype(jnp.bfloat16).astype(jnp.float32), 0.0)
    losses[...] = jnp.broadcast_to(jnp.sum(loss, axis=0, keepdims=True), losses.shape)
    grad_cond = grad_sum[...].astype(jnp.bfloat16)
    grad_rows[...] = right_trans(grad_cond, w_cond[...]).astype(jnp.bfloat16)
    tiles = Tiles(wide, tile_sems)

    def out_ada(j):
        tiles.put(j, rows_dot(cond_act[...], grad_mod[:, at_col(j, TILE)]), d_ada.at[:, at_col(j, TILE)])

    count = 3 * wide_cols // TILE
    loop(count, out_ada)
    half = wide_cols // TILE

    def out_inner(j):
        tiles.put(j + count, rows_dot(mlp_in[...], grad_inner[:, at_col(j, TILE)]), d_io.at[:, at_col(j, TILE)])

    def out_outer(j):
        tiles.put(j + count + half, rows_dot(inner_act[...], grad_branch[:, at_col(j, TILE)]), d_io.at[:, at_col(j + half, TILE)])

    loop(half, out_inner)
    loop(half, out_outer)
    d_cond[...] = rows_dot(acts[BUFFER:, :], grad_cond).astype(jnp.bfloat16)
    d_in[...] = rows_dot(noisy[...], grad_hidden[...])
    d_out[...] = rows_dot(grad_pred[...], final_in[...])
    tiles.flush(d_ada.at[:, pl.ds(0, TILE)])


def head_pass(acts, vis_row, targets, noise, steps, embeds, w_cond, w_ada, w_io, w_in, w_out):
    tokens, width = targets.shape[0], acts.shape[1]
    wide, flat = w_in.shape[1], noise.shape[0]
    f32, half = jnp.float32, jnp.bfloat16
    whole, anywhere = pl.BlockSpec(memory_space=pltpu.VMEM), pl.BlockSpec(memory_space=pl.ANY)
    shape = jax.ShapeDtypeStruct
    outs = [
        shape((tokens, width), half), shape((8, 128), f32), shape((CH, wide), f32), shape((CH, wide), f32),
        shape(w_cond.shape, half), shape(w_ada.shape, half), shape(w_io.shape, half),
    ]
    tile = lambda cols, kind=f32: pltpu.VMEM((tokens, cols), kind)
    long = lambda cols: pltpu.VMEM((flat, cols), half)
    return pl.pallas_call(
        head_kernel,
        out_shape=outs,
        in_specs=[whole] * 6 + [anywhere] * 3 + [whole] * 2,
        out_specs=[whole] * 5 + [anywhere] * 2,
        scratch_shapes=[pltpu.VMEM(w.shape, half) for w in (w_cond, w_ada, w_io)]
        + [
            tile(wide), tile(wide), tile(3 * wide), tile(wide), tile(wide), tile(1), tile(wide), tile(wide), tile(wide), tile(1),
            tile(wide), tile(wide), tile(wide),
            long(CH), long(wide), long(wide), long(wide), long(wide), long(CH), long(wide), long(wide), long(wide), long(3 * wide),
            pltpu.VMEM((2, wide, TILE), half),
            pltpu.SemaphoreType.DMA((3,)),
            pltpu.SemaphoreType.DMA((2,)),
        ],
        compiler_params=pltpu.CompilerParams(vmem_limit_bytes=SUM_VMEM),
        name="head_pass",
    )(acts, vis_row, targets, noise, steps, embeds, w_cond, w_ada, w_io, w_in, w_out)


class Slab:
    def __init__(self, rows, cols, by_rows, direct=False):
        self.rows, self.cols, self.by_rows, self.direct = rows, cols, by_rows, direct
        self.piece = (rows // 4, cols) if by_rows else (rows, cols // 4)

    def spot(self, shard, quarter, half=None):
        piece_rows, piece_cols = self.piece
        row = shard * self.rows
        if self.by_rows:
            row = row + quarter * piece_rows
        height = piece_rows
        if half is not None:
            height = piece_rows // 2
            row = row + half * height
        col = 0 if self.by_rows else quarter * piece_cols
        return (pl.ds(aligned(row, 16), height), pl.ds(aligned(col, 128), piece_cols))

    def shard(self, shard):
        return (pl.ds(aligned(shard * self.rows, 16), self.rows), pl.ds(0, self.cols))

    def within(self, quarter):
        return self.spot(0, quarter)


def aligned(value, multiple):
    return value if isinstance(value, int) else pl.multiple_of(value, multiple)


def place(depth):
    group, device = lax.axis_index("grp"), lax.axis_index("dev")
    level, core = device // 2, device % 2
    flip = lambda bit: group + (1 << bit) * (1 - 2 * ((group // (1 << bit)) % 2))
    return group, level, core, flip


def greet(peers):
    barrier = pltpu.get_barrier_semaphore()
    for peer in peers:
        pl.semaphore_signal(barrier, inc=1, device_id=peer, device_id_type=MESH)
    pl.semaphore_wait(barrier, len(peers))


def gather_kernel(slabs, depth, *refs):
    count = len(slabs)
    mine, whole = refs[:count], refs[count : 2 * count]
    sent, got, own_sent, own_got, own_copy = refs[2 * count :]
    group, level, core, flip = place(depth)
    x_peer, y_peer = (flip(0), 2 * level + core), (flip(1), 2 * level + core)
    partner = (group, 2 * level + 1 - core)

    def level_at(step):
        return lax.rem(level + step + depth, depth)

    z_peers = [(group, 2 * level_at(step) + core) for step in range(1, depth)]
    greet([x_peer, y_peer, partner] + z_peers)

    def move(kind, item, source, target, device):
        return pltpu.make_async_remote_copy(
            src_ref=source,
            dst_ref=target,
            send_sem=sent.at[kind, item],
            recv_sem=got.at[kind, item],
            device_id=device,
            device_id_type=MESH,
        )

    Z, X, Y, XH, YH, CORE = range(6)
    items = [(k, step) for k in range(count) for step in range(1, depth)]

    def by_z(item):
        k, step = items[item]
        slab = slabs[k]
        target = whole[k].at[slab.spot(2 * level + core, group)]
        return move(Z, item, mine[k].at[slab.within(group)], target, z_peers[step - 1])

    def shard_of(item):
        return 2 * level_at(-items[item][1]) + core

    def forward(kind, item, quarter, half, device):
        k = items[item][0]
        here = whole[k].at[slabs[k].spot(shard_of(item), quarter, half)]
        return move(kind, item, here, here, device)

    def core_copy(item, core_of):
        k, step = items[item]
        here = whole[k].at[slabs[k].shard(2 * level_at(-step) + core_of)]
        return move(CORE, item, here, here, partner)

    own = []
    for k, slab in enumerate(slabs):
        for step in range(1, depth):
            by_z(k * (depth - 1) + step - 1).start()
        target = whole[k].at[slab.shard(2 * level + core)]
        keep = pltpu.make_async_copy(mine[k], target, own_copy.at[k])
        keep.start()
        share = pltpu.make_async_remote_copy(
            src_ref=mine[k],
            dst_ref=target,
            send_sem=own_sent.at[k],
            recv_sem=own_got.at[k],
            device_id=partner,
            device_id_type=MESH,
        )
        share.start()
        own.append((keep, share))

    total = len(items)
    for turn in range(total + 2):
        if turn < total:
            k = items[turn][0]
            here = whole[k].at[slabs[k].spot(shard_of(turn), group)]
            move(Z, turn, here, here, x_peer).wait_recv()
            forward(X, turn, group, None, x_peer).start()
            forward(Y, turn, group, None, y_peer).start()
        item = turn - 1
        if 0 <= item < total:
            forward(X, item, flip(0), None, x_peer).wait_recv()
            forward(YH, item, flip(0), 0, y_peer).start()
            forward(Y, item, flip(1), None, y_peer).wait_recv()
            forward(XH, item, flip(1), 1, x_peer).start()
        item = turn - 2
        if 0 <= item < total:
            far = 3 - group
            forward(YH, item, far, 0, y_peer).wait_recv()
            forward(XH, item, far, 1, x_peer).wait_recv()
            core_copy(item, core).start()
    for item in range(total):
        by_z(item).wait_send()
        forward(X, item, group, None, x_peer).wait_send()
        forward(Y, item, group, None, y_peer).wait_send()
        forward(YH, item, flip(0), 0, y_peer).wait_send()
        forward(XH, item, flip(1), 1, x_peer).wait_send()
        core_copy(item, core).wait_send()
        core_copy(item, 1 - core).wait_recv()
    for keep, share in own:
        keep.wait()
        share.wait()


def gather_slabs(shards, slabs, depth):
    count, items = len(slabs), len(slabs) * (depth - 1)
    return pl.pallas_call(
        functools.partial(gather_kernel, slabs, depth),
        out_shape=[
            jax.ShapeDtypeStruct((2 * depth * s.rows, s.cols), jnp.bfloat16) for s in slabs
        ],
        in_specs=[pl.BlockSpec(memory_space=pl.ANY)] * count,
        out_specs=[pl.BlockSpec(memory_space=pl.ANY)] * count,
        scratch_shapes=[
            pltpu.SemaphoreType.DMA((6, items)),
            pltpu.SemaphoreType.DMA((6, items)),
            pltpu.SemaphoreType.DMA((count,)),
            pltpu.SemaphoreType.DMA((count,)),
            pltpu.SemaphoreType.DMA((count,)),
        ],
        compiler_params=pltpu.CompilerParams(collective_id=0, has_side_effects=True),
        name="gather_weights",
    )(*shards)


def sum_kernel(slabs, orders, depth, *refs):
    count = len(slabs)
    grads, outs = refs[:count], refs[count : 2 * count]
    rest = refs[2 * count :]
    take = lambda: (rest[:count], rest[count:])
    held, rest = take()
    from_first, rest = take()
    from_second, rest = take()
    from_level, rest = take()
    result, rest = take()
    stage, rest = take()
    stage_sem, out_sem, core_sent, core_got, sent, got, z_sent, z_got = rest
    group, level, core, flip = place(depth)
    me = 2 * level + core
    partner = (group, 2 * level + 1 - core)
    bit = lambda b: (group // (1 << b)) % 2

    def level_at(step):
        return lax.rem(level + step + depth, depth)

    z_peers = [(group, 2 * level_at(step) + core) for step in range(1, depth)]
    greet([(flip(0), me), (flip(1), me), partner] + z_peers)

    def move(pair, k, kind, source, target, device):
        send, receive = pair
        return pltpu.make_async_remote_copy(
            src_ref=source,
            dst_ref=target,
            send_sem=send.at[kind, k],
            recv_sem=receive.at[kind, k],
            device_id=device,
            device_id_type=MESH,
        )

    def core_move(k, lev):
        source = grads[k].at[slabs[k].shard(2 * lev + 1 - core)]
        return move((core_sent, core_got), k, lev, source, held[k].at[lev], partner)

    def rows_loop(height, body):
        step = 32 if height % 32 == 0 else 16

        def turn(i, carry):
            body(pl.ds(aligned(i * step, 16), step))
            return carry

        lax.fori_loop(0, height // step, turn, 0)

    def shifted(rows, by):
        return pl.ds(aligned(rows.start + by, 16), rows.size)

    def first_bit(k):
        return 1 if orders[k] == "yx" else 0

    def quarter(k, first, second):
        b = first_bit(k)
        return first * (1 << b) + second * (1 << (1 - b))

    def first_move(k, j):
        b = first_bit(k)
        where = slabs[k].within(quarter(k, 1 - bit(b), j))
        source = held[k].at[(level,) + where] if orders[k][0] == "z" else held[k].at[(slice(None),) + where]
        return move((sent, got), k, j, source, from_first[k].at[j], (flip(b), me))

    def second_move(k):
        b = first_bit(k)
        where = slabs[k].within(quarter(k, bit(b), 1 - bit(1 - b)))
        source = held[k].at[(level,) + where] if orders[k][0] == "z" else held[k].at[(slice(None),) + where]
        return move((sent, got), k, 2, source, from_second[k], (flip(1 - b), me))

    def level_move(k, step):
        lev = level_at(step)
        source = held[k].at[lev] if orders[k][0] == "z" else held[k].at[(lev,) + slabs[k].within(group)]
        return move((z_sent, z_got), k, step - 1, source, from_level[k].at[step - 1], z_peers[step - 1])

    def spread_second(k, whose):
        here = result[k].at[slabs[k].within(whose)]
        return move((sent, got), k, 3, here, here, (flip(1 - first_bit(k)), me))

    def spread_first(k, j, whose):
        here = result[k].at[slabs[k].within(whose)]
        return move((sent, got), k, 4 + j, here, here, (flip(first_bit(k)), me))

    def out_copy(k):
        return pltpu.make_async_copy(result[k], outs[k], out_sem.at[k])

    def stage_copy(k, lev):
        source = grads[k].at[slabs[k].shard(2 * lev + core)]
        return pltpu.make_async_copy(source, stage[k].at[lev % 2], stage_sem.at[k, lev % 2])

    def add_core(k):
        slab = slabs[k]
        stage_copy(k, 0).start()
        for lev in range(depth):
            if lev + 1 < depth:
                stage_copy(k, lev + 1).start()
            core_move(k, lev).wait_recv()
            stage_copy(k, lev).wait()

            def body(rows):
                total = held[k][lev, rows, :].astype(jnp.float32) + stage[k][lev % 2, rows, :].astype(jnp.float32)
                held[k][lev, rows, :] = total.astype(jnp.bfloat16)

            rows_loop(slab.rows, body)

    def levels_of(k):
        return [level] if orders[k][0] == "z" else list(range(depth))

    def add_first(k):
        slab = slabs[k]
        for j in range(2):
            first_move(k, j).wait_recv()
            rows_of, cols = slab.within(quarter(k, bit(first_bit(k)), j))
            for lev in levels_of(k):

                def body(rows):
                    at = (lev, shifted(rows, rows_of.start), cols)
                    extra = from_first[k][j, rows, :] if orders[k][0] == "z" else from_first[k][j, lev, rows, :]
                    held[k][at] = (held[k][at].astype(jnp.float32) + extra.astype(jnp.float32)).astype(jnp.bfloat16)

                rows_loop(slab.piece[0], body)

    def add_second(k):
        slab = slabs[k]
        second_move(k).wait_recv()
        rows_of, cols = slab.within(group)
        for lev in levels_of(k):

            def body(rows):
                at = (lev, shifted(rows, rows_of.start), cols)
                extra = from_second[k][rows, :] if orders[k][0] == "z" else from_second[k][lev, rows, :]
                total = held[k][at].astype(jnp.float32) + extra.astype(jnp.float32)
                target = result[k].at[shifted(rows, rows_of.start), cols] if orders[k][0] == "z" else held[k].at[at]
                target[...] = total.astype(jnp.bfloat16)

            rows_loop(slab.piece[0], body)

    def add_level(k):
        slab = slabs[k]
        for step in range(1, depth):
            level_move(k, step).wait_recv()
        if orders[k][0] == "z":

            def body(rows):
                total = held[k][level, rows, :].astype(jnp.float32)
                for step in range(depth - 1):
                    total = total + from_level[k][step, rows, :].astype(jnp.float32)
                held[k][level, rows, :] = total.astype(jnp.bfloat16)

            rows_loop(slab.rows, body)
            return
        rows_of, cols = slab.within(group)

        def body(rows):
            at = (shifted(rows, rows_of.start), cols)
            total = held[k][(level,) + at].astype(jnp.float32)
            for step in range(depth - 1):
                total = total + from_level[k][step, rows, :].astype(jnp.float32)
            result[k][at] = total.astype(jnp.bfloat16)

        rows_loop(slab.piece[0], body)

    def begin_core(k):
        for lev in range(depth):
            core_move(k, lev).start()

    def begin_first(k):
        first_move(k, 0).start()
        first_move(k, 1).start()

    def begin_level(k):
        for step in range(1, depth):
            level_move(k, step).start()

    def end_spread_second(k):
        spread_second(k, flip(1 - first_bit(k))).wait_recv()
        spread_first(k, 0, group).start()
        spread_first(k, 1, flip(1 - first_bit(k))).start()

    def end_spread_first(k):
        b = first_bit(k)
        spread_first(k, 0, flip(b)).wait_recv()
        spread_first(k, 1, 3 - group).wait_recv()
        out_copy(k).start()

    def steps(k):
        if orders[k][0] == "z":
            return [
                lambda: (add_core(k), begin_level(k)),
                lambda: (add_level(k), begin_first(k)),
                lambda: (add_first(k), second_move(k).start()),
                lambda: (add_second(k), spread_second(k, group).start()),
                lambda: end_spread_second(k),
                lambda: end_spread_first(k),
            ]
        return [
            lambda: (add_core(k), begin_first(k)),
            lambda: (add_first(k), second_move(k).start()),
            lambda: (add_second(k), begin_level(k)),
            lambda: (add_level(k), spread_second(k, group).start()),
            lambda: end_spread_second(k),
            lambda: end_spread_first(k),
        ]

    plans = [steps(k) for k in range(count)]
    begin_core(0)
    for turn in range(count + 5):
        if turn + 1 < count:
            begin_core(turn + 1)
        for place_in in range(6):
            k = turn - place_in
            if 0 <= k < count:
                plans[k][place_in]()
    for k in range(count):
        for lev in range(depth):
            core_move(k, lev).wait_send()
        first_move(k, 0).wait_send()
        first_move(k, 1).wait_send()
        second_move(k).wait_send()
        for step in range(1, depth):
            level_move(k, step).wait_send()
        spread_second(k, group).wait_send()
        spread_first(k, 0, group).wait_send()
        spread_first(k, 1, flip(1 - first_bit(k))).wait_send()
        out_copy(k).wait()


def sum_slabs(grads, slabs, orders, depth):
    count = len(slabs)
    half = jnp.bfloat16
    held, first, second, lev, result, stage = [], [], [], [], [], []
    for slab, order in zip(slabs, orders, strict=True):
        shard = (slab.rows, slab.cols)
        held.append(pltpu.VMEM((depth,) + shard, half))
        result.append(pltpu.VMEM(shard, half))
        stage.append(pltpu.VMEM((2,) + shard, half))
        if order[0] == "z":
            first.append(pltpu.VMEM((2,) + slab.piece, half))
            second.append(pltpu.VMEM(slab.piece, half))
            lev.append(pltpu.VMEM((depth - 1,) + shard, half))
        else:
            first.append(pltpu.VMEM((2, depth) + slab.piece, half))
            second.append(pltpu.VMEM((depth,) + slab.piece, half))
            lev.append(pltpu.VMEM((depth - 1,) + slab.piece, half))
    dma = pltpu.SemaphoreType.DMA
    return pl.pallas_call(
        functools.partial(sum_kernel, slabs, orders, depth),
        out_shape=[jax.ShapeDtypeStruct((s.rows, s.cols), half) for s in slabs],
        in_specs=[pl.BlockSpec(memory_space=pl.ANY)] * count,
        out_specs=[pl.BlockSpec(memory_space=pl.ANY)] * count,
        scratch_shapes=held
        + first
        + second
        + lev
        + result
        + stage
        + [
            dma((count, 2)),
            dma((count,)),
            dma((depth, count)),
            dma((depth, count)),
            dma((6, count)),
            dma((6, count)),
            dma((depth - 1, count)),
            dma((depth - 1, count)),
        ],
        compiler_params=pltpu.CompilerParams(
            collective_id=1, has_side_effects=True, vmem_limit_bytes=SUM_VMEM
        ),
        name="sum_gradients",
    )(*grads)


class Gathering:
    LAG, AHEAD, SKEW = 2, 2, 1

    def __init__(self, slabs, depth, mine, whole, near, sems):
        self.slabs, self.depth, self.mine, self.whole, self.near = slabs, depth, mine, whole, near
        self.sent, self.got, self.z_sent, self.z_got, self.own_sent, self.own_got, self.own_copy = sems
        self.group, self.level, self.core, self.flip = place(depth)
        me = 2 * self.level + self.core
        self.peers = ((self.flip(0), me), (self.flip(1), me), (self.group, 2 * self.level + 1 - self.core))
        by_way = [sorted((o for o in range(depth) if o != z), key=lambda o: (abs(o - z), o)) for z in range(depth)]
        self.sources = [sum((self.level == z) * by_way[z][i] for z in range(depth)) for i in range(depth - 1)]
        self.items = [(k, i) for k in range(len(slabs)) for i in range(depth - 1)]
        self.items.sort(key=lambda item: (item[0] + item[1] * self.SKEW, item[1]))
        self.turn = self.settled = 0
        self.turns = len(self.items) + 2 * self.LAG

    def move(self, kind, item, source, target, device):
        return pltpu.make_async_remote_copy(
            src_ref=source,
            dst_ref=target,
            send_sem=self.sent.at[kind, item],
            recv_sem=self.got.at[kind, item],
            device_id=device,
            device_id_type=MESH,
        )

    def z_part(self, k, source):
        slab, shard = self.slabs[k], 2 * source + self.core
        return self.whole[k].at[slab.shard(shard) if slab.direct else slab.spot(shard, self.group)]

    def mine_part(self, k):
        slab = self.slabs[k]
        return self.near[k] if slab.direct else self.near[k].at[slab.within(self.group)]

    def along_z(self, k, source, step):
        here = self.z_part(k, source)
        mine = source is self.level
        way = (1 - step) // 2
        return pltpu.make_async_remote_copy(
            src_ref=self.mine_part(k) if mine else here,
            dst_ref=here,
            send_sem=self.z_sent.at[way if mine else 2, k * self.depth + source],
            recv_sem=self.z_got.at[k * self.depth + source],
            device_id=(self.group, 2 * (self.level + step) + self.core),
            device_id_type=MESH,
        )

    def pass_on(self, item, act):
        k, i = self.items[item]
        source = self.sources[i]
        pl.when((source < self.level) & (self.level < self.depth - 1))(lambda: act(self.along_z(k, source, 1)))
        pl.when((source > self.level) & (self.level > 0))(lambda: act(self.along_z(k, source, -1)))

    def send_own(self, k, act):
        pl.when(self.level < self.depth - 1)(lambda: act(self.along_z(k, self.level, 1)))
        pl.when(self.level > 0)(lambda: act(self.along_z(k, self.level, -1)))

    def onward(self, kind, item, quarter, half, device):
        k, i = self.items[item]
        shard = 2 * self.sources[i] + self.core
        here = self.whole[k].at[self.slabs[k].spot(shard, quarter, half)]
        return self.move(kind, item, here, here, device)

    def direct(self, item):
        return self.slabs[self.items[item][0]].direct

    def to_core(self, item, core):
        k, i = self.items[item]
        here = self.whole[k].at[self.slabs[k].shard(2 * self.sources[i] + core)]
        return self.move(4, item, here, here, self.peers[2])

    def own(self, k):
        target = self.whole[k].at[self.slabs[k].shard(2 * self.level + self.core)]
        share = pltpu.make_async_remote_copy(
            src_ref=self.near[k],
            dst_ref=target,
            send_sem=self.own_sent.at[k],
            recv_sem=self.own_got.at[k],
            device_id=self.peers[2],
            device_id_type=MESH,
        )
        return pltpu.make_async_copy(self.near[k], target, self.own_copy.at[k, 0]), share

    def fetch_own(self, k):
        col = 0
        for i, array in enumerate(self.mine[k]):
            part = self.near[k].at[:, pl.ds(col, array.shape[1])]
            yield pltpu.make_async_copy(array, part, self.own_copy.at[k, i])
            col += array.shape[1]

    def start(self):
        for k in range(len(self.slabs)):
            for fetch in self.fetch_own(k):
                fetch.start()
        barrier = pltpu.get_barrier_semaphore()

        def greet_one(device):
            pl.semaphore_signal(barrier, inc=1, device_id=device, device_id_type=MESH)

        for peer in self.peers:
            greet_one(peer)
        up, down = self.level < self.depth - 1, self.level > 0
        pl.when(up)(lambda: greet_one((self.group, 2 * (self.level + 1) + self.core)))
        pl.when(down)(lambda: greet_one((self.group, 2 * (self.level - 1) + self.core)))
        pl.semaphore_wait(barrier, 3 + up.astype(jnp.int32) + down.astype(jnp.int32))
        self.begun = 0
        self.begin(self.AHEAD)

    def begin(self, until):
        while self.begun < min(until, len(self.slabs)):
            for fetch in self.fetch_own(self.begun):
                fetch.wait()
            self.send_own(self.begun, lambda copy: copy.start())
            for copy in self.own(self.begun):
                copy.start()
            self.begun += 1

    def pump(self, until):
        group, flip = self.group, self.flip
        x_peer, y_peer, _ = self.peers
        total = len(self.items)
        while self.turn < min(until, self.turns):
            item = self.turn
            if item < total:
                k, i = self.items[item]
                self.begin(k + i * self.SKEW + self.AHEAD)
                here = self.z_part(k, self.sources[i])
                pltpu.make_async_remote_copy(
                    src_ref=here,
                    dst_ref=here,
                    send_sem=self.z_sent.at[2, 0],
                    recv_sem=self.z_got.at[k * self.depth + self.sources[i]],
                    device_id=x_peer,
                    device_id_type=MESH,
                ).wait_recv()
                self.pass_on(item, lambda copy: copy.start())
                if self.direct(item):
                    self.to_core(item, self.core).start()
                else:
                    self.onward(0, item, group, None, x_peer).start()
                    self.onward(1, item, group, None, y_peer).start()
            item = self.turn - self.LAG
            if 0 <= item < total and not self.direct(item):
                self.onward(0, item, flip(0), None, x_peer).wait_recv()
                self.onward(3, item, flip(0), 0, y_peer).start()
                self.onward(1, item, flip(1), None, y_peer).wait_recv()
                self.onward(2, item, flip(1), 1, x_peer).start()
            item = self.turn - 2 * self.LAG
            if 0 <= item < total and not self.direct(item):
                self.onward(3, item, 3 - group, 0, y_peer).wait_recv()
                self.onward(2, item, 3 - group, 1, x_peer).wait_recv()
                self.to_core(item, self.core).start()
            if self.settled < self.turn - 2 * self.LAG - 2:
                self.settle(self.settled)
                self.settled += 1
            self.turn += 1

    def ready_at(self, k):
        return 1 + max(item for item, (slab, _) in enumerate(self.items) if slab == k) + 2 * self.LAG

    def take(self, k):
        self.pump(self.ready_at(k))
        for item, (slab, _) in enumerate(self.items):
            if slab == k:
                self.to_core(item, 1 - self.core).wait_recv()
        keep, share = self.own(k)
        keep.wait()
        share.wait_recv()

    def settle(self, item):
        group, flip = self.group, self.flip
        x_peer, y_peer, _ = self.peers
        self.pass_on(item, lambda copy: copy.wait_send())
        self.to_core(item, self.core).wait_send()
        if self.direct(item):
            return
        self.onward(0, item, group, None, x_peer).wait_send()
        self.onward(1, item, group, None, y_peer).wait_send()
        self.onward(3, item, flip(0), 0, y_peer).wait_send()
        self.onward(2, item, flip(1), 1, x_peer).wait_send()

    def finish(self):
        for item in range(self.settled, len(self.items)):
            self.settle(item)
        for k in range(len(self.slabs)):
            self.send_own(k, lambda copy: copy.wait_send())
            self.own(k)[1].wait_send()


def unpack_vectors(small, parts, width, vec):
    piece = width // parts
    vec[...] = jnp.zeros_like(vec)
    lane = lax.broadcasted_iota(jnp.int32, (128, width), 0)
    col = lax.broadcasted_iota(jnp.int32, (128, width), 1)
    for part in range(parts):
        spread = ((col == lane + part * piece) & (lane < piece)).astype(jnp.bfloat16)
        vec[...] += matmul(small[pl.ds(part * SMALL_ROWS, CH), :128], spread)


def first_kernel(slabs, depth, sizes, *refs):
    count, mine = len(slabs), []
    for size in sizes:
        mine.append(refs[:size])
        refs = refs[size:]
    embedded, vis_col, vis_row, steps, freqs = refs[:5]
    whole, refs = refs[5 : 5 + count], refs[5 + count :]
    kept_hbm, (acts, vec, w_in, w_out, embeds_hbm), refs = refs[:12], refs[12:17], refs[17:]
    sems, refs = refs[:7], refs[7:]
    near, refs = refs[:count], refs[count:]
    small, (e_a, e_u, e_d, d_a, d_u, d_d) = refs[0], refs[1:7]
    e_kept, d_kept = refs[7:13], refs[13:19]
    embeds, e_out, d_out, e_low, d_low, load_sems, kept_sems = refs[19:]
    width = embedded.shape[1]
    parts = 2 * depth
    gathering = Gathering(slabs, depth, mine, whole, near, sems)
    gathering.start()
    half, height = freqs.shape[1], 64
    pieces = steps.shape[0] // height
    enc_turn, dec_turn = gathering.ready_at(3), gathering.ready_at(6)
    encode(embedded, vis_col, None, e_kept[0])
    for piece in range(pieces):
        gathering.pump(piece * enc_turn // pieces)
        rows = pl.ds(piece * height, height)
        phase = steps[rows, :].astype(jnp.float32) * freqs[...]
        embeds[rows, :half] = jnp.cos(phase)
        embeds[rows, half:] = jnp.sin(phase)
    copies = [pltpu.make_async_copy(embeds, embeds_hbm, kept_sems.at[12])]
    copies[0].start()

    def fetch(slots):
        loads = []
        for slab, target in slots:
            gathering.take(slab)
            load = pltpu.make_async_copy(whole[slab], target, load_sems.at[slab])
            load.start()
            loads.append(load)
        return loads

    def run(steps_of, turn, last):
        steps_of = list(steps_of)
        for i, step in enumerate(steps_of):
            step()
            gathering.pump(turn + (last - turn) * (i + 1) // len(steps_of))

    def keep(kept, at):
        for i, buffer in enumerate(kept):
            copy = pltpu.make_async_copy(buffer, kept_hbm[at + i], kept_sems.at[at + i])
            copy.start()
            copies.append(copy)

    for load in fetch([(0, small), (1, e_a), (2, e_u), (3, e_d)]):
        load.wait()
    unpack_vectors(small, parts, width, vec)
    for part in range(parts):
        block = pl.ds(part * SMALL_ROWS, CH)
        w_in[:, pl.ds(part * 128, 128)] = small[block, pl.ds(128, 128)]
        w_out[:, pl.ds(part * 128, 128)] = small[block, pl.ds(256, 128)]
    live = live_keys(vis_row)
    run(forward_steps(width, e_kept[0], vec[0:1, :], vec[1:2, :], e_a, e_u, e_d, *e_kept[1:], e_out, e_low, live), enc_turn, dec_turn)
    keep(e_kept, 0)
    spread_rows(vis_row, e_out, vec, d_kept[0])
    for load in fetch([(4, d_a), (5, d_u), (6, d_d)]):
        load.wait()
    run(forward_steps(width, d_kept[0], vec[2:3, :], vec[3:4, :], d_a, d_u, d_d, *d_kept[1:], d_out, d_low), dec_turn, gathering.turns)
    keep(d_kept, 6)
    acts[...] = d_out[...].astype(jnp.bfloat16)
    for slab in range(7, count):
        gathering.take(slab)
    gathering.finish()
    for copy in copies:
        copy.wait()


def first_part(shards, slabs, depth, embedded, vis_col, vis_row, steps, freqs):
    tokens, width = embedded.shape
    count, items = len(slabs), len(slabs) * (depth - 1)
    inner = slabs[2].cols
    rows = BUFFER + vis_col.shape[0]
    flat, wide = steps.shape[0], 2 * freqs.shape[1]
    f32, half = jnp.float32, jnp.bfloat16
    whole, anywhere = pl.BlockSpec(memory_space=pltpu.VMEM), pl.BlockSpec(memory_space=pl.ANY)
    shape, dma = jax.ShapeDtypeStruct, pltpu.SemaphoreType.DMA
    gathered = [shape((2 * depth * s.rows, s.cols), half) for s in slabs]

    def kept(height):
        return [
            shape((height, width), f32),
            shape((height, 3 * width), half),
            shape((height, width), half),
            shape((height, width), f32),
            shape((height, inner), half),
            shape((height, inner), half),
        ]

    saved = kept(rows) + kept(tokens)
    outs = gathered + saved
    outs += [shape((tokens, width), half), shape((CH, width), f32), shape((CH, wide), half), shape((CH, wide), half), shape((flat, wide), f32)]
    found = pl.pallas_call(
        functools.partial(first_kernel, slabs, depth, [len(arrays) for arrays in shards]),
        out_shape=outs,
        in_specs=[anywhere] * sum(len(arrays) for arrays in shards) + [whole] * 5,
        out_specs=[anywhere] * (count + 12) + [whole] * 4 + [anywhere],
        scratch_shapes=[dma((5, items)), dma((5, items)), dma((3, count * depth)), dma((count * depth,)), dma((count,)), dma((count,)), dma((count, 2))]
        + [pltpu.VMEM((s.rows, s.cols), half) for s in slabs]
        + [pltpu.VMEM(s.shape, s.dtype) for s in (*gathered[:7], *saved)]
        + [
            pltpu.VMEM((flat, wide), f32),
            pltpu.VMEM((rows, width), f32),
            pltpu.VMEM((tokens, width), f32),
            pltpu.VMEM((rows, width), half),
            pltpu.VMEM((tokens, width), half),
            dma((count,)),
            dma((13,)),
        ],
        compiler_params=pltpu.CompilerParams(collective_id=0, has_side_effects=True, vmem_limit_bytes=SUM_VMEM),
        name="gather_and_forward",
    )(*(array for arrays in shards for array in arrays), embedded, vis_col, vis_row, steps, freqs)
    slabs_found, found = found[:count], found[count:]
    return slabs_found, found[:6], found[6:12], *found[12:]


SIDE = 256
BACK_TILE = 256


class Chunk:
    def __init__(self, parent, height, row, rows, col, cols, by_rows):
        self.parent, self.height = parent, height
        self.row, self.rows, self.col, self.cols, self.by_rows = row, rows, col, cols, by_rows
        self.piece = (rows // 4, cols) if by_rows else (rows, cols // 4)
        self.set_order(False, 0)

    def set_order(self, z_first, first_bit):
        self.z_first, self.first_bit = z_first, first_bit

    def shard(self, shard):
        return (pl.ds(aligned(shard * self.height + self.row, 16), self.rows), pl.ds(self.col, self.cols))

    def out(self):
        return (pl.ds(self.row, self.rows), pl.ds(self.col, self.cols))

    def within(self, quarter):
        rows, cols = self.piece
        if self.by_rows:
            return (pl.ds(aligned(quarter * rows, 16), rows), pl.ds(0, cols))
        return (pl.ds(0, rows), pl.ds(aligned(quarter * cols, 128), cols))


def cut(parent, slab, pieces):
    for i in range(pieces):
        if slab.by_rows:
            cols = slab.cols // pieces
            yield Chunk(parent, slab.rows, 0, slab.rows, i * cols, cols, True)
        else:
            rows = slab.rows // pieces
            yield Chunk(parent, slab.rows, i * rows, rows, 0, slab.cols, False)


class Summing:
    STAGES, LAG, AHEAD, BESIDE = 6, 5, 2, 5

    def __init__(self, chunks, depth, grads, outs, buffers, sems):
        self.chunks, self.depth, self.grads, self.outs = chunks, depth, grads, outs
        self.held, self.from_first, self.from_second, self.from_level, self.result, self.stage = buffers
        self.stage_sem, self.out_sem, self.core_pair, self.pair, self.z_pair = sems
        self.group, self.level, self.core, self.flip = place(depth)
        self.me = 2 * self.level + self.core
        self.partner = (self.group, 2 * self.level + 1 - self.core)
        self.z_peers = [(self.group, 2 * self.level_at(step) + self.core) for step in range(1, depth)]
        self.peers = [(self.flip(0), self.me), (self.flip(1), self.me), self.partner, *self.z_peers]

    def level_at(self, step):
        return lax.rem(self.level + step + self.depth, self.depth)

    def bit(self, b):
        return (self.group // (1 << b)) % 2

    def move(self, pair, k, kind, source, target, device):
        return pltpu.make_async_remote_copy(
            src_ref=source,
            dst_ref=target,
            send_sem=pair[0].at[kind, k],
            recv_sem=pair[1].at[kind, k],
            device_id=device,
            device_id_type=MESH,
        )

    def quarter(self, k, first, second):
        b = self.chunks[k].first_bit
        return first * (1 << b) + second * (1 << (1 - b))

    def core_move(self, k, lev):
        chunk = self.chunks[k]
        source = self.grads[chunk.parent].at[chunk.shard(2 * lev + 1 - self.core)]
        return self.move(self.core_pair, k, lev, source, self.held[k].at[lev], self.partner)

    def part(self, k, quarter):
        chunk, held = self.chunks[k], self.held[k]
        where = chunk.within(quarter)
        return held.at[(self.level,) + where] if chunk.z_first else held.at[(slice(None),) + where]

    def first_move(self, k, j):
        b = self.chunks[k].first_bit
        source = self.part(k, self.quarter(k, 1 - self.bit(b), j))
        return self.move(self.pair, k, j, source, self.from_first[k].at[j], (self.flip(b), self.me))

    def second_move(self, k):
        b = self.chunks[k].first_bit
        source = self.part(k, self.quarter(k, self.bit(b), 1 - self.bit(1 - b)))
        return self.move(self.pair, k, 2, source, self.from_second[k], (self.flip(1 - b), self.me))

    def level_move(self, k, step):
        chunk, held = self.chunks[k], self.held[k]
        lev = self.level_at(step)
        source = held.at[lev] if chunk.z_first else held.at[(lev,) + chunk.within(self.group)]
        target = self.from_level[k].at[step - 1]
        return self.move(self.z_pair, k, step - 1, source, target, self.z_peers[step - 1])

    def spread(self, k, kind, whose, b):
        here = self.result[k].at[self.chunks[k].within(whose)]
        return self.move(self.pair, k, kind, here, here, (self.flip(b), self.me))

    def spread_second(self, k, whose):
        return self.spread(k, 3, whose, 1 - self.chunks[k].first_bit)

    def spread_first(self, k, j, whose):
        return self.spread(k, 4 + j, whose, self.chunks[k].first_bit)

    def out_copy(self, k):
        chunk = self.chunks[k]
        target = self.outs[chunk.parent].at[chunk.out()]
        return pltpu.make_async_copy(self.result[k], target, self.out_sem.at[k])

    def stage_copy(self, k, lev):
        chunk = self.chunks[k]
        source = self.grads[chunk.parent].at[chunk.shard(2 * lev + self.core)]
        slot = self.stage[(chunk.rows, chunk.cols)].at[lev % 2]
        return pltpu.make_async_copy(source, slot, self.stage_sem.at[k, lev % 2])

    def rows_loop(self, height, body):
        step = 32 if height % 32 == 0 else 16
        loop(height // step + self.level // self.depth, lambda i: body(at_step(i, step)))

    def add_core(self, k):
        chunk, held = self.chunks[k], self.held[k]
        stage = self.stage[(chunk.rows, chunk.cols)]
        self.stage_copy(k, 0).start()
        for lev in range(self.depth):
            if lev + 1 < self.depth:
                self.stage_copy(k, lev + 1).start()
            self.core_move(k, lev).wait_recv()
            self.stage_copy(k, lev).wait()

            def body(rows):
                total = held[lev, rows, :].astype(jnp.float32) + stage[lev % 2, rows, :].astype(jnp.float32)
                held[lev, rows, :] = total.astype(jnp.bfloat16)

            self.rows_loop(chunk.rows, body)

    def levels_of(self, k):
        return [self.level] if self.chunks[k].z_first else list(range(self.depth))

    def shifted(self, rows, by):
        return pl.ds(aligned(rows.start + by, 16), rows.size)

    def add_first(self, k):
        chunk, slot = self.chunks[k], k
        held, arrived = self.held[slot], self.from_first[slot]
        for j in range(2):
            self.first_move(k, j).wait_recv()
            top, cols = chunk.within(self.quarter(k, self.bit(chunk.first_bit), j))
            for lev in self.levels_of(k):

                def body(rows):
                    at = (lev, self.shifted(rows, top.start), cols)
                    extra = arrived[j, rows, :] if chunk.z_first else arrived[j, lev, rows, :]
                    held[at] = (held[at].astype(jnp.float32) + extra.astype(jnp.float32)).astype(jnp.bfloat16)

                self.rows_loop(chunk.piece[0], body)

    def add_second(self, k):
        chunk, slot = self.chunks[k], k
        held, arrived, result = self.held[slot], self.from_second[slot], self.result[slot]
        self.second_move(k).wait_recv()
        top, cols = chunk.within(self.group)
        for lev in self.levels_of(k):

            def body(rows):
                at = (lev, self.shifted(rows, top.start), cols)
                extra = arrived[rows, :] if chunk.z_first else arrived[lev, rows, :]
                total = (held[at].astype(jnp.float32) + extra.astype(jnp.float32)).astype(jnp.bfloat16)
                if chunk.z_first:
                    result[at[1:]] = total
                else:
                    held[at] = total

            self.rows_loop(chunk.piece[0], body)

    def add_level(self, k):
        chunk, slot = self.chunks[k], k
        held, arrived, result = self.held[slot], self.from_level[slot], self.result[slot]
        for step in range(1, self.depth):
            self.level_move(k, step).wait_recv()
        top, cols = (pl.ds(0, chunk.rows), pl.ds(0, chunk.cols)) if chunk.z_first else chunk.within(self.group)

        def body(rows):
            at = (self.shifted(rows, top.start), cols)
            total = held[(self.level,) + at].astype(jnp.float32)
            for step in range(self.depth - 1):
                total = total + arrived[step, rows, :].astype(jnp.float32)
            if chunk.z_first:
                held[(self.level,) + at] = total.astype(jnp.bfloat16)
            else:
                result[at] = total.astype(jnp.bfloat16)

        self.rows_loop(top.size, body)

    def begin_core(self, k):
        for lev in range(self.depth):
            self.core_move(k, lev).start()

    def begin_first(self, k):
        self.first_move(k, 0).start()
        self.first_move(k, 1).start()

    def begin_level(self, k):
        for step in range(1, self.depth):
            self.level_move(k, step).start()

    def begin_spread(self, k):
        self.spread_second(k, self.group).start()

    def end_spread_second(self, k):
        other = self.flip(1 - self.chunks[k].first_bit)
        self.spread_second(k, other).wait_recv()
        self.spread_first(k, 0, self.group).start()
        self.spread_first(k, 1, other).start()

    def end_spread_first(self, k):
        self.spread_first(k, 0, self.flip(self.chunks[k].first_bit)).wait_recv()
        self.spread_first(k, 1, 3 - self.group).wait_recv()
        self.out_copy(k).start()

    def stages(self, k):
        if self.chunks[k].z_first:
            return [
                lambda: (self.add_core(k), self.begin_level(k)),
                lambda: (self.add_level(k), self.begin_first(k)),
                lambda: (self.add_first(k), self.second_move(k).start()),
                lambda: (self.add_second(k), self.begin_spread(k)),
                lambda: self.end_spread_second(k),
                lambda: self.end_spread_first(k),
            ]
        return [
            lambda: (self.add_core(k), self.begin_first(k)),
            lambda: (self.add_first(k), self.second_move(k).start()),
            lambda: (self.add_second(k), self.begin_level(k)),
            lambda: (self.add_level(k), self.begin_spread(k)),
            lambda: self.end_spread_second(k),
            lambda: self.end_spread_first(k),
        ]

    def settle(self, k):
        for lev in range(self.depth):
            self.core_move(k, lev).wait_send()
        self.first_move(k, 0).wait_send()
        self.first_move(k, 1).wait_send()
        self.second_move(k).wait_send()
        for step in range(1, self.depth):
            self.level_move(k, step).wait_send()
        self.spread_second(k, self.group).wait_send()
        self.spread_first(k, 0, self.group).wait_send()
        self.spread_first(k, 1, self.flip(1 - self.chunks[k].first_bit)).wait_send()
        self.out_copy(k).wait()

    def run(self, ready, beside):
        count = len(self.chunks)
        greet(self.peers)
        plans = [self.stages(k) for k in range(count)]
        for turn in range(-self.AHEAD, count + self.LAG * (self.STAGES - 1)):
            if turn + self.AHEAD < count:
                ready(turn + self.AHEAD)
                self.begin_core(turn + self.AHEAD)
            for stage in range(self.STAGES):
                if 0 <= turn - self.LAG * stage < count:
                    plans[turn - self.LAG * stage][stage]()
                if stage < self.BESIDE:
                    beside()
            done = turn - self.LAG * (self.STAGES - 1) - 2
            if 0 <= done < count:
                self.settle(done)
        for k in range(max(0, done + 1), count):
            self.settle(k)


class Saved:
    def __init__(self, kept, buffers, sems):
        rows = kept[0].shape[0]
        part = pl.ds(0, rows)
        self.wide, self.qkv, self.mixed = (b if b.shape[0] == rows else b.at[part] for b in buffers)
        places = (self.wide, self.qkv, self.mixed, self.wide)
        self.copies = [pltpu.make_async_copy(a, b, sems.at[i]) for i, (a, b) in enumerate(zip(kept, places, strict=True))]

    def start(self, which):
        self.copies[("x", "qkv", "mixed", "middle").index(which)].start()

    def wait(self, which):
        self.copies[("x", "qkv", "mixed", "middle").index(which)].wait()


class Stream:
    SLOTS = 3

    def __init__(self, sources, slots, sems):
        self.sources, self.slots, self.sems, self.used = sources, slots, sems, 0
        for i in range(self.SLOTS - 1):
            self.copy(i).start()

    def slot(self, i):
        height, slot = self.sources[i].shape[0], self.slots.at[i % self.SLOTS]
        return slot if height == slot.shape[0] else slot.at[pl.ds(0, height)]

    def copy(self, i):
        return pltpu.make_async_copy(self.sources[i], self.slot(i), self.sems.at[i % self.SLOTS])

    def next(self):
        i = self.used
        self.copy(i).wait()
        if i + self.SLOTS - 1 < len(self.sources):
            self.copy(i + self.SLOTS - 1).start()
        self.used += 1
        return self.slot(i)


def backward_steps(width, grad, gain_one, gain_two, saved, following, streams, d_a, d_up, d_down, d_one, d_two,
                   grad_low, low, grad_qkv, acc, grad_mid, out, tiles, live, reach, names):
    wide, narrow, square = tiles
    downs, ups, acts, slopes, heads = streams
    inner, side = d_up.shape[1], SIDE
    qkv, mixed, middle, stream = saved.qkv, saved.mixed, saved.wide, saved.wide

    def begin():
        saved.wait("middle")
        grad_low[...] = grad[...].astype(jnp.bfloat16)
        scale_norm(middle, gain_two, low)
        acc[...] = jnp.zeros_like(acc)

    yield begin
    def feed_down(j):
        narrow.put(j, rows_dot(acts.next()[...], grad_low[...]), d_down.at[pl.ds(j * BACK_TILE, BACK_TILE), :])

    def feed_slope(j):
        slope = slopes.next()[...].astype(jnp.float32)
        grad_qkv[:, :BACK_TILE] = (right_trans(grad_low[...], downs.next()[...]) * slope).astype(jnp.bfloat16)

    def feed_up(j):
        wide.put(j, rows_dot(low[...], grad_qkv[:, :BACK_TILE]), d_up.at[:, pl.ds(j * BACK_TILE, BACK_TILE)])
        acc[...] += right_trans(grad_qkv[:, :BACK_TILE], ups.next()[...])

    def down_done():
        narrow.flush(d_down.at[pl.ds(0, BACK_TILE), :])
        reach(names[0])

    for j in range(inner // BACK_TILE):
        yield functools.partial(feed_down, j)
    yield down_done
    for j in range(inner // BACK_TILE):
        yield functools.partial(feed_slope, j)
        yield functools.partial(feed_up, j)

    def middle_back():
        wide.flush(d_up.at[:, pl.ds(0, BACK_TILE)])
        reach(names[1])
        norm_back_into(acc, middle, gain_two, grad, grad_mid, d_two)
        saved.start("x")
        grad_low[...] = grad_mid[...].astype(jnp.bfloat16)
        saved.wait("mixed")

    yield middle_back

    def project_back(j):
        cols = pl.ds(j * side, side)
        square.put(j, rows_dot(mixed[...], grad_low[:, cols]), d_a.at[:, pl.ds(3 * width + j * side, side)])
        added = right_trans(grad_low[:, cols], heads.next()[...])
        acc[...] = added if j == 0 else acc[...] + added

    for j in range(width // side):
        yield functools.partial(project_back, j)

    def mixed_back():
        if following:
            following.start("mixed")
        low[...] = acc[...].astype(jnp.bfloat16)
        saved.wait("qkv")

    yield mixed_back

    def attend(pair):
        where = [pl.ds(pair * 128 + part * width, 128) for part in range(3)]
        query, key, value = (qkv[:, at] for at in where)
        grad_mixed = low[:, pl.ds(pair * 128, 128)]
        found = []
        for half in range(2):
            probs = probabilities(query, key, half, live)
            grad_half = keep_half(grad_mixed, half)
            grad_probs = right_trans(grad_half, value)
            dots = jnp.sum(grad_probs * probs, axis=-1, keepdims=True)
            grad_scores = (probs * (grad_probs - dots) * 0.125).astype(jnp.bfloat16)
            found.append(
                (matmul(grad_scores, key), rows_dot(grad_scores, query), rows_dot(probs.astype(jnp.bfloat16), grad_half))
            )
        for part in range(3):
            both = jnp.where(head_mask(0), found[0][part], found[1][part])
            grad_qkv[:, where[part]] = both.astype(jnp.bfloat16)

    for pair in range(width // 128):
        yield functools.partial(attend, pair)

    def normed():
        if following:
            following.start("qkv")
        saved.wait("x")
        scale_norm(stream, gain_one, low)

    yield normed

    def project(j):
        piece = grad_qkv[:, pl.ds(j * side, side)]
        square.put(j + width // side, rows_dot(low[...], piece), d_a.at[:, pl.ds(j * side, side)])
        added = right_trans(piece, heads.next()[...])
        acc[...] = added if j == 0 else acc[...] + added

    for j in range(3 * width // side):
        yield functools.partial(project, j)

    def end():
        square.flush(d_a.at[:, pl.ds(0, side)])
        reach(names[2])
        norm_back_into(acc, stream, gain_one, grad_mid, out, d_one)
        if following:
            following.start("middle")

    yield end


def last_kernel(chunks, stage_keys, depth, *refs):
    head_grads, refs = refs[:3], refs[3:]
    head_small, refs = refs[:2], refs[2:]
    (vis_col, vis_row, vec, grad_rows), e_kept, d_kept, refs = refs[:4], refs[4:10], refs[10:16], refs[16:]
    (e_a, e_u, e_d, d_a, d_u, d_d), refs = refs[:6], refs[6:]
    outs, refs = refs[:10], refs[10:]
    embed_grad, small_grad, refs = refs[0], refs[1], refs[2:]
    block_grads, refs = refs[:6], refs[6:]
    (small, small_pack, d_grad, low_a, low_b, grad_qkv, acc, grad_mid), refs = refs[:8], refs[8:]
    saved_buffers, saved_sems, refs = refs[:3], refs[3], refs[4:]
    (wide, narrow, square, down_slots, up_slots, act_slots, slope_slots, head_slots, tile_sems, load_sems, pack_sem), refs = refs[:11], refs[11:]
    count = len(chunks)
    buffers = [refs[i * count : (i + 1) * count] for i in range(5)]
    refs = refs[5 * count :]
    stage, refs = dict(zip(stage_keys, refs[: len(stage_keys)], strict=True)), refs[len(stage_keys) :]
    stage_sem, out_sem, core_sent, core_got, sent, got, z_sent, z_got = refs
    sems = (stage_sem, out_sem, (core_sent, core_got), (sent, got), (z_sent, z_got))
    tokens, width = d_kept[0].shape
    rows = e_kept[0].shape[0]
    parts = 2 * depth
    d_saved = Saved(d_kept[:4], saved_buffers, saved_sems.at[0])
    e_saved = Saved(e_kept[:4], saved_buffers, saved_sems.at[1])
    de_a, de_u, de_d, dd_a, dd_u, dd_d = block_grads
    grads = (small_grad, *block_grads, *head_grads)
    summing = Summing(chunks, depth, grads, outs, (*buffers, stage), sems)
    tiles = (Tiles(wide, tile_sems.at[0]), Tiles(narrow, tile_sems.at[1]), Tiles(square, tile_sems.at[2]))
    reached = {"head"}
    e_grad = d_grad.at[pl.ds(0, rows)]
    embed_copy = pltpu.make_async_copy(d_grad, embed_grad, pack_sem.at[1])

    def streams(inner, w_a, w_u, w_d, acted, sloped):
        tile = [pl.ds(j * BACK_TILE, BACK_TILE) for j in range(inner // BACK_TILE)]
        past = width // SIDE
        sides = [pl.ds((j + 3 * past) % (4 * past) * SIDE, SIDE) for j in range(4 * past)]
        return (
            Stream([w_d.at[t, :] for t in tile], down_slots, load_sems.at[0]),
            Stream([w_u.at[:, t] for t in tile], up_slots, load_sems.at[1]),
            Stream([acted.at[:, t] for t in tile], act_slots, load_sems.at[2]),
            Stream([sloped.at[:, t] for t in tile], slope_slots, load_sems.at[3]),
            Stream([w_a.at[:, t] for t in sides], head_slots, load_sems.at[4]),
        )

    def work():
        inner = d_u.shape[1]
        ready_streams = []

        def begin():
            for which in ("middle", "mixed", "qkv"):
                d_saved.start(which)
            ready_streams.append(streams(inner, d_a, d_u, d_d, *d_kept[4:]))
            arrived = low_b.at[pl.ds(BUFFER, tokens - BUFFER)]
            fetch = pltpu.make_async_copy(grad_rows, arrived, pack_sem.at[2])
            fetch.start()
            fetch.wait()
            d_grad[:BUFFER, :] = jnp.zeros((BUFFER, width), jnp.float32)
            d_grad[BUFFER:, :] = arrived[...].astype(jnp.float32)

        yield begin
        yield from lazy_steps(lambda: backward_steps(
            width, d_grad, vec[2:3, :], vec[3:4, :], d_saved, e_saved, ready_streams[0], dd_a, dd_u, dd_d,
            small.at[2], small.at[3], low_a, low_b, grad_qkv, acc, grad_mid, d_grad, tiles, None, reached.add, ("dec down", "dec up", "dec")))

        def between():
            ready_streams.append(streams(inner, e_a, e_u, e_d, *e_kept[4:]))
            hot = spot_hot(vis_row, tokens - BUFFER)
            masked = 1.0 - jnp.sum(hot.astype(jnp.float32), axis=1, keepdims=True)
            small[4] = jnp.broadcast_to(jnp.sum(d_grad[BUFFER:, :] * masked, axis=0, keepdims=True), (8, width))
            e_grad[BUFFER:, :] = exact_dot(token_hot(vis_col, tokens - BUFFER), d_grad[BUFFER:, :])

        yield between
        part = pl.ds(0, rows)
        yield from lazy_steps(lambda: backward_steps(
            width, e_grad, vec[0:1, :], vec[1:2, :], e_saved, None, ready_streams[1], de_a, de_u, de_d,
            small.at[0], small.at[1], low_a.at[part], low_b.at[part], grad_qkv.at[part], acc.at[part],
            grad_mid.at[part], e_grad, tiles, live_keys(vis_row), reached.add, ("enc down", "enc up", "enc")))

        def end():
            d_grad[BUFFER:, :] = exact_dot(spot_hot(vis_row, tokens - BUFFER), e_grad[BUFFER:, :])
            embed_copy.start()
            pack_gradients(small, head_small, parts, small_pack)
            copy = pltpu.make_async_copy(small_pack, small_grad, pack_sem.at[0])
            copy.start()
            copy.wait()
            reached.add("all")

        yield end

    steps = work()
    needs = ["all", "enc", "enc up", "enc down", "dec", "dec up", "dec down", "head", "head", "head"]

    def beside():
        step = next(steps, None)
        if step is not None:
            step()

    def ready(k):
        while needs[chunks[k].parent] not in reached:
            beside()

    summing.run(ready, beside)
    embed_copy.wait()


def lazy_steps(make):
    yield from make()


def pack_gradients(small, head_small, parts, target):
    count, _, width = small.shape
    piece = width // parts
    target[...] = jnp.zeros_like(target)
    lane = lax.broadcasted_iota(jnp.int32, (width, 128), 1)
    row = lax.broadcasted_iota(jnp.int32, (width, 128), 0)
    which = lax.broadcasted_iota(jnp.int32, (CH, width), 0)
    rows = jnp.zeros((CH, width), jnp.float32)
    for i in range(count):
        rows = jnp.where(which == i, jnp.concatenate([small[i], small[i]], axis=0), rows)
    low = rows.astype(jnp.bfloat16)
    for part in range(parts):
        block = pl.ds(part * SMALL_ROWS, CH)
        pick = ((row == lane + part * piece) & (lane < piece)).astype(jnp.bfloat16)
        target[block, :128] = matmul(low, pick).astype(jnp.bfloat16)
        for i in range(2):
            target[block, pl.ds(128 * (i + 1), 128)] = head_small[i][:, pl.ds(part * 128, 128)].astype(jnp.bfloat16)


def last_part(slabs, chunks, depth, head_grads, head_small, grad_rows, vis_col, vis_row, vec, enc_kept, dec_kept, weights):
    tokens, width = dec_kept[0].shape
    rows = enc_kept[0].shape[0]
    parts = 2 * depth
    f32, half = jnp.float32, jnp.bfloat16
    whole, anywhere = pl.BlockSpec(memory_space=pltpu.VMEM), pl.BlockSpec(memory_space=pl.ANY)
    shape, dma = jax.ShapeDtypeStruct, pltpu.SemaphoreType.DMA
    stage_keys = sorted({(c.rows, c.cols) for c in chunks})
    held, first, second, lev, result = [], [], [], [], []
    for chunk in chunks:
        part = (chunk.rows, chunk.cols)
        held.append(pltpu.VMEM((depth,) + part, half))
        result.append(pltpu.VMEM(part, half))
        if chunk.z_first:
            first.append(pltpu.VMEM((2,) + chunk.piece, half))
            second.append(pltpu.VMEM(chunk.piece, half))
            lev.append(pltpu.VMEM((depth - 1,) + part, half))
        else:
            first.append(pltpu.VMEM((2, depth) + chunk.piece, half))
            second.append(pltpu.VMEM((depth,) + chunk.piece, half))
            lev.append(pltpu.VMEM((depth - 1,) + chunk.piece, half))
    count = len(chunks)
    outs = [shape((s.rows, s.cols), half) for s in slabs]
    outs += [shape((tokens, width), f32), shape((parts * SMALL_ROWS, SMALL_COLS), half)]
    outs += [shape(w.shape, half) for w in weights]
    vmem = pltpu.VMEM
    found = pl.pallas_call(
        functools.partial(last_kernel, chunks, stage_keys, depth),
        out_shape=outs,
        in_specs=[anywhere] * 3 + [whole] * 5 + [anywhere] * 19,
        out_specs=[anywhere] * (len(slabs) + 8),
        scratch_shapes=[
            vmem((5, 8, width), f32),
            vmem((parts * SMALL_ROWS, SMALL_COLS), half),
            vmem((tokens, width), f32),
            vmem((tokens, width), half),
            vmem((tokens, width), half),
            vmem((tokens, 3 * width), half),
            vmem((tokens, width), f32),
            vmem((tokens, width), f32),
            vmem((tokens, width), f32),
            vmem((tokens, 3 * width), half),
            vmem((tokens, width), half),
            dma((2, 4)),
            vmem((2, width, BACK_TILE), half),
            vmem((2, BACK_TILE, width), half),
            vmem((2, width, SIDE), half),
            vmem((Stream.SLOTS, BACK_TILE, width), half),
            vmem((Stream.SLOTS, width, BACK_TILE), half),
            vmem((Stream.SLOTS, tokens, BACK_TILE), half),
            vmem((Stream.SLOTS, tokens, BACK_TILE), half),
            vmem((Stream.SLOTS, width, SIDE), half),
            dma((3, 2)),
            dma((5, Stream.SLOTS)),
            dma((3,)),
        ]
        + held
        + first
        + second
        + lev
        + result
        + [vmem((2,) + key, half) for key in stage_keys]
        + [
            dma((count, 2)),
            dma((count,)),
            dma((depth, count)),
            dma((depth, count)),
            dma((6, count)),
            dma((6, count)),
            dma((depth - 1, count)),
            dma((depth - 1, count)),
        ],
        compiler_params=pltpu.CompilerParams(collective_id=1, has_side_effects=True, vmem_limit_bytes=LAST_VMEM),
        name="backward_and_sum",
    )(*head_grads, *head_small, vis_col, vis_row, vec, grad_rows, *enc_kept, *dec_kept, *weights)
    return found[len(slabs)], found[: len(slabs)]


SMALL_ROWS, SMALL_COLS = 32, 512


def pack_small(vectors, first, last):
    parts = vectors[0].shape[0] // 96
    lanes = jnp.stack([v.reshape(parts, 96) for v in vectors], axis=1)
    lanes = jnp.pad(lanes, ((0, 0), (0, CH - len(vectors)), (0, 128 - 96)))
    wide = [w.reshape(CH, parts, 128).transpose(1, 0, 2) for w in (first, last)]
    packed = jnp.concatenate([lanes, *wide], axis=2)
    packed = jnp.pad(packed, ((0, 0), (0, SMALL_ROWS - CH), (0, SMALL_COLS - 384)))
    return packed.reshape(parts * SMALL_ROWS, SMALL_COLS)


def unpack_small(packed):
    parts = packed.shape[0] // SMALL_ROWS
    packed = packed.reshape(parts, SMALL_ROWS, SMALL_COLS)
    vectors = packed[:, :5, :96].transpose(1, 0, 2).reshape(5, parts * 96)
    wide = [packed[:, :CH, 128 * i : 128 * i + 128].transpose(1, 0, 2).reshape(CH, parts * 128) for i in (1, 2)]
    return vectors, wide[0], wide[1]


SLABS = (
    Slab(SMALL_ROWS, SMALL_COLS, False, True),
    Slab(96, 3072, False),
    Slab(96, 3072, False),
    Slab(384, 768, True),
    Slab(96, 3072, False),
    Slab(96, 3072, False),
    Slab(384, 768, True),
    Slab(128, 3072, False),
    Slab(128, 2048, False),
    Slab(96, 1024, False, True),
)


def chunks_of():
    plan = [(7, 4, ()), (8, 2, ()), (9, 1, ()), (6, 3, (0, 2)), (5, 3, ()), (4, 3, ()), (3, 3, (0, 2)), (2, 3, ()), (1, 3, ()), (0, 1, ())]
    found = []
    for parent, pieces, z_first in plan:
        for i, chunk in enumerate(cut(parent, SLABS[parent], pieces)):
            chunk.set_order(i in z_first, len(found) % 2)
            found.append(chunk)
    return found


def by_links():
    return lax.axis_size("dev") == 8 and lax.axis_size("grp") == 4


def packed_shards(shards):
    (e_one, e_qkv, e_proj, e_two, e_up, e_down, d_one, d_qkv, d_proj, d_two, d_up, d_down, fill, h_in, h_cond, h_ada, h_inner, h_outer, h_out) = shards
    large = ((e_qkv, e_proj), (e_up,), (e_down,), (d_qkv, d_proj), (d_up,), (d_down,), (h_ada,), (h_inner, h_outer), (h_cond,))
    return large, [e_one, e_two, d_one, d_two, fill], h_in, h_out


def gather_weights(shards):
    packed, vectors, h_in, h_out = packed_shards(shards)
    whole = lambda w, axis=0: lax.all_gather(w, "dev", axis=axis, tiled=True)
    return [whole(jnp.concatenate(w, axis=1)) for w in packed], whole(jnp.stack(vectors), 1), whole(h_in, 1), whole(h_out).T


def sum_gradients(slabs, vectors, d_in, d_out):
    def scatter(grad, axis=0):
        part = lax.psum_scatter(grad.astype(jnp.float32), "dev", scatter_dimension=axis, tiled=True)
        return lax.psum(part.astype(jnp.bfloat16), "grp")

    return unpack_gradients([scatter(g) for g in slabs], scatter(vectors, 1), scatter(d_in, 1), scatter(d_out, 1))


def widen_kernel(count, *refs):
    sources, targets = refs[:count], list(refs[count:])
    for source in sources:
        col = 0
        while col < source.shape[1]:
            target = targets.pop(0)
            width = target.shape[1]
            target[...] = source[:, col : col + width].astype(jnp.float32)
            col += width


def widen(slabs, cuts):
    shape = jax.ShapeDtypeStruct
    outs = [shape((s.shape[0], width), jnp.float32) for s, widths in zip(slabs, cuts, strict=True) for width in widths]
    whole = pl.BlockSpec(memory_space=pltpu.VMEM)
    return pl.pallas_call(
        functools.partial(widen_kernel, len(slabs)),
        out_shape=outs,
        in_specs=[whole] * len(slabs),
        out_specs=[whole] * len(outs),
        compiler_params=pltpu.CompilerParams(vmem_limit_bytes=SUM_VMEM),
        name="widen_gradients",
    )(*slabs)


def unpack_gradients(slabs, vectors, d_in, d_out):
    vectors, d_in, d_out = (s.astype(jnp.float32) for s in (vectors, d_in, d_out))
    width = slabs[2].shape[1]
    head = slabs[8].shape[1]
    cuts = [(3 * width, width), (4 * width,), (width,)] * 2 + [(3 * head,), (head, head), (head,)]
    e_qkv, e_proj, e_up, e_down, d_qkv, d_proj, d_up, d_down, ada, inner, outer, cond = widen(slabs, cuts)
    return (vectors[0], e_qkv, e_proj, vectors[1], e_up, e_down, vectors[2], d_qkv, d_proj, vectors[3], d_up, d_down,
            vectors[4], d_in, cond, ada, inner, outer, d_out.T)


def per_device(embedded, mask_order, counts, targets, noise_copies, timesteps, *shards):
    images, tokens, width = embedded.shape
    seq_len = mask_order.shape[1]
    linked = by_links() and images == 1
    if not linked:
        slabs, vectors, w_in, w_out = gather_weights(shards)
        vec = jnp.pad(vectors.astype(jnp.float32), ((0, CH - 5), (0, 0)))
    freqs = jnp.exp(-math.log(10000.0) * jnp.arange(HW // 2, dtype=jnp.float32) / (HW // 2)).reshape(1, HW // 2)
    losses, acts_of, embed_grads, totals = [], [], [], None
    for image in range(images):
        padded = jnp.concatenate([mask_order[image], jnp.full((SPOTS,), -1, jnp.int32)])
        seen = lax.dynamic_slice(padded, (counts[image],), (SPOTS,))
        vis_col, vis_row = seen.reshape(SPOTS, 1), seen.reshape(1, SPOTS)
        steps = timesteps[image].T.reshape(COPIES * seq_len, 1)
        noise = noise_copies[image].transpose(1, 0, 2).reshape(COPIES * seq_len, CH)
        if linked:
            packed, vectors, h_in, h_out = packed_shards(shards)
            (_, *slabs), enc_kept, dec_kept, acts, vec, w_in, w_out, embeds = first_part(
                ((pack_small(vectors, h_in, h_out.T),), *packed), SLABS, lax.axis_size("dev") // 2,
                embedded[image], vis_col, vis_row, steps, freqs,
            )
        else:
            phase = steps.astype(jnp.float32) * freqs
            embeds = jnp.concatenate([jnp.cos(phase), jnp.sin(phase)], axis=1)
            enc_kept, dec_kept, acts = forward_blocks(embedded[image], vis_col, vis_row, vec, slabs[:6])
        grad_rows, loss, d_in, d_out, d_cond, d_ada, d_io = head_pass(
            acts, vis_row, targets[image], noise, steps, embeds, slabs[8], slabs[6], slabs[7], w_in, w_out
        )
        head_grads = (d_ada, d_io, d_cond)
        if linked:
            embed_grad, sums = last_part(
                SLABS, chunks_of(), lax.axis_size("dev") // 2, head_grads, (d_in, d_out), grad_rows, vis_col, vis_row, vec,
                enc_kept, dec_kept, slabs[:6],
            )
        else:
            embed_grad, small, block_grads = backward_blocks(grad_rows, vis_col, vis_row, vec, enc_kept, dec_kept, slabs[:6])
            found = ([*block_grads, *head_grads], small[:5], d_in, d_out)
            totals = found if totals is None else jax.tree.map(jnp.add, totals, found)
        losses.append(loss[0, 0] / (counts[image].astype(jnp.float32) * (COPIES * CH)))
        acts_of.append(acts)
        embed_grads.append(embed_grad)
    if linked:
        small, *large = sums
        shares = unpack_gradients(large, *unpack_small(small))
    else:
        shares = sum_gradients(*totals)
    return (jnp.stack(losses), jnp.stack(acts_of), jnp.stack(embed_grads), *shares)


def solution(mesh):
    return jax.shard_map(
        per_device,
        mesh=mesh,
        in_specs=(
            P(("grp", "dev"), None, None),
            P(("grp", "dev"), None),
            P(("grp", "dev")),
            P(("grp", "dev"), None, None),
            P(("grp", "dev"), None, None, None),
            P(("grp", "dev"), None, None),
            P("dev"),
            P("dev", None),
            P("dev", None),
            P("dev"),
            P("dev", None),
            P("dev", None),
            P("dev"),
            P("dev", None),
            P("dev", None),
            P("dev"),
            P("dev", None),
            P("dev", None),
            P("dev"),
            P(None, "dev"),
            P("dev", None),
            P("dev", None),
            P("dev", None),
            P("dev", None),
            P("dev", None),
        ),
        out_specs=(
            P(("grp", "dev")),
            P(("grp", "dev"), None, None),
            P(("grp", "dev"), None, None),
            P("dev"),
            P("dev", None),
            P("dev", None),
            P("dev"),
            P("dev", None),
            P("dev", None),
            P("dev"),
            P("dev", None),
            P("dev", None),
            P("dev"),
            P("dev", None),
            P("dev", None),
            P("dev"),
            P(None, "dev"),
            P("dev", None),
            P("dev", None),
            P("dev", None),
            P("dev", None),
            P("dev", None),
        ),
        check_vma=False,
    )
```
